32 devices in a mesh: section: 2 (over y), batch: 16 (over z, x, core).
Axes of the slice: x: 2, y: 2, z: 4, core: 2. Of those that a mesh axis runs over, the one named last changes fastest.
Arguments:
- inputs: bfloat16 [2, 32, 256, 768], P('section', 'batch'), may hold values from -6 to 6
- cotangent: bfloat16 [2, 32, 256, 768], P('section', 'batch'), may hold values from -6 to 6
- segments: int32 [2, 32, 256], P(None, 'batch'), may hold values from 0 to 3, never falling along the last dimension, each value on 1 to 128 neighbouring positions
- buckets: int32 [511], replicated, may hold values from 0 to 31
- qkv_weight: bfloat16 [2, 768, 2304], P('section'), may hold values from -0.21875 to 0.21875
- out_weight: bfloat16 [2, 768, 768], P('section'), may hold values from -0.875 to 0.875
- in_weight: bfloat16 [2, 768, 3072], P('section'), may hold values from -0.21875 to 0.21875
- down_weight: bfloat16 [2, 3072, 768], P('section'), may hold values from -0.109375 to 0.109375
- cross_first: bfloat16 [2, 768, 768], P('section'), may hold values from -0.21875 to 0.21875
- cross_second: bfloat16 [2, 768, 768], P('section'), may hold values from -0.625 to 0.625
- vectors: float32 [2, 7, 768], P('section'), may hold values from -1.2 to 1.5, as said below
- ffn_bias: float32 [2, 3072], P('section'), may hold values from -3 to 3
- position_table: float32 [2, 32, 12], P('section'), may hold values from -4 to 4
Outputs:
- outputs: bfloat16 [2, 32, 256, 768], P('section', 'batch')
- input_grad: float32 [2, 32, 256, 768], P('section', 'batch')
- qkv_grad: float32 [2, 768, 2304], P('section', 'batch')
- out_grad: float32 [2, 768, 768], P('section', 'batch')
- in_grad: float32 [2, 768, 3072], P('section', 'batch')
- down_grad: float32 [2, 3072, 768], P('section', 'batch')
- cross_first_grad: float32 [2, 768, 768], P('section', 'batch')
- cross_second_grad: float32 [2, 768, 768], P('section', 'batch')
- vectors_grad: float32 [2, 7, 768], P('section', None, 'batch')
- ffn_bias_grad: float32 [2, 3072], P('section', 'batch')
- table_grad: float32 [2, 32, 12], P('section')
The draws below stay inside these ranges and needn't reach their ends.
Inputs may be any that keep to these rules, and one draw needn't show every extreme that they name: `segments`: each row numbers its packed sentences 0 to 3 in order, every sentence 1 to 128 tokens long and one exactly 128. `vectors`: gains lie in 0.5 to 1.5.
All inputs are finite; a program needn't handle non-finite values.
Results may differ from the reference program's by a relative error of at most 0.022.
Values may be sent and summed in bfloat16 or wider, within the bound.
No kernel may reach another device: no remote copies, remote signals or barrier semaphores. Data moves between devices by JAX's collectives and lax.ppermute only.
A program may use at most 512 MiB of HBM per device.

```python
import math
import jax
import jax.numpy as jnp
import numpy as np
from jax import lax

D = 768
H = 12
FF = 3072
NB = 32
S = 256
SEGS = 4
SEG_MOST = 128
ROWS_DEV = 2
ROWS = 32
N_BATCH = 16


def draw_vectors(key, part):
    key = jax.random.fold_in(key, 7)
    first_key, second_key = jax.random.split(key)
    gains = jax.random.uniform(first_key, (2, 7, D), jnp.float32, 0.5, 1.5)
    offsets = jnp.clip(0.3 * jax.random.normal(second_key, (2, 7, D), jnp.float32), -1.2, 1.2)
    row_index = jnp.arange(7)
    gain_rows = (row_index % 2 == 0) & (row_index < 6)
    return jnp.where(gain_rows[None, :, None], gains, offsets)


def set_ends(drawn, own_key, low, largest):
    index_at = [jax.random.randint(jax.random.fold_in(own_key, axis), (), 0, length) for axis, length in enumerate(drawn.shape)]
    main_axis = drawn.shape.index(max(drawn.shape))
    next_to = index_at[:main_axis] + [(index_at[main_axis] + 1) % drawn.shape[main_axis]] + index_at[main_axis + 1:]
    return drawn.at[tuple(index_at)].set(low).at[tuple(next_to)].set(largest)


def levels(own_key, dims, pieces, smallest, high):
    def one(axis_at, shards_of):
        draws = jax.random.uniform(jax.random.fold_in(jax.random.fold_in(own_key, 6), axis_at), (shards_of,), jnp.float32, smallest / len(pieces), high / len(pieces))
        return jnp.repeat(jnp.exp(draws), dims[axis_at] // shards_of).reshape((-1,) + (1,) * (len(dims) - axis_at - 1))

    factor_of = one(*pieces[0])
    for cut in pieces[1:]:
        factor_of = factor_of * one(*cut)
    return factor_of


def length_profile(number_of, total, reach, skew):
    loads = [(1 << 20) // math.isqrt(grade ** skew) + 1 for grade in range(2, number_of + 1)]
    rest, counts = total - reach - (number_of - 1), [1] * (number_of - 1)
    while rest > 0:
        movable = [i for i in range(number_of - 1) if counts[i] < reach]
        pool, remaining = sum([loads[i] for i in movable]), rest
        for i in movable:
            addition = min(reach - counts[i], max(1, remaining * loads[i] // pool), rest)
            counts[i] = counts[i] + addition
            rest = rest - addition
    return np.array([reach] + counts)


def uneven(key, amount, total, reach, lean):
    if amount == 2:
        one = jax.random.randint(key, (), max(1, total - reach), min(reach, total - 1) + 1)
        return jnp.stack([one, total - one])
    tallies = jnp.asarray(length_profile(amount, total, reach, lean), jnp.int32)
    twos = (amount - 1) // 2
    giver, receiver = tallies[1:1 + 2 * twos:2], tallies[2:2 + 2 * twos:2]
    room = jnp.minimum(giver - 1, reach - receiver)
    moved = jax.random.randint(jax.random.fold_in(key, 1), (twos,), 0, 1 << 20) % (room + 1)
    tallies = tallies.at[1:1 + 2 * twos:2].set(giver - moved).at[2:2 + 2 * twos:2].set(receiver + moved)
    return tallies[jax.random.permutation(jax.random.fold_in(key, 2), amount)]


def noise(rng, dims, scale, most, pieces=(), dtype=jnp.bfloat16):
    values = jax.random.normal(rng, dims, jnp.float32) * scale
    if len(pieces) > 0:
        values = levels(rng, dims, pieces, -0.22, 0.18) * values
    return jnp.clip(values, min=-most, max=most).astype(dtype)


def setup_inputs(seed: int = 0) -> dict:
    splits = jax.random.split(jax.random.key(seed), 14)
    inputs = noise(splits[0], (2, ROWS, S, D), 1.0, 6.0, ((0, 2), (1, 16)))
    cotangent = noise(splits[1], (2, ROWS, S, D), 1.0, 6.0, ((0, 2), (1, 16)))
    segments = jax.vmap(lambda own: jnp.searchsorted(jnp.cumsum(uneven(own, SEGS, S, SEG_MOST, 2)), jnp.arange(S), side="right"))(jax.random.split(splits[2], 2 * ROWS)).reshape((2, ROWS, S)).astype(jnp.int32)
    buckets = set_ends(jax.random.randint(splits[3], (2 * S - 1,), 0, NB), jax.random.fold_in(splits[3], 1), 0, NB - 1).astype(jnp.int32)
    qkv_weight = noise(splits[4], (2, D, 3 * D), D ** -0.5, 0.21875, ((0, 2),))
    out_weight = noise(splits[5], (2, D, D), (D // 16) ** -0.5, 0.875, ((0, 2),))
    in_weight = noise(splits[6], (2, D, FF), D ** -0.5, 0.21875, ((0, 2),))
    down_weight = noise(splits[7], (2, FF, D), FF ** -0.5, 0.109375, ((0, 2),))
    cross_first = noise(splits[8], (2, D, D), D ** -0.5, 0.21875, ((0, 2),))
    cross_second = noise(splits[9], (2, D, D), (D // 8) ** -0.5, 0.625, ((0, 2),))
    vectors = draw_vectors(jax.random.fold_in(splits[13], 71), 0)
    ffn_bias = noise(splits[11], (2, FF), 0.5, 3.0, ((0, 2),), jnp.float32)
    position_table = noise(splits[12], (2, NB, H), 1.0, 4.0, ((0, 2),), jnp.float32)
    return {"inputs": inputs, "cotangent": cotangent, "segments": segments, "buckets": buckets, "qkv_weight": qkv_weight, "out_weight": out_weight, "in_weight": in_weight, "down_weight": down_weight, "cross_first": cross_first, "cross_second": cross_second, "vectors": vectors, "ffn_bias": ffn_bias, "position_table": position_table}


@jax.custom_vjp
def low(v):
    return lax.optimization_barrier(v.astype(jnp.bfloat16)).astype(jnp.float32)

@jax.custom_vjp
def low_back(v):
    return v

def low_keep(v):
    return (low(v), None)

def low_pass(kept, grad):
    return (grad,)

def back_keep(v):
    return (v, None)

def back_low(kept, grad):
    return (low(grad),)
low.defvjp(low_keep, low_pass)
low_back.defvjp(back_keep, back_low)
norm_epsilon = 1e-05
masked_score = -1e+30
highest = lax.Precision.HIGHEST

def layer_norm(values, norm_gain, offset):
    centre = values - lax.optimization_barrier(jnp.mean(values, axis=-1, keepdims=True))
    spread = lax.optimization_barrier(jnp.mean(centre * centre, axis=-1, keepdims=True))
    return centre * lax.rsqrt(spread + norm_epsilon) * norm_gain + offset

def dense(left_side, weight):
    return jnp.einsum('rsd,de->rse', left_side, weight, precision=highest)

def attention(queries, key_rows, values, position_bias, allowed):
    batch_rows, length, model_width = queries.shape
    head_size = model_width // H
    query_heads = queries.reshape(batch_rows, length, H, head_size)
    key_heads = key_rows.reshape(batch_rows, key_rows.shape[1], H, head_size)
    value_heads = values.reshape(batch_rows, values.shape[1], H, head_size)
    raw_scores = low_back(jnp.einsum('rqhd,rkhd->rhqk', query_heads, key_heads, precision=highest))
    scores = raw_scores * head_size ** (-0.5) + position_bias
    scores = jnp.where(allowed[:, None], scores, masked_score)
    weights = jax.nn.softmax(scores, axis=-1)
    context = jnp.einsum('rhqk,rkhd->rqhd', low(weights), value_heads, precision=highest)
    return context.reshape(batch_rows, length, model_width)

def self_part(residual, qkv_matrix, out_matrix, norm_gain, norm_offset, position_bias, allowed):
    model_width = residual.shape[2]
    normed = low(layer_norm(residual, norm_gain, norm_offset))
    projected = dense(normed, qkv_matrix)
    queries = low_back(low(projected[..., :model_width]))
    key_rows = low_back(low(projected[..., model_width:2 * model_width]))
    values = low_back(low(projected[..., 2 * model_width:]))
    context = low_back(low(attention(queries, key_rows, values, position_bias, allowed)))
    return residual + low_back(dense(context, out_matrix))

def ffn_part(residual, in_matrix, in_bias, down_matrix, down_bias, norm_gain, norm_offset):
    normed = low(layer_norm(residual, norm_gain, norm_offset))
    hidden = low_back(dense(normed, in_matrix) + in_bias)
    activated = low(jax.nn.gelu(hidden, approximate=False))
    return residual + low_back(dense(activated, down_matrix) + down_bias)

def pair_forward(params, enc_rows, dec_rows, enc_ids, dec_ids, enc_bias, dec_bias):
    qkv_all = params[0]
    out_all = params[1]
    in_all = params[2]
    down_all = params[3]
    first_all = params[4]
    second_all = params[5]
    vector_all = params[6]
    fbias_all = params[7]
    enc_allowed = enc_ids[:, :, None] == enc_ids[:, None, :]
    positions = jnp.arange(S)
    causal = positions[:, None] >= positions[None, :]
    dec_allowed = (dec_ids[:, :, None] == dec_ids[:, None, :]) & causal[None]
    cross_allowed = dec_ids[:, :, None] == enc_ids[:, None, :]
    enc_first = self_part(enc_rows, qkv_all[0], out_all[0], vector_all[0, 0], vector_all[0, 1], enc_bias, enc_allowed)
    enc_second = ffn_part(enc_first, in_all[0], fbias_all[0], down_all[0], vector_all[0, 6], vector_all[0, 2], vector_all[0, 3])
    memory = layer_norm(enc_second, vector_all[0, 4], vector_all[0, 5])
    memory_low = low(memory)
    cross_keys = low_back(low(dense(memory_low, first_all[0])))
    cross_values = low_back(low(dense(memory_low, second_all[0])))
    dec_first = self_part(dec_rows, qkv_all[1], out_all[1], vector_all[1, 0], vector_all[1, 1], dec_bias, dec_allowed)
    cross_normed = low(layer_norm(dec_first, vector_all[1, 2], vector_all[1, 3]))
    cross_queries = low_back(low(dense(cross_normed, first_all[1])))
    cross_context = low_back(low(attention(cross_queries, cross_keys, cross_values, 0.0, cross_allowed)))
    dec_second = dec_first + low_back(dense(cross_context, second_all[1]))
    decoded = ffn_part(dec_second, in_all[1], fbias_all[1], down_all[1], vector_all[1, 6], vector_all[1, 4], vector_all[1, 5])
    return (memory, decoded)

def reference(inputs, cotangent, segments, buckets, qkv_weight, out_weight, in_weight, down_weight, cross_first, cross_second, vectors, ffn_bias, position_table):
    total_rows = ROWS_DEV * N_BATCH
    block_rows = math.gcd(total_rows, 16)
    block_count = total_rows // block_rows
    offsets = jnp.arange(S)[None, :] - jnp.arange(S)[:, None] + (S - 1)
    bucket_grid = buckets[offsets]
    one_hot = (bucket_grid[:, :, None] == jnp.arange(NB)[None, None, :]).astype(jnp.float32)
    params = (qkv_weight.astype(jnp.float32), out_weight.astype(jnp.float32), in_weight.astype(jnp.float32), down_weight.astype(jnp.float32), cross_first.astype(jnp.float32), cross_second.astype(jnp.float32), vectors.astype(jnp.float32), ffn_bias.astype(jnp.float32), position_table.astype(jnp.float32))
    enc_ids = segments[0].reshape(block_count, block_rows, S)
    dec_ids = segments[1].reshape(block_count, block_rows, S)

    def forward(weights, stacked):
        enc_bias = jnp.einsum('ijb,bh->hij', one_hot, weights[8][0], precision=highest)
        dec_bias = jnp.einsum('ijb,bh->hij', one_hot, weights[8][1], precision=highest)

        def run_block(item):
            return pair_forward(weights, item[0], item[1], item[2], item[3], enc_bias, dec_bias)
        memory, decoded = lax.map(jax.checkpoint(run_block), (stacked[0].reshape(block_count, block_rows, S, D), stacked[1].reshape(block_count, block_rows, S, D), enc_ids, dec_ids))
        return jnp.stack([memory.reshape(total_rows, S, D), decoded.reshape(total_rows, S, D)])
    result, pullback = jax.vjp(forward, params, inputs.astype(jnp.float32))
    param_grads, input_grad = pullback(cotangent.astype(jnp.float32))
    return (result.astype(jnp.bfloat16), input_grad, param_grads[0], param_grads[1], param_grads[2], param_grads[3], param_grads[4], param_grads[5], param_grads[6], param_grads[7], param_grads[8])
```

```python
import jax
import jax.numpy as jnp
from jax import lax
from jax.sharding import PartitionSpec as P

MICRO = 1


norm_epsilon = 1e-05
masked_score = -1e30


def passed_along(shard, axis, by):
    devices = lax.axis_size(axis)
    pairs = [(i, i + by) for i in range(devices) if 0 <= i + by < devices]
    return lax.ppermute(shard, axis, pairs)


def spread_offsets(offset_rows, length):
    heads = offset_rows.shape[0]
    turned = jnp.concatenate(
        [offset_rows[:, length - 1 :], jnp.zeros((heads, 1)), offset_rows[:, : length - 1]], axis=1
    )
    period = 2 * length
    tiled = jnp.broadcast_to(turned[:, None, :], (heads, length, period))
    flat = tiled.reshape(heads, length * period)[:, : length * (period - 1)]
    return flat.reshape(heads, length, period - 1)[:, :, :length]


def sum_offsets(grid):
    heads, length = grid.shape[0], grid.shape[1]
    period = 2 * length
    padded = jnp.pad(grid, ((0, 0), (0, 0), (0, length - 1)))
    flat = jnp.pad(padded.reshape(heads, length * (period - 1)), ((0, 0), (0, length)))
    turned = jnp.sum(flat.reshape(heads, length, period), axis=1)
    return jnp.concatenate([turned[:, length + 1 :], turned[:, :length]], axis=1)


def layer_norm(values, norm_gain, offset):
    centre = values - jnp.mean(values, axis=-1, keepdims=True)
    spread = jnp.mean(centre * centre, axis=-1, keepdims=True)
    return centre * lax.rsqrt(spread + norm_epsilon) * norm_gain + offset


def gelu_exact(values):
    return jax.nn.gelu(values, approximate=False)


def project(left_side, weight):
    return jnp.einsum("rsd,de->rse", left_side, weight, preferred_element_type=jnp.float32)


def project_back(grad_side, weight):
    return jnp.einsum("rse,de->rsd", grad_side, weight, preferred_element_type=jnp.float32)


def weight_grad(left_side, grad_side):
    return jnp.einsum("rsd,rse->de", left_side, grad_side, preferred_element_type=jnp.float32)


def scattered(total):
    low = lax.psum_scatter(total.astype(jnp.bfloat16), "batch", scatter_dimension=0, tiled=True)
    return low.astype(jnp.float32)


def split_heads(array, heads):
    return array.reshape(array.shape[0], array.shape[1], heads, array.shape[2] // heads)


def score_block(queries, key_rows, position_bias, allowed, heads):
    query_heads = split_heads(queries, heads)
    key_heads = split_heads(key_rows, heads)
    scale = query_heads.shape[3] ** (-0.5)
    raw_scores = jnp.einsum(
        "rqhd,rkhd->rhqk", query_heads, key_heads, preferred_element_type=jnp.float32
    )
    scores = raw_scores * scale + position_bias
    return (jnp.where(allowed[:, None], scores, masked_score), scale)


def attend(queries, key_rows, values, position_bias, allowed, heads):
    scores, scale = score_block(queries, key_rows, position_bias, allowed, heads)
    row_max = jnp.max(scores, axis=-1, keepdims=True)
    exponent = jnp.exp(scores - row_max)
    denominator = jnp.sum(exponent, axis=-1, keepdims=True)
    weights = exponent / denominator
    log_total = row_max + jnp.log(denominator)
    context = jnp.einsum(
        "rhqk,rkhd->rqhd",
        weights.astype(jnp.bfloat16),
        split_heads(values, heads),
        preferred_element_type=jnp.float32,
    )
    return (context.reshape(queries.shape), log_total)


def attend_back(grad_context, queries, key_rows, values, log_total, position_bias, allowed, heads):
    scores, scale = score_block(queries, key_rows, position_bias, allowed, heads)
    weights = jnp.exp(scores - log_total)
    grad_heads = split_heads(grad_context, heads)
    grad_weights = jnp.einsum(
        "rqhd,rkhd->rhqk",
        grad_heads,
        split_heads(values, heads),
        preferred_element_type=jnp.float32,
    )
    centred = jnp.sum(grad_weights * weights, axis=-1, keepdims=True)
    grad_scores = weights * (grad_weights - centred)
    grad_raw = (grad_scores * scale).astype(jnp.bfloat16)
    grad_queries = jnp.einsum(
        "rhqk,rkhd->rqhd",
        grad_raw,
        split_heads(key_rows, heads),
        preferred_element_type=jnp.float32,
    ).reshape(queries.shape)
    grad_keys = jnp.einsum(
        "rhqk,rqhd->rkhd", grad_raw, split_heads(queries, heads), preferred_element_type=jnp.float32
    ).reshape(key_rows.shape)
    grad_values = jnp.einsum(
        "rhqk,rqhd->rkhd",
        weights.astype(jnp.bfloat16),
        grad_heads,
        preferred_element_type=jnp.float32,
    ).reshape(values.shape)
    return (grad_queries, grad_keys, grad_values, jnp.sum(grad_scores, axis=0))


def self_forward(
    residual, qkv_matrix, out_matrix, norm_gain, norm_offset, position_bias, allowed, heads
):
    model_width = residual.shape[2]
    normed = layer_norm(residual, norm_gain, norm_offset).astype(jnp.bfloat16)
    projected = project(normed, qkv_matrix)
    queries = projected[..., :model_width].astype(jnp.bfloat16)
    key_rows = projected[..., model_width : 2 * model_width].astype(jnp.bfloat16)
    values = projected[..., 2 * model_width :].astype(jnp.bfloat16)
    context, log_total = attend(queries, key_rows, values, position_bias, allowed, heads)
    context_low = context.astype(jnp.bfloat16)
    updated = residual + project(context_low, out_matrix)
    return (updated, (residual, normed, queries, key_rows, values, log_total, context_low))


def self_backward(
    grad_out, saved, qkv_matrix, out_matrix, norm_gain, norm_offset, position_bias, allowed, heads
):
    residual, normed, queries, key_rows, values, log_total, context_low = saved
    grad_branch = grad_out.astype(jnp.bfloat16)
    out_grad = weight_grad(context_low, grad_branch)
    grad_context = project_back(grad_branch, out_matrix).astype(jnp.bfloat16)
    grad_queries, grad_keys, grad_values, bias_grad = attend_back(
        grad_context, queries, key_rows, values, log_total, position_bias, allowed, heads
    )
    grad_projected = jnp.concatenate(
        [
            grad_queries.astype(jnp.bfloat16),
            grad_keys.astype(jnp.bfloat16),
            grad_values.astype(jnp.bfloat16),
        ],
        axis=-1,
    )
    qkv_grad = weight_grad(normed, grad_projected)
    grad_normed = project_back(grad_projected, qkv_matrix)
    grad_residual, gain_grad, offset_grad = jax.vjp(layer_norm, residual, norm_gain, norm_offset)[
        1
    ](grad_normed)
    return (grad_out + grad_residual, qkv_grad, out_grad, gain_grad, offset_grad, bias_grad)


def feed_forward(residual, in_matrix, in_bias, down_matrix, down_bias, norm_gain, norm_offset):
    normed = layer_norm(residual, norm_gain, norm_offset).astype(jnp.bfloat16)
    hidden = project(normed, in_matrix) + in_bias
    activated = gelu_exact(hidden).astype(jnp.bfloat16)
    updated = residual + (project(activated, down_matrix) + down_bias)
    return (updated, (residual, normed, hidden, activated))


def feed_backward(grad_out, saved, in_matrix, down_matrix, norm_gain, norm_offset):
    residual, normed, hidden, activated = saved
    grad_branch = grad_out.astype(jnp.bfloat16)
    down_grad = weight_grad(activated, grad_branch)
    down_bias_grad = jnp.sum(grad_branch, axis=(0, 1), dtype=jnp.float32)
    grad_activated = project_back(grad_branch, down_matrix)
    grad_hidden = jax.vjp(gelu_exact, hidden)[1](grad_activated)[0].astype(jnp.bfloat16)
    in_bias_grad = jnp.sum(grad_hidden, axis=(0, 1), dtype=jnp.float32)
    in_grad = weight_grad(normed, grad_hidden)
    grad_normed = project_back(grad_hidden, in_matrix)
    grad_residual, gain_grad, offset_grad = jax.vjp(layer_norm, residual, norm_gain, norm_offset)[
        1
    ](grad_normed)
    return (
        grad_out + grad_residual,
        in_grad,
        in_bias_grad,
        down_grad,
        down_bias_grad,
        gain_grad,
        offset_grad,
    )


def encoder_forward(enc_rows, weights, position_bias, enc_ids, heads):
    (
        qkv_matrix,
        out_matrix,
        in_matrix,
        down_matrix,
        first_matrix,
        second_matrix,
        vector_rows,
        in_bias,
    ) = weights
    allowed = enc_ids[:, :, None] == enc_ids[:, None, :]
    residual = enc_rows.astype(jnp.float32)
    attended, saved_attention = self_forward(
        residual,
        qkv_matrix,
        out_matrix,
        vector_rows[0],
        vector_rows[1],
        position_bias,
        allowed,
        heads,
    )
    mixed, saved_feed = feed_forward(
        attended, in_matrix, in_bias, down_matrix, vector_rows[6], vector_rows[2], vector_rows[3]
    )
    memory = layer_norm(mixed, vector_rows[4], vector_rows[5])
    memory_low = memory.astype(jnp.bfloat16)
    key_rows = project(memory_low, first_matrix).astype(jnp.bfloat16)
    value_rows = project(memory_low, second_matrix).astype(jnp.bfloat16)
    return (memory, key_rows, value_rows, (saved_attention, saved_feed, mixed, memory_low))


def encoder_backward(
    cotangent_rows, grad_keys, grad_values, saved, weights, position_bias, enc_ids, heads
):
    (
        qkv_matrix,
        out_matrix,
        in_matrix,
        down_matrix,
        first_matrix,
        second_matrix,
        vector_rows,
        in_bias,
    ) = weights
    allowed = enc_ids[:, :, None] == enc_ids[:, None, :]
    saved_attention, saved_feed, mixed, memory_low = saved
    first_grad = weight_grad(memory_low, grad_keys)
    second_grad = weight_grad(memory_low, grad_values)
    grad_memory = (
        project_back(grad_keys, first_matrix)
        + project_back(grad_values, second_matrix)
        + cotangent_rows.astype(jnp.float32)
    )
    grad_mixed, final_gain, final_offset = jax.vjp(
        layer_norm, mixed, vector_rows[4], vector_rows[5]
    )[1](grad_memory)
    grad_attended, in_grad, in_bias_grad, down_grad, down_bias_grad, feed_gain, feed_offset = (
        feed_backward(
            grad_mixed, saved_feed, in_matrix, down_matrix, vector_rows[2], vector_rows[3]
        )
    )
    grad_input, qkv_grad, out_grad, self_gain, self_offset, bias_grad = self_backward(
        grad_attended,
        saved_attention,
        qkv_matrix,
        out_matrix,
        vector_rows[0],
        vector_rows[1],
        position_bias,
        allowed,
        heads,
    )
    vector_grad = jnp.stack(
        [self_gain, self_offset, feed_gain, feed_offset, final_gain, final_offset, down_bias_grad]
    )
    return (
        grad_input,
        (
            qkv_grad,
            out_grad,
            in_grad,
            down_grad,
            first_grad,
            second_grad,
            vector_grad,
            in_bias_grad,
        ),
        bias_grad,
    )


def decoder_step(
    dec_rows, cotangent_rows, key_rows, value_rows, weights, position_bias, dec_ids, enc_ids, heads
):
    (
        qkv_matrix,
        out_matrix,
        in_matrix,
        down_matrix,
        first_matrix,
        second_matrix,
        vector_rows,
        in_bias,
    ) = weights
    positions = jnp.arange(dec_rows.shape[1])
    causal = positions[:, None] >= positions[None, :]
    allowed = (dec_ids[:, :, None] == dec_ids[:, None, :]) & causal[None]
    cross_allowed = dec_ids[:, :, None] == enc_ids[:, None, :]
    residual = dec_rows.astype(jnp.float32)
    attended, saved_attention = self_forward(
        residual,
        qkv_matrix,
        out_matrix,
        vector_rows[0],
        vector_rows[1],
        position_bias,
        allowed,
        heads,
    )
    cross_normed = layer_norm(attended, vector_rows[2], vector_rows[3]).astype(jnp.bfloat16)
    cross_queries = project(cross_normed, first_matrix).astype(jnp.bfloat16)
    cross_context, cross_total = attend(
        cross_queries, key_rows, value_rows, 0.0, cross_allowed, heads
    )
    context_low = cross_context.astype(jnp.bfloat16)
    crossed = attended + project(context_low, second_matrix)
    decoded, saved_feed = feed_forward(
        crossed, in_matrix, in_bias, down_matrix, vector_rows[6], vector_rows[4], vector_rows[5]
    )
    grad_crossed, in_grad, in_bias_grad, down_grad, down_bias_grad, feed_gain, feed_offset = (
        feed_backward(
            cotangent_rows.astype(jnp.float32),
            saved_feed,
            in_matrix,
            down_matrix,
            vector_rows[4],
            vector_rows[5],
        )
    )
    grad_branch = grad_crossed.astype(jnp.bfloat16)
    second_grad = weight_grad(context_low, grad_branch)
    grad_context = project_back(grad_branch, second_matrix).astype(jnp.bfloat16)
    grad_queries, grad_keys, grad_values, unused_bias = attend_back(
        grad_context, cross_queries, key_rows, value_rows, cross_total, 0.0, cross_allowed, heads
    )
    grad_queries_low = grad_queries.astype(jnp.bfloat16)
    first_grad = weight_grad(cross_normed, grad_queries_low)
    grad_normed = project_back(grad_queries_low, first_matrix)
    grad_part, cross_gain, cross_offset = jax.vjp(
        layer_norm, attended, vector_rows[2], vector_rows[3]
    )[1](grad_normed)
    grad_attended = grad_crossed + grad_part
    grad_input, qkv_grad, out_grad, self_gain, self_offset, bias_grad = self_backward(
        grad_attended,
        saved_attention,
        qkv_matrix,
        out_matrix,
        vector_rows[0],
        vector_rows[1],
        position_bias,
        allowed,
        heads,
    )
    vector_grad = jnp.stack(
        [self_gain, self_offset, cross_gain, cross_offset, feed_gain, feed_offset, down_bias_grad]
    )
    grads = (
        qkv_grad,
        out_grad,
        in_grad,
        down_grad,
        first_grad,
        second_grad,
        vector_grad,
        in_bias_grad,
    )
    return (
        decoded,
        grad_input,
        grads,
        bias_grad,
        grad_keys.astype(jnp.bfloat16),
        grad_values.astype(jnp.bfloat16),
    )


def spare_branch(function):

    def zeros_only(*operands):
        return jax.tree.map(jnp.zeros_like, function(*operands))

    return zeros_only


def per_device(
    inputs,
    cotangent,
    segments,
    buckets,
    qkv_weight,
    out_weight,
    in_weight,
    down_weight,
    cross_first,
    cross_second,
    vectors,
    ffn_bias,
    position_table,
):
    heads = position_table.shape[2]
    length = inputs.shape[2]
    bucket_count = position_table.shape[1]
    on_encoder = lax.axis_index("section") == 0
    one_hot = (buckets[:, None] == jnp.arange(bucket_count)[None, :]).astype(jnp.float32)
    offset_bias = jnp.einsum(
        "ob,bh->ho", one_hot, position_table[0], precision=lax.Precision.HIGHEST
    )
    position_bias = spread_offsets(offset_bias, length)
    weights = (
        qkv_weight[0],
        out_weight[0],
        in_weight[0],
        down_weight[0],
        cross_first[0],
        cross_second[0],
        vectors[0],
        ffn_bias[0],
    )
    per_micro = inputs.shape[1] // MICRO

    def encode_rows(rows_part, enc_part):
        return encoder_forward(rows_part, weights, position_bias, enc_part, heads)

    def decode_rows(rows_part, cotangent_part, key_part, value_part, dec_part, enc_part):
        return decoder_step(
            rows_part,
            cotangent_part,
            key_part,
            value_part,
            weights,
            position_bias,
            dec_part,
            enc_part,
            heads,
        )

    def encode_back(cotangent_part, key_part, value_part, saved, enc_part):
        return encoder_backward(
            cotangent_part, key_part, value_part, saved, weights, position_bias, enc_part, heads
        )

    def pieces(micro):
        first_row = micro * per_micro
        return (
            inputs[0, first_row : first_row + per_micro],
            cotangent[0, first_row : first_row + per_micro],
            segments[0, first_row : first_row + per_micro],
            segments[1, first_row : first_row + per_micro],
        )

    def run_decoder(micro, got_keys, got_values):
        rows_part, cotangent_part, enc_part, dec_part = pieces(micro)
        return lax.cond(
            on_encoder,
            spare_branch(decode_rows),
            decode_rows,
            rows_part,
            cotangent_part,
            got_keys,
            got_values,
            dec_part,
            enc_part,
        )

    def run_backward(micro, ret_keys, ret_values, saved):
        rows_part, cotangent_part, enc_part, dec_part = pieces(micro)
        return lax.cond(
            on_encoder,
            encode_back,
            spare_branch(encode_back),
            cotangent_part,
            ret_keys,
            ret_values,
            saved,
            enc_part,
        )

    memories = [None] * MICRO
    decodes = [None] * MICRO
    enc_grads = [None] * MICRO
    dec_grads = [None] * MICRO
    enc_sets = [None] * MICRO
    dec_sets = [None] * MICRO
    enc_biases = [None] * MICRO
    dec_biases = [None] * MICRO
    kept = [None] * MICRO
    summed = None
    table_grad = jnp.zeros(position_table.shape[1:], jnp.float32)
    sent_rows = None
    sent_grads = None
    for tick in range(MICRO + 2):
        fresh_rows = None
        fresh_grads = None
        if tick < MICRO:
            run_rows_part, run_cotangent_part, run_enc_part, run_dec_part = pieces(tick)
            memory, key_rows, value_rows, saved = lax.cond(
                on_encoder, encode_rows, spare_branch(encode_rows), run_rows_part, run_enc_part
            )
            memories[tick] = memory
            kept[tick] = saved
            fresh_rows = (key_rows, value_rows)
        if tick >= 2:
            earlier = tick - 2
            enc_grads[earlier], enc_sets[earlier], enc_biases[earlier] = run_backward(
                earlier, sent_grads[0], sent_grads[1], kept[earlier]
            )
        if 1 <= tick <= MICRO:
            former = tick - 1
            decoded, dec_grad, dec_weights, dec_bias, back_keys, back_values = run_decoder(
                former, sent_rows[0], sent_rows[1]
            )
            decodes[former] = decoded
            dec_grads[former] = dec_grad
            dec_sets[former] = dec_weights
            dec_biases[former] = dec_bias
            fresh_grads = (back_keys, back_values)
        if fresh_rows is not None:
            sent_rows = passed_along((fresh_rows[0], fresh_rows[1]), "section", 1)
        if fresh_grads is not None:
            sent_grads = passed_along((fresh_grads[0], fresh_grads[1]), "section", -1)
        if tick >= 2:
            finish_micro = tick - 2
            finish_summed = summed
            finish_table_grad = table_grad
            micro_grads = jax.tree.map(jnp.add, enc_sets[finish_micro], dec_sets[finish_micro])
            finish_table_grad = finish_table_grad + jnp.einsum(
                "ho,ob->bh",
                sum_offsets(enc_biases[finish_micro] + dec_biases[finish_micro]),
                one_hot,
                precision=lax.Precision.HIGHEST,
            )
            finish_summed = (
                micro_grads
                if finish_summed is None
                else jax.tree.map(jnp.add, finish_summed, micro_grads)
            )
            summed = finish_summed
            table_grad = finish_table_grad
    summed = (
        scattered(summed[0]),
        scattered(summed[1]),
        scattered(summed[2]),
        scattered(summed[3]),
        scattered(summed[4]),
        scattered(summed[5]),
        lax.psum_scatter(summed[6], "batch", scatter_dimension=1, tiled=True),
        lax.psum_scatter(summed[7], "batch", scatter_dimension=0, tiled=True),
    )
    table_total = lax.psum(table_grad, "batch")
    output_parts = [
        (memories[micro] + decodes[micro]).astype(jnp.bfloat16) for micro in range(MICRO)
    ]
    grad_parts = [enc_grads[micro] + dec_grads[micro] for micro in range(MICRO)]
    return (
        jnp.concatenate(output_parts, axis=0)[None],
        jnp.concatenate(grad_parts, axis=0)[None],
        summed[0][None],
        summed[1][None],
        summed[2][None],
        summed[3][None],
        summed[4][None],
        summed[5][None],
        summed[6][None],
        summed[7][None],
        table_total[None],
    )


def solution(mesh):
    return jax.shard_map(
        per_device,
        mesh=mesh,
        in_specs=(
            P("section", "batch", None, None),
            P("section", "batch", None, None),
            P(None, "batch", None),
            P(),
            P("section", None, None),
            P("section", None, None),
            P("section", None, None),
            P("section", None, None),
            P("section", None, None),
            P("section", None, None),
            P("section", None, None),
            P("section", None),
            P("section", None, None),
        ),
        out_specs=(
            P("section", "batch", None, None),
            P("section", "batch", None, None),
            P("section", "batch", None),
            P("section", "batch", None),
            P("section", "batch", None),
            P("section", "batch", None),
            P("section", "batch", None),
            P("section", "batch", None),
            P("section", None, "batch"),
            P("section", "batch"),
            P("section", None, None),
        ),
        check_vma=False,
    )
```

```python
import functools

import jax
import jax.numpy as jnp
from jax import lax
from jax.experimental import pallas as pl
from jax.experimental.pallas import tpu as pltpu
from jax.sharding import PartitionSpec as P

norm_epsilon = 1e-05
masked_score = -1e30
half_root = 0.7071067811865476
density_scale = 0.3989422804014327
tile = 256
chunk = 64
vmem_bytes = 62 * 1024 * 1024

f32 = jnp.float32
bf16 = jnp.bfloat16
ANY = pl.BlockSpec(memory_space=pl.ANY)
SMEM = pl.BlockSpec(memory_space=pltpu.SMEM)
VMEM = pl.BlockSpec(memory_space=pltpu.VMEM)


def mm(left, right):
    return jnp.dot(left, right, preferred_element_type=f32)


def mm_nt(left, right):
    return lax.dot_general(left, right, (((1,), (1,)), ((), ())), preferred_element_type=f32)


def mm_tn(left, right):
    return lax.dot_general(left, right, (((0,), (0,)), ((), ())), preferred_element_type=f32)


def mean_of(values):
    return jnp.sum(values, axis=-1, keepdims=True) * (1.0 / values.shape[-1])


def normalised(values):
    centre = values - mean_of(values)
    rate = lax.rsqrt(mean_of(centre * centre) + norm_epsilon)
    return centre * rate, rate


def each_rows(count, body):
    @pl.loop(0, count // chunk)
    def _(step):
        body(pl.ds(pl.multiple_of(step * chunk, chunk), chunk))


def each_tile(count, body, width=tile):
    @pl.loop(0, count // width)
    def _(step):
        body(pl.ds(pl.multiple_of(step * width, width), width))


def norm_forward(source, gain, offset, target, also=None):
    def rows(at):
        unit, _ = normalised(source[at, :].astype(f32))
        normed = unit * gain + offset
        target[at, :] = normed.astype(target.dtype)

    each_rows(source.shape[0], rows)


def norm_backward(source, grad_normed, gain, upstream, target, gain_sum, offset_sum):
    gain_sum[...] = jnp.zeros_like(gain_sum)
    offset_sum[...] = jnp.zeros_like(offset_sum)

    def rows(at):
        unit, rate = normalised(source[at, :].astype(f32))
        upper = grad_normed[at, :]
        product = upper * unit
        gain_sum[...] += jnp.sum(product.reshape(-1, 8, product.shape[1]), axis=0)
        offset_sum[...] += jnp.sum(upper.reshape(-1, 8, upper.shape[1]), axis=0)
        scaled = upper * gain
        inner = mean_of(scaled)
        along = mean_of(product * gain)
        result = rate * (scaled - inner - unit * along)
        if upstream is not None:
            result = result + upstream[at, :].astype(f32)
        target[at, :] = result

    each_rows(source.shape[0], rows)


def column_sum(partial):
    return jnp.sum(partial[...], axis=0, keepdims=True)


def lower_lanes(shape):
    return lax.broadcasted_iota(jnp.int32, shape, 1) < shape[1] // 2


def split_pair(block):
    lower = lower_lanes(block.shape)
    zero = jnp.zeros_like(block)
    return jnp.concatenate([jnp.where(lower, block, zero), jnp.where(lower, zero, block)], axis=0)


def join_pair(stacked):
    rows = stacked.shape[0] // 2
    lower = lower_lanes((rows, stacked.shape[1]))
    return jnp.where(lower, stacked[:rows], stacked[rows:])


def attend_pair(queries, key_rows, values, additions, scale):
    length = queries.shape[0]
    scores = mm_nt(queries, split_pair(key_rows)) * scale
    parts = []
    for head in range(2):
        part = scores[:, head * length : (head + 1) * length] + additions[head]
        exponent = jnp.exp(part - jnp.max(part, axis=-1, keepdims=True))
        parts.append(exponent * (1.0 / jnp.sum(exponent, axis=-1, keepdims=True)))
    weights = jnp.concatenate(parts, axis=1).astype(bf16)
    return weights, mm(weights, split_pair(values))


def attend_pair_back(weights, queries, key_rows, values, grad_context, scale):
    length = queries.shape[0]
    grad_weights = mm_nt(grad_context, split_pair(values))
    parts = []
    for head in range(2):
        at = slice(head * length, (head + 1) * length)
        weight = weights[:, at].astype(f32)
        grad_weight = grad_weights[:, at]
        centred = jnp.sum(grad_weight * weight, axis=-1, keepdims=True)
        parts.append(weight * (grad_weight - centred))
    grad_raw = (jnp.concatenate(parts, axis=1) * scale).astype(bf16)
    grad_queries = mm(grad_raw, split_pair(key_rows))
    grad_keys = join_pair(mm_tn(grad_raw, queries))
    grad_values = join_pair(mm_tn(weights, grad_context))
    return grad_queries, grad_keys, grad_values, parts


def same_sentence(query_ids, key_ids):
    length = query_ids.shape[1]
    across = jnp.broadcast_to(key_ids.astype(f32), (length, length))
    down = jnp.broadcast_to(query_ids.astype(f32), (length, length)).T
    return across == down


class Mover:
    def __init__(self, semaphores):
        self.semaphores = semaphores
        self.used = 0

    def start(self, source, target):
        copy = pltpu.make_async_copy(source, target, self.semaphores.at[self.used])
        self.used += 1
        copy.start()
        return copy


def wait_all(copies):
    for copy in copies:
        copy.wait()


def gelu_parts(hidden):
    share = 0.5 + 0.5 * lax.erf(hidden * half_root)
    slope = share + hidden * (density_scale * jnp.exp(hidden * hidden * -0.5))
    return hidden * share, slope


def first_body(
    heads, flag, ids, turned, table, vectors, in_bias, rows_in, cot_in, qkv_in, out_in, ffn_in,
    down_in, first_in,
    x1_out, h1_out, qkv_out, weights_out, context_out, h2_out, u_out, slope_out, e2_out, low_out,
    hc_out, qc_out,
    rows, qkv_w, out_w, ffn_w, down_w, first_w, cot, normed, qkv, weights, context, x1, h2, u, slope,
    e2, low, bias_rows, mask, loads, stores,
):
    width = rows.shape[1]
    hidden_width = ffn_w.shape[1]
    row_count, length = ids.shape[1], ids.shape[2]
    on_encoder = flag[0] == 1
    load = Mover(loads)
    store = Mover(stores)
    got_rows = load.start(rows_in, rows)
    got_qkv = load.start(qkv_in, qkv_w)
    got_out = load.start(out_in, out_w)

    one_hot = (turned[...] == lax.broadcasted_iota(jnp.int32, (table.shape[0], 2 * length), 0)).astype(f32)
    bias_rows[...] = lax.dot_general(
        table[...], one_hot, (((0,), (0,)), ((), ())), precision=lax.Precision.HIGHEST,
        preferred_element_type=f32,
    )
    own_group = jnp.where(on_encoder, 0, 1)
    ahead = lax.broadcasted_iota(jnp.int32, (length, length), 0) >= lax.broadcasted_iota(
        jnp.int32, (length, length), 1
    )
    for row in range(row_count):
        own = ids[pl.ds(own_group, 1), row, :]
        allowed = same_sentence(own, own) & (ahead | on_encoder)
        mask[row] = jnp.where(allowed, 0.0, masked_score)

    got_rows.wait()
    norm_forward(rows, vectors[0:1, :], vectors[1:2, :], normed)
    got_qkv.wait()

    def project(at):
        qkv[:, at] = mm(normed[...], qkv_w[:, at]).astype(bf16)

    each_tile(3 * width, project)
    out_copies = [store.start(normed, h1_out), store.start(qkv, qkv_out)]
    scale = (width // heads) ** (-0.5)

    @pl.loop(0, heads // 2)
    def _(pair):
        lanes = pl.multiple_of(pair * 128, 128)
        biases = []
        for head in range(2):
            spread = jnp.broadcast_to(bias_rows[pl.ds(pair * 2 + head, 1), :], (length, 2 * length))
            skewed = pltpu.roll(spread, 0, 1, stride=1, stride_axis=0)
            biases.append(skewed[:, :length])
        for row in range(row_count):
            at = slice(row * length, (row + 1) * length)
            additions = [bias + mask[row] for bias in biases]
            part, mixed = attend_pair(
                qkv[at, pl.ds(lanes, 128)],
                qkv[at, pl.ds(width + lanes, 128)],
                qkv[at, pl.ds(2 * width + lanes, 128)],
                additions,
                scale,
            )
            weights[row, pair] = part
            context[at, pl.ds(lanes, 128)] = mixed.astype(bf16)

    out_copies += [store.start(weights, weights_out), store.start(context, context_out)]
    got_out.wait()

    def mix(at):
        x1[:, at] = rows[:, at].astype(f32) + mm(context[...], out_w[:, at])

    each_tile(width, mix)
    out_copies.append(store.start(x1, x1_out))

    @pl.when(on_encoder)
    def _():
        got_ffn = load.start(ffn_in, ffn_w)
        got_down = load.start(down_in, down_w)
        norm_forward(x1, vectors[2:3, :], vectors[3:4, :], h2)
        got_ffn.wait()

        def feed(at):
            value, rate = gelu_parts(mm(h2[...], ffn_w[:, at]) + in_bias[:, at])
            u[:, at] = value.astype(bf16)
            slope[:, at] = rate.astype(bf16)

        each_tile(hidden_width, feed)
        copies = [store.start(h2, h2_out), store.start(u, u_out), store.start(slope, slope_out)]
        got_down.wait()

        def down(at):
            e2[:, at] = x1[:, at] + (mm(u[...], down_w[:, at]) + vectors[6:7, at])

        each_tile(width, down)
        copies.append(store.start(e2, e2_out))
        norm_forward(e2, vectors[4:5, :], vectors[5:6, :], low)
        copies.append(store.start(low, low_out))
        wait_all(copies)

    @pl.when(jnp.logical_not(on_encoder))
    def _():
        got_down = load.start(down_in, down_w)
        got_first = load.start(first_in, first_w)
        got_cot = load.start(cot_in, cot)
        norm_forward(x1, vectors[2:3, :], vectors[3:4, :], h2)
        got_first.wait()

        def query(at):
            low[:, at] = mm(h2[...], first_w[:, at]).astype(bf16)

        each_tile(width, query)
        copies = [store.start(h2, hc_out), store.start(low, qc_out)]
        got_down.wait()
        got_cot.wait()

        def back(at):
            slope[:, at] = mm_nt(cot[...], down_w[at, :]).astype(bf16)

        each_tile(hidden_width, back)
        copies.append(store.start(slope, slope_out))
        wait_all(copies)

    wait_all(out_copies)


def cross_body(
    heads, flag, ids, vectors, in_bias, vec_in,
    memory_in, half_in, other_in, second_in, x1_in, qc_in, cot_in, ffn_in, h2_in, u_in, slope_in,
    vec_out, h2_out, u_out, slope_out, d2_out, grad_out, cc_out, dq_out, dk_out, dv_out, dm_out,
    memory, keys_w, values_w, second_w, x1, qc, cot, ffn_w, keys, values, weights, cc, d2, h2, u,
    slope, grad_normed, grad, grad_low, dq, dk, dv, dm, mask, gain_sum, offset_sum, loads, stores,
):
    width = memory.shape[1]
    hidden_width = ffn_w.shape[1]
    half = width // 2
    row_count, length = ids.shape[1], ids.shape[2]
    vec_out[...] = vec_in[...]

    @pl.when(flag[0] == 0)
    def _():
        load = Mover(loads)
        store = Mover(stores)
        core = flag[1]
        own_at = pl.ds(pl.multiple_of(core * half, half), half)
        other_at = pl.ds(pl.multiple_of((1 - core) * half, half), half)
        got_keys = [
            load.start(half_in.at[0], keys_w.at[own_at]),
            load.start(other_in.at[0], keys_w.at[other_at]),
            load.start(memory_in, memory),
        ]
        got_values = [
            load.start(half_in.at[1], values_w.at[own_at]),
            load.start(other_in.at[1], values_w.at[other_at]),
        ]
        got_query = load.start(qc_in, qc)
        got_second = [load.start(second_in, second_w), load.start(x1_in, x1)]
        got_ffn = [load.start(ffn_in, ffn_w), load.start(slope_in, slope)]
        got_cot = load.start(cot_in, cot)
        for row in range(row_count):
            mask[row] = jnp.where(
                same_sentence(ids[1:2, row, :], ids[0:1, row, :]), 0.0, masked_score
            )
        wait_all(got_keys)

        def project_keys(at):
            keys[:, at] = mm(memory[...], keys_w[:, at]).astype(bf16)

        each_tile(width, project_keys)
        wait_all(got_values)

        def project_values(at):
            values[:, at] = mm(memory[...], values_w[:, at]).astype(bf16)

        each_tile(width, project_values)
        got_query.wait()
        scale = (width // heads) ** (-0.5)

        @pl.loop(0, heads // 2)
        def _(pair):
            lanes = pl.ds(pl.multiple_of(pair * 128, 128), 128)
            for row in range(row_count):
                at = slice(row * length, (row + 1) * length)
                part, mixed = attend_pair(
                    qc[at, lanes], keys[at, lanes], values[at, lanes], [mask[row], mask[row]], scale
                )
                weights[row, pair] = part
                cc[at, lanes] = mixed.astype(bf16)

        copies = [store.start(cc, cc_out)]
        wait_all(got_second)

        def mix(at):
            d2[:, at] = x1[:, at] + mm(cc[...], second_w[:, at])

        each_tile(width, mix)
        copies.append(store.start(d2, d2_out))
        norm_forward(d2, vectors[4:5, :], vectors[5:6, :], h2)
        copies.append(store.start(h2, h2_out))
        wait_all(got_ffn)

        def feed(at):
            value, rate = gelu_parts(mm(h2[...], ffn_w[:, at]) + in_bias[:, at])
            u[:, at] = value.astype(bf16)
            slope[:, at] = (slope[:, at].astype(f32) * rate).astype(bf16)

        each_tile(hidden_width, feed)
        copies += [store.start(u, u_out), store.start(slope, slope_out)]

        def back(at):
            grad_normed[:, at] = mm_nt(slope[...], ffn_w[at, :])

        each_tile(width, back)
        got_cot.wait()
        norm_backward(d2, grad_normed, vectors[4:5, :], cot, grad, gain_sum, offset_sum)
        vec_out[4:5, :] = column_sum(gain_sum)
        vec_out[5:6, :] = column_sum(offset_sum)
        copies.append(store.start(grad, grad_out))

        def lower(at):
            grad_low[at, :] = grad[at, :].astype(bf16)

        each_rows(grad.shape[0], lower)

        def back_context(at):
            dm[:, at] = mm_nt(grad_low[...], second_w[at, :]).astype(bf16)

        each_tile(width, back_context)

        @pl.loop(0, heads // 2)
        def _(pair):
            lanes = pl.ds(pl.multiple_of(pair * 128, 128), 128)
            for row in range(row_count):
                at = slice(row * length, (row + 1) * length)
                grad_q, grad_k, grad_v, _ = attend_pair_back(
                    weights[row, pair], qc[at, lanes], keys[at, lanes], values[at, lanes],
                    dm[at, lanes], scale,
                )
                dq[at, lanes] = grad_q.astype(bf16)
                dk[at, lanes] = grad_k.astype(bf16)
                dv[at, lanes] = grad_v.astype(bf16)

        copies += [store.start(dq, dq_out), store.start(dk, dk_out), store.start(dv, dv_out)]

        def back_memory(at):
            dm[:, at] = (mm_nt(dk[...], keys_w[at, :]) + mm_nt(dv[...], values_w[at, :])).astype(bf16)

        each_tile(width, back_memory)
        copies.append(store.start(dm, dm_out))
        wait_all(copies)


def decoder_grads_body(
    flag, vectors, vec_in, fbias_in,
    u_in, slope_in, h2_in, cot_in, d2_in, down_in, cc_in, grad_in, hc_in, dq_in, memory_in, dk_in,
    dv_in, low_in,
    vec_out, fbias_out, low_out, down_out, ffn_out, cross_out,
    u, slope, h2, cot, d2, down_w, cc, grad, hc, dq, memory, dk, dv, low, down_g, ffn_g, cross_g,
    loads, stores,
):
    width = cot.shape[1]
    hidden_width = u.shape[1]
    vec_out[...] = vec_in[...]
    fbias_out[...] = fbias_in[...]

    @pl.when(flag[0] == 0)
    def _():
        load = Mover(loads)
        store = Mover(stores)
        got_down = [load.start(u_in, u), load.start(cot_in, cot)]
        got_ffn = [load.start(slope_in, slope), load.start(h2_in, h2)]
        got_cross = [
            load.start(hc_in, hc),
            load.start(dq_in, dq),
            load.start(cc_in, cc),
            load.start(grad_in, grad),
            load.start(memory_in, memory),
            load.start(dk_in, dk),
            load.start(dv_in, dv),
        ]
        got_out = [load.start(d2_in, d2), load.start(down_in, down_w)]
        wait_all(got_down)

        def down_grad(at):
            down_g[at, :] = mm_tn(u[:, at], cot[...]).astype(bf16)

        each_tile(hidden_width, down_grad)
        copies = [store.start(down_g, down_out)]
        vec_out[6:7, :] = jnp.sum(cot[...].astype(f32), axis=0, keepdims=True)
        wait_all(got_ffn)

        def ffn_grad(at):
            ffn_g[:, at] = mm_tn(h2[...], slope[:, at]).astype(bf16)
            fbias_out[:, at] = jnp.sum(slope[:, at].astype(f32), axis=0, keepdims=True)

        each_tile(hidden_width, ffn_grad)
        copies.append(store.start(ffn_g, ffn_out))
        wait_all(got_cross)

        def cross_grad(at):
            cross_g[0, :, at] = mm_tn(hc[...], dq[:, at]).astype(bf16)
            cross_g[1, :, at] = mm_tn(cc[...], grad[:, at].astype(bf16)).astype(bf16)
            cross_g[2, :, at] = mm_tn(memory[...], dk[:, at]).astype(bf16)
            cross_g[3, :, at] = mm_tn(memory[...], dv[:, at]).astype(bf16)

        each_tile(width, cross_grad)
        copies.append(store.start(cross_g, cross_out))
        wait_all(got_out)

        def down(at):
            value = d2[:, at] + (mm(u[...], down_w[:, at]) + vectors[6:7, at])
            low[:, at] = value.astype(bf16)

        each_tile(width, down)
        copies.append(store.start(low, low_out))
        wait_all(copies)


def encoder_down_body(
    flag, vectors, vec_in, dm_in, cot_in, e2_in, u_in, down_in,
    vec_out, grad_out, down_out,
    dm, cot, e2, u, grad, grad_low, down_g, gain_sum, offset_sum, loads, stores,
):
    hidden_width = u.shape[1]
    vec_out[...] = vec_in[...]

    @pl.when(flag[0] == 1)
    def _():
        load = Mover(loads)
        store = Mover(stores)
        got = [load.start(dm_in, dm), load.start(cot_in, cot), load.start(e2_in, e2)]
        got_u = load.start(u_in, u)
        wait_all(got)

        def total(at):
            grad[at, :] = dm[at, :].astype(f32) + cot[at, :].astype(f32)

        each_rows(grad.shape[0], total)
        norm_backward(e2, grad, vectors[4:5, :], None, grad, gain_sum, offset_sum)
        vec_out[4:5, :] = column_sum(gain_sum)
        vec_out[5:6, :] = column_sum(offset_sum)
        copies = [store.start(grad, grad_out)]

        def lower(at):
            grad_low[at, :] = grad[at, :].astype(bf16)

        each_rows(grad.shape[0], lower)
        vec_out[6:7, :] = jnp.sum(grad_low[...].astype(f32), axis=0, keepdims=True)
        got_u.wait()

        def down_grad(at):
            down_g[at, :] = mm_tn(u[:, at], grad_low[...]).astype(bf16)

        each_tile(hidden_width, down_grad)
        copies.append(store.start(down_g, down_out))
        wait_all(copies)


def encoder_ffn_body(
    flag, fbias_in, grad_in, down_in, slope_in, h2_in, ffn_old,
    fbias_out, slope_out, ffn_out,
    grad, grad_low, down_w, slope, h2, ffn_g, loads, stores,
):
    hidden_width = slope.shape[1]
    fbias_out[...] = fbias_in[...]

    @pl.when(flag[0] == 1)
    def _():
        load = Mover(loads)
        store = Mover(stores)
        got_grad = load.start(grad_in, grad)
        got = [load.start(down_in, down_w), load.start(slope_in, slope), load.start(h2_in, h2)]
        got_grad.wait()

        def lower(at):
            grad_low[at, :] = grad[at, :].astype(bf16)

        each_rows(grad.shape[0], lower)
        wait_all(got)

        def back(at):
            part = mm_nt(grad_low[...], down_w[at, :]) * slope[:, at].astype(f32)
            part = part.astype(bf16)
            slope[:, at] = part
            fbias_out[:, at] = jnp.sum(part.astype(f32), axis=0, keepdims=True)
            ffn_g[:, at] = mm_tn(h2[...], part).astype(bf16)

        each_tile(hidden_width, back)
        copies = [store.start(slope, slope_out), store.start(ffn_g, ffn_out)]
        wait_all(copies)


def tail_body(
    heads, wanted, flag, turned, vectors, vec_in, table_in,
    grad_in, part_in, matrix_in, x1_in, h1_in, qkv_in, weights_in, context_in, rows_in, qkvw_in,
    outw_in, result_in, out_old, qkv_old,
    vec_out, table_out, result_out, out_out, qkv_out,
    grad, part, matrix, x1, h1, qkv, weights, context, rows, qkv_w, out_w, grad_normed, grad_low,
    grad_context, grad_qkv, out_g, qkv_g, diagonals, gain_sum, offset_sum, loads, stores,
):
    width = x1.shape[1]
    row_count, length = weights.shape[0], weights.shape[2]
    vec_out[...] = vec_in[...]
    table_out[...] = table_in[...]

    @pl.when(flag[0] == wanted)
    def _():
        load = Mover(loads)
        store = Mover(stores)
        got_part = [load.start(part_in, part), load.start(matrix_in, matrix)]
        got_x1 = [load.start(x1_in, x1), load.start(grad_in, grad)]
        got_context = [load.start(context_in, context), load.start(outw_in, out_w)]
        got_attention = [load.start(weights_in, weights), load.start(qkv_in, qkv)]
        got_rest = [load.start(h1_in, h1), load.start(qkvw_in, qkv_w), load.start(rows_in, rows)]
        wait_all(got_part)

        def back(at):
            grad_normed[:, at] = mm_nt(part[...], matrix[at, :])

        each_tile(width, back)
        wait_all(got_x1)
        norm_backward(x1, grad_normed, vectors[2:3, :], grad, grad, gain_sum, offset_sum)
        vec_out[2:3, :] = column_sum(gain_sum)
        vec_out[3:4, :] = column_sum(offset_sum)

        def lower(at):
            grad_low[at, :] = grad[at, :].astype(bf16)

        each_rows(grad.shape[0], lower)
        wait_all(got_context)

        def back_out(at):
            grad_context[:, at] = mm_nt(grad_low[...], out_w[at, :]).astype(bf16)
            out_g[:, at] = mm_tn(context[...], grad_low[:, at]).astype(bf16)

        each_tile(width, back_out)
        copies = [store.start(out_g, out_out)]
        wait_all(got_attention)
        scale = (width // heads) ** (-0.5)

        @pl.loop(0, heads // 2)
        def _(pair):
            lanes = pl.multiple_of(pair * 128, 128)
            totals = [None, None]
            for row in range(row_count):
                at = slice(row * length, (row + 1) * length)
                grad_q, grad_k, grad_v, parts = attend_pair_back(
                    weights[row, pair],
                    qkv[at, pl.ds(lanes, 128)],
                    qkv[at, pl.ds(width + lanes, 128)],
                    qkv[at, pl.ds(2 * width + lanes, 128)],
                    grad_context[at, pl.ds(lanes, 128)],
                    scale,
                )
                grad_qkv[at, pl.ds(lanes, 128)] = grad_q.astype(bf16)
                grad_qkv[at, pl.ds(width + lanes, 128)] = grad_k.astype(bf16)
                grad_qkv[at, pl.ds(2 * width + lanes, 128)] = grad_v.astype(bf16)
                totals = [p if t is None else t + p for t, p in zip(totals, parts)]
            for head in range(2):
                padded = jnp.concatenate([totals[head], jnp.zeros((length, length), f32)], axis=1)
                folded = padded[0:8, :]
                for block in range(1, length // 8):
                    folded = folded + pltpu.roll(
                        padded[block * 8 : (block + 1) * 8, :], 2 * length - block * 8, 1
                    )
                line = folded[0:1, :]
                for sub in range(1, 8):
                    line = line + pltpu.roll(folded[sub : sub + 1, :], 2 * length - sub, 1)
                diagonals[pl.ds(pair * 2 + head, 1), :] = line

        one_hot = (
            turned[...] == lax.broadcasted_iota(jnp.int32, (table_out.shape[0], 2 * length), 0)
        ).astype(f32)
        table_out[...] = lax.dot_general(
            one_hot, diagonals[...], (((1,), (1,)), ((), ())), precision=lax.Precision.HIGHEST,
            preferred_element_type=f32,
        )
        wait_all(got_rest)

        def qkv_grad(at):
            qkv_g[:, at] = mm_tn(h1[...], grad_qkv[:, at]).astype(bf16)

        each_tile(3 * width, qkv_grad)
        copies.append(store.start(qkv_g, qkv_out))

        def back_normed(at):
            grad_normed[:, at] = mm_nt(grad_qkv[...], qkv_w[at, :])

        each_tile(width, back_normed)
        norm_backward(rows, grad_normed, vectors[0:1, :], grad, grad, gain_sum, offset_sum)
        vec_out[0:1, :] = column_sum(gain_sum)
        vec_out[1:2, :] = column_sum(offset_sum)
        copies.append(store.start(grad, result_out))
        wait_all(copies)


def shape_of(dims, dtype):
    return jax.ShapeDtypeStruct(tuple(dims), dtype)


def run_kernel(body, operands, places, outs, out_places, scratch, loads, stores, aliases, flops, name):
    return pl.pallas_call(
        body,
        in_specs=places,
        out_specs=out_places,
        out_shape=outs,
        scratch_shapes=[pltpu.VMEM(dims, dtype) for dims, dtype in scratch]
        + [pltpu.SemaphoreType.DMA((loads,)), pltpu.SemaphoreType.DMA((stores,))],
        input_output_aliases=aliases,
        compiler_params=pltpu.CompilerParams(vmem_limit_bytes=vmem_bytes),
        cost_estimate=pl.CostEstimate(flops=flops, bytes_accessed=flops // 400, transcendentals=0),
        name=name,
    )(*operands)


def scattered(total):
    low = lax.psum_scatter(total, "batch", scatter_dimension=0, tiled=True)
    return low.astype(f32)


def per_device(
    inputs, cotangent, segments, buckets, qkv_weight, out_weight, in_weight, down_weight,
    cross_first, cross_second, vectors, ffn_bias, position_table,
):
    row_count, length, width = inputs.shape[1:]
    heads = position_table.shape[2]
    bucket_count = position_table.shape[1]
    hidden = in_weight.shape[2]
    tokens = row_count * length
    pairs = heads // 2
    on_encoder = lax.axis_index("section") == 0
    place = lax.axis_index("batch")
    core = lax.rem(place, 2)
    devices = lax.axis_size("batch")
    flag = jnp.stack([on_encoder.astype(jnp.int32), core])
    turned = jnp.concatenate(
        [buckets[length - 1 :], jnp.full((1,), -1, jnp.int32), buckets[: length - 1]]
    )[None]
    rows = inputs.reshape(tokens, width)
    cot = cotangent.reshape(tokens, width)
    qkv_w, out_w, ffn_w, down_w = qkv_weight[0], out_weight[0], in_weight[0], down_weight[0]
    first_w, second_w = cross_first[0], cross_second[0]
    vec = jnp.concatenate([vectors[0], jnp.zeros((1, width), f32)])
    fbias = ffn_bias

    tw, th = (tokens, width), (tokens, hidden)
    wide = (tokens, 3 * width)
    square = (row_count, pairs, length, 2 * length)
    token_flops = 2 * tokens * width * width

    half = width // 2
    own_half = jnp.stack(
        [
            lax.dynamic_slice_in_dim(first_w, core * half, half),
            lax.dynamic_slice_in_dim(second_w, core * half, half),
        ]
    )
    half_sent = lax.ppermute(own_half, "section", [(0, 1)])
    half_other = lax.ppermute(half_sent, "batch", [(i, i ^ 1) for i in range(devices)])

    first_outs = [
        shape_of(tw, f32), shape_of(tw, bf16), shape_of(wide, bf16), shape_of(square, bf16),
        shape_of(tw, bf16), shape_of(tw, bf16), shape_of(th, bf16), shape_of(th, bf16),
        shape_of(tw, f32), shape_of(tw, bf16), shape_of(tw, bf16), shape_of(tw, bf16),
    ]
    x1, h1, qkv, weights, context, h2, u, slope, e2, low, hc, qc = run_kernel(
        functools.partial(first_body, heads),
        (flag, segments, turned, position_table[0], vec, fbias, rows, cot, qkv_w, out_w, ffn_w,
         down_w, first_w),
        [SMEM] + [VMEM] * 5 + [ANY] * 7,
        first_outs,
        [ANY] * 12,
        [
            (tw, bf16), ((width, 3 * width), bf16), ((width, width), bf16), ((width, hidden), bf16),
            ((hidden, width), bf16), ((width, width), bf16), (tw, bf16), (tw, bf16), (wide, bf16),
            (square, bf16), (tw, bf16), (tw, f32), (tw, bf16), (th, bf16), (th, bf16), (tw, f32),
            (tw, bf16), ((heads, 2 * length), f32), ((row_count, length, length), f32),
        ],
        8, 13, {}, 12 * token_flops, "first",
    )

    memory = lax.ppermute(low, "section", [(0, 1)])

    vec_grad = jnp.zeros((8, width), f32)
    fbias_grad = jnp.zeros((1, hidden), f32)
    table_grad = jnp.zeros((bucket_count, heads), f32)
    vec_grad, h2, u, slope, d2, grad, cc, dq, dk, dv, dm = run_kernel(
        functools.partial(cross_body, heads),
        (flag, segments, vec, fbias, vec_grad, memory, half_sent, half_other, second_w, x1, qc, cot,
         ffn_w, h2, u, slope),
        [SMEM] + [VMEM] * 4 + [ANY] * 11,
        [shape_of((8, width), f32), shape_of(tw, bf16), shape_of(th, bf16), shape_of(th, bf16),
         shape_of(tw, f32), shape_of(tw, f32)] + [shape_of(tw, bf16)] * 5,
        [VMEM] + [ANY] * 10,
        [
            (tw, bf16), ((width, width), bf16), ((width, width), bf16), ((width, width), bf16),
            (tw, f32), (tw, bf16), (tw, bf16), ((width, hidden), bf16), (tw, bf16), (tw, bf16),
            (square, bf16), (tw, bf16), (tw, f32), (tw, bf16), (th, bf16), (th, bf16), (tw, f32),
            (tw, f32), (tw, bf16), (tw, bf16), (tw, bf16), (tw, bf16), (tw, bf16),
            ((row_count, length, length), f32), ((8, width), f32), ((8, width), f32),
        ],
        11, 10, {4: 0, 13: 1, 14: 2, 15: 3}, 16 * token_flops, "cross",
    )

    returned = lax.ppermute(dm, "section", [(1, 0)])

    vec_grad, fbias_grad, low, down_g, ffn_g, cross_g = run_kernel(
        decoder_grads_body,
        (flag, vec, vec_grad, fbias_grad, u, slope, h2, cot, d2, down_w, cc, grad, hc, dq, memory,
         dk, dv, low),
        [SMEM] + [VMEM] * 3 + [ANY] * 14,
        [shape_of((8, width), f32), shape_of((1, hidden), f32), shape_of(tw, bf16),
         shape_of((hidden, width), bf16), shape_of((width, hidden), bf16),
         shape_of((4, width, width), bf16)],
        [VMEM, VMEM] + [ANY] * 4,
        [
            (th, bf16), (th, bf16), (tw, bf16), (tw, bf16), (tw, f32), ((hidden, width), bf16),
            (tw, bf16), (tw, f32), (tw, bf16), (tw, bf16), (tw, bf16), (tw, bf16), (tw, bf16),
            (tw, bf16), ((hidden, width), bf16), ((width, hidden), bf16),
            ((4, width, width), bf16),
        ],
        13, 4, {2: 0, 3: 1, 17: 2}, 16 * token_flops, "decoder_grads",
    )

    def tail(wanted, vec_grad, table_grad, grad, part, matrix, result, out_g, qkv_g, name):
        olds = () if result is None else (result, out_g, qkv_g)
        body = functools.partial(tail_body, heads, wanted)
        if result is None:

            def body(*refs):
                return tail_body(heads, wanted, *refs[:16], None, None, None, *refs[16:])

        depth = part.shape[1]
        return run_kernel(
            body,
            (flag, turned, vec, vec_grad, table_grad, grad, part, matrix, x1, h1, qkv, weights,
             context, rows, qkv_w, out_w) + olds,
            [SMEM] + [VMEM] * 4 + [ANY] * (11 + len(olds)),
            [shape_of((8, width), f32), shape_of((bucket_count, heads), f32), shape_of(tw, f32),
             shape_of((width, width), bf16), shape_of((width, 3 * width), bf16)],
            [VMEM, VMEM] + [ANY] * 3,
            [
                (tw, f32), ((tokens, depth), bf16), ((width, depth), bf16), (tw, f32), (tw, bf16),
                (wide, bf16), (square, bf16), (tw, bf16), (tw, bf16), ((width, 3 * width), bf16),
                ((width, width), bf16), (tw, f32), (tw, bf16), (tw, bf16), (wide, bf16),
                ((width, width), bf16), ((width, 3 * width), bf16), ((heads, 2 * length), f32),
                ((8, width), f32), ((8, width), f32),
            ],
            11, 3, {3: 0, 4: 1} | ({16: 2, 17: 3, 18: 4} if olds else {}), 16 * token_flops, name,
        )

    vec_grad, table_grad, result, out_g, qkv_g = tail(
        0, vec_grad, table_grad, grad, dq, first_w, None, None, None, "decoder_tail"
    )

    vec_grad, enc_grad, down_g = run_kernel(
        encoder_down_body,
        (flag, vec, vec_grad, returned, cot, e2, u, down_g),
        [SMEM] + [VMEM] * 2 + [ANY] * 5,
        [shape_of((8, width), f32), shape_of(tw, f32), shape_of((hidden, width), bf16)],
        [VMEM, ANY, ANY],
        [
            (tw, bf16), (tw, bf16), (tw, f32), (th, bf16), (tw, f32), (tw, bf16),
            ((hidden, width), bf16), ((8, width), f32), ((8, width), f32),
        ],
        4, 2, {2: 0, 7: 2}, 4 * token_flops, "encoder_down",
    )
    down_share = scattered(down_g)
    fbias_grad, slope, ffn_g = run_kernel(
        encoder_ffn_body,
        (flag, fbias_grad, enc_grad, down_w, slope, h2, ffn_g),
        [SMEM, VMEM] + [ANY] * 5,
        [shape_of((1, hidden), f32), shape_of(th, bf16), shape_of((width, hidden), bf16)],
        [VMEM, ANY, ANY],
        [
            (tw, f32), (tw, bf16), ((hidden, width), bf16), (th, bf16), (tw, bf16),
            ((width, hidden), bf16),
        ],
        4, 2, {1: 0, 4: 1, 6: 2}, 8 * token_flops, "encoder_ffn",
    )
    ffn_share = scattered(ffn_g)
    vec_grad, table_grad, result, out_g, qkv_g = tail(
        1, vec_grad, table_grad, enc_grad, slope, ffn_w, result, out_g, qkv_g, "encoder_tail"
    )
    out_share = scattered(out_g)
    qkv_share = scattered(qkv_g)
    cross_shares = lax.psum_scatter(cross_g, "batch", scatter_dimension=1, tiled=True)
    back_shares = lax.ppermute(cross_shares[2:], "section", [(1, 0)])
    cross_share = jnp.where(on_encoder, back_shares, cross_shares[:2]).astype(f32)
    vec_share = lax.psum_scatter(vec_grad[:7], "batch", scatter_dimension=1, tiled=True)
    fbias_share = lax.psum_scatter(fbias_grad, "batch", scatter_dimension=1, tiled=True)
    table_total = lax.psum(table_grad, "batch")
    return (
        low.reshape((1, row_count, length, width)),
        result.reshape((1, row_count, length, width)),
        qkv_share[None],
        out_share[None],
        ffn_share[None],
        down_share[None],
        cross_share[0][None],
        cross_share[1][None],
        vec_share[None],
        fbias_share,
        table_total[None],
    )


def solution(mesh):
    return jax.shard_map(
        per_device,
        mesh=mesh,
        in_specs=(
            P("section", "batch", None, None),
            P("section", "batch", None, None),
            P(None, "batch", None),
            P(),
            P("section", None, None),
            P("section", None, None),
            P("section", None, None),
            P("section", None, None),
            P("section", None, None),
            P("section", None, None),
            P("section", None, None),
            P("section", None),
            P("section", None, None),
        ),
        out_specs=(
            P("section", "batch", None, None),
            P("section", "batch", None, None),
            P("section", "batch", None),
            P("section", "batch", None),
            P("section", "batch", None),
            P("section", "batch", None),
            P("section", "batch", None),
            P("section", "batch", None),
            P("section", None, "batch"),
            P("section", "batch"),
            P("section", None, None),
        ),
        check_vma=False,
    )
```

```python
import functools

import jax
import jax.numpy as jnp
from jax import lax
from jax.experimental import pallas as pl
from jax.experimental.pallas import tpu as pltpu
from jax.sharding import PartitionSpec as P

norm_epsilon = 1e-05
masked_score = -1e30
half_root = 0.7071067811865476
density_scale = 0.3989422804014327
tile = 768
chunk = 64
spare_bytes = 8 * 1024 * 1024
all_bytes = 62 * 1024 * 1024

f32 = jnp.float32
bf16 = jnp.bfloat16
ANY = pl.BlockSpec(memory_space=pl.ANY)
SMEM = pl.BlockSpec(memory_space=pltpu.SMEM)
VMEM = pl.BlockSpec(memory_space=pltpu.VMEM)


def mm(left, right):
    return jnp.dot(left, right, preferred_element_type=f32)


def mm_nt(left, right):
    return lax.dot_general(left, right, (((1,), (1,)), ((), ())), preferred_element_type=f32)


def mm_tn(left, right):
    return lax.dot_general(left, right, (((0,), (0,)), ((), ())), preferred_element_type=f32)


def mean_of(values):
    return jnp.sum(values, axis=-1, keepdims=True) * (1.0 / values.shape[-1])


def normalised(values):
    centre = values - mean_of(values)
    rate = lax.rsqrt(mean_of(centre * centre) + norm_epsilon)
    return centre * rate, rate


def each_rows(count, body):
    @pl.loop(0, count // chunk)
    def _(step):
        body(pl.ds(pl.multiple_of(step * chunk, chunk), chunk))


def each_tile(count, body, width=tile):
    if count == width:
        body(pl.ds(0, width))
        return

    @pl.loop(0, count // width)
    def _(step):
        body(pl.ds(pl.multiple_of(step * width, width), width))


def norm_forward(source, gain, offset, target, also=None):
    def rows(at):
        unit, _ = normalised(source[at, :].astype(f32))
        normed = unit * gain + offset
        target[at, :] = normed.astype(target.dtype)

    each_rows(source.shape[0], rows)


def norm_backward(source, grad_normed, gain, upstream, target, gain_sum, offset_sum):
    gain_sum[...] = jnp.zeros_like(gain_sum)
    offset_sum[...] = jnp.zeros_like(offset_sum)

    def rows(at):
        unit, rate = normalised(source[at, :].astype(f32))
        upper = grad_normed[at, :]
        product = upper * unit
        gain_sum[...] += jnp.sum(product.reshape(-1, 8, product.shape[1]), axis=0)
        offset_sum[...] += jnp.sum(upper.reshape(-1, 8, upper.shape[1]), axis=0)
        scaled = upper * gain
        inner = mean_of(scaled)
        along = mean_of(product * gain)
        result = rate * (scaled - inner - unit * along)
        if upstream is not None:
            result = result + upstream[at, :].astype(f32)
        target[at, :] = result

    each_rows(source.shape[0], rows)


def column_sum(partial):
    return jnp.sum(partial[...], axis=0, keepdims=True)


def lower_lanes(shape):
    return lax.broadcasted_iota(jnp.int32, shape, 1) < shape[1] // 2


def split_pair(block):
    lower = lower_lanes(block.shape)
    zero = jnp.zeros_like(block)
    return jnp.concatenate([jnp.where(lower, block, zero), jnp.where(lower, zero, block)], axis=0)


def join_pair(stacked):
    rows = stacked.shape[0] // 2
    lower = lower_lanes((rows, stacked.shape[1]))
    return jnp.where(lower, stacked[:rows], stacked[rows:])


def attend_pair(queries, key_rows, values, additions, scale):
    length = queries.shape[0]
    scores = mm_nt(queries, split_pair(key_rows)) * scale
    parts = []
    for head in range(2):
        part = scores[:, head * length : (head + 1) * length] + additions[head]
        exponent = jnp.exp(part - jnp.max(part, axis=-1, keepdims=True))
        parts.append(exponent * (1.0 / jnp.sum(exponent, axis=-1, keepdims=True)))
    weights = jnp.concatenate(parts, axis=1).astype(bf16)
    return weights, mm(weights, split_pair(values))


def attend_pair_back(weights, queries, key_rows, values, grad_context, scale):
    length = queries.shape[0]
    grad_weights = mm_nt(grad_context, split_pair(values))
    parts = []
    for head in range(2):
        at = slice(head * length, (head + 1) * length)
        weight = weights[:, at].astype(f32)
        grad_weight = grad_weights[:, at]
        centred = jnp.sum(grad_weight * weight, axis=-1, keepdims=True)
        parts.append(weight * (grad_weight - centred))
    grad_raw = (jnp.concatenate(parts, axis=1) * scale).astype(bf16)
    grad_queries = mm(grad_raw, split_pair(key_rows))
    grad_keys = join_pair(mm_tn(grad_raw, queries))
    grad_values = join_pair(mm_tn(weights, grad_context))
    return grad_queries, grad_keys, grad_values, parts


def same_sentence(query_ids, key_ids):
    length = query_ids.shape[1]
    across = jnp.broadcast_to(key_ids.astype(f32), (length, length))
    down = jnp.broadcast_to(query_ids.astype(f32), (length, length)).T
    return across == down


class Mover:
    def __init__(self, semaphores):
        self.semaphores = semaphores
        self.used = 0

    def note(self, source, target):
        copy = pltpu.make_async_copy(source, target, self.semaphores.at[self.used])
        self.used += 1
        return copy

    def start(self, source, target):
        copy = self.note(source, target)
        copy.start()
        return copy


def wait_all(copies):
    for copy in copies:
        copy.wait()


def gelu_parts(hidden):
    share = 0.5 + 0.5 * lax.erf(hidden * half_root)
    slope = share + hidden * (density_scale * jnp.exp(hidden * hidden * -0.5))
    return hidden * share, slope


def first_body(
    heads, flag, ids, turned, table, vectors, in_bias, rows_in, cot_in, qkv_in, out_in, ffn_in,
    down_in, first_in,
    x1_out, h1_out, qkv_out, weights_out, context_out, h2_out, u_out, slope_out, e2_out, low_out,
    hc_out, qc_out,
    rows, qkv_w, out_w, ffn_w, down_w, first_w, cot, normed, qkv, weights, context, x1, h2, u, slope,
    e2, low, bias_rows, mask, loads, stores,
):
    width = rows.shape[1]
    hidden_width = ffn_w.shape[1]
    row_count, length = ids.shape[1], ids.shape[2]
    on_encoder = flag[0] == 1
    load = Mover(loads)
    store = Mover(stores)
    got_rows = load.start(rows_in, rows)
    got_qkv = load.start(qkv_in, qkv_w)
    got_out = load.start(out_in, out_w)

    one_hot = (turned[...] == lax.broadcasted_iota(jnp.int32, (table.shape[0], 2 * length), 0)).astype(f32)
    bias_rows[...] = lax.dot_general(
        table[...], one_hot, (((0,), (0,)), ((), ())), precision=lax.Precision.HIGHEST,
        preferred_element_type=f32,
    )
    own_group = jnp.where(on_encoder, 0, 1)
    ahead = lax.broadcasted_iota(jnp.int32, (length, length), 0) >= lax.broadcasted_iota(
        jnp.int32, (length, length), 1
    )
    for row in range(row_count):
        own = ids[pl.ds(own_group, 1), row, :]
        allowed = same_sentence(own, own) & (ahead | on_encoder)
        mask[row] = jnp.where(allowed, 0.0, masked_score)

    got_rows.wait()
    norm_forward(rows, vectors[0:1, :], vectors[1:2, :], normed)
    got_qkv.wait()

    def project(at):
        qkv[:, at] = mm(normed[...], qkv_w[:, at]).astype(bf16)

    each_tile(3 * width, project)
    out_copies = [store.start(normed, h1_out), store.start(qkv, qkv_out)]
    scale = (width // heads) ** (-0.5)

    @pl.loop(0, heads // 2, unroll=heads // 2)
    def _(pair):
        lanes = pl.multiple_of(pair * 128, 128)
        biases = []
        for head in range(2):
            spread = jnp.broadcast_to(bias_rows[pl.ds(pair * 2 + head, 1), :], (length, 2 * length))
            skewed = pltpu.roll(spread, 0, 1, stride=1, stride_axis=0)
            biases.append(skewed[:, :length])
        for row in range(row_count):
            at = slice(row * length, (row + 1) * length)
            additions = [bias + mask[row] for bias in biases]
            part, mixed = attend_pair(
                qkv[at, pl.ds(lanes, 128)],
                qkv[at, pl.ds(width + lanes, 128)],
                qkv[at, pl.ds(2 * width + lanes, 128)],
                additions,
                scale,
            )
            weights[row, pair] = part
            context[at, pl.ds(lanes, 128)] = mixed.astype(bf16)

    out_copies += [store.start(weights, weights_out), store.start(context, context_out)]
    got_out.wait()

    def mix(at):
        x1[:, at] = rows[:, at].astype(f32) + mm(context[...], out_w[:, at])

    each_tile(width, mix)
    out_copies.append(store.start(x1, x1_out))

    @pl.when(on_encoder)
    def _():
        got_ffn = load.start(ffn_in, ffn_w)
        got_down = load.start(down_in, down_w)
        norm_forward(x1, vectors[2:3, :], vectors[3:4, :], h2)
        got_ffn.wait()

        def feed(at):
            value, rate = gelu_parts(mm(h2[...], ffn_w[:, at]) + in_bias[:, at])
            u[:, at] = value.astype(bf16)
            slope[:, at] = rate.astype(bf16)

        each_tile(hidden_width, feed)
        copies = [store.start(h2, h2_out), store.start(u, u_out), store.start(slope, slope_out)]
        got_down.wait()

        def down(at):
            e2[:, at] = x1[:, at] + (mm(u[...], down_w[:, at]) + vectors[6:7, at])

        each_tile(width, down)
        copies.append(store.start(e2, e2_out))
        norm_forward(e2, vectors[4:5, :], vectors[5:6, :], low)
        copies.append(store.start(low, low_out))
        wait_all(copies)

    @pl.when(jnp.logical_not(on_encoder))
    def _():
        got_down = load.start(down_in, down_w)
        got_first = load.start(first_in, first_w)
        got_cot = load.start(cot_in, cot)
        norm_forward(x1, vectors[2:3, :], vectors[3:4, :], h2)
        got_first.wait()

        def query(at):
            low[:, at] = mm(h2[...], first_w[:, at]).astype(bf16)

        each_tile(width, query)
        copies = [store.start(h2, hc_out), store.start(low, qc_out)]
        got_down.wait()
        got_cot.wait()

        def back(at):
            slope[:, at] = mm_nt(cot[...], down_w[at, :]).astype(bf16)

        each_tile(hidden_width, back)
        copies.append(store.start(slope, slope_out))
        wait_all(copies)

    wait_all(out_copies)


def cross_body(
    heads, flag, ids, vectors, in_bias, vec_in,
    memory_in, sent_in, other_in, second_in, x1_in, qc_in, cot_in, ffn_in, h2_in, u_in, slope_in,
    vec_out, h2_out, u_out, slope_out, d2_out, grad_out, cc_out, dq_out, dk_out, dv_out, dm_out,
    memory, keys_w, values_w, second_w, x1, qc, cot, ffn_w, keys, values, weights, cc, d2, h2, u,
    slope, grad_normed, grad, grad_low, dq, dk, dv, dm, mask, gain_sum, offset_sum, loads, stores,
):
    width = memory.shape[1]
    hidden_width = ffn_w.shape[1]
    row_count, length = ids.shape[1], ids.shape[2]
    vec_out[...] = vec_in[...]

    @pl.when(flag[0] == 0)
    def _():
        load = Mover(loads)
        store = Mover(stores)
        got_keys = [load.start(memory_in, memory), load.note(sent_in, keys_w)]
        got_values = [load.note(sent_in, values_w)]
        for core, (keys_in, values_in) in enumerate(((sent_in, other_in), (other_in, sent_in))):

            @pl.when(flag[1] == core)
            def _(keys_in=keys_in, values_in=values_in):
                pltpu.make_async_copy(keys_in, keys_w, loads.at[1]).start()
                pltpu.make_async_copy(values_in, values_w, loads.at[2]).start()

        got_query = load.start(qc_in, qc)
        got_second = [load.start(second_in, second_w), load.start(x1_in, x1)]
        got_ffn = [load.start(ffn_in, ffn_w), load.start(slope_in, slope)]
        got_cot = load.start(cot_in, cot)
        for row in range(row_count):
            mask[row] = jnp.where(
                same_sentence(ids[1:2, row, :], ids[0:1, row, :]), 0.0, masked_score
            )
        wait_all(got_keys)

        def project_keys(at):
            keys[:, at] = mm(memory[...], keys_w[:, at]).astype(bf16)

        each_tile(width, project_keys)
        wait_all(got_values)

        def project_values(at):
            values[:, at] = mm(memory[...], values_w[:, at]).astype(bf16)

        each_tile(width, project_values)
        got_query.wait()
        scale = (width // heads) ** (-0.5)

        @pl.loop(0, heads // 2)
        def _(pair):
            lanes = pl.ds(pl.multiple_of(pair * 128, 128), 128)
            for row in range(row_count):
                at = slice(row * length, (row + 1) * length)
                part, mixed = attend_pair(
                    qc[at, lanes], keys[at, lanes], values[at, lanes], [mask[row], mask[row]], scale
                )
                weights[row, pair] = part
                cc[at, lanes] = mixed.astype(bf16)

        copies = [store.start(cc, cc_out)]
        wait_all(got_second)

        def mix(at):
            d2[:, at] = x1[:, at] + mm(cc[...], second_w[:, at])

        each_tile(width, mix)
        copies.append(store.start(d2, d2_out))
        norm_forward(d2, vectors[4:5, :], vectors[5:6, :], h2)
        copies.append(store.start(h2, h2_out))
        wait_all(got_ffn)

        def feed(at):
            value, rate = gelu_parts(mm(h2[...], ffn_w[:, at]) + in_bias[:, at])
            u[:, at] = value.astype(bf16)
            slope[:, at] = (slope[:, at].astype(f32) * rate).astype(bf16)

        each_tile(hidden_width, feed)
        copies += [store.start(u, u_out), store.start(slope, slope_out)]

        def back(at):
            grad_normed[:, at] = mm_nt(slope[...], ffn_w[at, :])

        each_tile(width, back)
        got_cot.wait()
        norm_backward(d2, grad_normed, vectors[4:5, :], cot, grad, gain_sum, offset_sum)
        vec_out[4:5, :] = column_sum(gain_sum)
        vec_out[5:6, :] = column_sum(offset_sum)
        copies.append(store.start(grad, grad_out))

        def lower(at):
            grad_low[at, :] = grad[at, :].astype(bf16)

        each_rows(grad.shape[0], lower)

        def back_context(at):
            dm[:, at] = mm_nt(grad_low[...], second_w[at, :]).astype(bf16)

        each_tile(width, back_context)

        @pl.loop(0, heads // 2)
        def _(pair):
            lanes = pl.ds(pl.multiple_of(pair * 128, 128), 128)
            for row in range(row_count):
                at = slice(row * length, (row + 1) * length)
                grad_q, grad_k, grad_v, _ = attend_pair_back(
                    weights[row, pair], qc[at, lanes], keys[at, lanes], values[at, lanes],
                    dm[at, lanes], scale,
                )
                dq[at, lanes] = grad_q.astype(bf16)
                dk[at, lanes] = grad_k.astype(bf16)
                dv[at, lanes] = grad_v.astype(bf16)

        copies += [store.start(dq, dq_out), store.start(dk, dk_out), store.start(dv, dv_out)]

        def back_memory(at):
            dm[:, at] = (mm_nt(dk[...], keys_w[at, :]) + mm_nt(dv[...], values_w[at, :])).astype(bf16)

        each_tile(width, back_memory)
        copies.append(store.start(dm, dm_out))
        wait_all(copies)


def put_rows(store, stage, targets, core, rows):
    if len(targets) == 1:
        return [store.start(stage.at[rows], targets[0].at[rows])]
    depth = targets[0].shape[1]
    copies = []
    for chip in range(rows.start // (2 * depth), (rows.start + rows.size) // (2 * depth)):
        for target, which in zip(targets, (core, 1 - core)):
            at = pl.multiple_of((2 * chip + which) * depth, depth)
            copies.append(store.start(stage.at[pl.ds(at, depth)], target.at[chip]))
    return copies


def put_columns(store, stage, targets, core, columns):
    if len(targets) == 1:
        return [store.start(stage.at[:, columns], targets[0].at[:, columns])]
    chips, depth = targets[0].shape[0], targets[0].shape[1]
    copies = []
    for chip in range(chips):
        for target, which in zip(targets, (core, 1 - core)):
            at = pl.multiple_of((2 * chip + which) * depth, depth)
            copies.append(
                store.start(stage.at[pl.ds(at, depth), columns], target.at[chip, :, columns])
            )
    return copies


def spans(count, width):
    return [pl.ds(start, width) for start in range(0, count, width)]


def cross_grads_body(flag, cc_in, grad_in, hc_in, dq_in, memory_in, dk_in, dv_in, *rest):
    *outs, cc, grad, hc, dq, memory, dk, dv, cross_g, loads, stores = rest
    width = cc.shape[1]

    @pl.when(flag[0] == 0)
    def _():
        load = Mover(loads)
        store = Mover(stores)
        got_query = [load.start(hc_in, hc), load.start(dq_in, dq)]
        got_keys = [load.start(memory_in, memory), load.start(dk_in, dk)]
        got_values = [load.start(dv_in, dv)]
        got_out = [load.start(cc_in, cc), load.start(grad_in, grad)]
        query, out, keys, values = spans(4 * width, width)
        wait_all(got_query)
        cross_g[:, query] = mm_tn(hc[...], dq[...]).astype(bf16)
        wait_all(got_keys)
        cross_g[:, keys] = mm_tn(memory[...], dk[...]).astype(bf16)
        wait_all(got_values)
        cross_g[:, values] = mm_tn(memory[...], dv[...]).astype(bf16)
        copies = put_columns(store, cross_g, outs, flag[1], pl.ds(2 * width, 2 * width))
        wait_all(got_out)
        cross_g[:, out] = mm_tn(cc[...], grad[...].astype(bf16)).astype(bf16)
        copies += put_columns(store, cross_g, outs, flag[1], pl.ds(0, 2 * width))
        wait_all(copies)


def down_body(flag, vectors, small_in, dm_in, cot_in, e2_in, u_in, *rest):
    small_out, grad_out, low_out, *rest = rest
    count = len(rest) - 11
    outs = rest[:count]
    dm, cot, e2, u, grad, grad_low, down_g, gain_sum, offset_sum, loads, stores = rest[count:]
    hidden_width, width = u.shape[1], cot.shape[1]
    small_out[...] = small_in[...]
    load = Mover(loads)
    store = Mover(stores)
    got_cot = load.start(cot_in, cot)
    got_u = load.start(u_in, u)
    moved = [load.note(dm_in, dm), load.note(e2_in, e2)]
    kept = [store.note(grad, grad_out), store.note(grad_low, low_out)]

    @pl.when(flag[0] == 1)
    def _():
        for copy in moved:
            copy.start()
        got_cot.wait()
        wait_all(moved)

        def total(at):
            grad[at, :] = dm[at, :].astype(f32) + cot[at, :].astype(f32)

        each_rows(grad.shape[0], total)
        norm_backward(e2, grad, vectors[4:5, :], None, grad, gain_sum, offset_sum)
        small_out[4:5, :] = column_sum(gain_sum)
        small_out[5:6, :] = column_sum(offset_sum)

        def lower(at):
            grad_low[at, :] = grad[at, :].astype(bf16)

        each_rows(grad.shape[0], lower)
        for copy in kept:
            copy.start()

    @pl.when(flag[0] == 0)
    def _():
        got_cot.wait()
        grad_low[...] = cot[...]

    got_u.wait()
    copies = []
    for rows in spans(hidden_width, tile):
        down_g[rows, :] = mm_tn(u[:, rows], grad_low[...]).astype(bf16)
        copies += put_rows(store, down_g, outs, flag[1], rows)
    small_out[6:7, :] = jnp.sum(grad_low[...].astype(f32), axis=0, keepdims=True)
    wait_all(copies)

    @pl.when(flag[0] == 1)
    def _():
        wait_all(kept)


def hidden_body(flag, low_in, down_in, slope_in, slope_out, grad_low, down_w, slope, loads, stores):
    @pl.when(flag[0] == 1)
    def _():
        load = Mover(loads)
        store = Mover(stores)
        hidden_width = slope.shape[1]
        got_low = load.start(low_in, grad_low)
        got_slope = load.start(slope_in, slope)
        got_down = [
            load.start(down_in.at[rows], down_w.at[rows]) for rows in spans(hidden_width, tile)
        ]
        got_low.wait()
        got_slope.wait()
        copies = []
        for at, got in zip(spans(hidden_width, tile), got_down):
            got.wait()
            part = mm_nt(grad_low[...], down_w[at, :]) * slope[:, at].astype(f32)
            slope[:, at] = part.astype(bf16)
            copies.append(store.start(slope.at[:, at], slope_out.at[:, at]))
        wait_all(copies)


def ffn_body(flag, small_in, enc_slope_in, dec_slope_in, h2_in, *rest):
    small_out, *rest = rest
    count = len(rest) - 5
    outs = rest[:count]
    slope, h2, ffn_g, loads, stores = rest[count:]
    width, hidden_width = h2.shape[1], slope.shape[1]
    small_out[...] = small_in[...]
    load = Mover(loads)
    store = Mover(stores)
    got_h2 = load.start(h2_in, h2)
    got = load.note(enc_slope_in, slope)
    for which, slope_in in enumerate((dec_slope_in, enc_slope_in)):

        @pl.when(flag[0] == which)
        def _(slope_in=slope_in):
            pltpu.make_async_copy(slope_in, slope, loads.at[1]).start()

    got_h2.wait()
    got.wait()
    copies = []
    for step, at in enumerate(spans(hidden_width, tile)):
        ffn_g[:, at] = mm_tn(h2[...], slope[:, at]).astype(bf16)
        if step % 2 == 1:
            both = pl.ds(at.start - tile, 2 * tile)
            copies += put_columns(store, ffn_g, outs, flag[1], both)
    for part in range(hidden_width // width):
        values = slope[:, part * width : (part + 1) * width].astype(f32)
        small_out[8 + part : 9 + part, :] = jnp.sum(values, axis=0, keepdims=True)
    wait_all(copies)


def hidden_back_body(
    flag, vectors, small_in, slope_in, ffn_in, dq_in, first_in, x1_in, enc_grad_in, dec_grad_in,
    small_out, grad_out,
    slope, ffn_w, dq, first_w, x1, grad, grad_normed, gain_sum, offset_sum, loads, stores,
):
    width = x1.shape[1]
    small_out[...] = small_in[...]
    load = Mover(loads)
    store = Mover(stores)
    got_x1 = load.note(x1_in, x1)
    got_grad = load.note(enc_grad_in, grad)

    @pl.when(flag[0] == 1)
    def _():
        got = [load.start(slope_in, slope), load.start(ffn_in, ffn_w)]
        got_x1.start()
        got_grad.start()
        wait_all(got)
        grad_normed[...] = mm_nt(slope[...], ffn_w[...])

    @pl.when(flag[0] == 0)
    def _():
        got = [load.start(dq_in, dq), load.start(first_in, first_w)]
        got_x1.start()
        pltpu.make_async_copy(dec_grad_in, grad, loads.at[1]).start()
        wait_all(got)
        grad_normed[...] = mm_nt(dq[...], first_w[...])

    got_x1.wait()
    got_grad.wait()
    norm_backward(x1, grad_normed, vectors[2:3, :], grad, grad, gain_sum, offset_sum)
    stored = store.start(grad, grad_out)
    small_out[2:3, :] = column_sum(gain_sum)
    small_out[3:4, :] = column_sum(offset_sum)
    stored.wait()


def attention_back_body(
    heads, flag, turned, small_in, grad_in, qkv_in, weights_in, context_in, outw_in, h1_in, *rest
):
    small_out, grad_qkv_out, *rest = rest
    count = len(rest) - 14
    outs = rest[:count]
    (
        grad, qkv, weights, context, out_w, h1, grad_low, grad_context, grad_qkv, mixed_g, diagonals,
        one_hot, loads, stores,
    ) = rest[count:]
    width = context.shape[1]
    row_count, length = weights.shape[0], weights.shape[2]
    bucket_count = one_hot.shape[0]
    small_out[...] = small_in[...]
    load = Mover(loads)
    store = Mover(stores)
    got_grad = [load.start(grad_in, grad), load.start(outw_in, out_w)]
    got_context = load.start(context_in, context)
    got_attention = [load.start(weights_in, weights), load.start(qkv_in, qkv)]
    got_h1 = load.start(h1_in, h1)
    wait_all(got_grad)

    def lower(at):
        grad_low[at, :] = grad[at, :].astype(bf16)

    each_rows(grad.shape[0], lower)
    grad_context[...] = mm_nt(grad_low[...], out_w[...]).astype(bf16)
    got_context.wait()
    mixed_g[:, pl.ds(0, width)] = mm_tn(context[...], grad_low[...]).astype(bf16)
    wait_all(got_attention)
    scale = (width // heads) ** (-0.5)

    @pl.loop(0, heads // 2, unroll=2)
    def _(pair):
        lanes = pl.multiple_of(pair * 128, 128)
        totals = [None, None]
        for row in range(row_count):
            at = slice(row * length, (row + 1) * length)
            grad_q, grad_k, grad_v, parts = attend_pair_back(
                weights[row, pair],
                qkv[at, pl.ds(lanes, 128)],
                qkv[at, pl.ds(width + lanes, 128)],
                qkv[at, pl.ds(2 * width + lanes, 128)],
                grad_context[at, pl.ds(lanes, 128)],
                scale,
            )
            grad_qkv[at, pl.ds(lanes, 128)] = grad_q.astype(bf16)
            grad_qkv[at, pl.ds(width + lanes, 128)] = grad_k.astype(bf16)
            grad_qkv[at, pl.ds(2 * width + lanes, 128)] = grad_v.astype(bf16)
            totals = [p if t is None else t + p for t, p in zip(totals, parts)]
        for head in range(2):
            padded = jnp.concatenate([totals[head], jnp.zeros((length, length), f32)], axis=1)
            folded = padded[0:8, :]
            for block in range(1, length // 8):
                folded = folded + pltpu.roll(
                    padded[block * 8 : (block + 1) * 8, :], 2 * length - block * 8, 1
                )
            line = folded[0:1, :]
            for sub in range(1, 8):
                line = line + pltpu.roll(folded[sub : sub + 1, :], 2 * length - sub, 1)
            diagonals[pl.ds(pair * 2 + head, 1), :] = line

    got_h1.wait()
    copies = []
    for step, at in enumerate(spans(3 * width, width)):
        mixed_g[:, pl.ds(width + at.start, width)] = mm_tn(h1[...], grad_qkv[:, at]).astype(bf16)
        if step != 1:
            both = pl.ds(0 if step == 0 else 2 * width, 2 * width)
            copies += put_columns(store, mixed_g, outs, flag[1], both)
    copies.append(store.start(grad_qkv, grad_qkv_out))
    one_hot[...] = (
        turned[...] == lax.broadcasted_iota(jnp.int32, (bucket_count, 2 * length), 0)
    ).astype(f32)
    small_out[pl.ds(12, heads), pl.ds(0, bucket_count)] = lax.dot_general(
        diagonals[...], one_hot[...], (((1,), (1,)), ((), ())), precision=lax.Precision.HIGHEST,
        preferred_element_type=f32,
    )
    wait_all(copies)


def last_body(
    flag, vectors, small_in, grad_in, grad_qkv_in, qkvw_in, rows_in, u_in, d2_in, down_in, low_in,
    small_out, result_out, low_out,
    grad, grad_qkv, qkv_w, rows, grad_normed, u, d2, down_w, low, gain_sum, offset_sum, loads, stores,
):
    small_out[...] = small_in[...]
    load = Mover(loads)
    store = Mover(stores)
    got = [load.start(grad_qkv_in, grad_qkv), load.start(qkvw_in, qkv_w)]
    got_rows = [load.start(rows_in, rows), load.start(grad_in, grad)]
    stored_low = store.note(low, low_out)
    got_low = load.note(low_in, low)

    @pl.when(flag[0] == 1)
    def _():
        got_low.start()

    wait_all(got)
    grad_normed[...] = mm_nt(grad_qkv[...], qkv_w[...])
    wait_all(got_rows)
    norm_backward(rows, grad_normed, vectors[0:1, :], grad, grad, gain_sum, offset_sum)
    small_out[0:1, :] = column_sum(gain_sum)
    small_out[1:2, :] = column_sum(offset_sum)
    stored = store.start(grad, result_out)

    @pl.when(flag[0] == 1)
    def _():
        got_low.wait()
        stored_low.start()

    @pl.when(flag[0] == 0)
    def _():
        wait_all([load.start(u_in, u), load.start(d2_in, d2), load.start(down_in, down_w)])
        value = d2[...] + (mm(u[...], down_w[...]) + vectors[6:7, :])
        low[...] = value.astype(bf16)
        stored_low.start()

    stored.wait()
    stored_low.wait()


def pair_sum_body(everywhere, flag, kept_in, got_in, out, kept, got, total, loads, stores):
    @pl.when(jnp.logical_or(flag[0] == 0, everywhere))
    def _():
        load = Mover(loads)
        store = Mover(stores)
        blocks = out.shape[0]
        ready = []
        for step in range(blocks):
            block = 2 * step + 1 - flag[2]
            ready.append(
                (load.start(kept_in.at[block], kept.at[step]), load.start(got_in.at[block], got.at[step]))
            )
        copies = []
        for step in range(blocks):
            wait_all(ready[step])
            total[step] = (kept[step].astype(f32) + got[step].astype(f32)).astype(bf16)
            copies.append(store.start(total.at[step], out.at[step]))
        wait_all(copies)


def pair_sum(flag, kept, got, everywhere):
    chips, depth, width = kept.shape
    part = (chips // 2, depth, width)
    return run_kernel(
        functools.partial(pair_sum_body, everywhere),
        (flag, kept, got),
        [SMEM, ANY, ANY],
        [shape_of(part, bf16)],
        [ANY],
        [(part, bf16)] * 3,
        chips, chips // 2, {}, "pair_sum",
    )[0]


def chip_sum_body(
    everywhere, flag, kept_in, got_in, far_in, first_out, second_out, third_out, own_out,
    kept, got, far, total, own, loads, stores,
):
    @pl.when(jnp.logical_or(flag[0] == 0, everywhere))
    def _():
        load = Mover(loads)
        store = Mover(stores)
        ready = []
        for step in range(4):
            place = lax.rem(flag[3] + step + 1, 4)
            block = 2 * place + flag[2]
            ready.append(
                [
                    load.start(kept_in.at[block], kept.at[step]),
                    load.start(got_in.at[block], got.at[step]),
                    load.start(far_in.at[place], far.at[step]),
                ]
            )
        copies = []
        for step, out in enumerate((first_out, second_out, third_out, own_out)):
            wait_all(ready[step])
            value = kept[step].astype(f32) + got[step].astype(f32) + far[step].astype(f32)
            if step < 3:
                total[step] = value.astype(bf16)
                copies.append(store.start(total.at[step], out))
            else:
                own[...] = value
                copies.append(store.start(own, out))
        wait_all(copies)


def chip_sum(flag, kept, got, far, everywhere):
    _, depth, width = kept.shape
    one = (depth, width)
    return run_kernel(
        functools.partial(chip_sum_body, everywhere),
        (flag, kept, got, far),
        [SMEM, ANY, ANY, ANY],
        [shape_of(one, bf16)] * 3 + [shape_of(one, f32)],
        [ANY] * 4,
        [((4,) + one, bf16)] * 3 + [((3,) + one, bf16), (one, f32)],
        12, 4, {}, "chip_sum",
    )


def shape_of(dims, dtype):
    return jax.ShapeDtypeStruct(tuple(dims), dtype)


def size_of(dims, dtype):
    total = jnp.dtype(dtype).itemsize
    for dim in dims:
        total *= dim
    return total


def run_kernel(
    body, operands, places, outs, out_places, scratch, loads, stores, aliases, name, alone=False
):
    held = sum(size_of(dims, dtype) for dims, dtype in scratch)
    return pl.pallas_call(
        body,
        in_specs=places,
        out_specs=out_places,
        out_shape=outs,
        scratch_shapes=[pltpu.VMEM(dims, dtype) for dims, dtype in scratch]
        + [pltpu.SemaphoreType.DMA((loads,)), pltpu.SemaphoreType.DMA((stores,))],
        input_output_aliases=aliases,
        compiler_params=pltpu.CompilerParams(vmem_limit_bytes=all_bytes if alone else held + spare_bytes),
        cost_estimate=pl.CostEstimate(flops=1, bytes_accessed=1, transcendentals=0),
        name=name,
    )(*operands)


def after(value, *others):
    return lax.optimization_barrier((value,) + others)[0]


def block_of(always, steps, *operands):
    shapes = jax.eval_shape(steps, *operands)

    def blank(*_):
        return jax.tree.map(lambda leaf: jnp.zeros(leaf.shape, leaf.dtype), shapes)

    return lax.cond(always, steps, blank, *operands)


class Ring:
    def __init__(self, devices, everywhere):
        self.devices = devices
        self.everywhere = everywhere

    def send(self, shard, moved):
        pairs = [(i, moved(i)) for i in range(self.devices)]
        if self.everywhere:
            return lax.ppermute(shard, "batch", pairs)
        pairs = [(self.devices + i, self.devices + j) for i, j in pairs]
        return lax.ppermute(shard, ("section", "batch"), pairs)

    def to_core(self, given):
        return self.send(given, lambda i: i ^ 1)

    def to_chip(self, out):
        return self.send(out, lambda i: i ^ 2)

    def sums(self, flag, *held):
        return chip_sum(flag, *held, self.everywhere)

    def along(self, outs):
        return [
            self.send(out, lambda i, away=away: (i + 4 * away) % 16)
            for away, out in zip((1, 2, 3), outs)
        ]


def per_device(
    inputs, cotangent, segments, buckets, qkv_weight, out_weight, in_weight, down_weight,
    cross_first, cross_second, vectors, ffn_bias, position_table,
):
    row_count, length, width = inputs.shape[1:]
    heads = position_table.shape[2]
    bucket_count = position_table.shape[1]
    hidden = in_weight.shape[2]
    tokens = row_count * length
    pairs = heads // 2
    on_encoder = lax.axis_index("section") == 0
    place = lax.axis_index("batch")
    core = lax.rem(place, 2)
    devices = lax.axis_size("batch")
    by_chip = devices == 16
    always = place < devices
    flag = jnp.stack(
        [on_encoder.astype(jnp.int32), core, lax.rem(lax.div(place, 2), 2), lax.div(place, 4)]
    )
    turned = jnp.concatenate(
        [buckets[length - 1 :], jnp.full((1,), -1, jnp.int32), buckets[: length - 1]]
    )[None]
    rows = inputs.reshape(tokens, width)
    cot = cotangent.reshape(tokens, width)
    qkv_w, out_w, ffn_w, down_w = qkv_weight[0], out_weight[0], in_weight[0], down_weight[0]
    first_w, second_w = cross_first[0], cross_second[0]
    vec = vectors[0]
    fbias = ffn_bias

    tw, th = (tokens, width), (tokens, hidden)
    wide = (tokens, 3 * width)
    square = (row_count, pairs, length, 2 * length)
    small = (24, width)

    sent = lax.ppermute(jnp.where(core == 0, first_w, second_w), "section", [(0, 1)])

    first_outs = [
        shape_of(tw, f32), shape_of(tw, bf16), shape_of(wide, bf16), shape_of(square, bf16),
        shape_of(tw, bf16), shape_of(tw, bf16), shape_of(th, bf16), shape_of(th, bf16),
        shape_of(tw, f32), shape_of(tw, bf16), shape_of(tw, bf16), shape_of(tw, bf16),
    ]
    x1, h1, qkv, weights, context, h2, u, slope, e2, low, hc, qc = run_kernel(
        functools.partial(first_body, heads),
        (flag, segments, turned, position_table[0], vec, fbias, rows, cot, qkv_w, out_w, ffn_w,
         down_w, first_w),
        [SMEM] + [VMEM] * 5 + [ANY] * 7,
        first_outs,
        [ANY] * 12,
        [
            (tw, bf16), ((width, 3 * width), bf16), ((width, width), bf16), ((width, hidden), bf16),
            ((hidden, width), bf16), ((width, width), bf16), (tw, bf16), (tw, bf16), (wide, bf16),
            (square, bf16), (tw, bf16), (tw, f32), (tw, bf16), (th, bf16), (th, bf16), (tw, f32),
            (tw, bf16), ((heads, 2 * length), f32), ((row_count, length, length), f32),
        ],
        8, 13, {}, "first", True,
    )

    memory = lax.ppermute(low, "section", [(0, 1)])
    sent = after(sent, low)
    sent_other = lax.ppermute(sent, "batch", [(i, i ^ 1) for i in range(devices)])

    small_grad = jnp.zeros(small, f32)
    small_grad, h2, u, slope, d2, grad, cc, dq, dk, dv, dm = run_kernel(
        functools.partial(cross_body, heads),
        (flag, segments, vec, fbias, small_grad, memory, sent, sent_other, second_w, x1, qc,
         cot, ffn_w, h2, u, slope),
        [SMEM] + [VMEM] * 4 + [ANY] * 11,
        [shape_of(small, f32), shape_of(tw, bf16), shape_of(th, bf16), shape_of(th, bf16),
         shape_of(tw, f32), shape_of(tw, f32)] + [shape_of(tw, bf16)] * 5,
        [VMEM] + [ANY] * 10,
        [
            (tw, bf16), ((width, width), bf16), ((width, width), bf16), ((width, width), bf16),
            (tw, f32), (tw, bf16), (tw, bf16), ((width, hidden), bf16), (tw, bf16), (tw, bf16),
            (square, bf16), (tw, bf16), (tw, f32), (tw, bf16), (th, bf16), (th, bf16), (tw, f32),
            (tw, f32), (tw, bf16), (tw, bf16), (tw, bf16), (tw, bf16), (tw, bf16),
            ((row_count, length, length), f32), ((8, width), f32), ((8, width), f32),
        ],
        9, 10, {4: 0, 13: 1, 14: 2, 15: 3}, "cross", True,
    )

    returned = lax.ppermute(dm, "section", [(1, 0)])

    def piece(depth_rows, columns):
        if not by_chip:
            return [shape_of((depth_rows, columns), bf16)]
        return [shape_of((devices // 2, depth_rows // devices, columns), bf16)] * 2

    down_piece, ffn_piece = piece(hidden, width), piece(width, hidden)
    mixed_piece = piece(width, 4 * width)
    count = len(down_piece)
    share_copies = devices if by_chip else 1
    cross, down, ffn, mixed = (
        Ring(devices, name != "cross") for name in ("cross", "down", "ffn", "mixed")
    )

    flag = after(flag, dm)
    cross_g = run_kernel(
        cross_grads_body,
        (flag, cc, grad, hc, dq, memory, dk, dv),
        [SMEM] + [ANY] * 7,
        mixed_piece,
        [ANY] * count,
        [(tw, bf16), (tw, f32)] + [(tw, bf16)] * 5 + [((width, 4 * width), bf16)],
        7, 2 * share_copies, {}, "cross_grads", True,
    )
    flag = after(flag, cross_g[0])

    def run_down(flag, vec, small_grad, returned, cot, e2, u):
        small_grad, enc_grad, enc_low, *pieces = run_kernel(
            down_body,
            (flag, vec, small_grad, returned, cot, e2, u),
            [SMEM] + [VMEM] * 2 + [ANY] * 4,
            [shape_of(small, f32), shape_of(tw, f32), shape_of(tw, bf16)] + down_piece,
            [VMEM] + [ANY] * (2 + count),
            [
                (tw, bf16), (tw, bf16), (tw, f32), (th, bf16), (tw, f32), (tw, bf16),
                ((hidden, width), bf16), ((8, width), f32), ((8, width), f32),
            ],
            4, 2 + max(share_copies, hidden // tile), {}, "down",
        )
        return small_grad, enc_grad, enc_low, pieces

    def run_hidden(flag, enc_low, down_w, slope):
        return run_kernel(
            hidden_body,
            (flag, enc_low, down_w, slope),
            [SMEM] + [ANY] * 3,
            [shape_of(th, bf16)],
            [ANY],
            [(tw, bf16), ((hidden, width), bf16), (th, bf16)],
            2 + hidden // tile, hidden // tile, {}, "hidden",
        )[0]

    def run_ffn(flag, small_grad, enc_slope, slope, h2):
        small_grad, *pieces = run_kernel(
            ffn_body,
            (flag, small_grad, enc_slope, slope, h2),
            [SMEM, VMEM] + [ANY] * 3,
            [shape_of(small, f32)] + ffn_piece,
            [VMEM] + [ANY] * count,
            [(th, bf16), (tw, bf16), ((width, hidden), bf16)],
            2, hidden // (2 * tile) * share_copies, {}, "ffn",
        )
        return small_grad, pieces

    def run_hidden_back(flag, vec, small_grad, slope, ffn_w, dq, first_w, x1, enc_grad, grad):
        return run_kernel(
            hidden_back_body,
            (flag, vec, small_grad, slope, ffn_w, dq, first_w, x1, enc_grad, grad),
            [SMEM] + [VMEM] * 2 + [ANY] * 7,
            [shape_of(small, f32), shape_of(tw, f32)],
            [VMEM, ANY],
            [
                (th, bf16), ((width, hidden), bf16), (tw, bf16), ((width, width), bf16), (tw, f32),
                (tw, f32), (tw, f32), ((8, width), f32), ((8, width), f32),
            ],
            6, 1, {}, "hidden_back",
        )

    def run_attention_back(flag, turned, small_grad, grad, qkv, weights, context, out_w, h1):
        small_grad, grad_qkv, *pieces = run_kernel(
            functools.partial(attention_back_body, heads),
            (flag, turned, small_grad, grad, qkv, weights, context, out_w, h1),
            [SMEM] + [VMEM] * 2 + [ANY] * 6,
            [shape_of(small, f32), shape_of(wide, bf16)] + mixed_piece,
            [VMEM] + [ANY] * (1 + count),
            [
                (tw, f32), (wide, bf16), (square, bf16), (tw, bf16), ((width, width), bf16),
                (tw, bf16), (tw, bf16), (tw, bf16), (wide, bf16), ((width, 4 * width), bf16),
                ((heads, 2 * length), f32), ((bucket_count, 2 * length), f32),
            ],
            6, 1 + 2 * share_copies, {}, "attention_back",
        )
        return small_grad, grad_qkv, pieces

    def run_last(flag, vec, small_grad, grad, grad_qkv, qkv_w, rows, u, d2, down_w, low):
        return run_kernel(
            last_body,
            (flag, vec, small_grad, grad, grad_qkv, qkv_w, rows, u, d2, down_w, low),
            [SMEM] + [VMEM] * 2 + [ANY] * 8,
            [shape_of(small, f32), shape_of(tw, f32), shape_of(tw, bf16)],
            [VMEM, ANY, ANY],
            [
                (tw, f32), (wide, bf16), ((width, 3 * width), bf16), (tw, bf16), (tw, f32),
                (th, bf16), (tw, f32), ((hidden, width), bf16), (tw, bf16), ((8, width), f32),
                ((8, width), f32),
            ],
            8, 2, {}, "last",
        )

    def beside(ring, pieces, kernel, *operands):
        def steps(kept, given, flag, *operands):
            got = ring.to_core(given)
            outs = kernel(flag, *operands)
            out = pair_sum(after(flag, *jax.tree.leaves(outs)), kept, got, ring.everywhere)
            return outs, got, out

        return block_of(always, steps, *pieces, *operands)

    if not by_chip:
        small_grad, enc_grad, enc_low, down_g = run_down(
            flag, vec, small_grad, returned, cot, e2, u
        )
        enc_slope = run_hidden(flag, enc_low, down_w, slope)
        small_grad, ffn_g = run_ffn(flag, small_grad, enc_slope, slope, h2)
        small_grad, grad = run_hidden_back(
            flag, vec, small_grad, enc_slope, ffn_w, dq, first_w, x1, enc_grad, grad
        )
        small_grad, grad_qkv, mixed_g = run_attention_back(
            flag, turned, small_grad, grad, qkv, weights, context, out_w, h1
        )
        small_grad, result, low = run_last(
            flag, vec, small_grad, grad, grad_qkv, qkv_w, rows, u, d2, down_w, low
        )
        small_grad = lax.psum(small_grad, "batch")
        cross_share, down_share, ffn_share, mixed_share = (
            lax.psum_scatter(pieces[0], "batch", scatter_dimension=0, tiled=True).astype(f32)
            for pieces in (cross_g, down_g, ffn_g, mixed_g)
        )
        cross_back = lax.ppermute(cross_share[:, 2 * width :], "section", [(1, 0)])
        cross_share = jnp.where(on_encoder, cross_back, cross_share[:, : 2 * width])
        out_share, qkv_share = mixed_share[:, :width], mixed_share[:, width:]
    else:

        def cross_steps(flag, kept, given):
            got = cross.to_core(given)
            return got, pair_sum(flag, kept, got, False)

        got, out = block_of(always, cross_steps, flag, *cross_g)
        flag = after(flag, out)

        def down_steps(out, kept, got, flag, *operands):
            vec, small_grad, returned, cot, e2, u, down_w, slope, h2, *operands = operands
            cross_far = cross.to_chip(out)
            small_grad, enc_grad, enc_low, pieces = run_down(
                flag, vec, small_grad, returned, cot, e2, u
            )
            flag = after(flag, small_grad)
            enc_slope, down_got, out = beside(
                down, pieces, run_hidden, flag, enc_low, down_w, slope
            )
            down_held = (pieces[0], down_got, down.to_chip(out))
            flag = after(flag, out)
            small_grad, pieces = run_ffn(flag, small_grad, enc_slope, slope, h2)
            flag = after(flag, small_grad)
            *outs, cross_own = cross.sums(flag, kept, got, cross_far)
            flag = after(flag, *outs)
            cross_last = (*cross.along(outs), cross_own)
            sums = beside(
                ffn, pieces, run_hidden_back, flag, vec, small_grad, enc_slope, *operands, enc_grad,
                grad,
            )
            return down_held, cross_last, pieces[0], sums

        down_held, cross_last, kept, sums = block_of(
            always, down_steps, out, cross_g[0], got, flag, vec, small_grad, returned, cot, e2, u,
            down_w, slope, h2, ffn_w, dq, first_w, x1,
        )
        (small_grad, grad), got, ffn_out = sums
        ffn_held = (kept, got)
        flag = after(flag, ffn_out)

        def attention_steps(flag, ffn_out, ffn_held, down_held, *operands):
            far = ffn.to_chip(ffn_out)
            *outs, down_own = down.sums(flag, *down_held)
            moved = down.along(outs)
            small_grad, grad_qkv, pieces = run_attention_back(after(flag, *outs), *operands)

            def swap(flag, kept, given, ffn_held):
                got = mixed.to_core(given)
                ffn_outs = ffn.sums(flag, *ffn_held)
                out = pair_sum(after(flag, *ffn_outs), kept, got, True)
                return got, out, ffn_outs

            flag = after(flag, small_grad)
            swapped = block_of(always, swap, flag, *pieces, (*ffn_held, far))
            return (*moved, down_own), small_grad, grad_qkv, pieces[0], swapped

        down_last, small_grad, grad_qkv, kept, swapped = block_of(
            always, attention_steps, flag, ffn_out, ffn_held, down_held, turned, small_grad, grad,
            qkv, weights, context, out_w, h1,
        )
        got, out, ffn_outs = swapped
        flag = after(flag, small_grad, out)

        def swapped_small(small_grad, away):
            pairs = [(i, i ^ away) for i in range(devices)]
            return small_grad + lax.ppermute(small_grad, "batch", pairs)

        def last_steps(flag, out, outs, *operands):
            far = mixed.to_chip(out)
            moved = ffn.along(outs)
            small_grad, result, low = run_last(flag, *operands)

            return far, moved, block_of(always, lambda s: swapped_small(s, 1), small_grad), result, low

        far, moved, small_grad, result, low = block_of(
            always, last_steps, flag, out, ffn_outs[:3], vec, small_grad, grad, grad_qkv, qkv_w, rows,
            u, d2, down_w, low,
        )
        flag = after(flag, small_grad)

        def mixed_steps(flag, small_grad, *held):
            small_grad = swapped_small(small_grad, 2)
            return mixed.sums(flag, *held), small_grad

        (*outs, own), small_grad = block_of(always, mixed_steps, flag, small_grad, kept, got, far)

        def end_steps(outs, small_grad, *parts):
            mixed_moved = mixed.along(outs)
            cross_share, down_share, ffn_share = (
                sum(part.astype(f32) for part in shares) for shares in after(parts, *outs)
            )
            cross_back = lax.ppermute(cross_share[:, 2 * width :], "section", [(1, 0)])

            def steps(small_grad):
                return swapped_small(swapped_small(small_grad, 4), 8)

            small_grad = block_of(always, steps, small_grad)
            return mixed_moved, cross_back, cross_share, down_share, ffn_share, small_grad

        mixed_moved, cross_back, cross_share, down_share, ffn_share, small_grad = block_of(
            always, end_steps, outs, small_grad, cross_last, down_last, (*moved, ffn_outs[3])
        )
        mixed_last = (*mixed_moved, own)
        out_share = sum(part[:, :width].astype(f32) for part in mixed_last)
        qkv_share = sum(part[:, width:].astype(f32) for part in mixed_last)
        cross_share = jnp.where(on_encoder, cross_back, cross_share[:, : 2 * width])
    vec_share = lax.dynamic_slice_in_dim(
        small_grad[:7], place * (width // devices), width // devices, 1
    )
    fbias_all = small_grad[8 : 8 + hidden // width].reshape(1, hidden)
    fbias_share = lax.dynamic_slice_in_dim(
        fbias_all, place * (hidden // devices), hidden // devices, 1
    )
    table_total = small_grad[12 : 12 + heads, :bucket_count].T
    return (
        low.reshape((1, row_count, length, width)),
        result.reshape((1, row_count, length, width)),
        qkv_share[None],
        out_share[None],
        ffn_share[None],
        down_share[None],
        cross_share[None, :, :width],
        cross_share[None, :, width:],
        vec_share[None],
        fbias_share,
        table_total[None],
    )


def solution(mesh):
    return jax.shard_map(
        per_device,
        mesh=mesh,
        in_specs=(
            P("section", "batch", None, None),
            P("section", "batch", None, None),
            P(None, "batch", None),
            P(),
            P("section", None, None),
            P("section", None, None),
            P("section", None, None),
            P("section", None, None),
            P("section", None, None),
            P("section", None, None),
            P("section", None, None),
            P("section", None),
            P("section", None, None),
        ),
        out_specs=(
            P("section", "batch", None, None),
            P("section", "batch", None, None),
            P("section", "batch", None),
            P("section", "batch", None),
            P("section", "batch", None),
            P("section", "batch", None),
            P("section", "batch", None),
            P("section", "batch", None),
            P("section", None, "batch"),
            P("section", "batch"),
            P("section", None, None),
        ),
        check_vma=False,
    )
```

```python
import functools

import jax
import jax.numpy as jnp
from jax import lax
from jax.experimental import pallas as pl
from jax.experimental.pallas import tpu as pltpu
from jax.sharding import PartitionSpec as P

norm_epsilon = 1e-05
masked_score = -1e30
half_root = 0.7071067811865476
density_scale = 0.3989422804014327
tile = 768
broad = 1536
chunk = 256
spare_bytes = 8 * 1024 * 1024
all_bytes = 62 * 1024 * 1024

f32 = jnp.float32
bf16 = jnp.bfloat16
ANY = pl.BlockSpec(memory_space=pl.ANY)
SMEM = pl.BlockSpec(memory_space=pltpu.SMEM)
VMEM = pl.BlockSpec(memory_space=pltpu.VMEM)


def mm(left, right):
    return jnp.dot(left, right, preferred_element_type=f32)


def mm_nt(left, right):
    return lax.dot_general(left, right, (((1,), (1,)), ((), ())), preferred_element_type=f32)


def mm_tn(left, right):
    return lax.dot_general(left, right, (((0,), (0,)), ((), ())), preferred_element_type=f32)


def mean_of(values):
    return jnp.sum(values, axis=-1, keepdims=True) * (1.0 / values.shape[-1])


def normalised(values):
    centre = values - mean_of(values)
    rate = lax.rsqrt(mean_of(centre * centre) + norm_epsilon)
    return centre * rate, rate


def each_rows(count, body):
    @pl.loop(0, count // chunk)
    def _(step):
        body(pl.ds(pl.multiple_of(step * chunk, chunk), chunk))


def each_tile(count, body, width=tile):
    if count == width:
        body(pl.ds(0, width))
        return

    @pl.loop(0, count // width)
    def _(step):
        body(pl.ds(pl.multiple_of(step * width, width), width))


def norm_forward(source, gain, offset, target, also=None):
    def rows(at):
        unit, _ = normalised(source[at, :].astype(f32))
        normed = unit * gain + offset
        target[at, :] = normed.astype(target.dtype)

    each_rows(source.shape[0], rows)


def norm_backward(
    source, grad_normed, gain, upstream, target, gain_sum, offset_sum, low=None
):
    gain_sum[...] = jnp.zeros_like(gain_sum)
    offset_sum[...] = jnp.zeros_like(offset_sum)

    def rows(at):
        unit, rate = normalised(source[at, :].astype(f32))
        upper = grad_normed[at, :]
        product = upper * unit
        gain_sum[...] += jnp.sum(product.reshape(-1, 8, product.shape[1]), axis=0)
        offset_sum[...] += jnp.sum(upper.reshape(-1, 8, upper.shape[1]), axis=0)
        scaled = upper * gain
        inner = mean_of(scaled)
        along = mean_of(product * gain)
        result = rate * (scaled - inner - unit * along)
        if upstream is not None:
            result = result + upstream[at, :].astype(f32)
        target[at, :] = result
        if low is not None:
            low[at, :] = result.astype(bf16)

    each_rows(source.shape[0], rows)


def column_sum(partial):
    return jnp.sum(partial[...], axis=0, keepdims=True)


def lower_lanes(shape):
    return lax.broadcasted_iota(jnp.int32, shape, 1) < shape[1] // 2


def split_pair(block):
    lower = lower_lanes(block.shape)
    zero = jnp.zeros_like(block)
    return jnp.concatenate([jnp.where(lower, block, zero), jnp.where(lower, zero, block)], axis=0)


def join_pair(stacked):
    rows = stacked.shape[0] // 2
    lower = lower_lanes((rows, stacked.shape[1]))
    return jnp.where(lower, stacked[:rows], stacked[rows:])


def attend_pair(queries, key_rows, values, additions, scale):
    length = queries.shape[0]
    scores = mm_nt(queries, split_pair(key_rows)) * scale
    parts = []
    for head in range(2):
        part = scores[:, head * length : (head + 1) * length] + additions[head]
        exponent = jnp.exp(part - jnp.max(part, axis=-1, keepdims=True))
        parts.append(exponent * (1.0 / jnp.sum(exponent, axis=-1, keepdims=True)))
    weights = jnp.concatenate(parts, axis=1).astype(bf16)
    return weights, mm(weights, split_pair(values))


def attend_pair_back(weights, queries, key_rows, values, grad_context, scale):
    length = queries.shape[0]
    grad_weights = mm_nt(grad_context, split_pair(values))
    parts = []
    for head in range(2):
        at = slice(head * length, (head + 1) * length)
        weight = weights[:, at].astype(f32)
        grad_weight = grad_weights[:, at]
        centred = jnp.sum(grad_weight * weight, axis=-1, keepdims=True)
        parts.append(weight * (grad_weight - centred))
    grad_raw = (jnp.concatenate(parts, axis=1) * scale).astype(bf16)
    grad_queries = mm(grad_raw, split_pair(key_rows))
    grad_keys = join_pair(mm_tn(grad_raw, queries))
    grad_values = join_pair(mm_tn(weights, grad_context))
    return grad_queries, grad_keys, grad_values, parts


def same_sentence(query_ids, key_ids):
    length = query_ids.shape[1]
    across = jnp.broadcast_to(key_ids.astype(f32), (length, length))
    down = jnp.broadcast_to(query_ids.astype(f32), (length, length)).T
    return across == down


class Move:
    def __init__(self, sources, target, semaphores):
        self.sources, self.target, self.semaphores = sources, target, semaphores

    def copies(self, sources):
        if not isinstance(sources, tuple):
            yield pltpu.make_async_copy(sources, self.target, self.semaphores[0])
            return
        rows = self.target.shape[0] // len(sources)
        for part, source in enumerate(sources):
            target = self.target.at[pl.ds(part * rows, rows)]
            yield pltpu.make_async_copy(source, target, self.semaphores[part])

    def start(self, sources=None):
        for copy in self.copies(self.sources if sources is None else sources):
            copy.start()

    def wait(self, sources=None):
        for copy in self.copies(self.sources if sources is None else sources):
            copy.wait()


class Mover:
    def __init__(self, semaphores):
        self.semaphores = semaphores
        self.used = 0

    def note(self, source, target):
        count = len(source) if isinstance(source, tuple) else 1
        semaphores = [self.semaphores.at[self.used + part] for part in range(count)]
        self.used += count
        return Move(source, target, semaphores)

    def start(self, source, target):
        move = self.note(source, target)
        move.start()
        return move


def wait_all(moves):
    for move in moves:
        move.wait()


def gelu_parts(hidden):
    share = 0.5 + 0.5 * lax.erf(hidden * half_root)
    slope = share + hidden * (density_scale * jnp.exp(hidden * hidden * -0.5))
    return hidden * share, slope


def first_body(
    heads, row, flag, ids, offsets, table, vectors, in_bias, rows_in, cot_in, qkv_in, out_in, ffn_in,
    down_in, first_in,
    x1_out, h1_out, qkv_out, weights_out, context_out, h2_out, u_out, slope_out, e2_out, low_out,
    hc_out, qc_out,
    rows, qkv_w, out_w, ffn_w, down_w, first_w, cot, normed, qkv, weights, context, x1, h2, u, slope,
    e2, low, bias_rows, mask, loads, stores,
):
    length, width = rows.shape
    hidden_width = ffn_w.shape[1]
    on_encoder = flag[0] == 1
    own_rows = pl.ds(row * length, length)
    load = Mover(loads)
    store = Mover(stores)
    got_rows = load.start(rows_in.at[own_rows], rows)
    got_qkv = load.start(qkv_in, qkv_w)
    got_out = load.start(out_in, out_w)
    got_down = load.note(down_in, down_w)
    got_ffn = load.note(ffn_in, ffn_w)
    got_first = load.note(first_in, first_w)
    got_cot = load.note(cot_in.at[own_rows], cot)

    @pl.when(on_encoder)
    def _():
        got_ffn.start()
        got_down.start()

    @pl.when(jnp.logical_not(on_encoder))
    def _():
        got_first.start()
        got_cot.start()
        got_down.start()

    one_hot = (offsets[...] == lax.broadcasted_iota(jnp.int32, (table.shape[1], 2 * length), 0)).astype(f32)
    by_offset = lax.dot_general(
        table[...], one_hot, (((1,), (0,)), ((), ())), precision=lax.Precision.HIGHEST,
        preferred_element_type=f32,
    )
    bias_rows[...] = pltpu.roll(by_offset, length + 1, 1)
    own_group = jnp.where(on_encoder, 0, 1)
    ahead = lax.broadcasted_iota(jnp.int32, (length, length), 0) >= lax.broadcasted_iota(
        jnp.int32, (length, length), 1
    )
    own = ids[pl.ds(own_group, 1), row, :]
    allowed = same_sentence(own, own) & (ahead | on_encoder)
    mask[...] = jnp.where(allowed, 0.0, masked_score)

    got_rows.wait()
    norm_forward(rows, vectors[0], vectors[1], normed)
    got_qkv.wait()

    def project(at):
        qkv[:, at] = mm(normed[...], qkv_w[:, at]).astype(bf16)

    each_tile(3 * width, project)
    out_copies = [store.start(normed, h1_out), store.start(qkv, qkv_out)]
    scale = (width // heads) ** (-0.5)

    @pl.loop(0, heads // 2, unroll=heads // 2)
    def _(pair):
        lanes = pl.multiple_of(pair * 128, 128)
        additions = []
        for head in range(2):
            spread = jnp.broadcast_to(bias_rows[pl.ds(pair * 2 + head, 1), :], (length, 2 * length))
            skewed = pltpu.roll(spread, 0, 1, stride=1, stride_axis=0)
            additions.append(skewed[:, :length] + mask[...])
        part, mixed = attend_pair(
            qkv[:, pl.ds(lanes, 128)],
            qkv[:, pl.ds(width + lanes, 128)],
            qkv[:, pl.ds(2 * width + lanes, 128)],
            additions,
            scale,
        )
        weights[0, pair] = part
        context[:, pl.ds(lanes, 128)] = mixed.astype(bf16)

    out_copies += [store.start(weights, weights_out), store.start(context, context_out)]
    got_out.wait()
    x1[...] = rows[...].astype(f32) + mm(context[...], out_w[...])
    out_copies.append(store.start(x1, x1_out))

    @pl.when(on_encoder)
    def _():
        norm_forward(x1, vectors[2], vectors[3], h2)
        got_ffn.wait()

        def feed(at):
            value, rate = gelu_parts(mm(h2[...], ffn_w[:, at]) + in_bias[:, at])
            u[:, at] = value.astype(bf16)
            slope[:, at] = rate.astype(bf16)

        each_tile(hidden_width, feed, broad)
        copies = [store.start(h2, h2_out), store.start(u, u_out), store.start(slope, slope_out)]
        got_down.wait()
        e2[...] = x1[...] + (mm(u[...], down_w[...]) + vectors[6])
        copies.append(store.start(e2, e2_out))
        norm_forward(e2, vectors[4], vectors[5], low)
        copies.append(store.start(low, low_out))
        wait_all(copies)

    @pl.when(jnp.logical_not(on_encoder))
    def _():
        norm_forward(x1, vectors[2], vectors[3], h2)
        got_first.wait()
        low[...] = mm(h2[...], first_w[...]).astype(bf16)
        copies = [store.start(h2, hc_out), store.start(low, qc_out)]
        got_down.wait()
        got_cot.wait()

        def back(at):
            slope[:, at] = mm_nt(cot[...], down_w[at, :]).astype(bf16)

        each_tile(hidden_width, back)
        copies.append(store.start(slope, slope_out))
        wait_all(copies)

    wait_all(out_copies)


def cross_body(
    heads, row, flag, ids, vectors, in_bias, small_in,
    memory_in, sent_in, other_in, second_in, x1_in, qc_in, cot_in, ffn_in, slope_in,
    small_out, h2_out, u_out, slope_out, d2_out, grad_out, cc_out, dq_out, dk_out, dv_out, dm_out,
    memory, keys_w, values_w, second_w, x1, qc, cot, ffn_w, keys, values, weights, cc, d2, h2, u,
    slope, grad_normed, grad, grad_low, dq, dk, dv, dm, mask, gain_sum, offset_sum, loads, stores,
):
    length, width = memory.shape
    hidden_width = ffn_w.shape[1]
    small_out[...] = jnp.zeros_like(small_out) if row == 0 else small_in[...]

    @pl.when(flag[0] == 0)
    def _():
        load = Mover(loads)
        store = Mover(stores)
        got_memory = load.start(memory_in, memory)
        got_keys = load.note(sent_in, keys_w)
        got_values = load.note(sent_in, values_w)
        for core, (keys_in, values_in) in enumerate(((sent_in, other_in), (other_in, sent_in))):

            @pl.when(flag[1] == core)
            def _(keys_in=keys_in, values_in=values_in):
                got_keys.start(keys_in)
                got_values.start(values_in)

        got_query = load.start(qc_in, qc)
        got_second = [load.start(second_in, second_w), load.start(x1_in, x1)]
        got_ffn = [load.start(ffn_in, ffn_w), load.start(slope_in, slope)]
        got_cot = load.start(cot_in.at[pl.ds(row * length, length)], cot)
        mask[...] = jnp.where(same_sentence(ids[1:2, row, :], ids[0:1, row, :]), 0.0, masked_score)
        got_memory.wait()
        got_keys.wait()
        keys[...] = mm(memory[...], keys_w[...]).astype(bf16)
        got_values.wait()
        values[...] = mm(memory[...], values_w[...]).astype(bf16)
        got_query.wait()
        scale = (width // heads) ** (-0.5)

        @pl.loop(0, heads // 2, unroll=2)
        def _(pair):
            lanes = pl.ds(pl.multiple_of(pair * 128, 128), 128)
            part, mixed = attend_pair(
                qc[:, lanes], keys[:, lanes], values[:, lanes], [mask[...], mask[...]], scale
            )
            weights[0, pair] = part
            cc[:, lanes] = mixed.astype(bf16)

        copies = [store.start(cc, cc_out)]
        wait_all(got_second)
        d2[...] = x1[...] + mm(cc[...], second_w[...])
        copies.append(store.start(d2, d2_out))
        norm_forward(d2, vectors[4], vectors[5], h2)
        copies.append(store.start(h2, h2_out))
        wait_all(got_ffn)

        def feed(at):
            value, rate = gelu_parts(mm(h2[...], ffn_w[:, at]) + in_bias[:, at])
            u[:, at] = value.astype(bf16)
            slope[:, at] = (slope[:, at].astype(f32) * rate).astype(bf16)

        each_tile(hidden_width, feed, broad)
        copies += [store.start(u, u_out), store.start(slope, slope_out)]
        grad_normed[...] = mm_nt(slope[...], ffn_w[...])
        got_cot.wait()
        norm_backward(
            d2, grad_normed, vectors[4], cot, grad, gain_sum, offset_sum, grad_low
        )
        small_out[4:5, :] += column_sum(gain_sum)
        small_out[5:6, :] += column_sum(offset_sum)
        copies.append(store.start(grad, grad_out))
        dm[...] = mm_nt(grad_low[...], second_w[...]).astype(bf16)

        @pl.loop(0, heads // 2, unroll=2)
        def _(pair):
            lanes = pl.ds(pl.multiple_of(pair * 128, 128), 128)
            grad_q, grad_k, grad_v, _ = attend_pair_back(
                weights[0, pair], qc[:, lanes], keys[:, lanes], values[:, lanes], dm[:, lanes], scale
            )
            dq[:, lanes] = grad_q.astype(bf16)
            dk[:, lanes] = grad_k.astype(bf16)
            dv[:, lanes] = grad_v.astype(bf16)

        copies += [store.start(dq, dq_out), store.start(dk, dk_out), store.start(dv, dv_out)]
        dm[...] = (mm_nt(dk[...], keys_w[...]) + mm_nt(dv[...], values_w[...])).astype(bf16)
        copies.append(store.start(dm, dm_out))
        wait_all(copies)


def put_rows(store, stage, targets, core, rows):
    if len(targets) == 1:
        return [store.start(stage.at[rows], targets[0].at[rows])]
    depth = targets[0].shape[1]
    copies = []
    for chip in range(rows.start // (2 * depth), (rows.start + rows.size) // (2 * depth)):
        for target, which in zip(targets, (core, 1 - core)):
            at = pl.multiple_of((2 * chip + which) * depth, depth)
            copies.append(store.start(stage.at[pl.ds(at, depth)], target.at[chip]))
    return copies


def put_columns(store, stage, targets, core, columns):
    if len(targets) == 1:
        return [store.start(stage.at[:, columns], targets[0].at[:, columns])]
    chips, depth = targets[0].shape[0], targets[0].shape[1]
    copies = []
    for chip in range(chips):
        for target, which in zip(targets, (core, 1 - core)):
            at = pl.multiple_of((2 * chip + which) * depth, depth)
            copies.append(
                store.start(stage.at[pl.ds(at, depth), columns], target.at[chip, :, columns])
            )
    return copies


def spans(count, width):
    return [pl.ds(start, width) for start in range(0, count, width)]


def cross_grads_body(flag, cc_in, grad_in, memory_in, dv_in, *rest):
    *outs, cc, grad, memory, dv, cross_g, loads, stores = rest
    width = cc.shape[1]

    @pl.when(flag[0] == 0)
    def _():
        load = Mover(loads)
        store = Mover(stores)
        got_values = [load.start(memory_in, memory), load.start(dv_in, dv)]
        got_out = [load.start(cc_in, cc), load.start(grad_in, grad)]
        out, values = spans(2 * width, width)
        wait_all(got_values)
        cross_g[:, values] = mm_tn(memory[...], dv[...]).astype(bf16)
        copies = put_columns(store, cross_g, outs, flag[1], values)
        wait_all(got_out)
        cross_g[:, out] = mm_tn(cc[...], grad[...].astype(bf16)).astype(bf16)
        copies += put_columns(store, cross_g, outs, flag[1], out)
        wait_all(copies)


def down_body(flag, vectors, small_in, dm_in, cot_in, e2_in, enc_u_in, dec_u_in, *rest):
    small_out, grad_out, low_out, *rest = rest
    count = len(rest) - 11
    outs = rest[:count]
    dm, cot, e2, u, grad, grad_low, down_g, gain_sum, offset_sum, loads, stores = rest[count:]
    hidden_width, width = u.shape[1], cot.shape[1]
    small_out[...] = small_in[...]
    load = Mover(loads)
    store = Mover(stores)
    got_cot = load.start(cot_in, cot)
    got_u = load.note(enc_u_in, u)
    moved = [load.note(dm_in, dm), load.note(e2_in, e2)]
    kept = [store.note(grad, grad_out), store.note(grad_low, low_out)]

    @pl.when(flag[0] == 1)
    def _():
        for copy in moved:
            copy.start()
        got_cot.wait()
        wait_all(moved)
        got_u.start(enc_u_in)

        def total(at):
            grad[at, :] = dm[at, :].astype(f32) + cot[at, :].astype(f32)

        each_rows(grad.shape[0], total)
        norm_backward(e2, grad, vectors[4], None, grad, gain_sum, offset_sum, grad_low)
        small_out[4:5, :] = column_sum(gain_sum)
        small_out[5:6, :] = column_sum(offset_sum)
        for copy in kept:
            copy.start()

    @pl.when(flag[0] == 0)
    def _():
        got_u.start(dec_u_in)
        got_cot.wait()
        grad_low[...] = cot[...]

    got_u.wait()
    copies = []
    for rows in spans(hidden_width, tile):
        down_g[rows, :] = mm_tn(u[:, rows], grad_low[...]).astype(bf16)
        copies += put_rows(store, down_g, outs, flag[1], rows)
    small_out[6:7, :] = jnp.sum(grad_low[...].astype(f32), axis=0, keepdims=True)
    wait_all(copies)

    @pl.when(flag[0] == 1)
    def _():
        wait_all(kept)


def hidden_body(flag, low_in, down_in, slope_in, slope_out, grad_low, down_w, slope, loads, stores):
    @pl.when(flag[0] == 1)
    def _():
        load = Mover(loads)
        store = Mover(stores)
        hidden_width = slope.shape[1]
        got_low = load.start(low_in, grad_low)
        got_slope = load.start(slope_in, slope)
        got_down = [
            load.start(down_in.at[rows], down_w.at[rows]) for rows in spans(hidden_width, tile)
        ]
        got_low.wait()
        got_slope.wait()
        copies = []
        for at, got in zip(spans(hidden_width, tile), got_down):
            got.wait()
            part = mm_nt(grad_low[...], down_w[at, :]) * slope[:, at].astype(f32)
            slope[:, at] = part.astype(bf16)
            copies.append(store.start(slope.at[:, at], slope_out.at[:, at]))
        wait_all(copies)


def ffn_body(flag, small_in, enc_ins, dec_ins, *rest):
    small_out, *rest = rest
    count = len(rest) - 7
    outs = rest[:count]
    slope, h2, left, right, ffn_g, loads, stores = rest[count:]
    width, hidden_width = h2.shape[1], slope.shape[1]
    small_out[...] = small_in[...]
    load = Mover(loads)
    store = Mover(stores)
    moves = [
        load.note(source, target) for source, target in zip(dec_ins, (h2, slope, left, right))
    ]
    for which, ins in enumerate((dec_ins, enc_ins)):

        @pl.when(flag[0] == which)
        def _(ins=ins):
            for move, source in zip(moves, ins):
                move.start(source)
            for move, source in zip(moves[:2], ins):
                move.wait(source)

    copies = []
    for step, at in enumerate(spans(hidden_width, tile)):
        ffn_g[:, at] = mm_tn(h2[...], slope[:, at]).astype(bf16)
        if step % 2 == 1:
            both = pl.ds(at.start - tile, 2 * tile)
            copies += put_columns(store, ffn_g, outs, flag[1], both)
    wait_all(moves[2:])
    at = pl.ds(hidden_width, width)
    ffn_g[:, at] = mm_tn(left[...], right[...]).astype(bf16)
    copies += put_columns(store, ffn_g, outs, flag[1], at)
    for part in range(hidden_width // width):
        values = slope[:, part * width : (part + 1) * width].astype(f32)
        small_out[8 + part : 9 + part, :] = jnp.sum(values, axis=0, keepdims=True)
    wait_all(copies)


def hidden_back_body(
    flag, vectors, small_in, slope_in, ffn_in, dq_in, first_in, x1_in, enc_grad_in, dec_grad_in,
    small_out, grad_out,
    slope, ffn_w, dq, first_w, x1, grad, grad_normed, gain_sum, offset_sum, loads, stores,
):
    width = x1.shape[1]
    small_out[...] = small_in[...]
    load = Mover(loads)
    store = Mover(stores)
    got_x1 = load.note(x1_in, x1)
    got_grad = load.note(dec_grad_in, grad)

    @pl.when(flag[0] == 1)
    def _():
        got = [load.start(slope_in, slope), load.start(ffn_in, ffn_w)]
        got_x1.start()
        got_grad.start(enc_grad_in)
        wait_all(got)
        grad_normed[...] = mm_nt(slope[...], ffn_w[...])
        got_grad.wait(enc_grad_in)

    @pl.when(flag[0] == 0)
    def _():
        got = [load.start(dq_in, dq), load.start(first_in, first_w)]
        got_x1.start()
        got_grad.start(dec_grad_in)
        wait_all(got)
        grad_normed[...] = mm_nt(dq[...], first_w[...])
        got_grad.wait()

    got_x1.wait()
    norm_backward(x1, grad_normed, vectors[2], grad, grad, gain_sum, offset_sum)
    stored = store.start(grad, grad_out)
    small_out[2:3, :] = column_sum(gain_sum)
    small_out[3:4, :] = column_sum(offset_sum)
    stored.wait()


def attention_back_body(
    heads, flag, offsets, small_in, grad_in, qkv_in, weights_in, context_in, outw_in, h1_in, *rest
):
    small_out, grad_qkv_out, *rest = rest
    count = len(rest) - 14
    outs = rest[:count]
    (
        grad, qkv, weights, context, out_w, h1, grad_low, grad_context, grad_qkv, mixed_g, diagonals,
        one_hot, loads, stores,
    ) = rest[count:]
    width = context.shape[1]
    row_count, length = weights.shape[0], weights.shape[2]
    bucket_count = one_hot.shape[0]
    small_out[...] = small_in[...]
    load = Mover(loads)
    store = Mover(stores)
    got_grad = [load.start(grad_in, grad), load.start(outw_in, out_w)]
    got_context = load.start(context_in, context)
    got_attention = [load.start(weights_in, weights), load.start(qkv_in, qkv)]
    got_h1 = load.start(h1_in, h1)
    wait_all(got_grad)

    def lower(at):
        grad_low[at, :] = grad[at, :].astype(bf16)

    each_rows(grad.shape[0], lower)
    grad_context[...] = mm_nt(grad_low[...], out_w[...]).astype(bf16)
    got_context.wait()
    mixed_g[:, pl.ds(0, width)] = mm_tn(context[...], grad_low[...]).astype(bf16)
    wait_all(got_attention)
    scale = (width // heads) ** (-0.5)

    @pl.loop(0, heads // 2, unroll=2)
    def _(pair):
        lanes = pl.multiple_of(pair * 128, 128)
        totals = [None, None]
        for row in range(row_count):
            at = slice(row * length, (row + 1) * length)
            grad_q, grad_k, grad_v, parts = attend_pair_back(
                weights[row, pair],
                qkv[at, pl.ds(lanes, 128)],
                qkv[at, pl.ds(width + lanes, 128)],
                qkv[at, pl.ds(2 * width + lanes, 128)],
                grad_context[at, pl.ds(lanes, 128)],
                scale,
            )
            grad_qkv[at, pl.ds(lanes, 128)] = grad_q.astype(bf16)
            grad_qkv[at, pl.ds(width + lanes, 128)] = grad_k.astype(bf16)
            grad_qkv[at, pl.ds(2 * width + lanes, 128)] = grad_v.astype(bf16)
            totals = [p if t is None else t + p for t, p in zip(totals, parts)]
        for head in range(2):
            padded = jnp.concatenate([totals[head], jnp.zeros((length, length), f32)], axis=1)
            folded = padded[0:8, :]
            for block in range(1, length // 8):
                folded = folded + pltpu.roll(
                    padded[block * 8 : (block + 1) * 8, :], 2 * length - block * 8, 1
                )
            line = folded[0:1, :]
            for sub in range(1, 8):
                line = line + pltpu.roll(folded[sub : sub + 1, :], 2 * length - sub, 1)
            diagonals[pl.ds(pair * 2 + head, 1), :] = line

    got_h1.wait()
    copies = []
    for step, at in enumerate(spans(3 * width, width)):
        mixed_g[:, pl.ds(width + at.start, width)] = mm_tn(h1[...], grad_qkv[:, at]).astype(bf16)
        if step != 1:
            both = pl.ds(0 if step == 0 else 2 * width, 2 * width)
            copies += put_columns(store, mixed_g, outs, flag[1], both)
    copies.append(store.start(grad_qkv, grad_qkv_out))
    one_hot[...] = (
        offsets[...] == lax.broadcasted_iota(jnp.int32, (bucket_count, 2 * length), 0)
    ).astype(f32)
    small_out[pl.ds(16, heads), pl.ds(0, bucket_count)] = lax.dot_general(
        pltpu.roll(diagonals[...], length - 1, 1), one_hot[...], (((1,), (1,)), ((), ())),
        precision=lax.Precision.HIGHEST,
        preferred_element_type=f32,
    )
    wait_all(copies)


def last_body(
    flag, vectors, small_in, grad_in, grad_qkv_in, qkvw_in, rows_in, u_in, d2_in, down_in, low_in,
    small_out, result_out, low_out,
    grad, grad_qkv, qkv_w, rows, grad_normed, u, d2, down_w, low, gain_sum, offset_sum, loads, stores,
):
    small_out[...] = small_in[...]
    load = Mover(loads)
    store = Mover(stores)
    got = [load.start(grad_qkv_in, grad_qkv), load.start(qkvw_in, qkv_w)]
    got_rows = [load.start(rows_in, rows), load.start(grad_in, grad)]
    stored_low = store.note(low, low_out)
    got_low = load.note(low_in, low)

    @pl.when(flag[0] == 1)
    def _():
        got_low.start()

    wait_all(got)
    grad_normed[...] = mm_nt(grad_qkv[...], qkv_w[...])
    wait_all(got_rows)
    norm_backward(rows, grad_normed, vectors[0], grad, grad, gain_sum, offset_sum)
    small_out[0:1, :] = column_sum(gain_sum)
    small_out[1:2, :] = column_sum(offset_sum)
    stored = store.start(grad, result_out)

    @pl.when(flag[0] == 1)
    def _():
        got_low.wait()
        stored_low.start()

    @pl.when(flag[0] == 0)
    def _():
        wait_all([load.start(u_in, u), load.start(d2_in, d2), load.start(down_in, down_w)])
        value = d2[...] + (mm(u[...], down_w[...]) + vectors[6])
        low[...] = value.astype(bf16)
        stored_low.start()

    stored.wait()
    stored_low.wait()


def pair_sum_body(everywhere, flag, kept_in, got_in, out, kept, got, total, loads, stores):
    @pl.when(jnp.logical_or(flag[0] == 0, everywhere))
    def _():
        load = Mover(loads)
        store = Mover(stores)
        blocks = out.shape[0]
        ready = []
        for step in range(blocks):
            block = 2 * step + 1 - flag[2]
            ready.append(
                (load.start(kept_in.at[block], kept.at[step]), load.start(got_in.at[block], got.at[step]))
            )
        copies = []
        for step in range(blocks):
            wait_all(ready[step])
            total[step] = (kept[step].astype(f32) + got[step].astype(f32)).astype(bf16)
            copies.append(store.start(total.at[step], out.at[step]))
        wait_all(copies)


def pair_sum(flag, kept, got, everywhere):
    chips, depth, width = kept.shape
    part = (chips // 2, depth, width)
    return run_kernel(
        functools.partial(pair_sum_body, everywhere),
        (flag, kept, got),
        [SMEM, ANY, ANY],
        [shape_of(part, bf16)],
        [ANY],
        [(part, bf16)] * 3,
        chips, chips // 2, "pair_sum",
    )[0]


def chip_sum_body(
    everywhere, flag, kept_in, got_in, far_in, first_out, second_out, third_out, own_out,
    kept, got, far, total, own, loads, stores,
):
    @pl.when(jnp.logical_or(flag[0] == 0, everywhere))
    def _():
        load = Mover(loads)
        store = Mover(stores)
        ready = []
        for step in range(4):
            place = lax.rem(flag[3] + step + 1, 4)
            block = 2 * place + flag[2]
            ready.append(
                [
                    load.start(kept_in.at[block], kept.at[step]),
                    load.start(got_in.at[block], got.at[step]),
                    load.start(far_in.at[place], far.at[step]),
                ]
            )
        copies = []
        for step, out in enumerate((first_out, second_out, third_out, own_out)):
            wait_all(ready[step])
            value = kept[step].astype(f32) + got[step].astype(f32) + far[step].astype(f32)
            if step < 3:
                total[step] = value.astype(bf16)
                copies.append(store.start(total.at[step], out))
            else:
                own[...] = value
                copies.append(store.start(own, out))
        wait_all(copies)


def chip_sum(flag, kept, got, far, everywhere):
    _, depth, width = kept.shape
    one = (depth, width)
    return run_kernel(
        functools.partial(chip_sum_body, everywhere),
        (flag, kept, got, far),
        [SMEM, ANY, ANY, ANY],
        [shape_of(one, bf16)] * 3 + [shape_of(one, f32)],
        [ANY] * 4,
        [((4,) + one, bf16)] * 3 + [((3,) + one, bf16), (one, f32)],
        12, 4, "chip_sum",
    )


def finish_body(
    place, first, second, third, own, small, qkv_out, out_out, vec_out, fbias_out, table_out
):
    width = out_out.shape[1]
    total = own[...]
    for part in (first, second, third):
        total = total + part[...].astype(f32)
    out_out[...] = total[:, :width]
    qkv_out[...] = total[:, width:]
    share = vec_out.shape[2]
    turned = pltpu.roll(small[0:8, :], lax.rem(width - place[0] * share, width), 1)
    for row in range(vec_out.shape[0]):
        vec_out[row] = turned[row : row + 1, :share]
    share = fbias_out.shape[1]
    per_row = width // share
    row = small[pl.ds(8 + lax.div(place[0], per_row), 1), :]
    turned = pltpu.roll(row, lax.rem(width - lax.rem(place[0], per_row) * share, width), 1)
    fbias_out[...] = turned[:, :share]
    for head in range(table_out.shape[0]):
        table_out[head] = small[16 + head : 17 + head, : table_out.shape[2]]


def shape_of(dims, dtype):
    return jax.ShapeDtypeStruct(tuple(dims), dtype)


def size_of(dims, dtype):
    total = jnp.dtype(dtype).itemsize
    for dim in dims:
        total *= dim
    return total


def run_kernel(
    body, operands, places, outs, out_places, scratch, loads, stores, name, alone=False
):
    held = sum(size_of(dims, dtype) for dims, dtype in scratch)
    flat, form = jax.tree.flatten(operands)
    flat_places = [
        place for place, operand in zip(places, operands, strict=True) for _ in jax.tree.leaves(operand)
    ]

    def kernel(*refs):
        return body(*form.unflatten(refs[: len(flat)]), *refs[len(flat) :])

    return pl.pallas_call(
        kernel,
        in_specs=flat_places,
        out_specs=out_places,
        out_shape=outs,
        scratch_shapes=[pltpu.VMEM(dims, dtype) for dims, dtype in scratch]
        + [pltpu.SemaphoreType.DMA((loads,)), pltpu.SemaphoreType.DMA((stores,))],
        compiler_params=pltpu.CompilerParams(
            vmem_limit_bytes=all_bytes if alone else held + spare_bytes
        ),
        cost_estimate=pl.CostEstimate(flops=1, bytes_accessed=1, transcendentals=0),
        name=name,
    )(*flat)


def after(value, *others):
    return lax.optimization_barrier((value,) + others)[0]


def block_of(always, steps, *operands):
    shapes = jax.eval_shape(steps, *operands)

    def blank(*_):
        return jax.tree.map(lambda leaf: jnp.zeros(leaf.shape, leaf.dtype), shapes)

    return lax.cond(always, steps, blank, *operands)


class Ring:
    def __init__(self, devices, everywhere):
        self.devices = devices
        self.everywhere = everywhere

    def send(self, shard, moved):
        pairs = [(i, moved(i)) for i in range(self.devices)]
        if self.everywhere:
            return lax.ppermute(shard, "batch", pairs)
        pairs = [(self.devices + i, self.devices + j) for i, j in pairs]
        return lax.ppermute(shard, ("section", "batch"), pairs)

    def to_core(self, given):
        return self.send(given, lambda i: i ^ 1)

    def to_chip(self, out):
        return self.send(out, lambda i: i ^ 2)

    def sums(self, flag, *held):
        return chip_sum(flag, *held, self.everywhere)

    def along(self, outs):
        return [
            self.send(out, lambda i, away=away: (i + 4 * away) % 16)
            for away, out in zip((2, 1, 3), (outs[1], outs[0], outs[2]))
        ]


def per_device(
    inputs, cotangent, segments, buckets, qkv_weight, out_weight, in_weight, down_weight,
    cross_first, cross_second, vectors, ffn_bias, position_table,
):
    row_count, length, width = inputs.shape[1:]
    heads = position_table.shape[2]
    bucket_count = position_table.shape[1]
    hidden = in_weight.shape[2]
    tokens = row_count * length
    pairs = heads // 2
    on_encoder = lax.axis_index("section") == 0
    place = lax.axis_index("batch")
    core = lax.rem(place, 2)
    devices = lax.axis_size("batch")
    by_chip = devices == 16
    always = place < devices
    flag = jnp.stack(
        [on_encoder.astype(jnp.int32), core, lax.rem(lax.div(place, 2), 2), lax.div(place, 4)]
    )
    offsets = jnp.pad(buckets, (0, 1), constant_values=-1)[None]
    table = jnp.transpose(position_table, (2, 0, 1))[:, 0]
    rows = inputs.reshape(tokens, width)
    cot = cotangent.reshape(tokens, width)
    qkv_w, out_w, ffn_w, down_w = qkv_weight[0], out_weight[0], in_weight[0], down_weight[0]
    first_w, second_w = cross_first[0], cross_second[0]
    vec = jnp.transpose(vectors, (1, 0, 2))
    fbias = ffn_bias

    tw, th = (tokens, width), (tokens, hidden)
    wide = (tokens, 3 * width)
    square = (row_count, pairs, length, 2 * length)
    row_tw, row_th, row_wide = (length, width), (length, hidden), (length, 3 * width)
    row_square = (1, pairs, length, 2 * length)
    small = (32, width)

    sent = lax.ppermute(jnp.where(core == 0, first_w, second_w), "section", [(0, 1)])

    def run_first(row, flag):
        return run_kernel(
            functools.partial(first_body, heads, row),
            (flag, segments, offsets, table, vec, fbias, rows, cot, qkv_w, out_w, ffn_w,
             down_w, first_w),
            [SMEM] + [VMEM] * 5 + [ANY] * 7,
            [
                shape_of(row_tw, f32), shape_of(row_tw, bf16), shape_of(row_wide, bf16),
                shape_of(row_square, bf16), shape_of(row_tw, bf16), shape_of(row_tw, bf16),
                shape_of(row_th, bf16), shape_of(row_th, bf16), shape_of(row_tw, f32),
                shape_of(row_tw, bf16), shape_of(row_tw, bf16), shape_of(row_tw, bf16),
            ],
            [ANY] * 12,
            [
                (row_tw, bf16), ((width, 3 * width), bf16), ((width, width), bf16),
                ((width, hidden), bf16), ((hidden, width), bf16), ((width, width), bf16),
                (row_tw, bf16), (row_tw, bf16), (row_wide, bf16), (row_square, bf16), (row_tw, bf16),
                (row_tw, f32), (row_tw, bf16), (row_th, bf16), (row_th, bf16), (row_tw, f32),
                (row_tw, bf16), ((heads, 2 * length), f32), ((length, length), f32),
            ],
            7, 13, "first", True,
        )

    def run_cross(row, flag, small_grad, memory, sent, sent_other, own):
        x1, qc, slope = own
        return run_kernel(
            functools.partial(cross_body, heads, row),
            (flag, segments, vec, fbias, small_grad, memory, sent, sent_other, second_w, x1, qc, cot,
             ffn_w, slope),
            [SMEM] + [VMEM] * 4 + [ANY] * 9,
            [shape_of(small, f32), shape_of(row_tw, bf16), shape_of(row_th, bf16),
             shape_of(row_th, bf16), shape_of(row_tw, f32), shape_of(row_tw, f32)]
            + [shape_of(row_tw, bf16)] * 5,
            [VMEM] + [ANY] * 10,
            [
                (row_tw, bf16), ((width, width), bf16), ((width, width), bf16),
                ((width, width), bf16), (row_tw, f32), (row_tw, bf16), (row_tw, bf16),
                ((width, hidden), bf16), (row_tw, bf16), (row_tw, bf16), (row_square, bf16),
                (row_tw, bf16), (row_tw, f32), (row_tw, bf16), (row_th, bf16), (row_th, bf16),
                (row_tw, f32), (row_tw, f32), (row_tw, bf16), (row_tw, bf16), (row_tw, bf16),
                (row_tw, bf16), (row_tw, bf16), ((length, length), f32), ((8, width), f32),
                ((8, width), f32),
            ],
            9, 10, "cross", True,
        )

    def to_decoder(value):
        return lax.ppermute(value, "section", [(0, 1)])

    def to_encoder(value):
        return lax.ppermute(value, "section", [(1, 0)])

    kept_rows = [run_first(0, flag)]
    for row in range(1, row_count):

        def first_steps(low, flag, row=row):
            memory = to_decoder(low)
            return memory, run_first(row, flag)

        low = kept_rows[-1][9]
        memory, outs = block_of(always, first_steps, low, after(flag, low))
        kept_rows.append(outs)
        memories = (*memories, memory) if row > 1 else (memory,)

    def cross_steps(low, flag, first_memory, sent, own):
        memory = to_decoder(low)
        other = lax.ppermute(sent, "batch", [(i, i ^ 1) for i in range(devices)])
        return memory, other, run_cross(0, flag, fbias, first_memory, sent, other, own)

    def own_of(row):
        outs = kept_rows[row]
        return outs[0], outs[11], outs[7]

    low = kept_rows[-1][9]
    memory, sent_other, outs = block_of(
        always, cross_steps, low, after(flag, low), memories[0], sent, own_of(0)
    )
    memories = (*memories, memory)
    small_grad, *outs = outs
    cross_rows, returned = [outs], ()
    for row in range(1, row_count):

        def return_steps(dm, flag, *operands, row=row):
            back = to_encoder(dm)
            return back, run_cross(row, flag, *operands)

        dm = cross_rows[-1][9]
        back, outs = block_of(
            always, return_steps, dm, after(flag, dm), small_grad, memories[row], sent, sent_other,
            own_of(row),
        )
        small_grad, *outs = outs
        cross_rows.append(outs)
        returned = (*returned, back)
    dm = cross_rows[-1][9]
    returned = (*returned, to_encoder(dm))
    x1, h1, qkv, weights, context, h2, u, slope, e2, low, hc, qc = zip(*kept_rows)
    dec_h2, dec_u, dec_slope, d2, grad, cc, dq, dk, dv, dm = zip(*cross_rows)

    def piece(depth_rows, columns):
        if not by_chip:
            return [shape_of((depth_rows, columns), bf16)]
        return [shape_of((devices // 2, depth_rows // devices, columns), bf16)] * 2

    down_piece, ffn_piece = piece(hidden, width), piece(width, hidden + width)
    mixed_piece, cross_piece = piece(width, 4 * width), piece(width, 2 * width)
    count = len(down_piece)
    share_copies = devices if by_chip else 1
    cross, down, ffn, mixed = (
        Ring(devices, name != "cross") for name in ("cross", "down", "ffn", "mixed")
    )

    flag = after(flag, *dm)
    cross_g = run_kernel(
        cross_grads_body,
        (flag, cc, grad, memories, dv),
        [SMEM] + [ANY] * 4,
        cross_piece,
        [ANY] * count,
        [(tw, bf16), (tw, f32), (tw, bf16), (tw, bf16), ((width, 2 * width), bf16)],
        4 * row_count, 2 * share_copies, "cross_grads", True,
    )
    flag = after(flag, cross_g[0])

    def run_down(flag, vec, small_grad, returned, cot, e2, u, dec_u):
        small_grad, enc_grad, enc_low, *pieces = run_kernel(
            down_body,
            (flag, vec, small_grad, returned, cot, e2, u, dec_u),
            [SMEM] + [VMEM] * 2 + [ANY] * 5,
            [shape_of(small, f32), shape_of(tw, f32), shape_of(tw, bf16)] + down_piece,
            [VMEM] + [ANY] * (2 + count),
            [
                (tw, bf16), (tw, bf16), (tw, f32), (th, bf16), (tw, f32), (tw, bf16),
                ((hidden, width), bf16), ((8, width), f32), ((8, width), f32),
            ],
            1 + 3 * row_count, 2 + max(share_copies, hidden // tile), "down",
        )
        return small_grad, enc_grad, enc_low, pieces

    def run_hidden(flag, enc_low, down_w, slope):
        return run_kernel(
            hidden_body,
            (flag, enc_low, down_w, slope),
            [SMEM] + [ANY] * 3,
            [shape_of(th, bf16)],
            [ANY],
            [(tw, bf16), ((hidden, width), bf16), (th, bf16)],
            1 + row_count + hidden // tile, hidden // tile, "hidden",
        )[0]

    def run_ffn(flag, small_grad, enc_slope, back_keys):
        small_grad, *pieces = run_kernel(
            ffn_body,
            (flag, small_grad, (h2, enc_slope, low, back_keys), (dec_h2, dec_slope, hc, dq)),
            [SMEM, VMEM, ANY, ANY],
            [shape_of(small, f32)] + ffn_piece,
            [VMEM] + [ANY] * count,
            [(th, bf16), (tw, bf16), (tw, bf16), (tw, bf16), ((width, hidden + width), bf16)],
            4 * row_count, (hidden // (2 * tile) + 1) * share_copies, "ffn",
        )
        return small_grad, pieces

    def run_hidden_back(flag, vec, small_grad, slope, ffn_w, dq, first_w, x1, enc_grad, grad):
        return run_kernel(
            hidden_back_body,
            (flag, vec, small_grad, slope, ffn_w, dq, first_w, x1, enc_grad, grad),
            [SMEM] + [VMEM] * 2 + [ANY] * 7,
            [shape_of(small, f32), shape_of(tw, f32)],
            [VMEM, ANY],
            [
                (th, bf16), ((width, hidden), bf16), (tw, bf16), ((width, width), bf16), (tw, f32),
                (tw, f32), (tw, f32), ((8, width), f32), ((8, width), f32),
            ],
            3 + 3 * row_count, 1, "hidden_back",
        )

    def run_attention_back(flag, offsets, small_grad, grad, qkv, weights, context, out_w, h1):
        small_grad, grad_qkv, *pieces = run_kernel(
            functools.partial(attention_back_body, heads),
            (flag, offsets, small_grad, grad, qkv, weights, context, out_w, h1),
            [SMEM] + [VMEM] * 2 + [ANY] * 6,
            [shape_of(small, f32), shape_of(wide, bf16)] + mixed_piece,
            [VMEM] + [ANY] * (1 + count),
            [
                (tw, f32), (wide, bf16), (square, bf16), (tw, bf16), ((width, width), bf16),
                (tw, bf16), (tw, bf16), (tw, bf16), (wide, bf16), ((width, 4 * width), bf16),
                ((heads, 2 * length), f32), ((bucket_count, 2 * length), f32),
            ],
            2 + 4 * row_count, 1 + 2 * share_copies, "attention_back",
        )
        return small_grad, grad_qkv, pieces

    def run_last(flag, vec, small_grad, grad, grad_qkv, qkv_w, rows, u, d2, down_w, low):
        return run_kernel(
            last_body,
            (flag, vec, small_grad, grad, grad_qkv, qkv_w, rows, u, d2, down_w, low),
            [SMEM] + [VMEM] * 2 + [ANY] * 8,
            [shape_of(small, f32), shape_of(tw, f32), shape_of(tw, bf16)],
            [VMEM, ANY, ANY],
            [
                (tw, f32), (wide, bf16), ((width, 3 * width), bf16), (tw, bf16), (tw, f32),
                (th, bf16), (tw, f32), ((hidden, width), bf16), (tw, bf16), ((8, width), f32),
                ((8, width), f32),
            ],
            5 + 3 * row_count, 2, "last",
        )

    def beside(ring, pieces, kernel, *operands):
        def steps(kept, given, flag, *operands):
            got = ring.to_core(given)
            outs = kernel(flag, *operands)
            out = pair_sum(after(flag, *jax.tree.leaves(outs)), kept, got, ring.everywhere)
            return outs, got, out

        return block_of(always, steps, *pieces, *operands)

    if not by_chip:
        small_grad, enc_grad, enc_low, down_g = run_down(
            flag, vec, small_grad, returned, cot, e2, u, dec_u
        )
        enc_slope = run_hidden(flag, enc_low, down_w, slope)
        back_keys = tuple(to_encoder(key) for key in dk)
        small_grad, ffn_g = run_ffn(flag, small_grad, enc_slope, back_keys)
        small_grad, grad = run_hidden_back(
            flag, vec, small_grad, enc_slope, ffn_w, dq, first_w, x1, enc_grad, grad
        )
        small_grad, grad_qkv, mixed_g = run_attention_back(
            flag, offsets, small_grad, grad, qkv, weights, context, out_w, h1
        )
        small_grad, result, low = run_last(
            flag, vec, small_grad, grad, grad_qkv, qkv_w, rows, dec_u, d2, down_w, low
        )
        small_grad = lax.psum(small_grad, "batch")
        cross_share, down_share, ffn_share, mixed_share = (
            lax.psum_scatter(pieces[0], "batch", scatter_dimension=0, tiled=True).astype(f32)
            for pieces in (cross_g, down_g, ffn_g, mixed_g)
        )
        cross_back = lax.ppermute(cross_share[:, width:], "section", [(1, 0)])
        cs_share = jnp.where(on_encoder, cross_back, cross_share[:, :width])
        ffn_share, cf_share = ffn_share[:, :hidden], ffn_share[:, hidden:]
        out_share, qkv_share = mixed_share[:, :width], mixed_share[:, width:]
        vec_share = lax.dynamic_slice_in_dim(
            small_grad[:7], place * (width // devices), width // devices, 1
        )
        fbias_all = small_grad[8 : 8 + hidden // width].reshape(1, hidden)
        fbias_share = lax.dynamic_slice_in_dim(
            fbias_all, place * (hidden // devices), hidden // devices, 1
        )
        table_total = small_grad[16 : 16 + heads, :bucket_count].T
    else:

        def cross_steps(flag, kept, given):
            got = cross.to_core(given)
            return got, pair_sum(flag, kept, got, False)

        got, out = block_of(always, cross_steps, flag, *cross_g)
        flag = after(flag, out)

        def down_steps(out, keys, flag, down_w, slope, *operands):
            cross_far = cross.to_chip(out)
            back_keys = tuple(to_encoder(key) for key in keys)
            small_grad, enc_grad, enc_low, pieces = run_down(flag, *operands)
            flag = after(flag, small_grad)
            sums = beside(down, pieces, run_hidden, flag, enc_low, down_w, slope)
            return cross_far, back_keys, small_grad, enc_grad, pieces[0], sums

        cross_far, back_keys, small_grad, enc_grad, kept, sums = block_of(
            always, down_steps, out, dk, flag, down_w, slope, vec, small_grad, returned, cot, e2,
            u, dec_u,
        )
        cross_held = (cross_g[0], got, cross_far)
        enc_slope, got, out = sums
        flag = after(flag, out)

        def ffn_steps(out, kept, got, flag, small_grad, cross_held, enc_slope, *operands):
            far = down.to_chip(out)
            small_grad, pieces = run_ffn(flag, small_grad, enc_slope, back_keys)
            flag = after(flag, small_grad)
            *outs, cross_own = cross.sums(flag, *cross_held)
            flag = after(flag, *outs)
            cross_last = (*cross.along(outs), cross_own)
            sums = beside(
                ffn, pieces, run_hidden_back, flag, vec, small_grad, enc_slope, *operands
            )
            return (kept, got, far), cross_last, pieces[0], sums

        down_held, cross_last, kept, sums = block_of(
            always, ffn_steps, out, kept, got, flag, small_grad, cross_held, enc_slope, ffn_w, dq,
            first_w, x1, enc_grad, grad,
        )
        (small_grad, grad), got, ffn_out = sums
        ffn_held = (kept, got)
        flag = after(flag, ffn_out)

        def attention_steps(flag, ffn_out, down_held, *operands):
            far = ffn.to_chip(ffn_out)
            *outs, own = down.sums(flag, *down_held)
            moved = (*down.along(outs), own)
            small_grad, grad_qkv, pieces = run_attention_back(after(flag, *outs), *operands)

            def swap(flag, kept, given):
                got = mixed.to_core(given)
                return got, pair_sum(flag, kept, got, True)

            swapped = block_of(always, swap, after(flag, small_grad), *pieces)
            return moved, far, small_grad, grad_qkv, pieces[0], swapped

        down_last, ffn_far, small_grad, grad_qkv, kept, swapped = block_of(
            always, attention_steps, flag, ffn_out, down_held, offsets, small_grad, grad,
            qkv, weights, context, out_w, h1,
        )
        got, out = swapped
        flag = after(flag, small_grad, out)

        def swapped_small(small_grad, away):
            pairs = [(i, i ^ away) for i in range(devices)]
            return small_grad + lax.ppermute(small_grad, "batch", pairs)

        def last_steps(flag, out, held, mixed_held, *operands):
            far = mixed.to_chip(out)
            *outs, own = ffn.sums(flag, *held)
            moved = (*ffn.along(outs), own)
            small_grad, result, low = run_last(after(flag, *outs), *operands)

            small_grad = block_of(always, lambda s: swapped_small(s, 1), small_grad)
            outs = mixed.sums(after(flag, small_grad), *mixed_held, far)
            return outs, moved, small_grad, result, low

        (*outs, own), ffn_last, small_grad, result, low = block_of(
            always, last_steps, flag, out, (*ffn_held, ffn_far), (kept, got), vec, small_grad, grad, grad_qkv, qkv_w, rows,
            dec_u, d2, down_w, low,
        )

        moved = mixed.along(outs)
        cross_last, down_last, ffn_last = after((cross_last, down_last, ffn_last), *outs)
        back = sum(part[:, width:].astype(f32) for part in cross_last)
        back = lax.ppermute(back, "section", [(1, 0)])
        shares = [
            sum(part[:, at].astype(f32) for part in parts)
            for parts, at in (
                (cross_last, slice(0, width)),
                (ffn_last, slice(hidden, hidden + width)),
                (down_last, slice(None)),
                (ffn_last, slice(0, hidden)),
            )
        ]

        def small_steps(small_grad):
            for away in (2, 4, 8):
                small_grad = swapped_small(small_grad, away)
            return small_grad

        small_grad = block_of(always, small_steps, after(small_grad, *outs))
        shares[0] = jnp.where(on_encoder, back, shares[0])
        cs_share, cf_share, down_share, ffn_share = shares
        qkv_share, out_share, vec_share, fbias_share, table_total = pl.pallas_call(
            finish_body,
            in_specs=[SMEM] + [VMEM] * 5,
            out_specs=[VMEM] * 5,
            out_shape=[
                shape_of((width // devices, 3 * width), f32), shape_of((width // devices, width), f32),
                shape_of((7, 1, width // devices), f32), shape_of((1, hidden // devices), f32),
                shape_of((heads, 1, bucket_count), f32),
            ],
            name="finish",
        )(place[None], *moved, own, small_grad)
        vec_share = vec_share[:, 0]
        table_total = table_total[:, 0].T
    return (
        low.reshape((1, row_count, length, width)),
        result.reshape((1, row_count, length, width)),
        qkv_share[None],
        out_share[None],
        ffn_share[None],
        down_share[None],
        cf_share[None],
        cs_share[None],
        vec_share[None],
        fbias_share,
        table_total[None],
    )


def solution(mesh):
    return jax.shard_map(
        per_device,
        mesh=mesh,
        in_specs=(
            P("section", "batch", None, None),
            P("section", "batch", None, None),
            P(None, "batch", None),
            P(),
            P("section", None, None),
            P("section", None, None),
            P("section", None, None),
            P("section", None, None),
            P("section", None, None),
            P("section", None, None),
            P("section", None, None),
            P("section", None),
            P("section", None, None),
        ),
        out_specs=(
            P("section", "batch", None, None),
            P("section", "batch", None, None),
            P("section", "batch", None),
            P("section", "batch", None),
            P("section", "batch", None),
            P("section", "batch", None),
            P("section", "batch", None),
            P("section", "batch", None),
            P("section", None, "batch"),
            P("section", "batch"),
            P("section", None, None),
        ),
        check_vma=False,
    )
```

```python
import functools

import jax
import jax.numpy as jnp
from jax import lax
from jax.experimental import pallas as pl
from jax.experimental.pallas import tpu as pltpu
from jax.sharding import PartitionSpec as P

norm_epsilon = 1e-05
masked_score = -1e30
half_root = 0.7071067811865476
density_scale = 0.3989422804014327
tile = 768
broad = 1536
chunk = 256
spare_bytes = 8 * 1024 * 1024
all_bytes = 62 * 1024 * 1024

f32 = jnp.float32
bf16 = jnp.bfloat16
ANY = pl.BlockSpec(memory_space=pl.ANY)
SMEM = pl.BlockSpec(memory_space=pltpu.SMEM)
VMEM = pl.BlockSpec(memory_space=pltpu.VMEM)


def mm(left, right):
    return jnp.dot(left, right, preferred_element_type=f32)


def mm_nt(left, right):
    return lax.dot_general(left, right, (((1,), (1,)), ((), ())), preferred_element_type=f32)


def mm_tn(left, right):
    return lax.dot_general(left, right, (((0,), (0,)), ((), ())), preferred_element_type=f32)


def mean_of(values):
    return jnp.sum(values, axis=-1, keepdims=True) * (1.0 / values.shape[-1])


def normalised(values):
    centre = values - mean_of(values)
    rate = lax.rsqrt(mean_of(centre * centre) + norm_epsilon)
    return centre * rate, rate


def each_rows(count, body):
    @pl.loop(0, count // chunk)
    def _(step):
        body(pl.ds(pl.multiple_of(step * chunk, chunk), chunk))


def each_tile(count, body, width=tile):
    if count == width:
        body(pl.ds(0, width))
        return

    @pl.loop(0, count // width)
    def _(step):
        body(pl.ds(pl.multiple_of(step * width, width), width))


def norm_forward(source, gain, offset, target, also=None):
    def rows(at):
        unit, _ = normalised(source[at, :].astype(f32))
        normed = unit * gain + offset
        target[at, :] = normed.astype(target.dtype)

    each_rows(source.shape[0], rows)


def norm_backward(
    source, grad_normed, gain, upstream, target, gain_sum, offset_sum, low=None
):
    gain_sum[...] = jnp.zeros_like(gain_sum)
    offset_sum[...] = jnp.zeros_like(offset_sum)

    def rows(at):
        unit, rate = normalised(source[at, :].astype(f32))
        upper = grad_normed[at, :]
        product = upper * unit
        gain_sum[...] += jnp.sum(product.reshape(-1, 8, product.shape[1]), axis=0)
        offset_sum[...] += jnp.sum(upper.reshape(-1, 8, upper.shape[1]), axis=0)
        scaled = upper * gain
        inner = mean_of(scaled)
        along = mean_of(product * gain)
        result = rate * (scaled - inner - unit * along)
        if upstream is not None:
            result = result + upstream[at, :].astype(f32)
        target[at, :] = result
        if low is not None:
            low[at, :] = result.astype(bf16)

    each_rows(source.shape[0], rows)


def column_sum(partial):
    return jnp.sum(partial[...], axis=0, keepdims=True)


def lower_lanes(shape):
    return lax.broadcasted_iota(jnp.int32, shape, 1) < shape[1] // 2


def split_pair(block):
    lower = lower_lanes(block.shape)
    zero = jnp.zeros_like(block)
    return jnp.concatenate([jnp.where(lower, block, zero), jnp.where(lower, zero, block)], axis=0)


def join_pair(stacked):
    rows = stacked.shape[0] // 2
    lower = lower_lanes((rows, stacked.shape[1]))
    return jnp.where(lower, stacked[:rows], stacked[rows:])


def attend_pair(queries, key_rows, values, additions, scale):
    length = queries.shape[0]
    scores = mm_nt((queries * scale).astype(bf16), split_pair(key_rows))
    parts = []
    for head in range(2):
        part = scores[:, head * length : (head + 1) * length] + additions[head]
        exponent = jnp.exp(part - jnp.max(part, axis=-1, keepdims=True))
        parts.append(exponent * (1.0 / jnp.sum(exponent, axis=-1, keepdims=True)))
    weights = jnp.concatenate(parts, axis=1).astype(bf16)
    return weights, mm(weights, split_pair(values))


def attend_pair_back(weights, queries, key_rows, values, context, grad_context, scale):
    length = queries.shape[0]
    grad_weights = mm_nt(grad_context, split_pair(values))
    product = grad_context.astype(f32) * context.astype(f32)
    lower = lower_lanes(product.shape)
    parts = []
    for head in range(2):
        at = slice(head * length, (head + 1) * length)
        own = jnp.where(lower, product, 0.0) if head == 0 else jnp.where(lower, 0.0, product)
        centred = jnp.sum(own, axis=-1, keepdims=True)
        parts.append(weights[:, at].astype(f32) * (grad_weights[:, at] - centred))
    grad_raw = jnp.concatenate(parts, axis=1).astype(bf16)
    grad_queries = mm(grad_raw, split_pair(key_rows)) * scale
    grad_keys = join_pair(mm_tn(grad_raw, queries)) * scale
    grad_values = join_pair(mm_tn(weights, grad_context))
    return grad_queries, grad_keys, grad_values, parts


def same_sentence(query_ids, key_ids):
    length = query_ids.shape[1]
    across = jnp.broadcast_to(key_ids.astype(f32), (length, length))
    down = jnp.broadcast_to(query_ids.astype(f32), (length, length)).T
    return across == down


class Move:
    def __init__(self, sources, target, semaphores):
        self.sources, self.target, self.semaphores = sources, target, semaphores

    def copies(self, sources):
        if not isinstance(sources, tuple):
            yield pltpu.make_async_copy(sources, self.target, self.semaphores[0])
            return
        rows = self.target.shape[0] // len(sources)
        for part, source in enumerate(sources):
            target = self.target.at[pl.ds(part * rows, rows)]
            yield pltpu.make_async_copy(source, target, self.semaphores[part])

    def start(self, sources=None):
        for copy in self.copies(self.sources if sources is None else sources):
            copy.start()

    def wait(self, sources=None):
        for copy in self.copies(self.sources if sources is None else sources):
            copy.wait()


class Mover:
    def __init__(self, semaphores):
        self.semaphores = semaphores
        self.used = 0

    def note(self, source, target):
        count = len(source) if isinstance(source, tuple) else 1
        semaphores = [self.semaphores.at[self.used + part] for part in range(count)]
        self.used += count
        return Move(source, target, semaphores)

    def start(self, source, target):
        move = self.note(source, target)
        move.start()
        return move


def wait_all(moves):
    for move in moves:
        move.wait()


def gelu_parts(hidden):
    share = 0.5 + 0.5 * lax.erf(hidden * half_root)
    slope = share + hidden * (density_scale * jnp.exp(hidden * hidden * -0.5))
    return hidden * share, slope


def first_body(
    heads, row, flag, ids, offsets, table, vectors, in_bias, rows_in, cot_in, qkv_in, out_in, ffn_in,
    down_in, first_in,
    x1_out, h1_out, qkv_out, weights_out, context_out, h2_out, u_out, slope_out, e2_out, low_out,
    hc_out, qc_out,
    rows, qkv_w, out_w, ffn_w, down_w, first_w, cot, normed, qkv, weights, context, x1, h2, u, slope,
    e2, low, bias_rows, mask, context_wide, loads, stores,
):
    length, width = rows.shape
    hidden_width = ffn_w.shape[1]
    on_encoder = flag[0] == 1
    own_rows = pl.ds(row * length, length)
    load = Mover(loads)
    store = Mover(stores)
    got_rows = load.start(rows_in.at[own_rows], rows)
    got_qkv = load.start(qkv_in, qkv_w)
    got_out = load.start(out_in, out_w)
    got_down = load.note(down_in, down_w)
    got_ffn = load.note(ffn_in, ffn_w)
    got_first = load.note(first_in, first_w)
    got_cot = load.note(cot_in.at[own_rows], cot)

    @pl.when(on_encoder)
    def _():
        got_ffn.start()
        got_down.start()

    @pl.when(jnp.logical_not(on_encoder))
    def _():
        got_first.start()
        got_cot.start()
        got_down.start()

    one_hot = (offsets[...] == lax.broadcasted_iota(jnp.int32, (table.shape[1], 2 * length), 0)).astype(f32)
    by_offset = lax.dot_general(
        table[...], one_hot, (((1,), (0,)), ((), ())), precision=lax.Precision.HIGHEST,
        preferred_element_type=f32,
    )
    bias_rows[...] = pltpu.roll(by_offset, length + 1, 1)
    own_group = jnp.where(on_encoder, 0, 1)
    ahead = lax.broadcasted_iota(jnp.int32, (length, length), 0) >= lax.broadcasted_iota(
        jnp.int32, (length, length), 1
    )
    own = ids[pl.ds(own_group, 1), row, :]
    allowed = same_sentence(own, own) & (ahead | on_encoder)
    mask[...] = jnp.where(allowed, 0.0, masked_score)

    got_rows.wait()
    norm_forward(rows, vectors[0], vectors[1], normed)
    got_qkv.wait()

    def project(at):
        qkv[:, at] = mm(normed[...], qkv_w[:, at]).astype(bf16)

    each_tile(3 * width, project)
    out_copies = [store.start(normed, h1_out), store.start(qkv, qkv_out)]
    scale = (width // heads) ** (-0.5)

    @pl.loop(0, heads // 2, unroll=heads // 2)
    def _(pair):
        lanes = pl.multiple_of(pair * 128, 128)
        additions = []
        for head in range(2):
            spread = jnp.broadcast_to(bias_rows[pl.ds(pair * 2 + head, 1), :], (length, 2 * length))
            skewed = pltpu.roll(spread, 0, 1, stride=1, stride_axis=0)
            additions.append(skewed[:, :length] + mask[...])
        part, mixed = attend_pair(
            qkv[:, pl.ds(lanes, 128)],
            qkv[:, pl.ds(width + lanes, 128)],
            qkv[:, pl.ds(2 * width + lanes, 128)],
            additions,
            scale,
        )
        weights[0, pair] = part
        context_wide[:, pl.ds(lanes, 128)] = mixed
        context[:, pl.ds(lanes, 128)] = mixed.astype(bf16)

    out_copies += [store.start(weights, weights_out), store.start(context_wide, context_out)]
    got_out.wait()
    x1[...] = rows[...].astype(f32) + mm(context[...], out_w[...])
    out_copies.append(store.start(x1, x1_out))

    @pl.when(on_encoder)
    def _():
        norm_forward(x1, vectors[2], vectors[3], h2)
        got_ffn.wait()

        def feed(at):
            value, rate = gelu_parts(mm(h2[...], ffn_w[:, at]) + in_bias[:, at])
            u[:, at] = value.astype(bf16)
            slope[:, at] = rate.astype(bf16)

        each_tile(hidden_width, feed, broad)
        copies = [store.start(h2, h2_out), store.start(u, u_out), store.start(slope, slope_out)]
        got_down.wait()
        e2[...] = x1[...] + (mm(u[...], down_w[...]) + vectors[6])
        copies.append(store.start(e2, e2_out))
        norm_forward(e2, vectors[4], vectors[5], low)
        copies.append(store.start(low, low_out))
        wait_all(copies)

    @pl.when(jnp.logical_not(on_encoder))
    def _():
        norm_forward(x1, vectors[2], vectors[3], h2)
        got_first.wait()
        low[...] = mm(h2[...], first_w[...]).astype(bf16)
        copies = [store.start(h2, hc_out), store.start(low, qc_out)]
        got_down.wait()
        got_cot.wait()

        def back(at):
            slope[:, at] = mm_nt(cot[...], down_w[at, :]).astype(bf16)

        each_tile(hidden_width, back)
        copies.append(store.start(slope, slope_out))
        wait_all(copies)

    wait_all(out_copies)


def cross_body(
    heads, row, flag, ids, vectors, in_bias, small_in,
    memory_in, sent_in, other_in, second_in, x1_in, qc_in, cot_in, ffn_in, slope_in, earlier,
    small_out, h2_out, u_out, slope_out, d2_out, grad_out, cc_out, dq_out, dk_out, dv_out, dm_out,
    low_out, pieces, memory, keys_w, values_w, second_w, x1, qc, cot, ffn_w, keys, values, weights, cc, d2, h2, u,
    slope, grad_normed, grad, grad_low, dq, dk, dv, dm, mask, gain_sum, offset_sum, cc_wide, *rest
):
    *products, loads, stores = rest
    length, width = memory.shape
    hidden_width = ffn_w.shape[1]
    small_out[...] = jnp.zeros_like(small_out) if row == 0 else small_in[...]

    @pl.when(flag[0] == 0)
    def _():
        load = Mover(loads)
        store = Mover(stores)
        got_memory = load.start(memory_in, memory)
        got_keys = load.note(sent_in, keys_w)
        got_values = load.note(sent_in, values_w)
        for core, (keys_in, values_in) in enumerate(((sent_in, other_in), (other_in, sent_in))):

            @pl.when(flag[1] == core)
            def _(keys_in=keys_in, values_in=values_in):
                got_keys.start(keys_in)
                got_values.start(values_in)

        got_query = load.start(qc_in, qc)
        got_second = [load.start(second_in, second_w), load.start(x1_in, x1)]
        got_ffn = [load.start(ffn_in, ffn_w), load.start(slope_in, slope)]
        got_cot = load.start(cot_in.at[pl.ds(row * length, length)], cot)
        if products:
            got_earlier = []
            for sources, whole in zip(earlier, products):
                if not sources:
                    continue
                rows = len(sources) * length
                got_earlier.append(load.start(tuple(sources), whole.at[pl.ds(0, rows)]))
        mask[...] = jnp.where(same_sentence(ids[1:2, row, :], ids[0:1, row, :]), 0.0, masked_score)
        got_memory.wait()
        got_keys.wait()
        keys[...] = mm(memory[...], keys_w[...]).astype(bf16)
        got_values.wait()
        values[...] = mm(memory[...], values_w[...]).astype(bf16)
        got_query.wait()
        scale = (width // heads) ** (-0.5)

        @pl.loop(0, heads // 2, unroll=3)
        def _(pair):
            lanes = pl.ds(pl.multiple_of(pair * 128, 128), 128)
            part, mixed = attend_pair(
                qc[:, lanes], keys[:, lanes], values[:, lanes], [mask[...], mask[...]], scale
            )
            weights[0, pair] = part
            cc_wide[:, lanes] = mixed
            cc[:, lanes] = mixed.astype(bf16)

        copies = [store.start(cc, cc_out)]
        wait_all(got_second)
        d2[...] = x1[...] + mm(cc[...], second_w[...])
        copies.append(store.start(d2, d2_out))
        norm_forward(d2, vectors[4], vectors[5], h2)
        copies.append(store.start(h2, h2_out))
        wait_all(got_ffn)

        def feed(at):
            value, rate = gelu_parts(mm(h2[...], ffn_w[:, at]) + in_bias[:, at])
            u[:, at] = value.astype(bf16)
            slope[:, at] = (slope[:, at].astype(f32) * rate).astype(bf16)

        each_tile(hidden_width, feed, broad)
        copies += [store.start(u, u_out), store.start(slope, slope_out)]
        grad_normed[...] = mm_nt(slope[...], ffn_w[...])
        got_cot.wait()
        norm_backward(
            d2, grad_normed, vectors[4], cot, grad, gain_sum, offset_sum, grad_low
        )
        small_out[4:5, :] += column_sum(gain_sum)
        small_out[5:6, :] += column_sum(offset_sum)
        copies += [store.start(grad, grad_out), store.start(grad_low, low_out)]
        dm[...] = mm_nt(grad_low[...], second_w[...]).astype(bf16)

        @pl.loop(0, heads // 2, unroll=3)
        def _(pair):
            lanes = pl.ds(pl.multiple_of(pair * 128, 128), 128)
            grad_q, grad_k, grad_v, _ = attend_pair_back(
                weights[0, pair], qc[:, lanes], keys[:, lanes], values[:, lanes], cc_wide[:, lanes],
                dm[:, lanes], scale,
            )
            dq[:, lanes] = grad_q.astype(bf16)
            dk[:, lanes] = grad_k.astype(bf16)
            dv[:, lanes] = grad_v.astype(bf16)

        copies += [store.start(dq, dq_out), store.start(dk, dk_out), store.start(dv, dv_out)]
        dm[...] = (mm_nt(dk[...], keys_w[...]) + mm_nt(dv[...], values_w[...])).astype(bf16)
        copies.append(store.start(dm, dm_out))
        if products:
            *wholes, cross_g = products
            hc, *others = wholes
            own = pl.ds(hc.shape[0] - length, length)
            for whole, part in zip(others, (dq, cc, grad_low, memory, dk, dv)):
                whole[own, :] = part[...]
            wait_all(got_earlier)
            hc, dq_all, cc_all, low_all, memory_all, dk_all, dv_all = wholes
            query, out, key, value = spans(4 * width, width)
            cross_g[:, query] = mm_tn(hc[...], dq_all[...]).astype(bf16)
            cross_g[:, out] = mm_tn(cc_all[...], low_all[...]).astype(bf16)
            copies += put_columns(store, cross_g, pieces, flag[1], pl.ds(0, 2 * width))
            cross_g[:, key] = mm_tn(memory_all[...], dk_all[...]).astype(bf16)
            cross_g[:, value] = mm_tn(memory_all[...], dv_all[...]).astype(bf16)
            copies += put_columns(store, cross_g, pieces, flag[1], pl.ds(2 * width, 2 * width))
        wait_all(copies)


def put_rows(store, stage, targets, core, rows):
    if len(targets) == 1:
        return [store.start(stage.at[rows], targets[0].at[rows])]
    depth = targets[0].shape[1]
    copies = []
    for chip in range(rows.start // (2 * depth), (rows.start + rows.size) // (2 * depth)):
        for target, which in zip(targets, (core, 1 - core)):
            at = pl.multiple_of((2 * chip + which) * depth, depth)
            copies.append(store.start(stage.at[pl.ds(at, depth)], target.at[chip]))
    return copies


def put_columns(store, stage, targets, core, columns):
    if len(targets) == 1:
        return [store.start(stage.at[:, columns], targets[0].at[:, columns])]
    chips, depth = targets[0].shape[0], targets[0].shape[1]
    copies = []
    for chip in range(chips):
        for target, which in zip(targets, (core, 1 - core)):
            at = pl.multiple_of((2 * chip + which) * depth, depth)
            copies.append(
                store.start(stage.at[pl.ds(at, depth), columns], target.at[chip, :, columns])
            )
    return copies


def spans(count, width):
    return [pl.ds(start, width) for start in range(0, count, width)]


def down_body(flag, vectors, small_in, dm_in, cot_in, e2_in, enc_u_in, dec_u_in, *rest):
    small_out, grad_out, low_out, *rest = rest
    count = len(rest) - 11
    outs = rest[:count]
    dm, cot, e2, u, grad, grad_low, down_g, gain_sum, offset_sum, loads, stores = rest[count:]
    hidden_width, width = u.shape[1], cot.shape[1]
    small_out[...] = small_in[...]
    load = Mover(loads)
    store = Mover(stores)
    got_cot = load.start(cot_in, cot)
    got_u = load.note(enc_u_in, u)
    moved = [load.note(dm_in, dm), load.note(e2_in, e2)]
    kept = [store.note(grad, grad_out), store.note(grad_low, low_out)]

    @pl.when(flag[0] == 1)
    def _():
        for copy in moved:
            copy.start()
        got_cot.wait()
        wait_all(moved)
        got_u.start(enc_u_in)

        def total(at):
            grad[at, :] = dm[at, :].astype(f32) + cot[at, :].astype(f32)

        each_rows(grad.shape[0], total)
        norm_backward(e2, grad, vectors[4], None, grad, gain_sum, offset_sum, grad_low)
        small_out[4:5, :] = column_sum(gain_sum)
        small_out[5:6, :] = column_sum(offset_sum)
        for copy in kept:
            copy.start()

    @pl.when(flag[0] == 0)
    def _():
        got_u.start(dec_u_in)
        got_cot.wait()
        grad_low[...] = cot[...]

    got_u.wait()
    copies = []
    for rows in spans(hidden_width, tile):
        down_g[rows, :] = mm_tn(u[:, rows], grad_low[...]).astype(bf16)
        copies += put_rows(store, down_g, outs, flag[1], rows)
    small_out[6:7, :] = jnp.sum(grad_low[...].astype(f32), axis=0, keepdims=True)
    wait_all(copies)

    @pl.when(flag[0] == 1)
    def _():
        wait_all(kept)


def hidden_body(flag, low_in, down_in, slope_in, slope_out, grad_low, down_w, slope, loads, stores):
    @pl.when(flag[0] == 1)
    def _():
        load = Mover(loads)
        store = Mover(stores)
        hidden_width = slope.shape[1]
        got_low = load.start(low_in, grad_low)
        got_slope = load.start(slope_in, slope)
        got_down = [
            load.start(down_in.at[rows], down_w.at[rows]) for rows in spans(hidden_width, tile)
        ]
        got_low.wait()
        got_slope.wait()
        copies = []
        for at, got in zip(spans(hidden_width, tile), got_down):
            got.wait()
            part = mm_nt(grad_low[...], down_w[at, :]) * slope[:, at].astype(f32)
            slope[:, at] = part.astype(bf16)
            copies.append(store.start(slope.at[:, at], slope_out.at[:, at]))
        wait_all(copies)


def ffn_body(flag, small_in, enc_ins, dec_ins, *rest):
    small_out, *rest = rest
    count = len(rest) - 5
    outs = rest[:count]
    slope, h2, ffn_g, loads, stores = rest[count:]
    width, hidden_width = h2.shape[1], slope.shape[1]
    small_out[...] = small_in[...]
    load = Mover(loads)
    store = Mover(stores)
    moves = [load.note(source, target) for source, target in zip(dec_ins, (h2, slope))]
    for which, ins in enumerate((dec_ins, enc_ins)):

        @pl.when(flag[0] == which)
        def _(ins=ins):
            for move, source in zip(moves, ins):
                move.start(source)
            for move, source in zip(moves, ins):
                move.wait(source)

    copies = []
    for step, at in enumerate(spans(hidden_width, tile)):
        ffn_g[:, at] = mm_tn(h2[...], slope[:, at]).astype(bf16)
        if step % 2 == 1:
            both = pl.ds(at.start - tile, 2 * tile)
            copies += put_columns(store, ffn_g, outs, flag[1], both)
    for part in range(hidden_width // width):
        values = slope[:, part * width : (part + 1) * width].astype(f32)
        small_out[8 + part : 9 + part, :] = jnp.sum(values, axis=0, keepdims=True)
    wait_all(copies)


def hidden_back_body(
    flag, vectors, small_in, slope_in, ffn_in, dq_in, first_in, x1_in, enc_grad_in, dec_grad_in,
    small_out, grad_out,
    slope, ffn_w, dq, first_w, x1, grad, grad_normed, gain_sum, offset_sum, loads, stores,
):
    width = x1.shape[1]
    small_out[...] = small_in[...]
    load = Mover(loads)
    store = Mover(stores)
    got_x1 = load.note(x1_in, x1)
    got_grad = load.note(dec_grad_in, grad)

    @pl.when(flag[0] == 1)
    def _():
        got = [load.start(slope_in, slope), load.start(ffn_in, ffn_w)]
        got_x1.start()
        got_grad.start(enc_grad_in)
        wait_all(got)
        grad_normed[...] = mm_nt(slope[...], ffn_w[...])
        got_grad.wait(enc_grad_in)

    @pl.when(flag[0] == 0)
    def _():
        got = [load.start(dq_in, dq), load.start(first_in, first_w)]
        got_x1.start()
        got_grad.start(dec_grad_in)
        wait_all(got)
        grad_normed[...] = mm_nt(dq[...], first_w[...])
        got_grad.wait()

    got_x1.wait()
    norm_backward(x1, grad_normed, vectors[2], grad, grad, gain_sum, offset_sum)
    stored = store.start(grad, grad_out)
    small_out[2:3, :] = column_sum(gain_sum)
    small_out[3:4, :] = column_sum(offset_sum)
    stored.wait()


def attention_back_body(
    heads, flag, grad_in, qkv_in, weights_in, context_in, outw_in, h1_in, *rest
):
    grad_qkv_out, scores_out, *rest = rest
    count = len(rest) - 14
    outs = rest[:count]
    (
        grad, qkv, weights, context, out_w, h1, grad_low, grad_context, grad_qkv, mixed_g,
        grad_scores, context_low, loads, stores,
    ) = rest[count:]
    width = context.shape[1]
    row_count, length = weights.shape[0], weights.shape[2]
    load = Mover(loads)
    store = Mover(stores)
    got_grad = [load.start(grad_in, grad), load.start(outw_in, out_w)]
    got_context = load.start(context_in, context)
    got_attention = [load.start(weights_in, weights), load.start(qkv_in, qkv)]
    got_h1 = load.start(h1_in, h1)
    wait_all(got_grad)

    def lower(at):
        grad_low[at, :] = grad[at, :].astype(bf16)

    each_rows(grad.shape[0], lower)
    grad_context[...] = mm_nt(grad_low[...], out_w[...]).astype(bf16)
    got_context.wait()
    context_low[...] = context[...].astype(bf16)
    mixed_g[:, pl.ds(0, width)] = mm_tn(context_low[...], grad_low[...]).astype(bf16)
    wait_all(got_attention)
    scale = (width // heads) ** (-0.5)

    @pl.loop(0, heads // 2, unroll=3)
    def _(pair):
        lanes = pl.multiple_of(pair * 128, 128)
        totals = [None, None]
        for row in range(row_count):
            at = slice(row * length, (row + 1) * length)
            grad_q, grad_k, grad_v, parts = attend_pair_back(
                weights[row, pair],
                qkv[at, pl.ds(lanes, 128)],
                qkv[at, pl.ds(width + lanes, 128)],
                qkv[at, pl.ds(2 * width + lanes, 128)],
                context[at, pl.ds(lanes, 128)],
                grad_context[at, pl.ds(lanes, 128)],
                scale,
            )
            grad_qkv[at, pl.ds(lanes, 128)] = grad_q.astype(bf16)
            grad_qkv[at, pl.ds(width + lanes, 128)] = grad_k.astype(bf16)
            grad_qkv[at, pl.ds(2 * width + lanes, 128)] = grad_v.astype(bf16)
            totals = [p if t is None else t + p for t, p in zip(totals, parts)]
        for head in range(2):
            grad_scores[pair * 2 + head] = totals[head]

    got_h1.wait()
    copies = [store.start(grad_qkv, grad_qkv_out), store.start(grad_scores, scores_out)]
    for step, at in enumerate(spans(3 * width, width)):
        mixed_g[:, pl.ds(width + at.start, width)] = mm_tn(h1[...], grad_qkv[:, at]).astype(bf16)
        if step != 1:
            both = pl.ds(0 if step == 0 else 2 * width, 2 * width)
            copies += put_columns(store, mixed_g, outs, flag[1], both)
    wait_all(copies)


def sum_diagonals(grid):
    length = grid.shape[0]
    padded = jnp.concatenate([grid, jnp.zeros((length, length), f32)], axis=1)
    folded = padded[0:8, :]
    for block in range(1, length // 8):
        folded = folded + pltpu.roll(
            padded[block * 8 : (block + 1) * 8, :], 2 * length - block * 8, 1
        )
    line = folded[0:1, :]
    for sub in range(1, 8):
        line = line + pltpu.roll(folded[sub : sub + 1, :], 2 * length - sub, 1)
    return pltpu.roll(line, length - 1, 1)


def last_body(
    flag, offsets, vectors, small_in, grad_in, grad_qkv_in, qkvw_in, rows_in, scores_in, u_in, d2_in,
    down_in, low_in,
    small_out, result_out, low_out,
    grad, grad_qkv, qkv_w, rows, grad_normed, grad_scores, diagonals, one_hot, u, d2, down_w, low,
    gain_sum, offset_sum, loads, stores,
):
    small_out[...] = small_in[...]
    heads, bucket_count = grad_scores.shape[0], one_hot.shape[0]
    load = Mover(loads)
    store = Mover(stores)
    got = [load.start(grad_qkv_in, grad_qkv), load.start(qkvw_in, qkv_w)]
    got_rows = [load.start(rows_in, rows), load.start(grad_in, grad)]
    got_scores = load.start(scores_in, grad_scores)
    stored_low = store.note(low, low_out)
    got_low = load.note(low_in, low)

    @pl.when(flag[0] == 1)
    def _():
        got_low.start()

    wait_all(got)
    grad_normed[...] = mm_nt(grad_qkv[...], qkv_w[...])
    wait_all(got_rows)
    norm_backward(rows, grad_normed, vectors[0], grad, grad, gain_sum, offset_sum)
    small_out[0:1, :] = column_sum(gain_sum)
    small_out[1:2, :] = column_sum(offset_sum)
    stored = store.start(grad, result_out)

    @pl.when(flag[0] == 1)
    def _():
        got_low.wait()
        stored_low.start()

    @pl.when(flag[0] == 0)
    def _():
        wait_all([load.start(u_in, u), load.start(d2_in, d2), load.start(down_in, down_w)])
        value = d2[...] + (mm(u[...], down_w[...]) + vectors[6])
        low[...] = value.astype(bf16)
        stored_low.start()

    got_scores.wait()

    @pl.loop(0, heads)
    def _(head):
        diagonals[pl.ds(head, 1), :] = sum_diagonals(grad_scores[head])

    one_hot[...] = (offsets[...] == lax.broadcasted_iota(jnp.int32, one_hot.shape, 0)).astype(f32)
    small_out[pl.ds(16, heads), pl.ds(0, bucket_count)] = lax.dot_general(
        diagonals[...], one_hot[...], (((1,), (1,)), ((), ())), precision=lax.Precision.HIGHEST,
        preferred_element_type=f32,
    )
    stored.wait()
    stored_low.wait()


def pair_sum_body(everywhere, flag, kept_in, got_in, out, kept, got, total, loads, stores):
    @pl.when(jnp.logical_or(flag[0] == 0, everywhere))
    def _():
        load = Mover(loads)
        store = Mover(stores)
        blocks = out.shape[0]
        ready = []
        for step in range(blocks):
            block = 2 * step + 1 - flag[2]
            ready.append(
                (load.start(kept_in.at[block], kept.at[step]), load.start(got_in.at[block], got.at[step]))
            )
        copies = []
        for step in range(blocks):
            wait_all(ready[step])
            total[step] = (kept[step].astype(f32) + got[step].astype(f32)).astype(bf16)
            copies.append(store.start(total.at[step], out.at[step]))
        wait_all(copies)


def pair_sum(flag, kept, got, everywhere):
    chips, depth, width = kept.shape
    part = (chips // 2, depth, width)
    return run_kernel(
        functools.partial(pair_sum_body, everywhere),
        (flag, kept, got),
        [SMEM, ANY, ANY],
        [shape_of(part, bf16)],
        [ANY],
        [(part, bf16)] * 3,
        chips, chips // 2, "pair_sum",
    )[0]


def chip_sum_body(
    everywhere, flag, kept_in, got_in, far_in, first_out, second_out, third_out, own_out,
    kept, got, far, total, own, loads, stores,
):
    @pl.when(jnp.logical_or(flag[0] == 0, everywhere))
    def _():
        load = Mover(loads)
        store = Mover(stores)
        ready = []
        for step in range(4):
            place = lax.rem(flag[3] + step + 1, 4)
            block = 2 * place + flag[2]
            ready.append(
                [
                    load.start(kept_in.at[block], kept.at[step]),
                    load.start(got_in.at[block], got.at[step]),
                    load.start(far_in.at[place], far.at[step]),
                ]
            )
        copies = []
        for step, out in enumerate((first_out, second_out, third_out, own_out)):
            wait_all(ready[step])
            value = kept[step].astype(f32) + got[step].astype(f32) + far[step].astype(f32)
            if step < 3:
                total[step] = value.astype(bf16)
                copies.append(store.start(total.at[step], out))
            else:
                own[...] = value
                copies.append(store.start(own, out))
        wait_all(copies)


def chip_sum(flag, kept, got, far, everywhere):
    _, depth, width = kept.shape
    one = (depth, width)
    return run_kernel(
        functools.partial(chip_sum_body, everywhere),
        (flag, kept, got, far),
        [SMEM, ANY, ANY, ANY],
        [shape_of(one, bf16)] * 3 + [shape_of(one, f32)],
        [ANY] * 4,
        [((4,) + one, bf16)] * 3 + [((3,) + one, bf16), (one, f32)],
        12, 4, "chip_sum",
    )


def finish_body(
    place, first, second, third, own, small, qkv_out, out_out, vec_out, fbias_out, table_out
):
    width = out_out.shape[1]
    total = own[...]
    for part in (first, second, third):
        total = total + part[...].astype(f32)
    out_out[...] = total[:, :width]
    qkv_out[...] = total[:, width:]
    share = vec_out.shape[2]
    turned = pltpu.roll(small[0:8, :], lax.rem(width - place[0] * share, width), 1)
    for row in range(vec_out.shape[0]):
        vec_out[row] = turned[row : row + 1, :share]
    share = fbias_out.shape[1]
    per_row = width // share
    row = small[pl.ds(8 + lax.div(place[0], per_row), 1), :]
    turned = pltpu.roll(row, lax.rem(width - lax.rem(place[0], per_row) * share, width), 1)
    fbias_out[...] = turned[:, :share]
    for head in range(table_out.shape[0]):
        table_out[head] = small[16 + head : 17 + head, : table_out.shape[2]]


def shape_of(dims, dtype):
    return jax.ShapeDtypeStruct(tuple(dims), dtype)


def size_of(dims, dtype):
    total = jnp.dtype(dtype).itemsize
    for dim in dims:
        total *= dim
    return total


def run_kernel(
    body, operands, places, outs, out_places, scratch, loads, stores, name, alone=False
):
    held = sum(size_of(dims, dtype) for dims, dtype in scratch)
    flat, form = jax.tree.flatten(operands)
    flat_places = [
        place for place, operand in zip(places, operands, strict=True) for _ in jax.tree.leaves(operand)
    ]

    flat_outs, out_form = jax.tree.flatten(outs)
    held_at = len(flat) + len(flat_outs)

    def kernel(*refs):
        results = out_form.unflatten(refs[len(flat) : held_at])
        return body(*form.unflatten(refs[: len(flat)]), *results, *refs[held_at:])

    results = pl.pallas_call(
        kernel,
        in_specs=flat_places,
        out_specs=out_places,
        out_shape=flat_outs,
        scratch_shapes=[pltpu.VMEM(dims, dtype) for dims, dtype in scratch]
        + [pltpu.SemaphoreType.DMA((loads,)), pltpu.SemaphoreType.DMA((stores,))],
        compiler_params=pltpu.CompilerParams(
            vmem_limit_bytes=all_bytes if alone else held + spare_bytes
        ),
        cost_estimate=pl.CostEstimate(flops=1, bytes_accessed=1, transcendentals=0),
        name=name,
    )(*flat)
    return out_form.unflatten(results)


def after(value, *others):
    return lax.optimization_barrier((value,) + others)[0]


def block_of(always, steps, *operands):
    shapes = jax.eval_shape(steps, *operands)

    def blank(*_):
        return jax.tree.map(lambda leaf: jnp.zeros(leaf.shape, leaf.dtype), shapes)

    return lax.cond(always, steps, blank, *operands)


class Ring:
    def __init__(self, devices, everywhere):
        self.devices = devices
        self.everywhere = everywhere

    def send(self, shard, moved):
        pairs = [(i, moved(i)) for i in range(self.devices)]
        if self.everywhere:
            return lax.ppermute(shard, "batch", pairs)
        pairs = [(self.devices + i, self.devices + j) for i, j in pairs]
        return lax.ppermute(shard, ("section", "batch"), pairs)

    def to_core(self, given):
        return self.send(given, lambda i: i ^ 1)

    def to_chip(self, out):
        return self.send(out, lambda i: i ^ 2)

    def sums(self, flag, *held):
        return chip_sum(flag, *held, self.everywhere)

    def along(self, outs):
        return [
            self.send(out, lambda i, away=away: (i + 4 * away) % 16)
            for away, out in zip((2, 1, 3), (outs[1], outs[0], outs[2]))
        ]


def per_device(
    inputs, cotangent, segments, buckets, qkv_weight, out_weight, in_weight, down_weight,
    cross_first, cross_second, vectors, ffn_bias, position_table,
):
    row_count, length, width = inputs.shape[1:]
    heads = position_table.shape[2]
    bucket_count = position_table.shape[1]
    hidden = in_weight.shape[2]
    tokens = row_count * length
    pairs = heads // 2
    on_encoder = lax.axis_index("section") == 0
    place = lax.axis_index("batch")
    core = lax.rem(place, 2)
    devices = lax.axis_size("batch")
    by_chip = devices == 16
    always = place < devices
    flag = jnp.stack(
        [on_encoder.astype(jnp.int32), core, lax.rem(lax.div(place, 2), 2), lax.div(place, 4)]
    )
    offsets = jnp.pad(buckets, (0, 1), constant_values=-1)[None]
    table = jnp.transpose(position_table, (2, 0, 1))[:, 0]
    rows = inputs.reshape(tokens, width)
    cot = cotangent.reshape(tokens, width)
    qkv_w, out_w, ffn_w, down_w = qkv_weight[0], out_weight[0], in_weight[0], down_weight[0]
    first_w, second_w = cross_first[0], cross_second[0]
    vec = jnp.transpose(vectors, (1, 0, 2))
    fbias = ffn_bias

    tw, th = (tokens, width), (tokens, hidden)
    wide = (tokens, 3 * width)
    square = (row_count, pairs, length, 2 * length)
    row_tw, row_th, row_wide = (length, width), (length, hidden), (length, 3 * width)
    row_square = (1, pairs, length, 2 * length)
    small = (32, width)

    sent = lax.ppermute(jnp.where(core == 0, first_w, second_w), "section", [(0, 1)])

    def piece(depth_rows, columns):
        if not by_chip:
            return [shape_of((depth_rows, columns), bf16)]
        return [shape_of((devices // 2, depth_rows // devices, columns), bf16)] * 2

    down_piece, ffn_piece = piece(hidden, width), piece(width, hidden)
    mixed_piece = piece(width, 4 * width)
    count = len(down_piece)
    share_copies = devices if by_chip else 1
    def run_first(row, flag):
        return run_kernel(
            functools.partial(first_body, heads, row),
            (flag, segments, offsets, table, vec, fbias, rows, cot, qkv_w, out_w, ffn_w,
             down_w, first_w),
            [SMEM] + [VMEM] * 5 + [ANY] * 7,
            [
                shape_of(row_tw, f32), shape_of(row_tw, bf16), shape_of(row_wide, bf16),
                shape_of(row_square, bf16), shape_of(row_tw, f32), shape_of(row_tw, bf16),
                shape_of(row_th, bf16), shape_of(row_th, bf16), shape_of(row_tw, f32),
                shape_of(row_tw, bf16), shape_of(row_tw, bf16), shape_of(row_tw, bf16),
            ],
            [ANY] * 12,
            [
                (row_tw, bf16), ((width, 3 * width), bf16), ((width, width), bf16),
                ((width, hidden), bf16), ((hidden, width), bf16), ((width, width), bf16),
                (row_tw, bf16), (row_tw, bf16), (row_wide, bf16), (row_square, bf16), (row_tw, bf16),
                (row_tw, f32), (row_tw, bf16), (row_th, bf16), (row_th, bf16), (row_tw, f32),
                (row_tw, bf16), ((heads, 2 * length), f32), ((length, length), f32),
                (row_tw, f32),
            ],
            7, 13, "first", True,
        )

    def run_cross(row, flag, small_grad, memory, sent, sent_other, own, earlier):
        x1, qc, slope = own
        last_row = row == row_count - 1
        products = [(tw, bf16)] * 7 + [((width, 4 * width), bf16)] if last_row else []
        return run_kernel(
            functools.partial(cross_body, heads, row),
            (flag, segments, vec, fbias, small_grad, memory, sent, sent_other, second_w, x1, qc, cot,
             ffn_w, slope, earlier if last_row else ()),
            [SMEM] + [VMEM] * 4 + [ANY] * 10,
            [shape_of(small, f32), shape_of(row_tw, bf16), shape_of(row_th, bf16),
             shape_of(row_th, bf16), shape_of(row_tw, f32), shape_of(row_tw, f32)]
            + [shape_of(row_tw, bf16)] * 6 + [mixed_piece if last_row else []],
            [VMEM] + [ANY] * (11 + (count if last_row else 0)),
            [
                (row_tw, bf16), ((width, width), bf16), ((width, width), bf16),
                ((width, width), bf16), (row_tw, f32), (row_tw, bf16), (row_tw, bf16),
                ((width, hidden), bf16), (row_tw, bf16), (row_tw, bf16), (row_square, bf16),
                (row_tw, bf16), (row_tw, f32), (row_tw, bf16), (row_th, bf16), (row_th, bf16),
                (row_tw, f32), (row_tw, f32), (row_tw, bf16), (row_tw, bf16), (row_tw, bf16),
                (row_tw, bf16), (row_tw, bf16), ((length, length), f32), ((8, width), f32),
                ((8, width), f32), (row_tw, f32),
            ] + products,
            9 + (7 * row_count if last_row else 0), 11 + 2 * share_copies, "cross", True,
        )

    def to_decoder(value):
        return lax.ppermute(value, "section", [(0, 1)])

    def to_encoder(value):
        return lax.ppermute(value, "section", [(1, 0)])

    kept_rows = [run_first(0, flag)]
    for row in range(1, row_count):

        def first_steps(low, flag, row=row):
            memory = to_decoder(low)
            return memory, run_first(row, flag)

        low = kept_rows[-1][9]
        memory, outs = block_of(always, first_steps, low, after(flag, low))
        kept_rows.append(outs)
        memories = (*memories, memory) if row > 1 else (memory,)

    def cross_steps(low, flag, first_memory, sent, own, first_earlier):
        memory = to_decoder(low)
        other = lax.ppermute(sent, "batch", [(i, i ^ 1) for i in range(devices)])
        return memory, other, run_cross(0, flag, fbias, first_memory, sent, other, own, first_earlier)

    def own_of(row):
        outs = kept_rows[row]
        return outs[0], outs[11], outs[7]

    def earlier_of(rows):
        hc = tuple(outs[10] for outs in kept_rows)
        return (
            hc,
            *(tuple(outs[part] for outs in rows) for part in (6, 5, 10)),
            tuple(memories[: len(rows)]),
            *(tuple(outs[part] for outs in rows) for part in (7, 8)),
        )

    low = kept_rows[-1][9]
    memory, sent_other, outs = block_of(
        always, cross_steps, low, after(flag, low), memories[0], sent, own_of(0), earlier_of(())
    )
    memories = (*memories, memory)
    small_grad, *outs = outs
    cross_rows, returned = [outs], ()
    for row in range(1, row_count):

        def return_steps(dm, flag, *operands, row=row):
            back = to_encoder(dm)
            return back, run_cross(row, flag, *operands)

        dm = cross_rows[-1][9]
        back, outs = block_of(
            always, return_steps, dm, after(flag, dm), small_grad, memories[row], sent, sent_other,
            own_of(row), earlier_of(cross_rows),
        )
        small_grad, *outs = outs
        cross_rows.append(outs)
        returned = (*returned, back)
    dm = cross_rows[-1][9]
    returned = (*returned, to_encoder(dm))
    x1, h1, qkv, weights, context, h2, u, slope, e2, low, hc, qc = zip(*kept_rows)
    dec_h2, dec_u, dec_slope, d2, grad, _, dq, _, _, dm, _, cross_gs = zip(*cross_rows)
    cross_g = cross_gs[-1]

    cross, down, ffn, mixed = (
        Ring(devices, name != "cross") for name in ("cross", "down", "ffn", "mixed")
    )

    flag = after(flag, *dm)

    def run_down(flag, vec, small_grad, returned, cot, e2, u, dec_u):
        small_grad, enc_grad, enc_low, *pieces = run_kernel(
            down_body,
            (flag, vec, small_grad, returned, cot, e2, u, dec_u),
            [SMEM] + [VMEM] * 2 + [ANY] * 5,
            [shape_of(small, f32), shape_of(tw, f32), shape_of(tw, bf16)] + down_piece,
            [VMEM] + [ANY] * (2 + count),
            [
                (tw, bf16), (tw, bf16), (tw, f32), (th, bf16), (tw, f32), (tw, bf16),
                ((hidden, width), bf16), ((8, width), f32), ((8, width), f32),
            ],
            1 + 3 * row_count, 2 + max(share_copies, hidden // tile), "down",
        )
        return small_grad, enc_grad, enc_low, pieces

    def run_hidden(flag, enc_low, down_w, slope):
        return run_kernel(
            hidden_body,
            (flag, enc_low, down_w, slope),
            [SMEM] + [ANY] * 3,
            [shape_of(th, bf16)],
            [ANY],
            [(tw, bf16), ((hidden, width), bf16), (th, bf16)],
            1 + row_count + hidden // tile, hidden // tile, "hidden",
        )[0]

    def run_ffn(flag, small_grad, enc_slope):
        small_grad, *pieces = run_kernel(
            ffn_body,
            (flag, small_grad, (h2, enc_slope), (dec_h2, dec_slope)),
            [SMEM, VMEM, ANY, ANY],
            [shape_of(small, f32)] + ffn_piece,
            [VMEM] + [ANY] * count,
            [(th, bf16), (tw, bf16), ((width, hidden), bf16)],
            2 * row_count, hidden // (2 * tile) * share_copies, "ffn",
        )
        return small_grad, pieces

    def run_hidden_back(flag, vec, small_grad, slope, ffn_w, dq, first_w, x1, enc_grad, grad):
        return run_kernel(
            hidden_back_body,
            (flag, vec, small_grad, slope, ffn_w, dq, first_w, x1, enc_grad, grad),
            [SMEM] + [VMEM] * 2 + [ANY] * 7,
            [shape_of(small, f32), shape_of(tw, f32)],
            [VMEM, ANY],
            [
                (th, bf16), ((width, hidden), bf16), (tw, bf16), ((width, width), bf16), (tw, f32),
                (tw, f32), (tw, f32), ((8, width), f32), ((8, width), f32),
            ],
            3 + 3 * row_count, 1, "hidden_back",
        )

    def run_attention_back(flag, grad, qkv, weights, context, out_w, h1):
        grad_qkv, grad_scores, *pieces = run_kernel(
            functools.partial(attention_back_body, heads),
            (flag, grad, qkv, weights, context, out_w, h1),
            [SMEM] + [ANY] * 6,
            [shape_of(wide, bf16), shape_of((heads, length, length), f32)] + mixed_piece,
            [ANY] * (2 + count),
            [
                (tw, f32), (wide, bf16), (square, bf16), (tw, f32), ((width, width), bf16),
                (tw, bf16), (tw, bf16), (tw, bf16), (wide, bf16), ((width, 4 * width), bf16),
                ((heads, length, length), f32), (tw, bf16),
            ],
            2 + 4 * row_count, 2 + 2 * share_copies, "attention_back",
        )
        return grad_qkv, grad_scores, pieces

    def run_last(
        flag, vec, small_grad, grad, grad_qkv, qkv_w, rows, grad_scores, u, d2, down_w, low
    ):
        return run_kernel(
            last_body,
            (flag, offsets, vec, small_grad, grad, grad_qkv, qkv_w, rows, grad_scores, u, d2, down_w,
             low),
            [SMEM] + [VMEM] * 3 + [ANY] * 9,
            [shape_of(small, f32), shape_of(tw, f32), shape_of(tw, bf16)],
            [VMEM, ANY, ANY],
            [
                (tw, f32), (wide, bf16), ((width, 3 * width), bf16), (tw, bf16), (tw, f32),
                ((heads, length, length), f32), ((heads, 2 * length), f32),
                ((bucket_count, 2 * length), f32), (th, bf16), (tw, f32), ((hidden, width), bf16),
                (tw, bf16), ((8, width), f32), ((8, width), f32),
            ],
            6 + 3 * row_count, 2, "last",
        )

    def beside(ring, pieces, kernel, *operands):
        def steps(kept, given, flag, *operands):
            got = ring.to_core(given)
            outs = kernel(flag, *operands)
            out = pair_sum(after(flag, *jax.tree.leaves(outs)), kept, got, ring.everywhere)
            return outs, got, out

        return block_of(always, steps, *pieces, *operands)

    if not by_chip:
        small_grad, enc_grad, enc_low, down_g = run_down(
            flag, vec, small_grad, returned, cot, e2, u, dec_u
        )
        enc_slope = run_hidden(flag, enc_low, down_w, slope)
        small_grad, ffn_g = run_ffn(flag, small_grad, enc_slope)
        small_grad, grad = run_hidden_back(
            flag, vec, small_grad, enc_slope, ffn_w, dq, first_w, x1, enc_grad, grad
        )
        grad_qkv, grad_scores, mixed_g = run_attention_back(
            flag, grad, qkv, weights, context, out_w, h1
        )
        small_grad, result, low = run_last(
            flag, vec, small_grad, grad, grad_qkv, qkv_w, rows, grad_scores, dec_u, d2, down_w, low
        )
        small_grad = lax.psum(small_grad, "batch")
        cross_share, down_share, ffn_share, mixed_share = (
            lax.psum_scatter(pieces[0], "batch", scatter_dimension=0, tiled=True).astype(f32)
            for pieces in (cross_g, down_g, ffn_g, mixed_g)
        )
        cross_back = lax.ppermute(cross_share[:, 2 * width :], "section", [(1, 0)])
        cross_share = jnp.where(on_encoder, cross_back, cross_share[:, : 2 * width])
        cf_share, cs_share = cross_share[:, :width], cross_share[:, width:]
        out_share, qkv_share = mixed_share[:, :width], mixed_share[:, width:]
        vec_share = lax.dynamic_slice_in_dim(
            small_grad[:7], place * (width // devices), width // devices, 1
        )
        fbias_all = small_grad[8 : 8 + hidden // width].reshape(1, hidden)
        fbias_share = lax.dynamic_slice_in_dim(
            fbias_all, place * (hidden // devices), hidden // devices, 1
        )
        table_total = small_grad[16 : 16 + heads, :bucket_count].T
    else:

        def cross_steps(flag, kept, given):
            got = cross.to_core(given)
            return got, pair_sum(flag, kept, got, False)

        got, out = block_of(always, cross_steps, flag, *cross_g)
        flag = after(flag, out)

        def down_steps(out, kept, got, flag, down_w, slope, ffn_ins, *operands):
            far = cross.to_chip(out)
            small_grad, enc_grad, enc_low, pieces = run_down(flag, *operands)
            flag = after(flag, small_grad)
            enc_slope, down_got, out = beside(
                down, pieces, run_hidden, flag, enc_low, down_w, slope
            )
            down_held = (pieces[0], down_got, down.to_chip(out))
            flag = after(flag, out)
            small_grad, pieces = run_ffn(flag, small_grad, enc_slope)
            flag = after(flag, small_grad)
            *outs, cross_own = cross.sums(flag, kept, got, far)
            flag = after(flag, *outs)
            cross_last = (*cross.along(outs), cross_own)
            sums = beside(
                ffn, pieces, run_hidden_back, flag, vec, small_grad, enc_slope, *ffn_ins[:4],
                enc_grad, ffn_ins[4],
            )
            outs = down.sums(after(flag, sums[2]), *down_held)
            return outs, cross_last, pieces[0], sums

        down_outs, cross_last, kept, sums = block_of(
            always, down_steps, out, cross_g[0], got, flag, down_w, slope,
            (ffn_w, dq, first_w, x1, grad), vec, small_grad, returned, cot, e2, u, dec_u,
        )
        (small_grad, grad), got, ffn_out = sums
        ffn_held = (kept, got)
        flag = after(flag, ffn_out, *down_outs)

        def attention_steps(flag, ffn_out, outs, *operands):
            far = ffn.to_chip(ffn_out)
            moved = down.along(outs)
            grad_qkv, grad_scores, pieces = run_attention_back(flag, *operands)

            def swap(flag, kept, given):
                got = mixed.to_core(given)
                return got, pair_sum(flag, kept, got, True)

            swapped = block_of(always, swap, after(flag, grad_qkv), *pieces)
            return moved, far, grad_qkv, grad_scores, pieces[0], swapped

        moved, ffn_far, grad_qkv, grad_scores, kept, swapped = block_of(
            always, attention_steps, flag, ffn_out, down_outs[:3], grad, qkv, weights, context, out_w,
            h1,
        )
        down_last = (*moved, down_outs[3])
        got, out = swapped
        flag = after(flag, out)

        def swapped_small(small_grad, away):
            pairs = [(i, i ^ away) for i in range(devices)]
            return small_grad + lax.ppermute(small_grad, "batch", pairs)

        def last_steps(flag, out, held, mixed_held, *operands):
            far = mixed.to_chip(out)
            *outs, own = ffn.sums(flag, *held)
            moved = (*ffn.along(outs), own)
            small_grad, result, low = run_last(after(flag, *outs), *operands)

            small_grad = block_of(always, lambda s: swapped_small(s, 1), small_grad)
            outs = mixed.sums(after(flag, small_grad), *mixed_held, far)
            return outs, moved, small_grad, result, low

        (*outs, own), ffn_last, small_grad, result, low = block_of(
            always, last_steps, flag, out, (*ffn_held, ffn_far), (kept, got), vec, small_grad,
            grad, grad_qkv, qkv_w, rows, grad_scores, dec_u, d2, down_w, low,
        )

        moved = mixed.along(outs)
        cross_last, down_last, ffn_last = after((cross_last, down_last, ffn_last), *outs)
        back = sum(part[:, 2 * width :].astype(f32) for part in cross_last)
        back = lax.ppermute(back, "section", [(1, 0)])
        shares = [
            sum(part[:, at].astype(f32) for part in parts)
            for parts, at in (
                (cross_last, slice(0, width)),
                (cross_last, slice(width, 2 * width)),
                (down_last, slice(None)),
                (ffn_last, slice(None)),
            )
        ]

        def small_steps(small_grad):
            for away in (2, 4, 8):
                small_grad = swapped_small(small_grad, away)
            return small_grad

        small_grad = block_of(always, small_steps, after(small_grad, *outs))
        shares[0] = jnp.where(on_encoder, back[:, :width], shares[0])
        shares[1] = jnp.where(on_encoder, back[:, width:], shares[1])
        cf_share, cs_share, down_share, ffn_share = shares
        small_grad = after(small_grad, cf_share, cs_share)
        qkv_share, out_share, vec_share, fbias_share, table_total = pl.pallas_call(
            finish_body,
            in_specs=[SMEM] + [VMEM] * 5,
            out_specs=[VMEM] * 5,
            out_shape=[
                shape_of((width // devices, 3 * width), f32), shape_of((width // devices, width), f32),
                shape_of((7, 1, width // devices), f32), shape_of((1, hidden // devices), f32),
                shape_of((heads, 1, bucket_count), f32),
            ],
            name="finish",
        )(place[None], *moved, own, small_grad)
        vec_share = vec_share[:, 0]
        table_total = table_total[:, 0].T
    return (
        low.reshape((1, row_count, length, width)),
        result.reshape((1, row_count, length, width)),
        qkv_share[None],
        out_share[None],
        ffn_share[None],
        down_share[None],
        cf_share[None],
        cs_share[None],
        vec_share[None],
        fbias_share,
        table_total[None],
    )


def solution(mesh):
    return jax.shard_map(
        per_device,
        mesh=mesh,
        in_specs=(
            P("section", "batch", None, None),
            P("section", "batch", None, None),
            P(None, "batch", None),
            P(),
            P("section", None, None),
            P("section", None, None),
            P("section", None, None),
            P("section", None, None),
            P("section", None, None),
            P("section", None, None),
            P("section", None, None),
            P("section", None),
            P("section", None, None),
        ),
        out_specs=(
            P("section", "batch", None, None),
            P("section", "batch", None, None),
            P("section", "batch", None),
            P("section", "batch", None),
            P("section", "batch", None),
            P("section", "batch", None),
            P("section", "batch", None),
            P("section", "batch", None),
            P("section", None, "batch"),
            P("section", "batch"),
            P("section", None, None),
        ),
        check_vma=False,
    )
```

```python
import functools

import jax
import jax.numpy as jnp
from jax import lax
from jax.experimental import pallas as pl
from jax.experimental.pallas import tpu as pltpu
from jax.sharding import PartitionSpec as P

norm_epsilon = 1e-05
masked_score = -1e30
half_root = 0.7071067811865476
density_scale = 0.3989422804014327
tile = 768
chunk = 256
spare_bytes = 8 * 1024 * 1024
all_bytes = 62 * 1024 * 1024

f32 = jnp.float32
bf16 = jnp.bfloat16
ANY = pl.BlockSpec(memory_space=pl.ANY)
SMEM = pl.BlockSpec(memory_space=pltpu.SMEM)
VMEM = pl.BlockSpec(memory_space=pltpu.VMEM)


def mm(left, right):
    return jnp.dot(left, right, preferred_element_type=f32)


def mm_nt(left, right):
    return lax.dot_general(left, right, (((1,), (1,)), ((), ())), preferred_element_type=f32)


def mm_tn(left, right):
    return lax.dot_general(left, right, (((0,), (0,)), ((), ())), preferred_element_type=f32)


def mean_of(values):
    return jnp.sum(values, axis=-1, keepdims=True) * (1.0 / values.shape[-1])


def normalised(values):
    centre = values - mean_of(values)
    rate = lax.rsqrt(mean_of(centre * centre) + norm_epsilon)
    return centre * rate, rate


def each_rows(count, body):
    @pl.loop(0, count // chunk)
    def _(step):
        body(pl.ds(pl.multiple_of(step * chunk, chunk), chunk))


def each_tile(count, body, width=tile):
    if count == width:
        body(pl.ds(0, width))
        return

    @pl.loop(0, count // width)
    def _(step):
        body(pl.ds(pl.multiple_of(step * width, width), width))


def norm_forward(source, gain, offset, target, also=None):
    def rows(at):
        unit, _ = normalised(source[at, :].astype(f32))
        normed = unit * gain + offset
        target[at, :] = normed.astype(target.dtype)

    each_rows(source.shape[0], rows)


def norm_backward(
    source, grad_normed, gain, upstream, target, gain_sum, offset_sum, low=None
):
    gain_sum[...] = jnp.zeros_like(gain_sum)
    offset_sum[...] = jnp.zeros_like(offset_sum)

    def rows(at):
        unit, rate = normalised(source[at, :].astype(f32))
        upper = grad_normed[at, :]
        product = upper * unit
        gain_sum[...] += jnp.sum(product.reshape(-1, 8, product.shape[1]), axis=0)
        offset_sum[...] += jnp.sum(upper.reshape(-1, 8, upper.shape[1]), axis=0)
        scaled = upper * gain
        inner = mean_of(scaled)
        along = mean_of(product * gain)
        result = rate * (scaled - inner - unit * along)
        if upstream is not None:
            result = result + upstream[at, :].astype(f32)
        target[at, :] = result
        if low is not None:
            low[at, :] = result.astype(bf16)

    each_rows(source.shape[0], rows)


def column_sum(partial):
    return jnp.sum(partial[...], axis=0, keepdims=True)


def lower_lanes(shape):
    return lax.broadcasted_iota(jnp.int32, shape, 1) < shape[1] // 2


def split_pair(block):
    lower = lower_lanes(block.shape)
    zero = jnp.zeros_like(block)
    return jnp.concatenate([jnp.where(lower, block, zero), jnp.where(lower, zero, block)], axis=0)


def join_pair(stacked):
    rows = stacked.shape[0] // 2
    lower = lower_lanes((rows, stacked.shape[1]))
    return jnp.where(lower, stacked[:rows], stacked[rows:])


def attend_pair(queries, key_rows, values, additions, scale):
    length = queries.shape[0]
    scores = mm_nt((queries * scale).astype(bf16), split_pair(key_rows))
    parts = []
    for head in range(2):
        part = scores[:, head * length : (head + 1) * length] + additions[head]
        exponent = jnp.exp(part - jnp.max(part, axis=-1, keepdims=True))
        parts.append(exponent * (1.0 / jnp.sum(exponent, axis=-1, keepdims=True)))
    weights = jnp.concatenate(parts, axis=1).astype(bf16)
    return weights, mm(weights, split_pair(values))


def attend_pair_back(weights, queries, key_rows, values, context, grad_context, scale):
    length = queries.shape[0]
    grad_weights = mm_nt(grad_context, split_pair(values))
    product = grad_context.astype(f32) * context.astype(f32)
    lower = lower_lanes(product.shape)
    parts = []
    for head in range(2):
        at = slice(head * length, (head + 1) * length)
        own = jnp.where(lower, product, 0.0) if head == 0 else jnp.where(lower, 0.0, product)
        centred = jnp.sum(own, axis=-1, keepdims=True)
        parts.append(weights[:, at].astype(f32) * (grad_weights[:, at] - centred))
    grad_raw = jnp.concatenate(parts, axis=1).astype(bf16)
    grad_queries = mm(grad_raw, split_pair(key_rows)) * scale
    grad_keys = join_pair(mm_tn(grad_raw, queries)) * scale
    grad_values = join_pair(mm_tn(weights, grad_context))
    return grad_queries, grad_keys, grad_values, parts


def same_sentence(query_ids, key_ids):
    length = query_ids.shape[1]
    across = jnp.broadcast_to(key_ids.astype(f32), (length, length))
    down = jnp.broadcast_to(query_ids.astype(f32), (length, length)).T
    return across == down


class Move:
    def __init__(self, sources, target, semaphores):
        self.sources, self.target, self.semaphores = sources, target, semaphores

    def copies(self, sources):
        if not isinstance(sources, tuple):
            yield pltpu.make_async_copy(sources, self.target, self.semaphores[0])
            return
        rows = self.target.shape[0] // len(sources)
        for part, source in enumerate(sources):
            target = self.target.at[pl.ds(part * rows, rows)]
            yield pltpu.make_async_copy(source, target, self.semaphores[part])

    def start(self, sources=None):
        for copy in self.copies(self.sources if sources is None else sources):
            copy.start()

    def wait(self, sources=None):
        for copy in self.copies(self.sources if sources is None else sources):
            copy.wait()


class Mover:
    def __init__(self, semaphores):
        self.semaphores = semaphores
        self.used = 0

    def note(self, source, target):
        count = len(source) if isinstance(source, tuple) else 1
        semaphores = [self.semaphores.at[self.used + part] for part in range(count)]
        self.used += count
        return Move(source, target, semaphores)

    def start(self, source, target):
        move = self.note(source, target)
        move.start()
        return move


def wait_all(moves):
    for move in moves:
        move.wait()


def gelu_parts(hidden):
    share = 0.5 + 0.5 * lax.erf(hidden * half_root)
    slope = share + hidden * (density_scale * jnp.exp(hidden * hidden * -0.5))
    return hidden * share, slope


def feed_forward(normed, ffn_w, in_bias, ahead, use):
    tiles = spans(ffn_w.shape[1], tile)
    ahead[0] = mm(normed[...], ffn_w[:, tiles[0]])
    for step, at in enumerate(tiles):
        if step + 1 < len(tiles):
            ahead[(step + 1) % 2] = mm(normed[...], ffn_w[:, tiles[step + 1]])
        use(at, ahead[step % 2] + in_bias[:, at])


def first_body(
    heads, row, flag, ids, offsets, table, vectors, in_bias, rows_in, cot_in, qkv_in, out_in, ffn_in,
    down_in, first_in,
    x1_out, h1_out, qkv_out, weights_out, context_out, h2_out, u_out, slope_out, e2_out, low_out,
    hc_out, qc_out,
    rows, qkv_w, out_w, ffn_w, down_w, first_w, cot, normed, qkv, weights, context, x1, h2, u, slope,
    e2, low, bias_rows, mask, context_wide, ahead, loads, stores,
):
    length, width = rows.shape
    hidden_width = ffn_w.shape[1]
    on_encoder = flag[0] == 1
    own_rows = pl.ds(row * length, length)
    load = Mover(loads)
    store = Mover(stores)
    got_rows = load.start(rows_in.at[own_rows], rows)
    got_qkv = load.start(qkv_in, qkv_w)
    got_out = load.start(out_in, out_w)
    got_down = load.note(down_in, down_w)
    got_ffn = load.note(ffn_in, ffn_w)
    got_first = load.note(first_in, first_w)
    got_cot = load.note(cot_in.at[own_rows], cot)

    @pl.when(on_encoder)
    def _():
        got_ffn.start()
        got_down.start()

    @pl.when(jnp.logical_not(on_encoder))
    def _():
        got_first.start()
        got_cot.start()
        got_down.start()

    one_hot = (offsets[...] == lax.broadcasted_iota(jnp.int32, (table.shape[1], 2 * length), 0)).astype(f32)
    by_offset = lax.dot_general(
        table[...], one_hot, (((1,), (0,)), ((), ())), precision=lax.Precision.HIGHEST,
        preferred_element_type=f32,
    )
    bias_rows[...] = pltpu.roll(by_offset, length + 1, 1)
    own_group = jnp.where(on_encoder, 0, 1)
    causal = lax.broadcasted_iota(jnp.int32, (length, length), 0) >= lax.broadcasted_iota(
        jnp.int32, (length, length), 1
    )
    own = ids[pl.ds(own_group, 1), row, :]
    allowed = same_sentence(own, own) & (causal | on_encoder)
    mask[...] = jnp.where(allowed, 0.0, masked_score)

    got_rows.wait()
    norm_forward(rows, vectors[0], vectors[1], normed)
    got_qkv.wait()

    def project(at):
        qkv[:, at] = mm(normed[...], qkv_w[:, at]).astype(bf16)

    each_tile(3 * width, project)
    out_copies = [store.start(normed, h1_out), store.start(qkv, qkv_out)]
    scale = (width // heads) ** (-0.5)

    @pl.loop(0, heads // 2, unroll=heads // 2)
    def _(pair):
        lanes = pl.multiple_of(pair * 128, 128)
        additions = []
        for head in range(2):
            spread = jnp.broadcast_to(bias_rows[pl.ds(pair * 2 + head, 1), :], (length, 2 * length))
            skewed = pltpu.roll(spread, 0, 1, stride=1, stride_axis=0)
            additions.append(skewed[:, :length] + mask[...])
        part, mixed = attend_pair(
            qkv[:, pl.ds(lanes, 128)],
            qkv[:, pl.ds(width + lanes, 128)],
            qkv[:, pl.ds(2 * width + lanes, 128)],
            additions,
            scale,
        )
        weights[0, pair] = part
        context_wide[:, pl.ds(lanes, 128)] = mixed
        context[:, pl.ds(lanes, 128)] = mixed.astype(bf16)

    out_copies += [store.start(weights, weights_out), store.start(context_wide, context_out)]
    got_out.wait()
    x1[...] = rows[...].astype(f32) + mm(context[...], out_w[...])
    out_copies.append(store.start(x1, x1_out))

    @pl.when(on_encoder)
    def _():
        norm_forward(x1, vectors[2], vectors[3], h2)
        got_ffn.wait()

        def feed(at, hidden):
            value, rate = gelu_parts(hidden)
            u[:, at] = value.astype(bf16)
            slope[:, at] = rate.astype(bf16)

        feed_forward(h2, ffn_w, in_bias, ahead, feed)
        copies = [store.start(h2, h2_out), store.start(u, u_out), store.start(slope, slope_out)]
        got_down.wait()
        e2[...] = x1[...] + (mm(u[...], down_w[...]) + vectors[6])
        copies.append(store.start(e2, e2_out))
        norm_forward(e2, vectors[4], vectors[5], low)
        copies.append(store.start(low, low_out))
        wait_all(copies)

    @pl.when(jnp.logical_not(on_encoder))
    def _():
        norm_forward(x1, vectors[2], vectors[3], h2)
        got_first.wait()
        low[...] = mm(h2[...], first_w[...]).astype(bf16)
        copies = [store.start(h2, hc_out), store.start(low, qc_out)]
        got_down.wait()
        got_cot.wait()

        def back(at):
            slope[:, at] = mm_nt(cot[...], down_w[at, :]).astype(bf16)

        each_tile(hidden_width, back)
        copies.append(store.start(slope, slope_out))
        wait_all(copies)

    wait_all(out_copies)


def cross_body(
    heads, row, flag, ids, vectors, in_bias, small_in,
    memory_in, sent_in, other_in, second_in, x1_in, qc_in, cot_in, ffn_in, slope_in, earlier,
    small_out, h2_out, u_out, slope_out, d2_out, grad_out, cc_out, dq_out, dk_out, dv_out, dm_out,
    low_out, pieces, memory, keys_w, values_w, second_w, x1, qc, cot, ffn_w, keys, values, weights, cc, d2, h2, u,
    slope, grad_normed, grad, grad_low, dq, dk, dv, dm, mask, gain_sum, offset_sum, cc_wide, ahead, *rest
):
    *products, loads, stores = rest
    length, width = memory.shape
    small_out[...] = jnp.zeros_like(small_out) if row == 0 else small_in[...]

    @pl.when(flag[0] == 0)
    def _():
        load = Mover(loads)
        store = Mover(stores)
        got_memory = load.start(memory_in, memory)
        got_keys = load.note(sent_in, keys_w)
        got_values = load.note(sent_in, values_w)
        for core, (keys_in, values_in) in enumerate(((sent_in, other_in), (other_in, sent_in))):

            @pl.when(flag[1] == core)
            def _(keys_in=keys_in, values_in=values_in):
                got_keys.start(keys_in)
                got_values.start(values_in)

        got_query = load.start(qc_in, qc)
        got_second = [load.start(second_in, second_w), load.start(x1_in, x1)]
        got_ffn = [load.start(ffn_in, ffn_w), load.start(slope_in, slope)]
        got_cot = load.start(cot_in.at[pl.ds(row * length, length)], cot)
        if products:
            got_earlier = []
            for sources, whole in zip(earlier, products):
                if not sources:
                    continue
                rows = len(sources) * length
                got_earlier.append(load.start(tuple(sources), whole.at[pl.ds(0, rows)]))
        mask[...] = jnp.where(same_sentence(ids[1:2, row, :], ids[0:1, row, :]), 0.0, masked_score)
        got_memory.wait()
        got_keys.wait()
        keys[...] = mm(memory[...], keys_w[...]).astype(bf16)
        got_values.wait()
        values[...] = mm(memory[...], values_w[...]).astype(bf16)
        got_query.wait()
        scale = (width // heads) ** (-0.5)

        @pl.loop(0, heads // 2, unroll=3)
        def _(pair):
            lanes = pl.ds(pl.multiple_of(pair * 128, 128), 128)
            part, mixed = attend_pair(
                qc[:, lanes], keys[:, lanes], values[:, lanes], [mask[...], mask[...]], scale
            )
            weights[0, pair] = part
            cc_wide[:, lanes] = mixed
            cc[:, lanes] = mixed.astype(bf16)

        copies = [store.start(cc, cc_out)]
        wait_all(got_second)
        d2[...] = x1[...] + mm(cc[...], second_w[...])
        copies.append(store.start(d2, d2_out))
        norm_forward(d2, vectors[4], vectors[5], h2)
        copies.append(store.start(h2, h2_out))
        wait_all(got_ffn)

        def feed(at, hidden):
            value, rate = gelu_parts(hidden)
            u[:, at] = value.astype(bf16)
            slope[:, at] = (slope[:, at].astype(f32) * rate).astype(bf16)

        feed_forward(h2, ffn_w, in_bias, ahead, feed)
        copies += [store.start(u, u_out), store.start(slope, slope_out)]
        grad_normed[...] = mm_nt(slope[...], ffn_w[...])
        got_cot.wait()
        norm_backward(
            d2, grad_normed, vectors[4], cot, grad, gain_sum, offset_sum, grad_low
        )
        small_out[4:5, :] += column_sum(gain_sum)
        small_out[5:6, :] += column_sum(offset_sum)
        copies += [store.start(grad, grad_out), store.start(grad_low, low_out)]
        dm[...] = mm_nt(grad_low[...], second_w[...]).astype(bf16)

        @pl.loop(0, heads // 2, unroll=3)
        def _(pair):
            lanes = pl.ds(pl.multiple_of(pair * 128, 128), 128)
            grad_q, grad_k, grad_v, _ = attend_pair_back(
                weights[0, pair], qc[:, lanes], keys[:, lanes], values[:, lanes], cc_wide[:, lanes],
                dm[:, lanes], scale,
            )
            dq[:, lanes] = grad_q.astype(bf16)
            dk[:, lanes] = grad_k.astype(bf16)
            dv[:, lanes] = grad_v.astype(bf16)

        copies += [store.start(dq, dq_out), store.start(dk, dk_out), store.start(dv, dv_out)]
        dm[...] = (mm_nt(dk[...], keys_w[...]) + mm_nt(dv[...], values_w[...])).astype(bf16)
        copies.append(store.start(dm, dm_out))
        if products:
            *wholes, cross_g = products
            hc, *others = wholes
            own = pl.ds(hc.shape[0] - length, length)
            for whole, part in zip(others, (dq, cc, grad_low, memory, dk, dv)):
                whole[own, :] = part[...]
            wait_all(got_earlier)
            hc, dq_all, cc_all, low_all, memory_all, dk_all, dv_all = wholes
            query, out, key, value = spans(4 * width, width)
            cross_g[:, query] = mm_tn(hc[...], dq_all[...]).astype(bf16)
            cross_g[:, out] = mm_tn(cc_all[...], low_all[...]).astype(bf16)
            copies += put_columns(store, cross_g, pieces, flag[1], pl.ds(0, 2 * width))
            cross_g[:, key] = mm_tn(memory_all[...], dk_all[...]).astype(bf16)
            cross_g[:, value] = mm_tn(memory_all[...], dv_all[...]).astype(bf16)
            copies += put_columns(store, cross_g, pieces, flag[1], pl.ds(2 * width, 2 * width))
        wait_all(copies)


def put_rows(store, stage, targets, core, rows):
    if len(targets) == 1:
        return [store.start(stage.at[rows], targets[0].at[rows])]
    depth = targets[0].shape[1]
    copies = []
    for chip in range(rows.start // (2 * depth), (rows.start + rows.size) // (2 * depth)):
        for target, which in zip(targets, (core, 1 - core)):
            at = pl.multiple_of((2 * chip + which) * depth, depth)
            copies.append(store.start(stage.at[pl.ds(at, depth)], target.at[chip]))
    return copies


def put_columns(store, stage, targets, core, columns):
    if len(targets) == 1:
        return [store.start(stage.at[:, columns], targets[0].at[:, columns])]
    chips, depth = targets[0].shape[0], targets[0].shape[1]
    copies = []
    for chip in range(chips):
        for target, which in zip(targets, (core, 1 - core)):
            at = pl.multiple_of((2 * chip + which) * depth, depth)
            copies.append(
                store.start(stage.at[pl.ds(at, depth), columns], target.at[chip, :, columns])
            )
    return copies


def spans(count, width):
    return [pl.ds(start, width) for start in range(0, count, width)]


def down_body(flag, vectors, small_in, dm_in, cot_in, e2_in, enc_u_in, dec_u_in, *rest):
    small_out, grad_out, low_out, *rest = rest
    count = len(rest) - 11
    outs = rest[:count]
    dm, cot, e2, u, grad, grad_low, down_g, gain_sum, offset_sum, loads, stores = rest[count:]
    hidden_width, width = u.shape[1], cot.shape[1]
    small_out[...] = small_in[...]
    load = Mover(loads)
    store = Mover(stores)
    got_cot = load.start(cot_in, cot)
    got_u = load.note(enc_u_in, u)
    moved = [load.note(dm_in, dm), load.note(e2_in, e2)]
    kept = [store.note(grad, grad_out), store.note(grad_low, low_out)]

    @pl.when(flag[0] == 1)
    def _():
        for copy in moved:
            copy.start()
        got_cot.wait()
        wait_all(moved)
        got_u.start(enc_u_in)

        def total(at):
            grad[at, :] = dm[at, :].astype(f32) + cot[at, :].astype(f32)

        each_rows(grad.shape[0], total)
        norm_backward(e2, grad, vectors[4], None, grad, gain_sum, offset_sum, grad_low)
        small_out[4:5, :] = column_sum(gain_sum)
        small_out[5:6, :] = column_sum(offset_sum)
        for copy in kept:
            copy.start()

    @pl.when(flag[0] == 0)
    def _():
        got_u.start(dec_u_in)
        got_cot.wait()
        grad_low[...] = cot[...]

    got_u.wait()
    copies = []
    for rows in spans(hidden_width, tile):
        down_g[rows, :] = mm_tn(u[:, rows], grad_low[...]).astype(bf16)
        copies += put_rows(store, down_g, outs, flag[1], rows)
    small_out[6:7, :] = jnp.sum(grad_low[...].astype(f32), axis=0, keepdims=True)
    wait_all(copies)

    @pl.when(flag[0] == 1)
    def _():
        wait_all(kept)


def hidden_body(flag, low_in, down_in, slope_in, slope_out, grad_low, down_w, slope, loads, stores):
    @pl.when(flag[0] == 1)
    def _():
        load = Mover(loads)
        store = Mover(stores)
        hidden_width = slope.shape[1]
        got_low = load.start(low_in, grad_low)
        got_slope = load.start(slope_in, slope)
        got_down = [
            load.start(down_in.at[rows], down_w.at[rows]) for rows in spans(hidden_width, tile)
        ]
        got_low.wait()
        got_slope.wait()
        copies = []
        for at, got in zip(spans(hidden_width, tile), got_down):
            got.wait()
            part = mm_nt(grad_low[...], down_w[at, :]) * slope[:, at].astype(f32)
            slope[:, at] = part.astype(bf16)
            copies.append(store.start(slope.at[:, at], slope_out.at[:, at]))
        wait_all(copies)


def ffn_body(flag, small_in, enc_ins, dec_ins, *rest):
    small_out, *rest = rest
    count = len(rest) - 5
    outs = rest[:count]
    slope, h2, ffn_g, loads, stores = rest[count:]
    width, hidden_width = h2.shape[1], slope.shape[1]
    small_out[...] = small_in[...]
    load = Mover(loads)
    store = Mover(stores)
    moves = [load.note(source, target) for source, target in zip(dec_ins, (h2, slope))]
    for which, ins in enumerate((dec_ins, enc_ins)):

        @pl.when(flag[0] == which)
        def _(ins=ins):
            for move, source in zip(moves, ins):
                move.start(source)
            for move, source in zip(moves, ins):
                move.wait(source)

    copies = []
    for step, at in enumerate(spans(hidden_width, tile)):
        ffn_g[:, at] = mm_tn(h2[...], slope[:, at]).astype(bf16)
        if step % 2 == 1:
            both = pl.ds(at.start - tile, 2 * tile)
            copies += put_columns(store, ffn_g, outs, flag[1], both)
    for part in range(hidden_width // width):
        values = slope[:, part * width : (part + 1) * width].astype(f32)
        small_out[8 + part : 9 + part, :] = jnp.sum(values, axis=0, keepdims=True)
    wait_all(copies)


def hidden_back_body(
    flag, vectors, small_in, slope_in, ffn_in, dq_in, first_in, x1_in, enc_grad_in, dec_grad_in,
    small_out, grad_out,
    slope, ffn_w, dq, first_w, x1, grad, grad_normed, gain_sum, offset_sum, loads, stores,
):
    width = x1.shape[1]
    small_out[...] = small_in[...]
    load = Mover(loads)
    store = Mover(stores)
    got_x1 = load.note(x1_in, x1)
    got_grad = load.note(dec_grad_in, grad)

    @pl.when(flag[0] == 1)
    def _():
        got = [load.start(slope_in, slope), load.start(ffn_in, ffn_w)]
        got_x1.start()
        got_grad.start(enc_grad_in)
        wait_all(got)
        grad_normed[...] = mm_nt(slope[...], ffn_w[...])
        got_grad.wait(enc_grad_in)

    @pl.when(flag[0] == 0)
    def _():
        got = [load.start(dq_in, dq), load.start(first_in, first_w)]
        got_x1.start()
        got_grad.start(dec_grad_in)
        wait_all(got)
        grad_normed[...] = mm_nt(dq[...], first_w[...])
        got_grad.wait()

    got_x1.wait()
    norm_backward(x1, grad_normed, vectors[2], grad, grad, gain_sum, offset_sum)
    stored = store.start(grad, grad_out)
    small_out[2:3, :] = column_sum(gain_sum)
    small_out[3:4, :] = column_sum(offset_sum)
    stored.wait()


def attention_back_body(
    heads, flag, grad_in, qkv_in, weights_in, context_in, outw_in, h1_in, *rest
):
    grad_qkv_out, scores_out, *rest = rest
    count = len(rest) - 14
    outs = rest[:count]
    (
        grad, qkv, weights, context, out_w, h1, grad_low, grad_context, grad_qkv, mixed_g,
        grad_scores, context_low, loads, stores,
    ) = rest[count:]
    width = context.shape[1]
    row_count, length = weights.shape[0], weights.shape[2]
    load = Mover(loads)
    store = Mover(stores)
    got_grad = [load.start(grad_in, grad), load.start(outw_in, out_w)]
    got_context = load.start(context_in, context)
    got_attention = [load.start(weights_in, weights), load.start(qkv_in, qkv)]
    got_h1 = load.start(h1_in, h1)
    wait_all(got_grad)

    def lower(at):
        grad_low[at, :] = grad[at, :].astype(bf16)

    each_rows(grad.shape[0], lower)
    grad_context[...] = mm_nt(grad_low[...], out_w[...]).astype(bf16)
    got_context.wait()
    context_low[...] = context[...].astype(bf16)
    mixed_g[:, pl.ds(0, width)] = mm_tn(context_low[...], grad_low[...]).astype(bf16)
    wait_all(got_attention)
    scale = (width // heads) ** (-0.5)

    @pl.loop(0, heads // 2, unroll=3)
    def _(pair):
        lanes = pl.multiple_of(pair * 128, 128)
        totals = [None, None]
        for row in range(row_count):
            at = slice(row * length, (row + 1) * length)
            grad_q, grad_k, grad_v, parts = attend_pair_back(
                weights[row, pair],
                qkv[at, pl.ds(lanes, 128)],
                qkv[at, pl.ds(width + lanes, 128)],
                qkv[at, pl.ds(2 * width + lanes, 128)],
                context[at, pl.ds(lanes, 128)],
                grad_context[at, pl.ds(lanes, 128)],
                scale,
            )
            grad_qkv[at, pl.ds(lanes, 128)] = grad_q.astype(bf16)
            grad_qkv[at, pl.ds(width + lanes, 128)] = grad_k.astype(bf16)
            grad_qkv[at, pl.ds(2 * width + lanes, 128)] = grad_v.astype(bf16)
            totals = [p if t is None else t + p for t, p in zip(totals, parts)]
        for head in range(2):
            grad_scores[pair * 2 + head] = totals[head]

    got_h1.wait()
    copies = [store.start(grad_qkv, grad_qkv_out), store.start(grad_scores, scores_out)]
    for step, at in enumerate(spans(3 * width, width)):
        mixed_g[:, pl.ds(width + at.start, width)] = mm_tn(h1[...], grad_qkv[:, at]).astype(bf16)
        if step != 1:
            both = pl.ds(0 if step == 0 else 2 * width, 2 * width)
            copies += put_columns(store, mixed_g, outs, flag[1], both)
    wait_all(copies)


def sum_diagonals(grid):
    length = grid.shape[0]
    padded = jnp.concatenate([grid, jnp.zeros((length, length), f32)], axis=1)
    folded = padded[0:8, :]
    for block in range(1, length // 8):
        folded = folded + pltpu.roll(
            padded[block * 8 : (block + 1) * 8, :], 2 * length - block * 8, 1
        )
    line = folded[0:1, :]
    for sub in range(1, 8):
        line = line + pltpu.roll(folded[sub : sub + 1, :], 2 * length - sub, 1)
    return pltpu.roll(line, length - 1, 1)


def last_body(
    flag, offsets, vectors, small_in, grad_in, grad_qkv_in, qkvw_in, rows_in, scores_in,
    small_out, result_out,
    grad, grad_qkv, qkv_w, rows, grad_normed, grad_scores, diagonals, one_hot, gain_sum, offset_sum,
    loads, stores,
):
    small_out[...] = small_in[...]
    heads, bucket_count = grad_scores.shape[0], one_hot.shape[0]
    load = Mover(loads)
    store = Mover(stores)
    got = [load.start(grad_qkv_in, grad_qkv), load.start(qkvw_in, qkv_w)]
    got_rows = [load.start(rows_in, rows), load.start(grad_in, grad)]
    got_scores = load.start(scores_in, grad_scores)
    wait_all(got)
    grad_normed[...] = mm_nt(grad_qkv[...], qkv_w[...])
    wait_all(got_rows)
    norm_backward(rows, grad_normed, vectors[0], grad, grad, gain_sum, offset_sum)
    small_out[0:1, :] = column_sum(gain_sum)
    small_out[1:2, :] = column_sum(offset_sum)
    stored = store.start(grad, result_out)

    got_scores.wait()

    @pl.loop(0, heads)
    def _(head):
        diagonals[pl.ds(head, 1), :] = sum_diagonals(grad_scores[head])

    one_hot[...] = (offsets[...] == lax.broadcasted_iota(jnp.int32, one_hot.shape, 0)).astype(f32)
    small_out[pl.ds(16, heads), pl.ds(0, bucket_count)] = lax.dot_general(
        diagonals[...], one_hot[...], (((1,), (1,)), ((), ())), precision=lax.Precision.HIGHEST,
        preferred_element_type=f32,
    )
    stored.wait()


def output_body(
    flag, vectors, u_in, d2_in, down_in, low_in, low_out, u, d2, down_w, low, loads, stores
):
    load = Mover(loads)
    stored = Mover(stores).note(low, low_out)
    got_low = load.note(low_in, low)

    @pl.when(flag[0] == 1)
    def _():
        got_low.start()
        got_low.wait()
        stored.start()

    @pl.when(flag[0] == 0)
    def _():
        wait_all([load.start(u_in, u), load.start(d2_in, d2), load.start(down_in, down_w)])
        value = d2[...] + (mm(u[...], down_w[...]) + vectors[6])
        low[...] = value.astype(bf16)
        stored.start()

    stored.wait()


def pair_sum_body(everywhere, flag, kept_in, got_in, out, kept, got, total, loads, stores):
    @pl.when(jnp.logical_or(flag[0] == 0, everywhere))
    def _():
        load = Mover(loads)
        store = Mover(stores)
        blocks = out.shape[0]
        ready = []
        for step in range(blocks):
            block = 2 * step + 1 - flag[2]
            ready.append(
                (load.start(kept_in.at[block], kept.at[step]), load.start(got_in.at[block], got.at[step]))
            )
        copies = []
        for step in range(blocks):
            wait_all(ready[step])
            total[step] = (kept[step].astype(f32) + got[step].astype(f32)).astype(bf16)
            copies.append(store.start(total.at[step], out.at[step]))
        wait_all(copies)


def pair_sum(flag, kept, got, everywhere):
    chips, depth, width = kept.shape
    part = (chips // 2, depth, width)
    return run_kernel(
        functools.partial(pair_sum_body, everywhere),
        (flag, kept, got),
        [SMEM, ANY, ANY],
        [shape_of(part, bf16)],
        [ANY],
        [(part, bf16)] * 3,
        chips, chips // 2, "pair_sum",
    )[0]


def chip_sum_body(
    everywhere, flag, kept_in, got_in, far_in, first_out, second_out, third_out, own_out,
    kept, got, far, total, own, loads, stores,
):
    @pl.when(jnp.logical_or(flag[0] == 0, everywhere))
    def _():
        load = Mover(loads)
        store = Mover(stores)
        ready = []
        for step in range(4):
            place = lax.rem(flag[3] + step + 1, 4)
            block = 2 * place + flag[2]
            ready.append(
                [
                    load.start(kept_in.at[block], kept.at[step]),
                    load.start(got_in.at[block], got.at[step]),
                    load.start(far_in.at[place], far.at[step]),
                ]
            )
        copies = []
        for step, out in enumerate((first_out, second_out, third_out, own_out)):
            wait_all(ready[step])
            value = kept[step].astype(f32) + got[step].astype(f32) + far[step].astype(f32)
            if step < 3:
                total[step] = value.astype(bf16)
                copies.append(store.start(total.at[step], out))
            else:
                own[...] = value
                copies.append(store.start(own, out))
        wait_all(copies)


def chip_sum(flag, kept, got, far, everywhere):
    _, depth, width = kept.shape
    one = (depth, width)
    return run_kernel(
        functools.partial(chip_sum_body, everywhere),
        (flag, kept, got, far),
        [SMEM, ANY, ANY, ANY],
        [shape_of(one, bf16)] * 3 + [shape_of(one, f32)],
        [ANY] * 4,
        [((4,) + one, bf16)] * 3 + [((3,) + one, bf16), (one, f32)],
        12, 4, "chip_sum",
    )


def pick_body(flag, first_in, second_in, out, held, loads, stores):
    @pl.when(flag[0] == 1)
    def _():
        got = Mover(loads).note(first_in, held)
        for core, source in enumerate((first_in, second_in)):

            @pl.when(flag[1] == core)
            def _(source=source):
                got.start(source)

        got.wait()
        Mover(stores).start(held, out).wait()


def finish_body(
    place, flag, first, second, third, own, cross, back, small,
    qkv_out, out_out, cf_out, cs_out, vec_out, fbias_out, table_out,
):
    width = out_out.shape[1]
    total = own[...]
    for part in (first, second, third):
        total = total + part[...].astype(f32)
    out_out[...] = total[:, :width]
    qkv_out[...] = total[:, width:]
    chosen = jnp.where(flag[0] == 1, back[...], cross[...])
    cf_out[...] = chosen[:, :width]
    cs_out[...] = chosen[:, width:]
    share = vec_out.shape[2]
    turned = pltpu.roll(small[0:8, :], lax.rem(width - place[0] * share, width), 1)
    for row in range(vec_out.shape[0]):
        vec_out[row] = turned[row : row + 1, :share]
    share = fbias_out.shape[1]
    per_row = width // share
    row = small[pl.ds(8 + lax.div(place[0], per_row), 1), :]
    turned = pltpu.roll(row, lax.rem(width - lax.rem(place[0], per_row) * share, width), 1)
    fbias_out[...] = turned[:, :share]
    for head in range(table_out.shape[0]):
        table_out[head] = small[16 + head : 17 + head, : table_out.shape[2]]


def shape_of(dims, dtype):
    return jax.ShapeDtypeStruct(tuple(dims), dtype)


def size_of(dims, dtype):
    total = jnp.dtype(dtype).itemsize
    for dim in dims:
        total *= dim
    return total


def run_kernel(
    body, operands, places, outs, out_places, scratch, loads, stores, name, alone=False
):
    held = sum(size_of(dims, dtype) for dims, dtype in scratch)
    flat, form = jax.tree.flatten(operands)
    flat_places = [
        place for place, operand in zip(places, operands, strict=True) for _ in jax.tree.leaves(operand)
    ]

    flat_outs, out_form = jax.tree.flatten(outs)
    held_at = len(flat) + len(flat_outs)

    def kernel(*refs):
        results = out_form.unflatten(refs[len(flat) : held_at])
        return body(*form.unflatten(refs[: len(flat)]), *results, *refs[held_at:])

    results = pl.pallas_call(
        kernel,
        in_specs=flat_places,
        out_specs=out_places,
        out_shape=flat_outs,
        scratch_shapes=[pltpu.VMEM(dims, dtype) for dims, dtype in scratch]
        + [pltpu.SemaphoreType.DMA((loads,)), pltpu.SemaphoreType.DMA((stores,))],
        compiler_params=pltpu.CompilerParams(
            vmem_limit_bytes=all_bytes if alone else held + spare_bytes
        ),
        cost_estimate=pl.CostEstimate(flops=1, bytes_accessed=1, transcendentals=0),
        name=name,
    )(*flat)
    return out_form.unflatten(results)


def after(value, *others):
    return lax.optimization_barrier((value,) + others)[0]


def block_of(always, steps, *operands):
    shapes = jax.eval_shape(steps, *operands)

    def blank(*_):
        return jax.tree.map(lambda leaf: jnp.zeros(leaf.shape, leaf.dtype), shapes)

    return lax.cond(always, steps, blank, *operands)


class Ring:
    def __init__(self, devices, everywhere):
        self.devices = devices
        self.everywhere = everywhere

    def send(self, shard, moved):
        pairs = [(i, moved(i)) for i in range(self.devices)]
        if self.everywhere:
            return lax.ppermute(shard, "batch", pairs)
        pairs = [(self.devices + i, self.devices + j) for i, j in pairs]
        return lax.ppermute(shard, ("section", "batch"), pairs)

    def to_core(self, given):
        return self.send(given, lambda i: i ^ 1)

    def to_chip(self, out):
        return self.send(out, lambda i: i ^ 2)

    def sums(self, flag, *held):
        return chip_sum(flag, *held, self.everywhere)

    def along(self, outs):
        return [
            self.send(out, lambda i, away=away: (i + 4 * away) % 16)
            for away, out in zip((2, 1, 3), (outs[1], outs[0], outs[2]))
        ]


def per_device(
    inputs, cotangent, segments, buckets, qkv_weight, out_weight, in_weight, down_weight,
    cross_first, cross_second, vectors, ffn_bias, position_table,
):
    row_count, length, width = inputs.shape[1:]
    heads = position_table.shape[2]
    bucket_count = position_table.shape[1]
    hidden = in_weight.shape[2]
    tokens = row_count * length
    pairs = heads // 2
    on_encoder = lax.axis_index("section") == 0
    place = lax.axis_index("batch")
    core = lax.rem(place, 2)
    devices = lax.axis_size("batch")
    by_chip = devices == 16
    always = place < devices
    flag = jnp.stack(
        [on_encoder.astype(jnp.int32), core, lax.rem(lax.div(place, 2), 2), lax.div(place, 4)]
    )
    offsets = jnp.pad(buckets, (0, 1), constant_values=-1)[None]
    table = jnp.transpose(position_table, (2, 0, 1))[:, 0]
    rows = inputs.reshape(tokens, width)
    cot = cotangent.reshape(tokens, width)
    qkv_w, out_w, ffn_w, down_w = qkv_weight[0], out_weight[0], in_weight[0], down_weight[0]
    first_w, second_w = cross_first[0], cross_second[0]
    vec = jnp.transpose(vectors, (1, 0, 2))
    fbias = ffn_bias

    tw, th = (tokens, width), (tokens, hidden)
    wide = (tokens, 3 * width)
    square = (row_count, pairs, length, 2 * length)
    row_tw, row_th, row_wide = (length, width), (length, hidden), (length, 3 * width)
    row_square = (1, pairs, length, 2 * length)
    small = (32, width)

    (picked,) = run_kernel(
        pick_body, (flag, first_w, second_w), [SMEM, ANY, ANY], [shape_of((width, width), bf16)],
        [ANY], [((width, width), bf16)], 1, 1, "pick",
    )
    sent = lax.ppermute(picked, "section", [(0, 1)])
    flag = after(flag, picked)

    def piece(depth_rows, columns):
        if not by_chip:
            return [shape_of((depth_rows, columns), bf16)]
        return [shape_of((devices // 2, depth_rows // devices, columns), bf16)] * 2

    down_piece, ffn_piece = piece(hidden, width), piece(width, hidden)
    mixed_piece = piece(width, 4 * width)
    count = len(down_piece)
    share_copies = devices if by_chip else 1
    def run_first(row, flag):
        return run_kernel(
            functools.partial(first_body, heads, row),
            (flag, segments, offsets, table, vec, fbias, rows, cot, qkv_w, out_w, ffn_w,
             down_w, first_w),
            [SMEM] + [VMEM] * 5 + [ANY] * 7,
            [
                shape_of(row_tw, f32), shape_of(row_tw, bf16), shape_of(row_wide, bf16),
                shape_of(row_square, bf16), shape_of(row_tw, f32), shape_of(row_tw, bf16),
                shape_of(row_th, bf16), shape_of(row_th, bf16), shape_of(row_tw, f32),
                shape_of(row_tw, bf16), shape_of(row_tw, bf16), shape_of(row_tw, bf16),
            ],
            [ANY] * 12,
            [
                (row_tw, bf16), ((width, 3 * width), bf16), ((width, width), bf16),
                ((width, hidden), bf16), ((hidden, width), bf16), ((width, width), bf16),
                (row_tw, bf16), (row_tw, bf16), (row_wide, bf16), (row_square, bf16), (row_tw, bf16),
                (row_tw, f32), (row_tw, bf16), (row_th, bf16), (row_th, bf16), (row_tw, f32),
                (row_tw, bf16), ((heads, 2 * length), f32), ((length, length), f32),
                (row_tw, f32), ((2, length, tile), f32),
            ],
            7, 13, "first", True,
        )

    def run_cross(row, flag, small_grad, memory, sent, sent_other, own, earlier):
        x1, qc, slope = own
        last_row = row == row_count - 1
        products = [(tw, bf16)] * 7 + [((width, 4 * width), bf16)] if last_row else []
        return run_kernel(
            functools.partial(cross_body, heads, row),
            (flag, segments, vec, fbias, small_grad, memory, sent, sent_other, second_w, x1, qc, cot,
             ffn_w, slope, earlier if last_row else ()),
            [SMEM] + [VMEM] * 4 + [ANY] * 10,
            [shape_of(small, f32), shape_of(row_tw, bf16), shape_of(row_th, bf16),
             shape_of(row_th, bf16), shape_of(row_tw, f32), shape_of(row_tw, f32)]
            + [shape_of(row_tw, bf16)] * 6 + [mixed_piece if last_row else []],
            [VMEM] + [ANY] * (11 + (count if last_row else 0)),
            [
                (row_tw, bf16), ((width, width), bf16), ((width, width), bf16),
                ((width, width), bf16), (row_tw, f32), (row_tw, bf16), (row_tw, bf16),
                ((width, hidden), bf16), (row_tw, bf16), (row_tw, bf16), (row_square, bf16),
                (row_tw, bf16), (row_tw, f32), (row_tw, bf16), (row_th, bf16), (row_th, bf16),
                (row_tw, f32), (row_tw, f32), (row_tw, bf16), (row_tw, bf16), (row_tw, bf16),
                (row_tw, bf16), (row_tw, bf16), ((length, length), f32), ((8, width), f32),
                ((8, width), f32), (row_tw, f32), ((2, length, tile), f32),
            ] + products,
            9 + (7 * row_count if last_row else 0), 11 + 2 * share_copies, "cross", True,
        )

    def to_decoder(value):
        return lax.ppermute(value, "section", [(0, 1)])

    def to_encoder(value):
        return lax.ppermute(value, "section", [(1, 0)])

    kept_rows = [run_first(0, flag)]
    for row in range(1, row_count):

        def first_steps(low, flag, row=row):
            memory = to_decoder(low)
            return memory, run_first(row, flag)

        low = kept_rows[-1][9]
        memory, outs = block_of(always, first_steps, low, after(flag, low))
        kept_rows.append(outs)
        memories = (*memories, memory) if row > 1 else (memory,)

    def cross_steps(low, flag, first_memory, sent, own, first_earlier):
        memory = to_decoder(low)
        other = lax.ppermute(sent, "batch", [(i, i ^ 1) for i in range(devices)])
        return memory, other, run_cross(0, flag, fbias, first_memory, sent, other, own, first_earlier)

    def own_of(row):
        outs = kept_rows[row]
        return outs[0], outs[11], outs[7]

    def earlier_of(rows):
        hc = tuple(outs[10] for outs in kept_rows)
        return (
            hc,
            *(tuple(outs[part] for outs in rows) for part in (6, 5, 10)),
            tuple(memories[: len(rows)]),
            *(tuple(outs[part] for outs in rows) for part in (7, 8)),
        )

    low = kept_rows[-1][9]
    memory, sent_other, outs = block_of(
        always, cross_steps, low, after(flag, low), memories[0], sent, own_of(0), earlier_of(())
    )
    memories = (*memories, memory)
    small_grad, *outs = outs
    cross_rows, returned = [outs], ()
    for row in range(1, row_count):

        def return_steps(dm, flag, *operands, row=row):
            back = to_encoder(dm)
            return back, run_cross(row, flag, *operands)

        dm = cross_rows[-1][9]
        back, outs = block_of(
            always, return_steps, dm, after(flag, dm), small_grad, memories[row], sent, sent_other,
            own_of(row), earlier_of(cross_rows),
        )
        small_grad, *outs = outs
        cross_rows.append(outs)
        returned = (*returned, back)
    dm = cross_rows[-1][9]
    returned = (*returned, to_encoder(dm))
    x1, h1, qkv, weights, context, h2, u, slope, e2, low, hc, qc = zip(*kept_rows)
    dec_h2, dec_u, dec_slope, d2, grad, _, dq, _, _, dm, _, cross_gs = zip(*cross_rows)
    cross_g = cross_gs[-1]

    cross, down, ffn, mixed = (
        Ring(devices, name != "cross") for name in ("cross", "down", "ffn", "mixed")
    )

    flag = after(flag, *dm)

    def run_down(flag, vec, small_grad, returned, cot, e2, u, dec_u):
        small_grad, enc_grad, enc_low, *pieces = run_kernel(
            down_body,
            (flag, vec, small_grad, returned, cot, e2, u, dec_u),
            [SMEM] + [VMEM] * 2 + [ANY] * 5,
            [shape_of(small, f32), shape_of(tw, f32), shape_of(tw, bf16)] + down_piece,
            [VMEM] + [ANY] * (2 + count),
            [
                (tw, bf16), (tw, bf16), (tw, f32), (th, bf16), (tw, f32), (tw, bf16),
                ((hidden, width), bf16), ((8, width), f32), ((8, width), f32),
            ],
            1 + 3 * row_count, 2 + max(share_copies, hidden // tile), "down",
        )
        return small_grad, enc_grad, enc_low, pieces

    def run_hidden(flag, enc_low, down_w, slope):
        return run_kernel(
            hidden_body,
            (flag, enc_low, down_w, slope),
            [SMEM] + [ANY] * 3,
            [shape_of(th, bf16)],
            [ANY],
            [(tw, bf16), ((hidden, width), bf16), (th, bf16)],
            1 + row_count + hidden // tile, hidden // tile, "hidden",
        )[0]

    def run_ffn(flag, small_grad, enc_slope):
        small_grad, *pieces = run_kernel(
            ffn_body,
            (flag, small_grad, (h2, enc_slope), (dec_h2, dec_slope)),
            [SMEM, VMEM, ANY, ANY],
            [shape_of(small, f32)] + ffn_piece,
            [VMEM] + [ANY] * count,
            [(th, bf16), (tw, bf16), ((width, hidden), bf16)],
            2 * row_count, hidden // (2 * tile) * share_copies, "ffn",
        )
        return small_grad, pieces

    def run_hidden_back(flag, vec, small_grad, slope, ffn_w, dq, first_w, x1, enc_grad, grad):
        return run_kernel(
            hidden_back_body,
            (flag, vec, small_grad, slope, ffn_w, dq, first_w, x1, enc_grad, grad),
            [SMEM] + [VMEM] * 2 + [ANY] * 7,
            [shape_of(small, f32), shape_of(tw, f32)],
            [VMEM, ANY],
            [
                (th, bf16), ((width, hidden), bf16), (tw, bf16), ((width, width), bf16), (tw, f32),
                (tw, f32), (tw, f32), ((8, width), f32), ((8, width), f32),
            ],
            3 + 3 * row_count, 1, "hidden_back",
        )

    def run_attention_back(flag, grad, qkv, weights, context, out_w, h1):
        grad_qkv, grad_scores, *pieces = run_kernel(
            functools.partial(attention_back_body, heads),
            (flag, grad, qkv, weights, context, out_w, h1),
            [SMEM] + [ANY] * 6,
            [shape_of(wide, bf16), shape_of((heads, length, length), f32)] + mixed_piece,
            [ANY] * (2 + count),
            [
                (tw, f32), (wide, bf16), (square, bf16), (tw, f32), ((width, width), bf16),
                (tw, bf16), (tw, bf16), (tw, bf16), (wide, bf16), ((width, 4 * width), bf16),
                ((heads, length, length), f32), (tw, bf16),
            ],
            2 + 4 * row_count, 2 + 2 * share_copies, "attention_back",
        )
        return grad_qkv, grad_scores, pieces

    def run_last(flag, vec, small_grad, grad, grad_qkv, qkv_w, rows, grad_scores):
        return run_kernel(
            last_body,
            (flag, offsets, vec, small_grad, grad, grad_qkv, qkv_w, rows, grad_scores),
            [SMEM] + [VMEM] * 3 + [ANY] * 5,
            [shape_of(small, f32), shape_of(tw, f32)],
            [VMEM, ANY],
            [
                (tw, f32), (wide, bf16), ((width, 3 * width), bf16), (tw, bf16), (tw, f32),
                ((heads, length, length), f32), ((heads, 2 * length), f32),
                ((bucket_count, 2 * length), f32), ((8, width), f32), ((8, width), f32),
            ],
            5, 1, "last",
        )

    def run_output(flag, vec, dec_u, d2, down_w, low):
        return run_kernel(
            output_body,
            (flag, vec, dec_u, d2, down_w, low),
            [SMEM, VMEM] + [ANY] * 4,
            [shape_of(tw, bf16)],
            [ANY],
            [(th, bf16), (tw, f32), ((hidden, width), bf16), (tw, bf16)],
            1 + 3 * row_count, 1, "output",
        )[0]

    def beside(ring, pieces, kernel, *operands):
        def steps(kept, given, flag, *operands):
            got = ring.to_core(given)
            outs = kernel(flag, *operands)
            out = pair_sum(after(flag, *jax.tree.leaves(outs)), kept, got, ring.everywhere)
            return outs, got, out

        return block_of(always, steps, *pieces, *operands)

    if not by_chip:
        small_grad, enc_grad, enc_low, down_g = run_down(
            flag, vec, small_grad, returned, cot, e2, u, dec_u
        )
        enc_slope = run_hidden(flag, enc_low, down_w, slope)
        small_grad, ffn_g = run_ffn(flag, small_grad, enc_slope)
        small_grad, grad = run_hidden_back(
            flag, vec, small_grad, enc_slope, ffn_w, dq, first_w, x1, enc_grad, grad
        )
        grad_qkv, grad_scores, mixed_g = run_attention_back(
            flag, grad, qkv, weights, context, out_w, h1
        )
        small_grad, result = run_last(
            flag, vec, small_grad, grad, grad_qkv, qkv_w, rows, grad_scores
        )
        low = run_output(flag, vec, dec_u, d2, down_w, low)
        small_grad = lax.psum(small_grad, "batch")
        cross_share, down_share, ffn_share, mixed_share = (
            lax.psum_scatter(pieces[0], "batch", scatter_dimension=0, tiled=True).astype(f32)
            for pieces in (cross_g, down_g, ffn_g, mixed_g)
        )
        cross_back = lax.ppermute(cross_share[:, 2 * width :], "section", [(1, 0)])
        cross_share = jnp.where(on_encoder, cross_back, cross_share[:, : 2 * width])
        cf_share, cs_share = cross_share[:, :width], cross_share[:, width:]
        out_share, qkv_share = mixed_share[:, :width], mixed_share[:, width:]
        vec_share = lax.dynamic_slice_in_dim(
            small_grad[:7], place * (width // devices), width // devices, 1
        )
        fbias_all = small_grad[8 : 8 + hidden // width].reshape(1, hidden)
        fbias_share = lax.dynamic_slice_in_dim(
            fbias_all, place * (hidden // devices), hidden // devices, 1
        )
        table_total = small_grad[16 : 16 + heads, :bucket_count].T
    else:

        def cross_steps(flag, kept, given):
            got = cross.to_core(given)
            return got, pair_sum(flag, kept, got, False)

        got, out = block_of(always, cross_steps, flag, *cross_g)
        flag = after(flag, out)

        def down_steps(out, kept, got, flag, down_w, slope, ffn_ins, *operands):
            far = cross.to_chip(out)
            small_grad, enc_grad, enc_low, pieces = run_down(flag, *operands)
            flag = after(flag, small_grad)
            enc_slope, down_got, out = beside(
                down, pieces, run_hidden, flag, enc_low, down_w, slope
            )
            down_held = (pieces[0], down_got, down.to_chip(out))
            flag = after(flag, out)
            small_grad, pieces = run_ffn(flag, small_grad, enc_slope)
            flag = after(flag, small_grad)
            *outs, cross_own = cross.sums(flag, kept, got, far)
            flag = after(flag, *outs)
            cross_last = (*cross.along(outs), cross_own)
            sums = beside(
                ffn, pieces, run_hidden_back, flag, vec, small_grad, enc_slope, *ffn_ins[:4],
                enc_grad, ffn_ins[4],
            )
            outs = down.sums(after(flag, sums[2]), *down_held)
            return outs, cross_last, pieces[0], sums

        down_outs, cross_last, kept, sums = block_of(
            always, down_steps, out, cross_g[0], got, flag, down_w, slope,
            (ffn_w, dq, first_w, x1, grad), vec, small_grad, returned, cot, e2, u, dec_u,
        )
        (small_grad, grad), got, ffn_out = sums
        ffn_held = (kept, got)
        flag = after(flag, ffn_out, *down_outs)

        def attention_steps(flag, ffn_out, outs, *operands):
            far = ffn.to_chip(ffn_out)
            moved = down.along(outs)
            grad_qkv, grad_scores, pieces = run_attention_back(flag, *operands)

            def swap(flag, kept, given):
                got = mixed.to_core(given)
                return got, pair_sum(flag, kept, got, True)

            swapped = block_of(always, swap, after(flag, grad_qkv), *pieces)
            return moved, far, grad_qkv, grad_scores, pieces[0], swapped

        moved, ffn_far, grad_qkv, grad_scores, kept, swapped = block_of(
            always, attention_steps, flag, ffn_out, down_outs[:3], grad, qkv, weights, context, out_w,
            h1,
        )
        down_last = (*moved, down_outs[3])
        got, out = swapped
        flag = after(flag, out)

        def swapped_small(small_grad, away):
            pairs = [(i, i ^ away) for i in range(devices)]
            return small_grad + lax.ppermute(small_grad, "batch", pairs)

        def last_steps(flag, out, held, mixed_held, *operands):
            far = mixed.to_chip(out)
            *outs, own = ffn.sums(flag, *held)
            moved = (*ffn.along(outs), own)
            small_grad, result = run_last(after(flag, *outs), *operands)

            small_grad = block_of(always, lambda s: swapped_small(s, 1), small_grad)
            outs = mixed.sums(after(flag, small_grad), *mixed_held, far)
            return outs, moved, small_grad, result

        (*outs, own), ffn_last, small_grad, result = block_of(
            always, last_steps, flag, out, (*ffn_held, ffn_far), (kept, got), vec, small_grad,
            grad, grad_qkv, qkv_w, rows, grad_scores,
        )

        moved = mixed.along(outs)

        def end_steps(small_grad, cross_last, down_last, ffn_last, flag, *operands):
            back, cross_share, down_share, ffn_share = [
                sum(part[:, at].astype(f32) for part in parts)
                for parts, at in (
                    (cross_last, slice(2 * width, 4 * width)),
                    (cross_last, slice(0, 2 * width)),
                    (down_last, slice(None)),
                    (ffn_last, slice(None)),
                )
            ]
            back = lax.ppermute(back, "section", [(1, 0)])
            small_grad = swapped_small(small_grad, 2)
            low = run_output(after(flag, small_grad), *operands)
            small_grad = swapped_small(small_grad, 4)
            small_grad = swapped_small(after(small_grad, low, down_share, ffn_share), 8)
            return small_grad, low, back, cross_share, down_share, ffn_share

        small_grad, low, back, cross_share, down_share, ffn_share = block_of(
            always, end_steps, after(small_grad, *outs), cross_last, down_last, ffn_last, flag, vec,
            dec_u, d2, down_w, low,
        )
        one = (width // devices, width)
        qkv_share, out_share, cf_share, cs_share, vec_share, fbias_share, table_total = pl.pallas_call(
            finish_body,
            in_specs=[SMEM] * 2 + [VMEM] * 7,
            out_specs=[VMEM] * 7,
            out_shape=[
                shape_of((width // devices, 3 * width), f32), shape_of(one, f32), shape_of(one, f32),
                shape_of(one, f32), shape_of((7, 1, width // devices), f32),
                shape_of((1, hidden // devices), f32), shape_of((heads, 1, bucket_count), f32),
            ],
            name="finish",
        )(place[None], flag, *moved, own, cross_share, back, small_grad)
        vec_share = jnp.transpose(vec_share, (1, 0, 2))[0]
        table_total = jnp.transpose(table_total, (1, 2, 0))[0]
    return (
        low.reshape((1, row_count, length, width)),
        result.reshape((1, row_count, length, width)),
        qkv_share[None],
        out_share[None],
        ffn_share[None],
        down_share[None],
        cf_share[None],
        cs_share[None],
        vec_share[None],
        fbias_share,
        table_total[None],
    )


def solution(mesh):
    return jax.shard_map(
        per_device,
        mesh=mesh,
        in_specs=(
            P("section", "batch", None, None),
            P("section", "batch", None, None),
            P(None, "batch", None),
            P(),
            P("section", None, None),
            P("section", None, None),
            P("section", None, None),
            P("section", None, None),
            P("section", None, None),
            P("section", None, None),
            P("section", None, None),
            P("section", None),
            P("section", None, None),
        ),
        out_specs=(
            P("section", "batch", None, None),
            P("section", "batch", None, None),
            P("section", "batch", None),
            P("section", "batch", None),
            P("section", "batch", None),
            P("section", "batch", None),
            P("section", "batch", None),
            P("section", "batch", None),
            P("section", None, "batch"),
            P("section", "batch"),
            P("section", None, None),
        ),
        check_vma=False,
    )
```

```python
import functools

import jax
import jax.numpy as jnp
from jax import lax
from jax.experimental import pallas as pl
from jax.experimental.pallas import tpu as pltpu
from jax.sharding import PartitionSpec as P

norm_epsilon = 1e-05
masked_score = -1e30
half_root = 0.7071067811865476
density_scale = 0.3989422804014327
tile = 768
chunk = 256
rotations = (2, 3, 1)
spare_bytes = 8 * 1024 * 1024
all_bytes = 62 * 1024 * 1024

f32 = jnp.float32
bf16 = jnp.bfloat16
ANY = pl.BlockSpec(memory_space=pl.ANY)
SMEM = pl.BlockSpec(memory_space=pltpu.SMEM)
VMEM = pl.BlockSpec(memory_space=pltpu.VMEM)


def mm(left, right):
    return jnp.dot(left, right, preferred_element_type=f32)


def mm_nt(left, right):
    return lax.dot_general(left, right, (((1,), (1,)), ((), ())), preferred_element_type=f32)


def mm_tn(left, right):
    return lax.dot_general(left, right, (((0,), (0,)), ((), ())), preferred_element_type=f32)


def mean_of(values):
    return jnp.sum(values, axis=-1, keepdims=True) * (1.0 / values.shape[-1])


def normalised(values):
    centre = values - mean_of(values)
    rate = lax.rsqrt(mean_of(centre * centre) + norm_epsilon)
    return centre * rate, rate


def each_rows(count, body):
    @pl.loop(0, count // chunk)
    def _(step):
        body(pl.ds(pl.multiple_of(step * chunk, chunk), chunk))


def each_tile(count, body, width=tile):
    if count == width:
        body(pl.ds(0, width))
        return

    @pl.loop(0, count // width)
    def _(step):
        body(pl.ds(pl.multiple_of(step * width, width), width))


def norm_forward(source, gain, offset, target, also=None):
    def rows(at):
        unit, _ = normalised(source[at, :].astype(f32))
        normed = unit * gain + offset
        target[at, :] = normed.astype(target.dtype)

    each_rows(source.shape[0], rows)


def norm_backward(
    source, grad_normed, gain, upstream, target, gain_sum, offset_sum, low=None
):
    gain_sum[...] = jnp.zeros_like(gain_sum)
    offset_sum[...] = jnp.zeros_like(offset_sum)

    def rows(at):
        unit, rate = normalised(source[at, :].astype(f32))
        upper = grad_normed[at, :]
        product = upper * unit
        gain_sum[...] += jnp.sum(product.reshape(-1, 8, product.shape[1]), axis=0)
        offset_sum[...] += jnp.sum(upper.reshape(-1, 8, upper.shape[1]), axis=0)
        scaled = upper * gain
        inner = mean_of(scaled)
        along = mean_of(product * gain)
        result = rate * (scaled - inner - unit * along)
        if upstream is not None:
            result = result + upstream[at, :].astype(f32)
        target[at, :] = result
        if low is not None:
            low[at, :] = result.astype(bf16)

    each_rows(source.shape[0], rows)


def column_sum(partial):
    return jnp.sum(partial[...], axis=0, keepdims=True)


def lower_lanes(shape):
    return lax.broadcasted_iota(jnp.int32, shape, 1) < shape[1] // 2


def split_pair(block):
    lower = lower_lanes(block.shape)
    zero = jnp.zeros_like(block)
    return jnp.concatenate([jnp.where(lower, block, zero), jnp.where(lower, zero, block)], axis=0)


def join_pair(stacked):
    rows = stacked.shape[0] // 2
    lower = lower_lanes((rows, stacked.shape[1]))
    return jnp.where(lower, stacked[:rows], stacked[rows:])


def attend_pair(queries, key_rows, values, additions, scale):
    length = queries.shape[0]
    scores = mm_nt((queries * scale).astype(bf16), split_pair(key_rows))
    parts = []
    for head in range(2):
        part = scores[:, head * length : (head + 1) * length] + additions[head]
        exponent = jnp.exp(part - jnp.max(part, axis=-1, keepdims=True))
        parts.append(exponent * (1.0 / jnp.sum(exponent, axis=-1, keepdims=True)))
    weights = jnp.concatenate(parts, axis=1).astype(bf16)
    return weights, mm(weights, split_pair(values))


def attend_pair_back(weights, queries, key_rows, values, context, grad_context, scale):
    length = queries.shape[0]
    grad_weights = mm_nt(grad_context, split_pair(values))
    product = grad_context.astype(f32) * context.astype(f32)
    lower = lower_lanes(product.shape)
    parts = []
    for head in range(2):
        at = slice(head * length, (head + 1) * length)
        own = jnp.where(lower, product, 0.0) if head == 0 else jnp.where(lower, 0.0, product)
        centred = jnp.sum(own, axis=-1, keepdims=True)
        parts.append(weights[:, at].astype(f32) * (grad_weights[:, at] - centred))
    grad_raw = jnp.concatenate(parts, axis=1).astype(bf16)
    grad_queries = mm(grad_raw, split_pair(key_rows)) * scale
    grad_keys = join_pair(mm_tn(grad_raw, queries)) * scale
    grad_values = join_pair(mm_tn(weights, grad_context))
    return grad_queries, grad_keys, grad_values, parts


def same_sentence(query_ids, key_ids):
    length = query_ids.shape[1]
    across = jnp.broadcast_to(key_ids.astype(f32), (length, length))
    down = jnp.broadcast_to(query_ids.astype(f32), (length, length)).T
    return across == down


class Move:
    def __init__(self, sources, target, semaphores):
        self.sources, self.target, self.semaphores = sources, target, semaphores

    def copies(self, sources):
        if not isinstance(sources, tuple):
            yield pltpu.make_async_copy(sources, self.target, self.semaphores[0])
            return
        rows = self.target.shape[0] // len(sources)
        for part, source in enumerate(sources):
            target = self.target.at[pl.ds(part * rows, rows)]
            yield pltpu.make_async_copy(source, target, self.semaphores[part])

    def start(self, sources=None):
        for copy in self.copies(self.sources if sources is None else sources):
            copy.start()

    def wait(self, sources=None):
        for copy in self.copies(self.sources if sources is None else sources):
            copy.wait()


class Mover:
    def __init__(self, semaphores):
        self.semaphores = semaphores
        self.used = 0

    def note(self, source, target):
        count = len(source) if isinstance(source, tuple) else 1
        semaphores = [self.semaphores.at[self.used + part] for part in range(count)]
        self.used += count
        return Move(source, target, semaphores)

    def start(self, source, target):
        move = self.note(source, target)
        move.start()
        return move


def wait_all(moves):
    for move in moves:
        move.wait()


def gelu_parts(hidden):
    share = 0.5 + 0.5 * lax.erf(hidden * half_root)
    slope = share + hidden * (density_scale * jnp.exp(hidden * hidden * -0.5))
    return hidden * share, slope


def feed_forward(normed, ffn_w, in_bias, ahead, use):
    tiles = spans(ffn_w.shape[1], tile)
    ahead[0] = mm(normed[...], ffn_w[:, tiles[0]])
    for step, at in enumerate(tiles):
        if step + 1 < len(tiles):
            ahead[(step + 1) % 2] = mm(normed[...], ffn_w[:, tiles[step + 1]])
        use(at, ahead[step % 2] + in_bias[:, at])


def first_body(
    heads, row, flag, ids, offsets, table, vectors, in_bias, rows_in, cot_in, qkv_in, out_in, ffn_in,
    down_in, first_in,
    x1_out, h1_out, qkv_out, weights_out, context_out, h2_out, u_out, slope_out, e2_out, low_out,
    hc_out, qc_out,
    rows, qkv_w, out_w, ffn_w, down_w, first_w, cot, normed, qkv, weights, context, x1, h2, u, slope,
    e2, low, bias_rows, mask, context_wide, ahead, loads, stores,
):
    length, width = rows.shape
    hidden_width = ffn_w.shape[1]
    on_encoder = flag[0] == 1
    own_rows = pl.ds(row * length, length)
    load = Mover(loads)
    store = Mover(stores)
    got_rows = load.start(rows_in.at[own_rows], rows)
    got_qkv = load.start(qkv_in, qkv_w)
    got_out = load.start(out_in, out_w)
    got_down = load.note(down_in, down_w)
    got_ffn = load.note(ffn_in, ffn_w)
    got_first = load.note(first_in, first_w)
    got_cot = load.note(cot_in.at[own_rows], cot)

    @pl.when(on_encoder)
    def _():
        got_ffn.start()
        got_down.start()

    @pl.when(jnp.logical_not(on_encoder))
    def _():
        got_first.start()
        got_cot.start()
        got_down.start()

    one_hot = (offsets[...] == lax.broadcasted_iota(jnp.int32, (table.shape[1], 2 * length), 0)).astype(f32)
    by_offset = lax.dot_general(
        table[...], one_hot, (((1,), (0,)), ((), ())), precision=lax.Precision.HIGHEST,
        preferred_element_type=f32,
    )
    bias_rows[...] = pltpu.roll(by_offset, length + 1, 1)
    own_group = jnp.where(on_encoder, 0, 1)
    causal = lax.broadcasted_iota(jnp.int32, (length, length), 0) >= lax.broadcasted_iota(
        jnp.int32, (length, length), 1
    )
    own = ids[pl.ds(own_group, 1), row, :]
    allowed = same_sentence(own, own) & (causal | on_encoder)
    mask[...] = jnp.where(allowed, 0.0, masked_score)

    got_rows.wait()
    norm_forward(rows, vectors[0], vectors[1], normed)
    got_qkv.wait()

    def project(at):
        qkv[:, at] = mm(normed[...], qkv_w[:, at]).astype(bf16)

    each_tile(3 * width, project)
    out_copies = [store.start(normed, h1_out), store.start(qkv, qkv_out)]
    scale = (width // heads) ** (-0.5)

    @pl.loop(0, heads // 2, unroll=heads // 2)
    def _(pair):
        lanes = pl.multiple_of(pair * 128, 128)
        additions = []
        for head in range(2):
            spread = jnp.broadcast_to(bias_rows[pl.ds(pair * 2 + head, 1), :], (length, 2 * length))
            skewed = pltpu.roll(spread, 0, 1, stride=1, stride_axis=0)
            additions.append(skewed[:, :length] + mask[...])
        part, mixed = attend_pair(
            qkv[:, pl.ds(lanes, 128)],
            qkv[:, pl.ds(width + lanes, 128)],
            qkv[:, pl.ds(2 * width + lanes, 128)],
            additions,
            scale,
        )
        weights[0, pair] = part
        context_wide[:, pl.ds(lanes, 128)] = mixed
        context[:, pl.ds(lanes, 128)] = mixed.astype(bf16)

    out_copies += [store.start(weights, weights_out), store.start(context_wide, context_out)]
    got_out.wait()
    x1[...] = rows[...].astype(f32) + mm(context[...], out_w[...])
    out_copies.append(store.start(x1, x1_out))

    @pl.when(on_encoder)
    def _():
        norm_forward(x1, vectors[2], vectors[3], h2)
        got_ffn.wait()

        def feed(at, hidden):
            value, rate = gelu_parts(hidden)
            u[:, at] = value.astype(bf16)
            slope[:, at] = rate.astype(bf16)

        feed_forward(h2, ffn_w, in_bias, ahead, feed)
        copies = [store.start(h2, h2_out), store.start(u, u_out), store.start(slope, slope_out)]
        got_down.wait()
        e2[...] = x1[...] + (mm(u[...], down_w[...]) + vectors[6])
        copies.append(store.start(e2, e2_out))
        norm_forward(e2, vectors[4], vectors[5], low)
        copies.append(store.start(low, low_out))
        wait_all(copies)

    @pl.when(jnp.logical_not(on_encoder))
    def _():
        norm_forward(x1, vectors[2], vectors[3], h2)
        got_first.wait()
        low[...] = mm(h2[...], first_w[...]).astype(bf16)
        copies = [store.start(h2, hc_out), store.start(low, qc_out)]
        got_down.wait()
        got_cot.wait()

        def back(at):
            slope[:, at] = mm_nt(cot[...], down_w[at, :]).astype(bf16)

        each_tile(hidden_width, back)
        copies.append(store.start(slope, slope_out))
        wait_all(copies)

    wait_all(out_copies)


def cross_body(
    heads, row, flag, ids, vectors, in_bias, small_in,
    memory_in, sent_in, other_in, second_in, x1_in, qc_in, cot_in, ffn_in, slope_in, earlier,
    small_out, h2_out, u_out, slope_out, d2_out, grad_out, cc_out, dq_out, dk_out, dv_out, dm_out,
    low_out, pieces, memory, keys_w, values_w, second_w, x1, qc, cot, ffn_w, keys, values, weights, cc, d2, h2, u,
    slope, grad_normed, grad, grad_low, dq, dk, dv, dm, mask, gain_sum, offset_sum, cc_wide, ahead, *rest
):
    *products, loads, stores = rest
    length, width = memory.shape
    small_out[...] = jnp.zeros_like(small_out) if row == 0 else small_in[...]

    @pl.when(flag[0] == 0)
    def _():
        load = Mover(loads)
        store = Mover(stores)
        got_memory = load.start(memory_in, memory)
        got_keys = load.note(sent_in, keys_w)
        got_values = load.note(sent_in, values_w)
        for core, (keys_in, values_in) in enumerate(((sent_in, other_in), (other_in, sent_in))):

            @pl.when(flag[1] == core)
            def _(keys_in=keys_in, values_in=values_in):
                got_keys.start(keys_in)
                got_values.start(values_in)

        got_query = load.start(qc_in, qc)
        got_second = [load.start(second_in, second_w), load.start(x1_in, x1)]
        got_ffn = [load.start(ffn_in, ffn_w), load.start(slope_in, slope)]
        got_cot = load.start(cot_in.at[pl.ds(row * length, length)], cot)
        if products:
            got_earlier = []
            for sources, whole in zip(earlier, products):
                if not sources:
                    continue
                rows = len(sources) * length
                got_earlier.append(load.start(tuple(sources), whole.at[pl.ds(0, rows)]))
        mask[...] = jnp.where(same_sentence(ids[1:2, row, :], ids[0:1, row, :]), 0.0, masked_score)
        got_memory.wait()
        got_keys.wait()
        keys[...] = mm(memory[...], keys_w[...]).astype(bf16)
        got_values.wait()
        values[...] = mm(memory[...], values_w[...]).astype(bf16)
        got_query.wait()
        scale = (width // heads) ** (-0.5)

        @pl.loop(0, heads // 2, unroll=3)
        def _(pair):
            lanes = pl.ds(pl.multiple_of(pair * 128, 128), 128)
            part, mixed = attend_pair(
                qc[:, lanes], keys[:, lanes], values[:, lanes], [mask[...], mask[...]], scale
            )
            weights[0, pair] = part
            cc_wide[:, lanes] = mixed
            cc[:, lanes] = mixed.astype(bf16)

        copies = [store.start(cc, cc_out)]
        wait_all(got_second)
        d2[...] = x1[...] + mm(cc[...], second_w[...])
        copies.append(store.start(d2, d2_out))
        norm_forward(d2, vectors[4], vectors[5], h2)
        copies.append(store.start(h2, h2_out))
        wait_all(got_ffn)

        def feed(at, hidden):
            value, rate = gelu_parts(hidden)
            u[:, at] = value.astype(bf16)
            slope[:, at] = (slope[:, at].astype(f32) * rate).astype(bf16)

        feed_forward(h2, ffn_w, in_bias, ahead, feed)
        copies += [store.start(u, u_out), store.start(slope, slope_out)]
        grad_normed[...] = mm_nt(slope[...], ffn_w[...])
        got_cot.wait()
        norm_backward(
            d2, grad_normed, vectors[4], cot, grad, gain_sum, offset_sum, grad_low
        )
        small_out[4:5, :] += column_sum(gain_sum)
        small_out[5:6, :] += column_sum(offset_sum)
        copies += [store.start(grad, grad_out), store.start(grad_low, low_out)]
        dm[...] = mm_nt(grad_low[...], second_w[...]).astype(bf16)

        @pl.loop(0, heads // 2, unroll=3)
        def _(pair):
            lanes = pl.ds(pl.multiple_of(pair * 128, 128), 128)
            grad_q, grad_k, grad_v, _ = attend_pair_back(
                weights[0, pair], qc[:, lanes], keys[:, lanes], values[:, lanes], cc_wide[:, lanes],
                dm[:, lanes], scale,
            )
            dq[:, lanes] = grad_q.astype(bf16)
            dk[:, lanes] = grad_k.astype(bf16)
            dv[:, lanes] = grad_v.astype(bf16)

        copies += [store.start(dq, dq_out), store.start(dk, dk_out), store.start(dv, dv_out)]
        dm[...] = (mm_nt(dk[...], keys_w[...]) + mm_nt(dv[...], values_w[...])).astype(bf16)
        copies.append(store.start(dm, dm_out))
        if products:
            *wholes, cross_g = products
            hc, *others = wholes
            own = pl.ds(hc.shape[0] - length, length)
            for whole, part in zip(others, (dq, cc, grad_low, memory, dk, dv)):
                whole[own, :] = part[...]
            wait_all(got_earlier)
            hc, dq_all, cc_all, low_all, memory_all, dk_all, dv_all = wholes
            query, out, key, value = spans(4 * width, width)
            cross_g[:, query] = mm_tn(hc[...], dq_all[...]).astype(bf16)
            cross_g[:, out] = mm_tn(cc_all[...], low_all[...]).astype(bf16)
            copies += put_columns(store, cross_g, pieces, flag[1], pl.ds(0, 2 * width))
            cross_g[:, key] = mm_tn(memory_all[...], dk_all[...]).astype(bf16)
            cross_g[:, value] = mm_tn(memory_all[...], dv_all[...]).astype(bf16)
            copies += put_columns(store, cross_g, pieces, flag[1], pl.ds(2 * width, 2 * width))
        wait_all(copies)


def put_rows(store, stage, targets, core, rows):
    if len(targets) == 1:
        return [store.start(stage.at[rows], targets[0].at[rows])]
    depth = targets[0].shape[1]
    copies = []
    for chip in range(rows.start // (2 * depth), (rows.start + rows.size) // (2 * depth)):
        for target, which in zip(targets, (core, 1 - core)):
            at = pl.multiple_of((2 * chip + which) * depth, depth)
            copies.append(store.start(stage.at[pl.ds(at, depth)], target.at[chip]))
    return copies


def put_columns(store, stage, targets, core, columns):
    if len(targets) == 1:
        return [store.start(stage.at[:, columns], targets[0].at[:, columns])]
    chips, depth = targets[0].shape[0], targets[0].shape[1]
    copies = []
    for chip in range(chips):
        for target, which in zip(targets, (core, 1 - core)):
            at = pl.multiple_of((2 * chip + which) * depth, depth)
            copies.append(
                store.start(stage.at[pl.ds(at, depth), columns], target.at[chip, :, columns])
            )
    return copies


def spans(count, width):
    return [pl.ds(start, width) for start in range(0, count, width)]


def down_body(flag, vectors, small_in, dm_in, cot_in, e2_in, enc_u_in, dec_u_in, *rest):
    small_out, grad_out, low_out, *rest = rest
    count = len(rest) - 11
    outs = rest[:count]
    dm, cot, e2, u, grad, grad_low, down_g, gain_sum, offset_sum, loads, stores = rest[count:]
    hidden_width, width = u.shape[1], cot.shape[1]
    small_out[...] = small_in[...]
    load = Mover(loads)
    store = Mover(stores)
    got_cot = load.start(cot_in, cot)
    got_u = load.note(enc_u_in, u)
    moved = [load.note(dm_in, dm), load.note(e2_in, e2)]
    kept = [store.note(grad, grad_out), store.note(grad_low, low_out)]

    @pl.when(flag[0] == 1)
    def _():
        for copy in moved:
            copy.start()
        got_cot.wait()
        wait_all(moved)
        got_u.start(enc_u_in)

        def total(at):
            grad[at, :] = dm[at, :].astype(f32) + cot[at, :].astype(f32)

        each_rows(grad.shape[0], total)
        norm_backward(e2, grad, vectors[4], None, grad, gain_sum, offset_sum, grad_low)
        small_out[4:5, :] = column_sum(gain_sum)
        small_out[5:6, :] = column_sum(offset_sum)
        for copy in kept:
            copy.start()

    @pl.when(flag[0] == 0)
    def _():
        got_u.start(dec_u_in)
        got_cot.wait()
        grad_low[...] = cot[...]

    got_u.wait()
    copies = []
    for rows in spans(hidden_width, tile):
        down_g[rows, :] = mm_tn(u[:, rows], grad_low[...]).astype(bf16)
        copies += put_rows(store, down_g, outs, flag[1], rows)
    small_out[6:7, :] = jnp.sum(grad_low[...].astype(f32), axis=0, keepdims=True)
    wait_all(copies)

    @pl.when(flag[0] == 1)
    def _():
        wait_all(kept)


def hidden_body(flag, low_in, down_in, slope_in, slope_out, grad_low, down_w, slope, loads, stores):
    @pl.when(flag[0] == 1)
    def _():
        load = Mover(loads)
        store = Mover(stores)
        hidden_width = slope.shape[1]
        got_low = load.start(low_in, grad_low)
        got_slope = load.start(slope_in, slope)
        got_down = [
            load.start(down_in.at[rows], down_w.at[rows]) for rows in spans(hidden_width, tile)
        ]
        got_low.wait()
        got_slope.wait()
        copies = []
        for at, got in zip(spans(hidden_width, tile), got_down):
            got.wait()
            part = mm_nt(grad_low[...], down_w[at, :]) * slope[:, at].astype(f32)
            slope[:, at] = part.astype(bf16)
            copies.append(store.start(slope.at[:, at], slope_out.at[:, at]))
        wait_all(copies)


def ffn_body(flag, small_in, enc_ins, dec_ins, *rest):
    small_out, *rest = rest
    count = len(rest) - 5
    outs = rest[:count]
    slope, h2, ffn_g, loads, stores = rest[count:]
    width, hidden_width = h2.shape[1], slope.shape[1]
    small_out[...] = small_in[...]
    load = Mover(loads)
    store = Mover(stores)
    moves = [load.note(source, target) for source, target in zip(dec_ins, (h2, slope))]
    for which, ins in enumerate((dec_ins, enc_ins)):

        @pl.when(flag[0] == which)
        def _(ins=ins):
            for move, source in zip(moves, ins):
                move.start(source)
            for move, source in zip(moves, ins):
                move.wait(source)

    copies = []
    for step, at in enumerate(spans(hidden_width, tile)):
        ffn_g[:, at] = mm_tn(h2[...], slope[:, at]).astype(bf16)
        if step % 2 == 1:
            both = pl.ds(at.start - tile, 2 * tile)
            copies += put_columns(store, ffn_g, outs, flag[1], both)
    for part in range(hidden_width // width):
        values = slope[:, part * width : (part + 1) * width].astype(f32)
        small_out[8 + part : 9 + part, :] = jnp.sum(values, axis=0, keepdims=True)
    wait_all(copies)


def hidden_back_body(
    flag, vectors, small_in, slope_in, ffn_in, dq_in, first_in, x1_in, enc_grad_in, dec_grad_in,
    small_out, grad_out,
    slope, ffn_w, dq, first_w, x1, grad, grad_normed, gain_sum, offset_sum, loads, stores,
):
    width = x1.shape[1]
    small_out[...] = small_in[...]
    load = Mover(loads)
    store = Mover(stores)
    got_x1 = load.note(x1_in, x1)
    got_grad = load.note(dec_grad_in, grad)

    @pl.when(flag[0] == 1)
    def _():
        got = [load.start(slope_in, slope), load.start(ffn_in, ffn_w)]
        got_x1.start()
        got_grad.start(enc_grad_in)
        wait_all(got)
        grad_normed[...] = mm_nt(slope[...], ffn_w[...])
        got_grad.wait(enc_grad_in)

    @pl.when(flag[0] == 0)
    def _():
        got = [load.start(dq_in, dq), load.start(first_in, first_w)]
        got_x1.start()
        got_grad.start(dec_grad_in)
        wait_all(got)
        grad_normed[...] = mm_nt(dq[...], first_w[...])
        got_grad.wait()

    got_x1.wait()
    norm_backward(x1, grad_normed, vectors[2], grad, grad, gain_sum, offset_sum)
    stored = store.start(grad, grad_out)
    small_out[2:3, :] = column_sum(gain_sum)
    small_out[3:4, :] = column_sum(offset_sum)
    stored.wait()


def attention_back_body(
    heads, flag, grad_in, qkv_in, weights_in, context_in, outw_in, h1_in, *rest
):
    grad_qkv_out, scores_out, *rest = rest
    count = len(rest) - 14
    outs = rest[:count]
    (
        grad, qkv, weights, context, out_w, h1, grad_low, grad_context, grad_qkv, mixed_g,
        grad_scores, context_low, loads, stores,
    ) = rest[count:]
    width = context.shape[1]
    row_count, length = weights.shape[0], weights.shape[2]
    load = Mover(loads)
    store = Mover(stores)
    got_grad = [load.start(grad_in, grad), load.start(outw_in, out_w)]
    got_context = load.start(context_in, context)
    got_attention = [load.start(weights_in, weights), load.start(qkv_in, qkv)]
    got_h1 = load.start(h1_in, h1)
    wait_all(got_grad)

    def lower(at):
        grad_low[at, :] = grad[at, :].astype(bf16)

    each_rows(grad.shape[0], lower)
    grad_context[...] = mm_nt(grad_low[...], out_w[...]).astype(bf16)
    got_context.wait()
    context_low[...] = context[...].astype(bf16)
    mixed_g[:, pl.ds(0, width)] = mm_tn(context_low[...], grad_low[...]).astype(bf16)
    wait_all(got_attention)
    scale = (width // heads) ** (-0.5)

    @pl.loop(0, heads // 2, unroll=3)
    def _(pair):
        lanes = pl.multiple_of(pair * 128, 128)
        totals = [None, None]
        for row in range(row_count):
            at = slice(row * length, (row + 1) * length)
            grad_q, grad_k, grad_v, parts = attend_pair_back(
                weights[row, pair],
                qkv[at, pl.ds(lanes, 128)],
                qkv[at, pl.ds(width + lanes, 128)],
                qkv[at, pl.ds(2 * width + lanes, 128)],
                context[at, pl.ds(lanes, 128)],
                grad_context[at, pl.ds(lanes, 128)],
                scale,
            )
            grad_qkv[at, pl.ds(lanes, 128)] = grad_q.astype(bf16)
            grad_qkv[at, pl.ds(width + lanes, 128)] = grad_k.astype(bf16)
            grad_qkv[at, pl.ds(2 * width + lanes, 128)] = grad_v.astype(bf16)
            totals = [p if t is None else t + p for t, p in zip(totals, parts)]
        for head in range(2):
            grad_scores[pair * 2 + head] = totals[head]

    got_h1.wait()
    copies = [store.start(grad_qkv, grad_qkv_out), store.start(grad_scores, scores_out)]
    for step, at in enumerate(spans(3 * width, width)):
        mixed_g[:, pl.ds(width + at.start, width)] = mm_tn(h1[...], grad_qkv[:, at]).astype(bf16)
        if step != 1:
            both = pl.ds(0 if step == 0 else 2 * width, 2 * width)
            copies += put_columns(store, mixed_g, outs, flag[1], both)
    wait_all(copies)


def sum_diagonals(grid):
    length = grid.shape[0]
    padded = jnp.concatenate([grid, jnp.zeros((length, length), f32)], axis=1)
    folded = padded[0:8, :]
    for block in range(1, length // 8):
        folded = folded + pltpu.roll(
            padded[block * 8 : (block + 1) * 8, :], 2 * length - block * 8, 1
        )
    line = folded[0:1, :]
    for sub in range(1, 8):
        line = line + pltpu.roll(folded[sub : sub + 1, :], 2 * length - sub, 1)
    return pltpu.roll(line, length - 1, 1)


def last_body(
    flag, offsets, vectors, small_in, grad_in, grad_qkv_in, qkvw_in, rows_in, scores_in,
    small_out, result_out,
    grad, grad_qkv, qkv_w, rows, grad_normed, grad_scores, diagonals, one_hot, gain_sum, offset_sum,
    loads, stores,
):
    small_out[...] = small_in[...]
    heads, bucket_count = grad_scores.shape[0], one_hot.shape[0]
    load = Mover(loads)
    store = Mover(stores)
    got = [load.start(grad_qkv_in, grad_qkv), load.start(qkvw_in, qkv_w)]
    got_rows = [load.start(rows_in, rows), load.start(grad_in, grad)]
    got_scores = load.start(scores_in, grad_scores)
    wait_all(got)
    grad_normed[...] = mm_nt(grad_qkv[...], qkv_w[...])
    wait_all(got_rows)
    norm_backward(rows, grad_normed, vectors[0], grad, grad, gain_sum, offset_sum)
    small_out[0:1, :] = column_sum(gain_sum)
    small_out[1:2, :] = column_sum(offset_sum)
    stored = store.start(grad, result_out)

    got_scores.wait()

    @pl.loop(0, heads)
    def _(head):
        diagonals[pl.ds(head, 1), :] = sum_diagonals(grad_scores[head])

    one_hot[...] = (offsets[...] == lax.broadcasted_iota(jnp.int32, one_hot.shape, 0)).astype(f32)
    small_out[pl.ds(16, heads), pl.ds(0, bucket_count)] = lax.dot_general(
        diagonals[...], one_hot[...], (((1,), (1,)), ((), ())), precision=lax.Precision.HIGHEST,
        preferred_element_type=f32,
    )
    stored.wait()


def output_body(
    flag, vectors, u_in, d2_in, down_in, low_in, low_out, u, d2, down_w, low, loads, stores
):
    load = Mover(loads)
    stored = Mover(stores).note(low, low_out)
    got_low = load.note(low_in, low)

    @pl.when(flag[0] == 1)
    def _():
        got_low.start()
        got_low.wait()
        stored.start()

    @pl.when(flag[0] == 0)
    def _():
        wait_all([load.start(u_in, u), load.start(d2_in, d2), load.start(down_in, down_w)])
        value = d2[...] + (mm(u[...], down_w[...]) + vectors[6])
        low[...] = value.astype(bf16)
        stored.start()

    stored.wait()


def pair_sum_body(everywhere, flag, kept_in, got_in, out, kept, got, total, loads, stores):
    @pl.when(jnp.logical_or(flag[0] == 0, everywhere))
    def _():
        load = Mover(loads)
        store = Mover(stores)
        blocks = out.shape[0]
        ready = []
        for step in range(blocks):
            block = 2 * step + 1 - flag[2]
            ready.append(
                (load.start(kept_in.at[block], kept.at[step]), load.start(got_in.at[block], got.at[step]))
            )
        copies = []
        for step in range(blocks):
            wait_all(ready[step])
            total[step] = (kept[step].astype(f32) + got[step].astype(f32)).astype(bf16)
            copies.append(store.start(total.at[step], out.at[step]))
        wait_all(copies)


def pair_sum(flag, kept, got, everywhere):
    chips, depth, width = kept.shape
    part = (chips // 2, depth, width)
    return run_kernel(
        functools.partial(pair_sum_body, everywhere),
        (flag, kept, got),
        [SMEM, ANY, ANY],
        [shape_of(part, bf16)],
        [ANY],
        [(part, bf16)] * 3,
        chips, chips // 2, "pair_sum",
    )[0]


def chip_sum_body(
    everywhere, flag, kept_in, got_in, far_in, first_out, second_out, third_out, own_out,
    kept, got, far, total, own, loads, stores,
):
    @pl.when(jnp.logical_or(flag[0] == 0, everywhere))
    def _():
        load = Mover(loads)
        store = Mover(stores)
        ready = []
        for step, away in enumerate((*rotations, 0)):
            place = lax.rem(flag[3] + away, 4)
            block = 2 * place + flag[2]
            ready.append(
                [
                    load.start(kept_in.at[block], kept.at[step]),
                    load.start(got_in.at[block], got.at[step]),
                    load.start(far_in.at[place], far.at[step]),
                ]
            )
        copies = []
        for step, out in enumerate((first_out, second_out, third_out, own_out)):
            wait_all(ready[step])
            value = kept[step].astype(f32) + got[step].astype(f32) + far[step].astype(f32)
            if step < 3:
                total[step] = value.astype(bf16)
                copies.append(store.start(total.at[step], out))
            else:
                own[...] = value
                copies.append(store.start(own, out))
        wait_all(copies)


def chip_sum(flag, kept, got, far, everywhere):
    _, depth, width = kept.shape
    one = (depth, width)
    return run_kernel(
        functools.partial(chip_sum_body, everywhere),
        (flag, kept, got, far),
        [SMEM, ANY, ANY, ANY],
        [shape_of(one, bf16)] * 3 + [shape_of(one, f32)],
        [ANY] * 4,
        [((4,) + one, bf16)] * 3 + [((3,) + one, bf16), (one, f32)],
        12, 4, "chip_sum",
    )


def pick_body(flag, first_in, second_in, out, held, loads, stores):
    @pl.when(flag[0] == 1)
    def _():
        got = Mover(loads).note(first_in, held)
        for core, source in enumerate((first_in, second_in)):

            @pl.when(flag[1] == core)
            def _(source=source):
                got.start(source)

        got.wait()
        Mover(stores).start(held, out).wait()


def finish_body(
    flag, first, second, third, own, cross, back, qkv_out, out_out, cf_out, cs_out
):
    width = out_out.shape[1]
    total = own[...]
    for part in (first, second, third):
        total = total + part[...].astype(f32)
    out_out[...] = total[:, :width]
    qkv_out[...] = total[:, width:]
    chosen = jnp.where(flag[0] == 1, back[...], cross[...])
    cf_out[...] = chosen[:, :width]
    cs_out[...] = chosen[:, width:]


def small_body(place, mine, other, vec_out, fbias_out, table_out):
    small = mine[...] + other[...]
    width = small.shape[1]
    share = vec_out.shape[2]
    turned = pltpu.roll(small[0:8, :], lax.rem(width - place[0] * share, width), 1)
    for row in range(vec_out.shape[0]):
        vec_out[row] = turned[row : row + 1, :share]
    share = fbias_out.shape[1]
    per_row = width // share
    row = mine[pl.ds(8 + lax.div(place[0], per_row), 1), :]
    row = row + other[pl.ds(8 + lax.div(place[0], per_row), 1), :]
    turned = pltpu.roll(row, lax.rem(width - lax.rem(place[0], per_row) * share, width), 1)
    fbias_out[...] = turned[:, :share]
    for head in range(table_out.shape[0]):
        table_out[head] = small[16 + head : 17 + head, : table_out.shape[2]]


def shape_of(dims, dtype):
    return jax.ShapeDtypeStruct(tuple(dims), dtype)


def size_of(dims, dtype):
    total = jnp.dtype(dtype).itemsize
    for dim in dims:
        total *= dim
    return total


def run_kernel(
    body, operands, places, outs, out_places, scratch, loads, stores, name, alone=False
):
    held = sum(size_of(dims, dtype) for dims, dtype in scratch)
    flat, form = jax.tree.flatten(operands)
    flat_places = [
        place for place, operand in zip(places, operands, strict=True) for _ in jax.tree.leaves(operand)
    ]

    flat_outs, out_form = jax.tree.flatten(outs)
    held_at = len(flat) + len(flat_outs)

    def kernel(*refs):
        results = out_form.unflatten(refs[len(flat) : held_at])
        return body(*form.unflatten(refs[: len(flat)]), *results, *refs[held_at:])

    results = pl.pallas_call(
        kernel,
        in_specs=flat_places,
        out_specs=out_places,
        out_shape=flat_outs,
        scratch_shapes=[pltpu.VMEM(dims, dtype) for dims, dtype in scratch]
        + [pltpu.SemaphoreType.DMA((loads,)), pltpu.SemaphoreType.DMA((stores,))],
        compiler_params=pltpu.CompilerParams(
            vmem_limit_bytes=all_bytes if alone else held + spare_bytes
        ),
        cost_estimate=pl.CostEstimate(flops=1, bytes_accessed=1, transcendentals=0),
        name=name,
    )(*flat)
    return out_form.unflatten(results)


def after(value, *others):
    return lax.optimization_barrier((value,) + others)[0]


def block_of(always, steps, *operands):
    shapes = jax.eval_shape(steps, *operands)

    def blank(*_):
        return jax.tree.map(lambda leaf: jnp.zeros(leaf.shape, leaf.dtype), shapes)

    return lax.cond(always, steps, blank, *operands)


class Ring:
    def __init__(self, devices, everywhere):
        self.devices = devices
        self.everywhere = everywhere

    def send(self, shard, moved):
        pairs = [(i, moved(i)) for i in range(self.devices)]
        if self.everywhere:
            return lax.ppermute(shard, "batch", pairs)
        pairs = [(self.devices + i, self.devices + j) for i, j in pairs]
        return lax.ppermute(shard, ("section", "batch"), pairs)

    def to_core(self, given):
        return self.send(given, lambda i: i ^ 1)

    def to_chip(self, out):
        return self.send(out, lambda i: i ^ 2)

    def sums(self, flag, *held):
        return chip_sum(flag, *held, self.everywhere)

    def along(self, outs):
        return [
            self.send(out, lambda i, away=away: (i + 4 * away) % 16)
            for away, out in zip(rotations, outs)
        ]


def per_device(
    inputs, cotangent, segments, buckets, qkv_weight, out_weight, in_weight, down_weight,
    cross_first, cross_second, vectors, ffn_bias, position_table,
):
    row_count, length, width = inputs.shape[1:]
    heads = position_table.shape[2]
    bucket_count = position_table.shape[1]
    hidden = in_weight.shape[2]
    tokens = row_count * length
    pairs = heads // 2
    on_encoder = lax.axis_index("section") == 0
    place = lax.axis_index("batch")
    core = lax.rem(place, 2)
    devices = lax.axis_size("batch")
    by_chip = devices == 16
    always = place < devices
    flag = jnp.stack(
        [on_encoder.astype(jnp.int32), core, lax.rem(lax.div(place, 2), 2), lax.div(place, 4)]
    )
    offsets = jnp.pad(buckets, (0, 1), constant_values=-1)[None]
    table = jnp.transpose(position_table, (2, 0, 1))[:, 0]
    rows = inputs.reshape(tokens, width)
    cot = cotangent.reshape(tokens, width)
    qkv_w, out_w, ffn_w, down_w = qkv_weight[0], out_weight[0], in_weight[0], down_weight[0]
    first_w, second_w = cross_first[0], cross_second[0]
    vec = jnp.transpose(vectors, (1, 0, 2))
    fbias = ffn_bias

    tw, th = (tokens, width), (tokens, hidden)
    wide = (tokens, 3 * width)
    square = (row_count, pairs, length, 2 * length)
    row_tw, row_th, row_wide = (length, width), (length, hidden), (length, 3 * width)
    row_square = (1, pairs, length, 2 * length)
    small = (32, width)

    (picked,) = run_kernel(
        pick_body, (flag, first_w, second_w), [SMEM, ANY, ANY], [shape_of((width, width), bf16)],
        [ANY], [((width, width), bf16)], 1, 1, "pick",
    )
    sent = lax.ppermute(picked, "section", [(0, 1)])
    flag = after(flag, picked)

    def piece(depth_rows, columns):
        if not by_chip:
            return [shape_of((depth_rows, columns), bf16)]
        return [shape_of((devices // 2, depth_rows // devices, columns), bf16)] * 2

    down_piece, ffn_piece = piece(hidden, width), piece(width, hidden)
    mixed_piece = piece(width, 4 * width)
    count = len(down_piece)
    share_copies = devices if by_chip else 1
    def run_first(row, flag):
        return run_kernel(
            functools.partial(first_body, heads, row),
            (flag, segments, offsets, table, vec, fbias, rows, cot, qkv_w, out_w, ffn_w,
             down_w, first_w),
            [SMEM] + [VMEM] * 5 + [ANY] * 7,
            [
                shape_of(row_tw, f32), shape_of(row_tw, bf16), shape_of(row_wide, bf16),
                shape_of(row_square, bf16), shape_of(row_tw, f32), shape_of(row_tw, bf16),
                shape_of(row_th, bf16), shape_of(row_th, bf16), shape_of(row_tw, f32),
                shape_of(row_tw, bf16), shape_of(row_tw, bf16), shape_of(row_tw, bf16),
            ],
            [ANY] * 12,
            [
                (row_tw, bf16), ((width, 3 * width), bf16), ((width, width), bf16),
                ((width, hidden), bf16), ((hidden, width), bf16), ((width, width), bf16),
                (row_tw, bf16), (row_tw, bf16), (row_wide, bf16), (row_square, bf16), (row_tw, bf16),
                (row_tw, f32), (row_tw, bf16), (row_th, bf16), (row_th, bf16), (row_tw, f32),
                (row_tw, bf16), ((heads, 2 * length), f32), ((length, length), f32),
                (row_tw, f32), ((2, length, tile), f32),
            ],
            7, 13, "first", True,
        )

    def run_cross(row, flag, small_grad, memory, sent, sent_other, own, earlier):
        x1, qc, slope = own
        last_row = row == row_count - 1
        products = [(tw, bf16)] * 7 + [((width, 4 * width), bf16)] if last_row else []
        return run_kernel(
            functools.partial(cross_body, heads, row),
            (flag, segments, vec, fbias, small_grad, memory, sent, sent_other, second_w, x1, qc, cot,
             ffn_w, slope, earlier if last_row else ()),
            [SMEM] + [VMEM] * 4 + [ANY] * 10,
            [shape_of(small, f32), shape_of(row_tw, bf16), shape_of(row_th, bf16),
             shape_of(row_th, bf16), shape_of(row_tw, f32), shape_of(row_tw, f32)]
            + [shape_of(row_tw, bf16)] * 6 + [mixed_piece if last_row else []],
            [VMEM] + [ANY] * (11 + (count if last_row else 0)),
            [
                (row_tw, bf16), ((width, width), bf16), ((width, width), bf16),
                ((width, width), bf16), (row_tw, f32), (row_tw, bf16), (row_tw, bf16),
                ((width, hidden), bf16), (row_tw, bf16), (row_tw, bf16), (row_square, bf16),
                (row_tw, bf16), (row_tw, f32), (row_tw, bf16), (row_th, bf16), (row_th, bf16),
                (row_tw, f32), (row_tw, f32), (row_tw, bf16), (row_tw, bf16), (row_tw, bf16),
                (row_tw, bf16), (row_tw, bf16), ((length, length), f32), ((8, width), f32),
                ((8, width), f32), (row_tw, f32), ((2, length, tile), f32),
            ] + products,
            9 + (7 * row_count if last_row else 0), 11 + 2 * share_copies, "cross", True,
        )

    def to_decoder(value):
        return lax.ppermute(value, "section", [(0, 1)])

    def to_encoder(value):
        return lax.ppermute(value, "section", [(1, 0)])

    kept_rows = [run_first(0, flag)]
    for row in range(1, row_count):

        def first_steps(low, flag, row=row):
            memory = to_decoder(low)
            return memory, run_first(row, flag)

        low = kept_rows[-1][9]
        memory, outs = block_of(always, first_steps, low, after(flag, low))
        kept_rows.append(outs)
        memories = (*memories, memory) if row > 1 else (memory,)

    def cross_steps(low, flag, first_memory, sent, own, first_earlier):
        memory = to_decoder(low)
        other = lax.ppermute(sent, "batch", [(i, i ^ 1) for i in range(devices)])
        return memory, other, run_cross(0, flag, fbias, first_memory, sent, other, own, first_earlier)

    def own_of(row):
        outs = kept_rows[row]
        return outs[0], outs[11], outs[7]

    def earlier_of(rows):
        hc = tuple(outs[10] for outs in kept_rows)
        return (
            hc,
            *(tuple(outs[part] for outs in rows) for part in (6, 5, 10)),
            tuple(memories[: len(rows)]),
            *(tuple(outs[part] for outs in rows) for part in (7, 8)),
        )

    low = kept_rows[-1][9]
    memory, sent_other, outs = block_of(
        always, cross_steps, low, after(flag, low), memories[0], sent, own_of(0), earlier_of(())
    )
    memories = (*memories, memory)
    small_grad, *outs = outs
    cross_rows, returned = [outs], ()
    for row in range(1, row_count):

        def return_steps(dm, flag, *operands, row=row):
            back = to_encoder(dm)
            return back, run_cross(row, flag, *operands)

        dm = cross_rows[-1][9]
        back, outs = block_of(
            always, return_steps, dm, after(flag, dm), small_grad, memories[row], sent, sent_other,
            own_of(row), earlier_of(cross_rows),
        )
        small_grad, *outs = outs
        cross_rows.append(outs)
        returned = (*returned, back)
    dm = cross_rows[-1][9]
    returned = (*returned, to_encoder(dm))
    x1, h1, qkv, weights, context, h2, u, slope, e2, low, hc, qc = zip(*kept_rows)
    dec_h2, dec_u, dec_slope, d2, grad, _, dq, _, _, dm, _, cross_gs = zip(*cross_rows)
    cross_g = cross_gs[-1]

    cross, down, ffn, mixed = (
        Ring(devices, name != "cross") for name in ("cross", "down", "ffn", "mixed")
    )

    flag = after(flag, *dm)

    def run_down(flag, vec, small_grad, returned, cot, e2, u, dec_u):
        small_grad, enc_grad, enc_low, *pieces = run_kernel(
            down_body,
            (flag, vec, small_grad, returned, cot, e2, u, dec_u),
            [SMEM] + [VMEM] * 2 + [ANY] * 5,
            [shape_of(small, f32), shape_of(tw, f32), shape_of(tw, bf16)] + down_piece,
            [VMEM] + [ANY] * (2 + count),
            [
                (tw, bf16), (tw, bf16), (tw, f32), (th, bf16), (tw, f32), (tw, bf16),
                ((hidden, width), bf16), ((8, width), f32), ((8, width), f32),
            ],
            1 + 3 * row_count, 2 + max(share_copies, hidden // tile), "down",
        )
        return small_grad, enc_grad, enc_low, pieces

    def run_hidden(flag, enc_low, down_w, slope):
        return run_kernel(
            hidden_body,
            (flag, enc_low, down_w, slope),
            [SMEM] + [ANY] * 3,
            [shape_of(th, bf16)],
            [ANY],
            [(tw, bf16), ((hidden, width), bf16), (th, bf16)],
            1 + row_count + hidden // tile, hidden // tile, "hidden",
        )[0]

    def run_ffn(flag, small_grad, enc_slope):
        small_grad, *pieces = run_kernel(
            ffn_body,
            (flag, small_grad, (h2, enc_slope), (dec_h2, dec_slope)),
            [SMEM, VMEM, ANY, ANY],
            [shape_of(small, f32)] + ffn_piece,
            [VMEM] + [ANY] * count,
            [(th, bf16), (tw, bf16), ((width, hidden), bf16)],
            2 * row_count, hidden // (2 * tile) * share_copies, "ffn",
        )
        return small_grad, pieces

    def run_hidden_back(flag, vec, small_grad, slope, ffn_w, dq, first_w, x1, enc_grad, grad):
        return run_kernel(
            hidden_back_body,
            (flag, vec, small_grad, slope, ffn_w, dq, first_w, x1, enc_grad, grad),
            [SMEM] + [VMEM] * 2 + [ANY] * 7,
            [shape_of(small, f32), shape_of(tw, f32)],
            [VMEM, ANY],
            [
                (th, bf16), ((width, hidden), bf16), (tw, bf16), ((width, width), bf16), (tw, f32),
                (tw, f32), (tw, f32), ((8, width), f32), ((8, width), f32),
            ],
            3 + 3 * row_count, 1, "hidden_back",
        )

    def run_attention_back(flag, grad, qkv, weights, context, out_w, h1):
        grad_qkv, grad_scores, *pieces = run_kernel(
            functools.partial(attention_back_body, heads),
            (flag, grad, qkv, weights, context, out_w, h1),
            [SMEM] + [ANY] * 6,
            [shape_of(wide, bf16), shape_of((heads, length, length), f32)] + mixed_piece,
            [ANY] * (2 + count),
            [
                (tw, f32), (wide, bf16), (square, bf16), (tw, f32), ((width, width), bf16),
                (tw, bf16), (tw, bf16), (tw, bf16), (wide, bf16), ((width, 4 * width), bf16),
                ((heads, length, length), f32), (tw, bf16),
            ],
            2 + 4 * row_count, 2 + 2 * share_copies, "attention_back",
        )
        return grad_qkv, grad_scores, pieces

    def run_last(flag, vec, small_grad, grad, grad_qkv, qkv_w, rows, grad_scores):
        return run_kernel(
            last_body,
            (flag, offsets, vec, small_grad, grad, grad_qkv, qkv_w, rows, grad_scores),
            [SMEM] + [VMEM] * 3 + [ANY] * 5,
            [shape_of(small, f32), shape_of(tw, f32)],
            [VMEM, ANY],
            [
                (tw, f32), (wide, bf16), ((width, 3 * width), bf16), (tw, bf16), (tw, f32),
                ((heads, length, length), f32), ((heads, 2 * length), f32),
                ((bucket_count, 2 * length), f32), ((8, width), f32), ((8, width), f32),
            ],
            5, 1, "last",
        )

    def run_output(flag, vec, dec_u, d2, down_w, low):
        return run_kernel(
            output_body,
            (flag, vec, dec_u, d2, down_w, low),
            [SMEM, VMEM] + [ANY] * 4,
            [shape_of(tw, bf16)],
            [ANY],
            [(th, bf16), (tw, f32), ((hidden, width), bf16), (tw, bf16)],
            1 + 3 * row_count, 1, "output",
        )[0]

    def beside(ring, pieces, kernel, *operands):
        def steps(kept, given, flag, *operands):
            got = ring.to_core(given)
            outs = kernel(flag, *operands)
            out = pair_sum(after(flag, *jax.tree.leaves(outs)), kept, got, ring.everywhere)
            return outs, got, out

        return block_of(always, steps, *pieces, *operands)

    if not by_chip:
        small_grad, enc_grad, enc_low, down_g = run_down(
            flag, vec, small_grad, returned, cot, e2, u, dec_u
        )
        enc_slope = run_hidden(flag, enc_low, down_w, slope)
        small_grad, ffn_g = run_ffn(flag, small_grad, enc_slope)
        small_grad, grad = run_hidden_back(
            flag, vec, small_grad, enc_slope, ffn_w, dq, first_w, x1, enc_grad, grad
        )
        grad_qkv, grad_scores, mixed_g = run_attention_back(
            flag, grad, qkv, weights, context, out_w, h1
        )
        small_grad, result = run_last(
            flag, vec, small_grad, grad, grad_qkv, qkv_w, rows, grad_scores
        )
        low = run_output(flag, vec, dec_u, d2, down_w, low)
        small_grad = lax.psum(small_grad, "batch")
        cross_share, down_share, ffn_share, mixed_share = (
            lax.psum_scatter(pieces[0], "batch", scatter_dimension=0, tiled=True).astype(f32)
            for pieces in (cross_g, down_g, ffn_g, mixed_g)
        )
        cross_back = lax.ppermute(cross_share[:, 2 * width :], "section", [(1, 0)])
        cross_share = jnp.where(on_encoder, cross_back, cross_share[:, : 2 * width])
        cf_share, cs_share = cross_share[:, :width], cross_share[:, width:]
        out_share, qkv_share = mixed_share[:, :width], mixed_share[:, width:]
        vec_share = lax.dynamic_slice_in_dim(
            small_grad[:7], place * (width // devices), width // devices, 1
        )
        fbias_all = small_grad[8 : 8 + hidden // width].reshape(1, hidden)
        fbias_share = lax.dynamic_slice_in_dim(
            fbias_all, place * (hidden // devices), hidden // devices, 1
        )
        table_total = small_grad[16 : 16 + heads, :bucket_count].T
    else:

        def cross_steps(flag, kept, given):
            got = cross.to_core(given)
            return got, pair_sum(flag, kept, got, False)

        got, out = block_of(always, cross_steps, flag, *cross_g)
        flag = after(flag, out)

        def down_steps(out, kept, got, flag, down_w, slope, ffn_ins, *operands):
            far = cross.to_chip(out)
            small_grad, enc_grad, enc_low, pieces = run_down(flag, *operands)
            flag = after(flag, small_grad)
            enc_slope, down_got, out = beside(
                down, pieces, run_hidden, flag, enc_low, down_w, slope
            )
            down_held = (pieces[0], down_got, down.to_chip(out))
            flag = after(flag, out)
            small_grad, pieces = run_ffn(flag, small_grad, enc_slope)
            flag = after(flag, small_grad)
            *outs, cross_own = cross.sums(flag, kept, got, far)
            flag = after(flag, *outs)
            cross_last = (*cross.along(outs), cross_own)
            sums = beside(
                ffn, pieces, run_hidden_back, flag, vec, small_grad, enc_slope, *ffn_ins[:4],
                enc_grad, ffn_ins[4],
            )
            outs = down.sums(after(flag, sums[2]), *down_held)
            return outs, cross_last, pieces[0], sums

        down_outs, cross_last, kept, sums = block_of(
            always, down_steps, out, cross_g[0], got, flag, down_w, slope,
            (ffn_w, dq, first_w, x1, grad), vec, small_grad, returned, cot, e2, u, dec_u,
        )
        (small_grad, grad), got, ffn_out = sums
        ffn_held = (kept, got)
        flag = after(flag, ffn_out, *down_outs)

        def attention_steps(flag, ffn_out, outs, *operands):
            far = ffn.to_chip(ffn_out)
            moved = down.along(outs)
            grad_qkv, grad_scores, pieces = run_attention_back(flag, *operands)

            def swap(flag, kept, given):
                got = mixed.to_core(given)
                return got, pair_sum(flag, kept, got, True)

            swapped = block_of(always, swap, after(flag, grad_qkv), *pieces)
            return moved, far, grad_qkv, grad_scores, pieces[0], swapped

        moved, ffn_far, grad_qkv, grad_scores, kept, swapped = block_of(
            always, attention_steps, flag, ffn_out, down_outs[:3], grad, qkv, weights, context, out_w,
            h1,
        )
        down_last = (*moved, down_outs[3])
        got, out = swapped
        flag = after(flag, out)

        def swapped_small(small_grad, away):
            pairs = [(i, i ^ away) for i in range(devices)]
            return small_grad + lax.ppermute(small_grad, "batch", pairs)

        def last_steps(flag, out, held, mixed_held, *operands):
            far = mixed.to_chip(out)
            *outs, own = ffn.sums(flag, *held)
            moved = (*ffn.along(outs), own)
            small_grad, result = run_last(after(flag, *outs), *operands)

            small_grad = block_of(always, lambda s: swapped_small(s, 1), small_grad)
            outs = mixed.sums(after(flag, small_grad), *mixed_held, far)
            return outs, moved, small_grad, result

        (*outs, own), ffn_last, small_grad, result = block_of(
            always, last_steps, flag, out, (*ffn_held, ffn_far), (kept, got), vec, small_grad,
            grad, grad_qkv, qkv_w, rows, grad_scores,
        )

        moved = mixed.along(outs)

        def end_steps(small_grad, cross_last, down_last, ffn_last, flag, *operands):
            back, cross_share, down_share, ffn_share = [
                sum(part[:, at].astype(f32) for part in parts)
                for parts, at in (
                    (cross_last, slice(2 * width, 4 * width)),
                    (cross_last, slice(0, 2 * width)),
                    (down_last, slice(None)),
                    (ffn_last, slice(None)),
                )
            ]
            back = lax.ppermute(back, "section", [(1, 0)])
            small_grad = swapped_small(small_grad, 2)
            low = run_output(after(flag, small_grad), *operands)
            small_grad = swapped_small(small_grad, 4)
            return small_grad, low, back, cross_share, down_share, ffn_share

        small_grad, low, back, cross_share, down_share, ffn_share = block_of(
            always, end_steps, after(small_grad, *outs), cross_last, down_last, ffn_last, flag, vec,
            dec_u, d2, down_w, low,
        )
        small_other = lax.ppermute(small_grad, "batch", [(i, i ^ 8) for i in range(devices)])
        one = (width // devices, width)
        qkv_share, out_share, cf_share, cs_share = pl.pallas_call(
            finish_body,
            in_specs=[SMEM] + [VMEM] * 6,
            out_specs=[VMEM] * 4,
            out_shape=[shape_of((width // devices, 3 * width), f32)] + [shape_of(one, f32)] * 3,
            name="finish",
        )(flag, *moved, own, cross_share, back)
        small_other = after(small_other, qkv_share)
        vec_share, fbias_share, table_total = pl.pallas_call(
            small_body,
            in_specs=[SMEM] + [VMEM] * 2,
            out_specs=[VMEM] * 3,
            out_shape=[
                shape_of((7, 1, width // devices), f32), shape_of((1, hidden // devices), f32),
                shape_of((heads, 1, bucket_count), f32),
            ],
            name="small",
        )(place[None], small_grad, small_other)
        vec_share = jnp.transpose(vec_share, (1, 0, 2))[0]
        table_total = jnp.transpose(table_total, (1, 2, 0))[0]
    return (
        low.reshape((1, row_count, length, width)),
        result.reshape((1, row_count, length, width)),
        qkv_share[None],
        out_share[None],
        ffn_share[None],
        down_share[None],
        cf_share[None],
        cs_share[None],
        vec_share[None],
        fbias_share,
        table_total[None],
    )


def solution(mesh):
    return jax.shard_map(
        per_device,
        mesh=mesh,
        in_specs=(
            P("section", "batch", None, None),
            P("section", "batch", None, None),
            P(None, "batch", None),
            P(),
            P("section", None, None),
            P("section", None, None),
            P("section", None, None),
            P("section", None, None),
            P("section", None, None),
            P("section", None, None),
            P("section", None, None),
            P("section", None),
            P("section", None, None),
        ),
        out_specs=(
            P("section", "batch", None, None),
            P("section", "batch", None, None),
            P("section", "batch", None),
            P("section", "batch", None),
            P("section", "batch", None),
            P("section", "batch", None),
            P("section", "batch", None),
            P("section", "batch", None),
            P("section", None, "batch"),
            P("section", "batch"),
            P("section", None, None),
        ),
        check_vma=False,
    )
```

```python
import functools

import jax
import jax.numpy as jnp
from jax import lax
from jax.experimental import pallas as pl
from jax.experimental.pallas import tpu as pltpu
from jax.sharding import PartitionSpec as P

norm_epsilon = 1e-05
masked_score = -1e30
half_root = 0.7071067811865476
density_scale = 0.3989422804014327
tile = 768
chunk = 256
rotations = (2, 3, 1)
spare_bytes = 8 * 1024 * 1024
all_bytes = 62 * 1024 * 1024

f32 = jnp.float32
bf16 = jnp.bfloat16
ANY = pl.BlockSpec(memory_space=pl.ANY)
SMEM = pl.BlockSpec(memory_space=pltpu.SMEM)
VMEM = pl.BlockSpec(memory_space=pltpu.VMEM)


def mm(left, right):
    return jnp.dot(left, right, preferred_element_type=f32)


def mm_nt(left, right):
    return lax.dot_general(left, right, (((1,), (1,)), ((), ())), preferred_element_type=f32)


def mm_tn(left, right):
    return lax.dot_general(left, right, (((0,), (0,)), ((), ())), preferred_element_type=f32)


def mean_of(values):
    return jnp.sum(values, axis=-1, keepdims=True) * (1.0 / values.shape[-1])


def normalised(values):
    centre = values - mean_of(values)
    rate = lax.rsqrt(mean_of(centre * centre) + norm_epsilon)
    return centre * rate, rate


def each_rows(count, body):
    @pl.loop(0, count // chunk)
    def _(step):
        body(pl.ds(pl.multiple_of(step * chunk, chunk), chunk))


def each_tile(count, body, width=tile):
    if count == width:
        body(pl.ds(0, width))
        return

    @pl.loop(0, count // width)
    def _(step):
        body(pl.ds(pl.multiple_of(step * width, width), width))


def norm_forward(source, gain, offset, target, also=None):
    def rows(at):
        unit, _ = normalised(source[at, :].astype(f32))
        normed = unit * gain + offset
        target[at, :] = normed.astype(target.dtype)

    each_rows(source.shape[0], rows)


def norm_backward(
    source, grad_normed, gain, upstream, target, gain_sum, offset_sum, low=None
):
    gain_sum[...] = jnp.zeros_like(gain_sum)
    offset_sum[...] = jnp.zeros_like(offset_sum)

    def rows(at):
        unit, rate = normalised(source[at, :].astype(f32))
        upper = grad_normed[at, :]
        product = upper * unit
        gain_sum[...] += jnp.sum(product.reshape(-1, 8, product.shape[1]), axis=0)
        offset_sum[...] += jnp.sum(upper.reshape(-1, 8, upper.shape[1]), axis=0)
        scaled = upper * gain
        inner = mean_of(scaled)
        along = mean_of(product * gain)
        result = rate * (scaled - inner - unit * along)
        if upstream is not None:
            result = result + upstream[at, :].astype(f32)
        target[at, :] = result
        if low is not None:
            low[at, :] = result.astype(bf16)

    each_rows(source.shape[0], rows)


def column_sum(partial):
    return jnp.sum(partial[...], axis=0, keepdims=True)


def lower_lanes(shape):
    return lax.broadcasted_iota(jnp.int32, shape, 1) < shape[1] // 2


def split_pair(block):
    lower = lower_lanes(block.shape)
    zero = jnp.zeros_like(block)
    return jnp.concatenate([jnp.where(lower, block, zero), jnp.where(lower, zero, block)], axis=0)


def join_pair(stacked):
    rows = stacked.shape[0] // 2
    lower = lower_lanes((rows, stacked.shape[1]))
    return jnp.where(lower, stacked[:rows], stacked[rows:])


def attend_pair(queries, key_rows, values, additions, scale):
    length = queries.shape[0]
    scores = mm_nt((queries * scale).astype(bf16), split_pair(key_rows))
    parts = []
    for head in range(2):
        part = scores[:, head * length : (head + 1) * length] + additions[head]
        exponent = jnp.exp(part - jnp.max(part, axis=-1, keepdims=True))
        parts.append(exponent * (1.0 / jnp.sum(exponent, axis=-1, keepdims=True)))
    weights = jnp.concatenate(parts, axis=1).astype(bf16)
    return weights, mm(weights, split_pair(values))


def attend_pair_back(weights, queries, key_rows, values, context, grad_context, scale):
    length = queries.shape[0]
    grad_weights = mm_nt(grad_context, split_pair(values))
    product = grad_context.astype(f32) * context.astype(f32)
    lower = lower_lanes(product.shape)
    parts = []
    for head in range(2):
        at = slice(head * length, (head + 1) * length)
        own = jnp.where(lower, product, 0.0) if head == 0 else jnp.where(lower, 0.0, product)
        centred = jnp.sum(own, axis=-1, keepdims=True)
        parts.append(weights[:, at].astype(f32) * (grad_weights[:, at] - centred))
    grad_raw = jnp.concatenate(parts, axis=1).astype(bf16)
    grad_queries = mm(grad_raw, split_pair(key_rows)) * scale
    grad_keys = join_pair(mm_tn(grad_raw, queries)) * scale
    grad_values = join_pair(mm_tn(weights, grad_context))
    return grad_queries, grad_keys, grad_values, parts


def same_sentence(query_ids, key_ids):
    length = query_ids.shape[1]
    across = jnp.broadcast_to(key_ids.astype(f32), (length, length))
    down = jnp.broadcast_to(query_ids.astype(f32), (length, length)).T
    return across == down


class Move:
    def __init__(self, sources, target, semaphores):
        self.sources, self.target, self.semaphores = sources, target, semaphores

    def copies(self, sources):
        if not isinstance(sources, tuple):
            yield pltpu.make_async_copy(sources, self.target, self.semaphores[0])
            return
        rows = self.target.shape[0] // len(sources)
        for part, source in enumerate(sources):
            target = self.target.at[pl.ds(part * rows, rows)]
            yield pltpu.make_async_copy(source, target, self.semaphores[part])

    def start(self, sources=None):
        for copy in self.copies(self.sources if sources is None else sources):
            copy.start()

    def wait(self, sources=None):
        for copy in self.copies(self.sources if sources is None else sources):
            copy.wait()


class Mover:
    def __init__(self, semaphores):
        self.semaphores = semaphores
        self.used = 0

    def note(self, source, target):
        count = len(source) if isinstance(source, tuple) else 1
        semaphores = [self.semaphores.at[self.used + part] for part in range(count)]
        self.used += count
        return Move(source, target, semaphores)

    def start(self, source, target):
        move = self.note(source, target)
        move.start()
        return move


def wait_all(moves):
    for move in moves:
        move.wait()


def gelu_parts(hidden):
    share = 0.5 + 0.5 * lax.erf(hidden * half_root)
    slope = share + hidden * (density_scale * jnp.exp(hidden * hidden * -0.5))
    return hidden * share, slope


def feed_forward(normed, ffn_w, in_bias, ahead, use):
    tiles = spans(ffn_w.shape[1], tile)
    ahead[0] = mm(normed[...], ffn_w[:, tiles[0]])
    for step, at in enumerate(tiles):
        if step + 1 < len(tiles):
            ahead[(step + 1) % 2] = mm(normed[...], ffn_w[:, tiles[step + 1]])
        use(at, ahead[step % 2] + in_bias[:, at])


def first_body(
    heads, row, flag, ids, offsets, table, vectors, in_bias, rows_in, cot_in, qkv_in, out_in, ffn_in,
    down_in, first_in,
    x1_out, h1_out, qkv_out, weights_out, context_out, h2_out, u_out, slope_out, e2_out, low_out,
    hc_out, qc_out,
    rows, qkv_w, out_w, ffn_w, down_w, first_w, cot, normed, qkv, weights, context, x1, h2, u, slope,
    e2, low, bias_rows, mask, context_wide, ahead, loads, stores,
):
    length, width = rows.shape
    hidden_width = ffn_w.shape[1]
    on_encoder = flag[0] == 1
    own_rows = pl.ds(row * length, length)
    load = Mover(loads)
    store = Mover(stores)
    got_rows = load.start(rows_in.at[own_rows], rows)
    got_qkv = load.start(qkv_in, qkv_w)
    got_out = load.start(out_in, out_w)
    got_down = load.note(down_in, down_w)
    got_ffn = load.note(ffn_in, ffn_w)
    got_first = load.note(first_in, first_w)
    got_cot = load.note(cot_in.at[own_rows], cot)

    @pl.when(on_encoder)
    def _():
        got_ffn.start()
        got_down.start()

    @pl.when(jnp.logical_not(on_encoder))
    def _():
        got_first.start()
        got_cot.start()
        got_down.start()

    one_hot = (offsets[...] == lax.broadcasted_iota(jnp.int32, (table.shape[1], 2 * length), 0)).astype(f32)
    by_offset = lax.dot_general(
        table[...], one_hot, (((1,), (0,)), ((), ())), precision=lax.Precision.HIGHEST,
        preferred_element_type=f32,
    )
    bias_rows[...] = pltpu.roll(by_offset, length + 1, 1)
    own_group = jnp.where(on_encoder, 0, 1)
    causal = lax.broadcasted_iota(jnp.int32, (length, length), 0) >= lax.broadcasted_iota(
        jnp.int32, (length, length), 1
    )
    own = ids[pl.ds(own_group, 1), row, :]
    allowed = same_sentence(own, own) & (causal | on_encoder)
    mask[...] = jnp.where(allowed, 0.0, masked_score)

    got_rows.wait()
    norm_forward(rows, vectors[0], vectors[1], normed)
    got_qkv.wait()

    def project(at):
        qkv[:, at] = mm(normed[...], qkv_w[:, at]).astype(bf16)

    each_tile(3 * width, project)
    out_copies = [store.start(normed, h1_out), store.start(qkv, qkv_out)]
    scale = (width // heads) ** (-0.5)

    @pl.loop(0, heads // 2, unroll=heads // 2)
    def _(pair):
        lanes = pl.multiple_of(pair * 128, 128)
        additions = []
        for head in range(2):
            spread = jnp.broadcast_to(bias_rows[pl.ds(pair * 2 + head, 1), :], (length, 2 * length))
            skewed = pltpu.roll(spread, 0, 1, stride=1, stride_axis=0)
            additions.append(skewed[:, :length] + mask[...])
        part, mixed = attend_pair(
            qkv[:, pl.ds(lanes, 128)],
            qkv[:, pl.ds(width + lanes, 128)],
            qkv[:, pl.ds(2 * width + lanes, 128)],
            additions,
            scale,
        )
        weights[0, pair] = part
        context_wide[:, pl.ds(lanes, 128)] = mixed
        context[:, pl.ds(lanes, 128)] = mixed.astype(bf16)

    out_copies += [store.start(weights, weights_out), store.start(context_wide, context_out)]
    got_out.wait()
    x1[...] = rows[...].astype(f32) + mm(context[...], out_w[...])
    out_copies.append(store.start(x1, x1_out))

    @pl.when(on_encoder)
    def _():
        norm_forward(x1, vectors[2], vectors[3], h2)
        got_ffn.wait()

        def feed(at, hidden):
            value, rate = gelu_parts(hidden)
            u[:, at] = value.astype(bf16)
            slope[:, at] = rate.astype(bf16)

        feed_forward(h2, ffn_w, in_bias, ahead, feed)
        copies = [store.start(h2, h2_out), store.start(u, u_out), store.start(slope, slope_out)]
        got_down.wait()
        e2[...] = x1[...] + (mm(u[...], down_w[...]) + vectors[6])
        copies.append(store.start(e2, e2_out))
        norm_forward(e2, vectors[4], vectors[5], low)
        copies.append(store.start(low, low_out))
        wait_all(copies)

    @pl.when(jnp.logical_not(on_encoder))
    def _():
        norm_forward(x1, vectors[2], vectors[3], h2)
        got_first.wait()
        low[...] = mm(h2[...], first_w[...]).astype(bf16)
        copies = [store.start(h2, hc_out), store.start(low, qc_out)]
        got_down.wait()
        got_cot.wait()

        def back(at):
            slope[:, at] = mm_nt(cot[...], down_w[at, :]).astype(bf16)

        each_tile(hidden_width, back)
        copies.append(store.start(slope, slope_out))
        wait_all(copies)

    wait_all(out_copies)


def cross_body(
    heads, row, flag, ids, vectors, in_bias, small_in,
    memory_in, sent_in, other_in, second_in, x1_in, qc_in, cot_in, ffn_in, slope_in, earlier,
    small_out, h2_out, u_out, slope_out, d2_out, grad_out, cc_out, dq_out, dk_out, dv_out, dm_out,
    low_out, pieces, memory, keys_w, values_w, second_w, x1, qc, cot, ffn_w, keys, values, weights, cc, d2, h2, u,
    slope, grad_normed, grad, grad_low, dq, dk, dv, dm, mask, gain_sum, offset_sum, cc_wide, ahead, *rest
):
    *products, loads, stores = rest
    length, width = memory.shape
    small_out[...] = jnp.zeros_like(small_out) if row == 0 else small_in[...]

    @pl.when(flag[0] == 0)
    def _():
        load = Mover(loads)
        store = Mover(stores)
        got_memory = load.start(memory_in, memory)
        got_keys = load.note(sent_in, keys_w)
        got_values = load.note(sent_in, values_w)
        for core, (keys_in, values_in) in enumerate(((sent_in, other_in), (other_in, sent_in))):

            @pl.when(flag[1] == core)
            def _(keys_in=keys_in, values_in=values_in):
                got_keys.start(keys_in)
                got_values.start(values_in)

        got_query = load.start(qc_in, qc)
        got_second = [load.start(second_in, second_w), load.start(x1_in, x1)]
        got_ffn = [load.start(ffn_in, ffn_w), load.start(slope_in, slope)]
        got_cot = load.start(cot_in.at[pl.ds(row * length, length)], cot)
        if products:
            got_earlier = []
            for sources, whole in zip(earlier, products):
                if not sources:
                    continue
                rows = len(sources) * length
                got_earlier.append(load.start(tuple(sources), whole.at[pl.ds(0, rows)]))
        mask[...] = jnp.where(same_sentence(ids[1:2, row, :], ids[0:1, row, :]), 0.0, masked_score)
        got_memory.wait()
        got_keys.wait()
        keys[...] = mm(memory[...], keys_w[...]).astype(bf16)
        got_values.wait()
        values[...] = mm(memory[...], values_w[...]).astype(bf16)
        got_query.wait()
        scale = (width // heads) ** (-0.5)

        @pl.loop(0, heads // 2, unroll=3)
        def _(pair):
            lanes = pl.ds(pl.multiple_of(pair * 128, 128), 128)
            part, mixed = attend_pair(
                qc[:, lanes], keys[:, lanes], values[:, lanes], [mask[...], mask[...]], scale
            )
            weights[0, pair] = part
            cc_wide[:, lanes] = mixed
            cc[:, lanes] = mixed.astype(bf16)

        copies = [store.start(cc, cc_out)]
        wait_all(got_second)
        d2[...] = x1[...] + mm(cc[...], second_w[...])
        copies.append(store.start(d2, d2_out))
        norm_forward(d2, vectors[4], vectors[5], h2)
        copies.append(store.start(h2, h2_out))
        wait_all(got_ffn)

        def feed(at, hidden):
            value, rate = gelu_parts(hidden)
            u[:, at] = value.astype(bf16)
            slope[:, at] = (slope[:, at].astype(f32) * rate).astype(bf16)

        feed_forward(h2, ffn_w, in_bias, ahead, feed)
        copies += [store.start(u, u_out), store.start(slope, slope_out)]
        grad_normed[...] = mm_nt(slope[...], ffn_w[...])
        got_cot.wait()
        norm_backward(
            d2, grad_normed, vectors[4], cot, grad, gain_sum, offset_sum, grad_low
        )
        small_out[4:5, :] += column_sum(gain_sum)
        small_out[5:6, :] += column_sum(offset_sum)
        copies += [store.start(grad, grad_out), store.start(grad_low, low_out)]
        dm[...] = mm_nt(grad_low[...], second_w[...]).astype(bf16)

        @pl.loop(0, heads // 2, unroll=3)
        def _(pair):
            lanes = pl.ds(pl.multiple_of(pair * 128, 128), 128)
            grad_q, grad_k, grad_v, _ = attend_pair_back(
                weights[0, pair], qc[:, lanes], keys[:, lanes], values[:, lanes], cc_wide[:, lanes],
                dm[:, lanes], scale,
            )
            dq[:, lanes] = grad_q.astype(bf16)
            dk[:, lanes] = grad_k.astype(bf16)
            dv[:, lanes] = grad_v.astype(bf16)

        copies += [store.start(dq, dq_out), store.start(dk, dk_out), store.start(dv, dv_out)]
        dm[...] = (mm_nt(dk[...], keys_w[...]) + mm_nt(dv[...], values_w[...])).astype(bf16)
        copies.append(store.start(dm, dm_out))
        if products:
            *wholes, cross_g = products
            hc, *others = wholes
            own = pl.ds(hc.shape[0] - length, length)
            for whole, part in zip(others, (dq, cc, grad_low, memory, dk, dv)):
                whole[own, :] = part[...]
            wait_all(got_earlier)
            hc, dq_all, cc_all, low_all, memory_all, dk_all, dv_all = wholes
            query, out, key, value = spans(4 * width, width)
            cross_g[:, query] = mm_tn(hc[...], dq_all[...]).astype(bf16)
            cross_g[:, out] = mm_tn(cc_all[...], low_all[...]).astype(bf16)
            copies += put_columns(store, cross_g, pieces, flag[1], pl.ds(0, 2 * width))
            cross_g[:, key] = mm_tn(memory_all[...], dk_all[...]).astype(bf16)
            cross_g[:, value] = mm_tn(memory_all[...], dv_all[...]).astype(bf16)
            copies += put_columns(store, cross_g, pieces, flag[1], pl.ds(2 * width, 2 * width))
        wait_all(copies)


def put_rows(store, stage, targets, core, rows):
    if len(targets) == 1:
        return [store.start(stage.at[rows], targets[0].at[rows])]
    depth = targets[0].shape[1]
    copies = []
    for chip in range(rows.start // (2 * depth), (rows.start + rows.size) // (2 * depth)):
        for target, which in zip(targets, (core, 1 - core)):
            at = pl.multiple_of((2 * chip + which) * depth, depth)
            copies.append(store.start(stage.at[pl.ds(at, depth)], target.at[chip]))
    return copies


def put_columns(store, stage, targets, core, columns):
    if len(targets) == 1:
        return [store.start(stage.at[:, columns], targets[0].at[:, columns])]
    chips, depth = targets[0].shape[0], targets[0].shape[1]
    copies = []
    for chip in range(chips):
        for target, which in zip(targets, (core, 1 - core)):
            at = pl.multiple_of((2 * chip + which) * depth, depth)
            copies.append(
                store.start(stage.at[pl.ds(at, depth), columns], target.at[chip, :, columns])
            )
    return copies


def spans(count, width):
    return [pl.ds(start, width) for start in range(0, count, width)]


def down_body(flag, vectors, small_in, dm_in, cot_in, e2_in, enc_u_in, dec_u_in, *rest):
    small_out, grad_out, low_out, *rest = rest
    count = len(rest) - 11
    outs = rest[:count]
    dm, cot, e2, u, grad, grad_low, down_g, gain_sum, offset_sum, loads, stores = rest[count:]
    hidden_width, width = u.shape[1], cot.shape[1]
    small_out[...] = small_in[...]
    load = Mover(loads)
    store = Mover(stores)
    got_cot = load.start(cot_in, cot)
    got_u = load.note(enc_u_in, u)
    moved = [load.note(dm_in, dm), load.note(e2_in, e2)]
    kept = [store.note(grad, grad_out), store.note(grad_low, low_out)]

    @pl.when(flag[0] == 1)
    def _():
        for copy in moved:
            copy.start()
        got_cot.wait()
        wait_all(moved)
        got_u.start(enc_u_in)

        def total(at):
            grad[at, :] = dm[at, :].astype(f32) + cot[at, :].astype(f32)

        each_rows(grad.shape[0], total)
        norm_backward(e2, grad, vectors[4], None, grad, gain_sum, offset_sum, grad_low)
        small_out[4:5, :] = column_sum(gain_sum)
        small_out[5:6, :] = column_sum(offset_sum)
        for copy in kept:
            copy.start()

    @pl.when(flag[0] == 0)
    def _():
        got_u.start(dec_u_in)
        got_cot.wait()
        grad_low[...] = cot[...]

    got_u.wait()
    copies = []
    for rows in spans(hidden_width, tile):
        down_g[rows, :] = mm_tn(u[:, rows], grad_low[...]).astype(bf16)
        copies += put_rows(store, down_g, outs, flag[1], rows)
    small_out[6:7, :] = jnp.sum(grad_low[...].astype(f32), axis=0, keepdims=True)
    wait_all(copies)

    @pl.when(flag[0] == 1)
    def _():
        wait_all(kept)


def hidden_body(flag, low_in, down_in, slope_in, slope_out, grad_low, down_w, slope, loads, stores):
    @pl.when(flag[0] == 1)
    def _():
        load = Mover(loads)
        store = Mover(stores)
        hidden_width = slope.shape[1]
        got_low = load.start(low_in, grad_low)
        got_slope = load.start(slope_in, slope)
        got_down = [
            load.start(down_in.at[rows], down_w.at[rows]) for rows in spans(hidden_width, tile)
        ]
        got_low.wait()
        got_slope.wait()
        copies = []
        for at, got in zip(spans(hidden_width, tile), got_down):
            got.wait()
            part = mm_nt(grad_low[...], down_w[at, :]) * slope[:, at].astype(f32)
            slope[:, at] = part.astype(bf16)
            copies.append(store.start(slope.at[:, at], slope_out.at[:, at]))
        wait_all(copies)


def ffn_body(flag, small_in, enc_ins, dec_ins, *rest):
    small_out, *rest = rest
    count = len(rest) - 5
    outs = rest[:count]
    slope, h2, ffn_g, loads, stores = rest[count:]
    width, hidden_width = h2.shape[1], slope.shape[1]
    small_out[...] = small_in[...]
    load = Mover(loads)
    store = Mover(stores)
    moves = [load.note(source, target) for source, target in zip(dec_ins, (h2, slope))]
    for which, ins in enumerate((dec_ins, enc_ins)):

        @pl.when(flag[0] == which)
        def _(ins=ins):
            for move, source in zip(moves, ins):
                move.start(source)
            for move, source in zip(moves, ins):
                move.wait(source)

    copies = []
    for step, at in enumerate(spans(hidden_width, tile)):
        ffn_g[:, at] = mm_tn(h2[...], slope[:, at]).astype(bf16)
        if step % 2 == 1:
            both = pl.ds(at.start - tile, 2 * tile)
            copies += put_columns(store, ffn_g, outs, flag[1], both)
    for part in range(hidden_width // width):
        values = slope[:, part * width : (part + 1) * width].astype(f32)
        small_out[8 + part : 9 + part, :] = jnp.sum(values, axis=0, keepdims=True)
    wait_all(copies)


def hidden_back_body(
    flag, vectors, small_in, slope_in, ffn_in, dq_in, first_in, x1_in, enc_grad_in, dec_grad_in,
    small_out, grad_out,
    slope, ffn_w, dq, first_w, x1, grad, grad_normed, gain_sum, offset_sum, loads, stores,
):
    width = x1.shape[1]
    small_out[...] = small_in[...]
    load = Mover(loads)
    store = Mover(stores)
    got_x1 = load.note(x1_in, x1)
    got_grad = load.note(dec_grad_in, grad)

    @pl.when(flag[0] == 1)
    def _():
        got = [load.start(slope_in, slope), load.start(ffn_in, ffn_w)]
        got_x1.start()
        got_grad.start(enc_grad_in)
        wait_all(got)
        grad_normed[...] = mm_nt(slope[...], ffn_w[...])
        got_grad.wait(enc_grad_in)

    @pl.when(flag[0] == 0)
    def _():
        got = [load.start(dq_in, dq), load.start(first_in, first_w)]
        got_x1.start()
        got_grad.start(dec_grad_in)
        wait_all(got)
        grad_normed[...] = mm_nt(dq[...], first_w[...])
        got_grad.wait()

    got_x1.wait()
    norm_backward(x1, grad_normed, vectors[2], grad, grad, gain_sum, offset_sum)
    stored = store.start(grad, grad_out)
    small_out[2:3, :] = column_sum(gain_sum)
    small_out[3:4, :] = column_sum(offset_sum)
    stored.wait()


def attention_back_body(
    heads, flag, grad_in, qkv_in, weights_in, context_in, outw_in, h1_in, *rest
):
    grad_qkv_out, scores_out, *rest = rest
    count = len(rest) - 14
    outs = rest[:count]
    (
        grad, qkv, weights, context, out_w, h1, grad_low, grad_context, grad_qkv, mixed_g,
        grad_scores, context_low, loads, stores,
    ) = rest[count:]
    width = context.shape[1]
    row_count, length = weights.shape[0], weights.shape[2]
    load = Mover(loads)
    store = Mover(stores)
    got_grad = [load.start(grad_in, grad), load.start(outw_in, out_w)]
    got_context = load.start(context_in, context)
    got_attention = [load.start(weights_in, weights), load.start(qkv_in, qkv)]
    got_h1 = load.start(h1_in, h1)
    wait_all(got_grad)

    def lower(at):
        grad_low[at, :] = grad[at, :].astype(bf16)

    each_rows(grad.shape[0], lower)
    grad_context[...] = mm_nt(grad_low[...], out_w[...]).astype(bf16)
    got_context.wait()
    context_low[...] = context[...].astype(bf16)
    mixed_g[:, pl.ds(0, width)] = mm_tn(context_low[...], grad_low[...]).astype(bf16)
    wait_all(got_attention)
    scale = (width // heads) ** (-0.5)

    @pl.loop(0, heads // 2, unroll=3)
    def _(pair):
        lanes = pl.multiple_of(pair * 128, 128)
        totals = [None, None]
        for row in range(row_count):
            at = slice(row * length, (row + 1) * length)
            grad_q, grad_k, grad_v, parts = attend_pair_back(
                weights[row, pair],
                qkv[at, pl.ds(lanes, 128)],
                qkv[at, pl.ds(width + lanes, 128)],
                qkv[at, pl.ds(2 * width + lanes, 128)],
                context[at, pl.ds(lanes, 128)],
                grad_context[at, pl.ds(lanes, 128)],
                scale,
            )
            grad_qkv[at, pl.ds(lanes, 128)] = grad_q.astype(bf16)
            grad_qkv[at, pl.ds(width + lanes, 128)] = grad_k.astype(bf16)
            grad_qkv[at, pl.ds(2 * width + lanes, 128)] = grad_v.astype(bf16)
            totals = [p if t is None else t + p for t, p in zip(totals, parts)]
        for head in range(2):
            grad_scores[pair * 2 + head] = totals[head]

    got_h1.wait()
    copies = [store.start(grad_qkv, grad_qkv_out), store.start(grad_scores, scores_out)]
    for step, at in enumerate(spans(3 * width, width)):
        mixed_g[:, pl.ds(width + at.start, width)] = mm_tn(h1[...], grad_qkv[:, at]).astype(bf16)
        if step != 1:
            both = pl.ds(0 if step == 0 else 2 * width, 2 * width)
            copies += put_columns(store, mixed_g, outs, flag[1], both)
    wait_all(copies)


def sum_diagonals(grid):
    length = grid.shape[0]
    padded = jnp.concatenate([grid, jnp.zeros((length, length), f32)], axis=1)
    folded = padded[0:8, :]
    for block in range(1, length // 8):
        folded = folded + pltpu.roll(
            padded[block * 8 : (block + 1) * 8, :], 2 * length - block * 8, 1
        )
    line = folded[0:1, :]
    for sub in range(1, 8):
        line = line + pltpu.roll(folded[sub : sub + 1, :], 2 * length - sub, 1)
    return pltpu.roll(line, length - 1, 1)


def last_body(
    flag, offsets, vectors, small_in, grad_in, grad_qkv_in, qkvw_in, rows_in, scores_in,
    small_out, result_out,
    grad, grad_qkv, qkv_w, rows, grad_normed, grad_scores, diagonals, one_hot, gain_sum, offset_sum,
    loads, stores,
):
    small_out[...] = small_in[...]
    heads, bucket_count = grad_scores.shape[0], one_hot.shape[0]
    load = Mover(loads)
    store = Mover(stores)
    got = [load.start(grad_qkv_in, grad_qkv), load.start(qkvw_in, qkv_w)]
    got_rows = [load.start(rows_in, rows), load.start(grad_in, grad)]
    got_scores = load.start(scores_in, grad_scores)
    wait_all(got)
    grad_normed[...] = mm_nt(grad_qkv[...], qkv_w[...])
    wait_all(got_rows)
    norm_backward(rows, grad_normed, vectors[0], grad, grad, gain_sum, offset_sum)
    small_out[0:1, :] = column_sum(gain_sum)
    small_out[1:2, :] = column_sum(offset_sum)
    stored = store.start(grad, result_out)

    got_scores.wait()

    @pl.loop(0, heads)
    def _(head):
        diagonals[pl.ds(head, 1), :] = sum_diagonals(grad_scores[head])

    one_hot[...] = (offsets[...] == lax.broadcasted_iota(jnp.int32, one_hot.shape, 0)).astype(f32)
    small_out[pl.ds(16, heads), pl.ds(0, bucket_count)] = lax.dot_general(
        diagonals[...], one_hot[...], (((1,), (1,)), ((), ())), precision=lax.Precision.HIGHEST,
        preferred_element_type=f32,
    )
    stored.wait()


def output_body(
    flag, vectors, u_in, d2_in, down_in, low_in, low_out, u, d2, down_w, low, loads, stores
):
    load = Mover(loads)
    stored = Mover(stores).note(low, low_out)
    got_low = load.note(low_in, low)

    @pl.when(flag[0] == 1)
    def _():
        got_low.start()
        got_low.wait()
        stored.start()

    @pl.when(flag[0] == 0)
    def _():
        wait_all([load.start(u_in, u), load.start(d2_in, d2), load.start(down_in, down_w)])
        value = d2[...] + (mm(u[...], down_w[...]) + vectors[6])
        low[...] = value.astype(bf16)
        stored.start()

    stored.wait()


def pair_sum_body(everywhere, flag, kept_in, got_in, out, kept, got, total, loads, stores):
    @pl.when(jnp.logical_or(flag[0] == 0, everywhere))
    def _():
        load = Mover(loads)
        store = Mover(stores)
        blocks = out.shape[0]
        ready = []
        for step in range(blocks):
            block = 2 * step + 1 - flag[2]
            ready.append(
                (load.start(kept_in.at[block], kept.at[step]), load.start(got_in.at[block], got.at[step]))
            )
        copies = []
        for step in range(blocks):
            wait_all(ready[step])
            total[step] = (kept[step].astype(f32) + got[step].astype(f32)).astype(bf16)
            copies.append(store.start(total.at[step], out.at[step]))
        wait_all(copies)


def pair_sum(flag, kept, got, everywhere):
    chips, depth, width = kept.shape
    part = (chips // 2, depth, width)
    return run_kernel(
        functools.partial(pair_sum_body, everywhere),
        (flag, kept, got),
        [SMEM, ANY, ANY],
        [shape_of(part, bf16)],
        [ANY],
        [(part, bf16)] * 3,
        chips, chips // 2, "pair_sum",
    )[0]


def chip_sum_body(
    everywhere, flag, kept_in, got_in, far_in, first_out, second_out, third_out, own_out,
    kept, got, far, total, own, loads, stores,
):
    @pl.when(jnp.logical_or(flag[0] == 0, everywhere))
    def _():
        load = Mover(loads)
        store = Mover(stores)
        ready = []
        for step, away in enumerate((*rotations, 0)):
            place = lax.rem(flag[3] + away, 4)
            block = 2 * place + flag[2]
            ready.append(
                [
                    load.start(kept_in.at[block], kept.at[step]),
                    load.start(got_in.at[block], got.at[step]),
                    load.start(far_in.at[place], far.at[step]),
                ]
            )
        copies = []
        for step, out in enumerate((first_out, second_out, third_out, own_out)):
            wait_all(ready[step])
            value = kept[step].astype(f32) + got[step].astype(f32) + far[step].astype(f32)
            if step < 3:
                total[step] = value.astype(bf16)
                copies.append(store.start(total.at[step], out))
            else:
                own[...] = value
                copies.append(store.start(own, out))
        wait_all(copies)


def chip_sum(flag, kept, got, far, everywhere):
    _, depth, width = kept.shape
    one = (depth, width)
    return run_kernel(
        functools.partial(chip_sum_body, everywhere),
        (flag, kept, got, far),
        [SMEM, ANY, ANY, ANY],
        [shape_of(one, bf16)] * 3 + [shape_of(one, f32)],
        [ANY] * 4,
        [((4,) + one, bf16)] * 3 + [((3,) + one, bf16), (one, f32)],
        12, 4, "chip_sum",
    )


def pick_body(flag, first_in, second_in, out, held, loads, stores):
    @pl.when(flag[0] == 1)
    def _():
        got = Mover(loads).note(first_in, held)
        for core, source in enumerate((first_in, second_in)):

            @pl.when(flag[1] == core)
            def _(source=source):
                got.start(source)

        got.wait()
        Mover(stores).start(held, out).wait()


def finish_body(
    flag, first, second, third, own, cross, back, qkv_out, out_out, cf_out, cs_out
):
    width = out_out.shape[1]
    total = own[...]
    for part in (first, second, third):
        total = total + part[...].astype(f32)
    out_out[...] = total[:, :width]
    qkv_out[...] = total[:, width:]
    chosen = jnp.where(flag[0] == 1, back[...], cross[...])
    cf_out[...] = chosen[:, :width]
    cs_out[...] = chosen[:, width:]


def small_body(place, mine, other, vec_out, fbias_out, table_out):
    small = mine[...] + other[...]
    width = small.shape[1]
    share = vec_out.shape[2]
    turned = pltpu.roll(small[0:8, :], lax.rem(width - place[0] * share, width), 1)
    for row in range(vec_out.shape[0]):
        vec_out[row] = turned[row : row + 1, :share]
    share = fbias_out.shape[1]
    per_row = width // share
    row = mine[pl.ds(8 + lax.div(place[0], per_row), 1), :]
    row = row + other[pl.ds(8 + lax.div(place[0], per_row), 1), :]
    turned = pltpu.roll(row, lax.rem(width - lax.rem(place[0], per_row) * share, width), 1)
    fbias_out[...] = turned[:, :share]
    for head in range(table_out.shape[0]):
        table_out[head] = small[16 + head : 17 + head, : table_out.shape[2]]


def shape_of(dims, dtype):
    return jax.ShapeDtypeStruct(tuple(dims), dtype)


def size_of(dims, dtype):
    total = jnp.dtype(dtype).itemsize
    for dim in dims:
        total *= dim
    return total


def run_kernel(
    body, operands, places, outs, out_places, scratch, loads, stores, name, alone=False
):
    held = sum(size_of(dims, dtype) for dims, dtype in scratch)
    flat, form = jax.tree.flatten(operands)
    flat_places = [
        place for place, operand in zip(places, operands, strict=True) for _ in jax.tree.leaves(operand)
    ]

    flat_outs, out_form = jax.tree.flatten(outs)
    held_at = len(flat) + len(flat_outs)

    def kernel(*refs):
        results = out_form.unflatten(refs[len(flat) : held_at])
        return body(*form.unflatten(refs[: len(flat)]), *results, *refs[held_at:])

    results = pl.pallas_call(
        kernel,
        in_specs=flat_places,
        out_specs=out_places,
        out_shape=flat_outs,
        scratch_shapes=[pltpu.VMEM(dims, dtype) for dims, dtype in scratch]
        + [pltpu.SemaphoreType.DMA((loads,)), pltpu.SemaphoreType.DMA((stores,))],
        compiler_params=pltpu.CompilerParams(
            vmem_limit_bytes=all_bytes
        ),
        cost_estimate=pl.CostEstimate(flops=1, bytes_accessed=1, transcendentals=0),
        name=name,
    )(*flat)
    return out_form.unflatten(results)


def after(value, *others):
    return lax.optimization_barrier((value,) + others)[0]


def block_of(always, steps, *operands):
    shapes = jax.eval_shape(steps, *operands)

    def blank(*_):
        return jax.tree.map(lambda leaf: jnp.zeros(leaf.shape, leaf.dtype), shapes)

    return lax.cond(always, steps, blank, *operands)


class Ring:
    def __init__(self, devices, everywhere):
        self.devices = devices
        self.everywhere = everywhere

    def send(self, shard, moved):
        pairs = [(i, moved(i)) for i in range(self.devices)]
        if self.everywhere:
            return lax.ppermute(shard, "batch", pairs)
        pairs = [(self.devices + i, self.devices + j) for i, j in pairs]
        return lax.ppermute(shard, ("section", "batch"), pairs)

    def to_core(self, given):
        return self.send(given, lambda i: i ^ 1)

    def to_chip(self, out):
        return self.send(out, lambda i: i ^ 2)

    def sums(self, flag, *held):
        return chip_sum(flag, *held, self.everywhere)

    def along(self, outs):
        return [
            self.send(out, lambda i, away=away: (i + 4 * away) % 16)
            for away, out in zip(rotations, outs)
        ]


def per_device(
    inputs, cotangent, segments, buckets, qkv_weight, out_weight, in_weight, down_weight,
    cross_first, cross_second, vectors, ffn_bias, position_table,
):
    row_count, length, width = inputs.shape[1:]
    heads = position_table.shape[2]
    bucket_count = position_table.shape[1]
    hidden = in_weight.shape[2]
    tokens = row_count * length
    pairs = heads // 2
    on_encoder = lax.axis_index("section") == 0
    place = lax.axis_index("batch")
    core = lax.rem(place, 2)
    devices = lax.axis_size("batch")
    by_chip = devices == 16
    always = place < devices
    flag = jnp.stack(
        [on_encoder.astype(jnp.int32), core, lax.rem(lax.div(place, 2), 2), lax.div(place, 4)]
    )
    offsets = jnp.pad(buckets, (0, 1), constant_values=-1)[None]
    table = jnp.transpose(position_table, (2, 0, 1))[:, 0]
    rows = inputs.reshape(tokens, width)
    cot = cotangent.reshape(tokens, width)
    qkv_w, out_w, ffn_w, down_w = qkv_weight[0], out_weight[0], in_weight[0], down_weight[0]
    first_w, second_w = cross_first[0], cross_second[0]
    vec = jnp.transpose(vectors, (1, 0, 2))
    fbias = ffn_bias

    tw, th = (tokens, width), (tokens, hidden)
    wide = (tokens, 3 * width)
    square = (row_count, pairs, length, 2 * length)
    row_tw, row_th, row_wide = (length, width), (length, hidden), (length, 3 * width)
    row_square = (1, pairs, length, 2 * length)
    small = (32, width)

    (picked,) = run_kernel(
        pick_body, (flag, first_w, second_w), [SMEM, ANY, ANY], [shape_of((width, width), bf16)],
        [ANY], [((width, width), bf16)], 1, 1, "pick",
    )
    sent = lax.ppermute(picked, "section", [(0, 1)])
    flag = after(flag, picked)

    def piece(depth_rows, columns):
        if not by_chip:
            return [shape_of((depth_rows, columns), bf16)]
        return [shape_of((devices // 2, depth_rows // devices, columns), bf16)] * 2

    down_piece, ffn_piece = piece(hidden, width), piece(width, hidden)
    mixed_piece = piece(width, 4 * width)
    count = len(down_piece)
    share_copies = devices if by_chip else 1
    def run_first(row, flag):
        return run_kernel(
            functools.partial(first_body, heads, row),
            (flag, segments, offsets, table, vec, fbias, rows, cot, qkv_w, out_w, ffn_w,
             down_w, first_w),
            [SMEM] + [VMEM] * 5 + [ANY] * 7,
            [
                shape_of(row_tw, f32), shape_of(row_tw, bf16), shape_of(row_wide, bf16),
                shape_of(row_square, bf16), shape_of(row_tw, f32), shape_of(row_tw, bf16),
                shape_of(row_th, bf16), shape_of(row_th, bf16), shape_of(row_tw, f32),
                shape_of(row_tw, bf16), shape_of(row_tw, bf16), shape_of(row_tw, bf16),
            ],
            [ANY] * 12,
            [
                (row_tw, bf16), ((width, 3 * width), bf16), ((width, width), bf16),
                ((width, hidden), bf16), ((hidden, width), bf16), ((width, width), bf16),
                (row_tw, bf16), (row_tw, bf16), (row_wide, bf16), (row_square, bf16), (row_tw, bf16),
                (row_tw, f32), (row_tw, bf16), (row_th, bf16), (row_th, bf16), (row_tw, f32),
                (row_tw, bf16), ((heads, 2 * length), f32), ((length, length), f32),
                (row_tw, f32), ((2, length, tile), f32),
            ],
            7, 13, "first", True,
        )

    def run_cross(row, flag, small_grad, memory, sent, sent_other, own, earlier):
        x1, qc, slope = own
        last_row = row == row_count - 1
        products = [(tw, bf16)] * 7 + [((width, 4 * width), bf16)] if last_row else []
        return run_kernel(
            functools.partial(cross_body, heads, row),
            (flag, segments, vec, fbias, small_grad, memory, sent, sent_other, second_w, x1, qc, cot,
             ffn_w, slope, earlier if last_row else ()),
            [SMEM] + [VMEM] * 4 + [ANY] * 10,
            [shape_of(small, f32), shape_of(row_tw, bf16), shape_of(row_th, bf16),
             shape_of(row_th, bf16), shape_of(row_tw, f32), shape_of(row_tw, f32)]
            + [shape_of(row_tw, bf16)] * 6 + [mixed_piece if last_row else []],
            [VMEM] + [ANY] * (11 + (count if last_row else 0)),
            [
                (row_tw, bf16), ((width, width), bf16), ((width, width), bf16),
                ((width, width), bf16), (row_tw, f32), (row_tw, bf16), (row_tw, bf16),
                ((width, hidden), bf16), (row_tw, bf16), (row_tw, bf16), (row_square, bf16),
                (row_tw, bf16), (row_tw, f32), (row_tw, bf16), (row_th, bf16), (row_th, bf16),
                (row_tw, f32), (row_tw, f32), (row_tw, bf16), (row_tw, bf16), (row_tw, bf16),
                (row_tw, bf16), (row_tw, bf16), ((length, length), f32), ((8, width), f32),
                ((8, width), f32), (row_tw, f32), ((2, length, tile), f32),
            ] + products,
            9 + (7 * row_count if last_row else 0), 11 + 2 * share_copies, "cross", True,
        )

    def to_decoder(value):
        return lax.ppermute(value, "section", [(0, 1)])

    def to_encoder(value):
        return lax.ppermute(value, "section", [(1, 0)])

    kept_rows = [run_first(0, flag)]
    for row in range(1, row_count):

        def first_steps(low, flag, row=row):
            memory = to_decoder(low)
            return memory, run_first(row, flag)

        low = kept_rows[-1][9]
        memory, outs = block_of(always, first_steps, low, after(flag, low))
        kept_rows.append(outs)
        memories = (*memories, memory) if row > 1 else (memory,)

    def cross_steps(low, flag, first_memory, sent, own, first_earlier):
        memory = to_decoder(low)
        other = lax.ppermute(sent, "batch", [(i, i ^ 1) for i in range(devices)])
        return memory, other, run_cross(0, flag, fbias, first_memory, sent, other, own, first_earlier)

    def own_of(row):
        outs = kept_rows[row]
        return outs[0], outs[11], outs[7]

    def earlier_of(rows):
        hc = tuple(outs[10] for outs in kept_rows)
        return (
            hc,
            *(tuple(outs[part] for outs in rows) for part in (6, 5, 10)),
            tuple(memories[: len(rows)]),
            *(tuple(outs[part] for outs in rows) for part in (7, 8)),
        )

    low = kept_rows[-1][9]
    memory, sent_other, outs = block_of(
        always, cross_steps, low, after(flag, low), memories[0], sent, own_of(0), earlier_of(())
    )
    memories = (*memories, memory)
    small_grad, *outs = outs
    cross_rows, returned = [outs], ()
    for row in range(1, row_count):

        def return_steps(dm, flag, *operands, row=row):
            back = to_encoder(dm)
            return back, run_cross(row, flag, *operands)

        dm = cross_rows[-1][9]
        back, outs = block_of(
            always, return_steps, dm, after(flag, dm), small_grad, memories[row], sent, sent_other,
            own_of(row), earlier_of(cross_rows),
        )
        small_grad, *outs = outs
        cross_rows.append(outs)
        returned = (*returned, back)
    dm = cross_rows[-1][9]
    returned = (*returned, to_encoder(dm))
    x1, h1, qkv, weights, context, h2, u, slope, e2, low, hc, qc = zip(*kept_rows)
    dec_h2, dec_u, dec_slope, d2, grad, _, dq, _, _, dm, _, cross_gs = zip(*cross_rows)
    cross_g = cross_gs[-1]

    cross, down, ffn, mixed = (
        Ring(devices, name != "cross") for name in ("cross", "down", "ffn", "mixed")
    )

    flag = after(flag, *dm)

    def run_down(flag, vec, small_grad, returned, cot, e2, u, dec_u):
        small_grad, enc_grad, enc_low, *pieces = run_kernel(
            down_body,
            (flag, vec, small_grad, returned, cot, e2, u, dec_u),
            [SMEM] + [VMEM] * 2 + [ANY] * 5,
            [shape_of(small, f32), shape_of(tw, f32), shape_of(tw, bf16)] + down_piece,
            [VMEM] + [ANY] * (2 + count),
            [
                (tw, bf16), (tw, bf16), (tw, f32), (th, bf16), (tw, f32), (tw, bf16),
                ((hidden, width), bf16), ((8, width), f32), ((8, width), f32),
            ],
            1 + 3 * row_count, 2 + max(share_copies, hidden // tile), "down",
        )
        return small_grad, enc_grad, enc_low, pieces

    def run_hidden(flag, enc_low, down_w, slope):
        return run_kernel(
            hidden_body,
            (flag, enc_low, down_w, slope),
            [SMEM] + [ANY] * 3,
            [shape_of(th, bf16)],
            [ANY],
            [(tw, bf16), ((hidden, width), bf16), (th, bf16)],
            1 + row_count + hidden // tile, hidden // tile, "hidden",
        )[0]

    def run_ffn(flag, small_grad, enc_slope):
        small_grad, *pieces = run_kernel(
            ffn_body,
            (flag, small_grad, (h2, enc_slope), (dec_h2, dec_slope)),
            [SMEM, VMEM, ANY, ANY],
            [shape_of(small, f32)] + ffn_piece,
            [VMEM] + [ANY] * count,
            [(th, bf16), (tw, bf16), ((width, hidden), bf16)],
            2 * row_count, hidden // (2 * tile) * share_copies, "ffn",
        )
        return small_grad, pieces

    def run_hidden_back(flag, vec, small_grad, slope, ffn_w, dq, first_w, x1, enc_grad, grad):
        return run_kernel(
            hidden_back_body,
            (flag, vec, small_grad, slope, ffn_w, dq, first_w, x1, enc_grad, grad),
            [SMEM] + [VMEM] * 2 + [ANY] * 7,
            [shape_of(small, f32), shape_of(tw, f32)],
            [VMEM, ANY],
            [
                (th, bf16), ((width, hidden), bf16), (tw, bf16), ((width, width), bf16), (tw, f32),
                (tw, f32), (tw, f32), ((8, width), f32), ((8, width), f32),
            ],
            3 + 3 * row_count, 1, "hidden_back",
        )

    def run_attention_back(flag, grad, qkv, weights, context, out_w, h1):
        grad_qkv, grad_scores, *pieces = run_kernel(
            functools.partial(attention_back_body, heads),
            (flag, grad, qkv, weights, context, out_w, h1),
            [SMEM] + [ANY] * 6,
            [shape_of(wide, bf16), shape_of((heads, length, length), f32)] + mixed_piece,
            [ANY] * (2 + count),
            [
                (tw, f32), (wide, bf16), (square, bf16), (tw, f32), ((width, width), bf16),
                (tw, bf16), (tw, bf16), (tw, bf16), (wide, bf16), ((width, 4 * width), bf16),
                ((heads, length, length), f32), (tw, bf16),
            ],
            2 + 4 * row_count, 2 + 2 * share_copies, "attention_back",
        )
        return grad_qkv, grad_scores, pieces

    def run_last(flag, vec, small_grad, grad, grad_qkv, qkv_w, rows, grad_scores):
        return run_kernel(
            last_body,
            (flag, offsets, vec, small_grad, grad, grad_qkv, qkv_w, rows, grad_scores),
            [SMEM] + [VMEM] * 3 + [ANY] * 5,
            [shape_of(small, f32), shape_of(tw, f32)],
            [VMEM, ANY],
            [
                (tw, f32), (wide, bf16), ((width, 3 * width), bf16), (tw, bf16), (tw, f32),
                ((heads, length, length), f32), ((heads, 2 * length), f32),
                ((bucket_count, 2 * length), f32), ((8, width), f32), ((8, width), f32),
            ],
            5, 1, "last",
        )

    def run_output(flag, vec, dec_u, d2, down_w, low):
        return run_kernel(
            output_body,
            (flag, vec, dec_u, d2, down_w, low),
            [SMEM, VMEM] + [ANY] * 4,
            [shape_of(tw, bf16)],
            [ANY],
            [(th, bf16), (tw, f32), ((hidden, width), bf16), (tw, bf16)],
            1 + 3 * row_count, 1, "output",
        )[0]

    def beside(ring, pieces, kernel, *operands):
        def steps(kept, given, flag, *operands):
            got = ring.to_core(given)
            outs = kernel(flag, *operands)
            out = pair_sum(after(flag, *jax.tree.leaves(outs)), kept, got, ring.everywhere)
            return outs, got, out

        return block_of(always, steps, *pieces, *operands)

    if not by_chip:
        small_grad, enc_grad, enc_low, down_g = run_down(
            flag, vec, small_grad, returned, cot, e2, u, dec_u
        )
        enc_slope = run_hidden(flag, enc_low, down_w, slope)
        small_grad, ffn_g = run_ffn(flag, small_grad, enc_slope)
        small_grad, grad = run_hidden_back(
            flag, vec, small_grad, enc_slope, ffn_w, dq, first_w, x1, enc_grad, grad
        )
        grad_qkv, grad_scores, mixed_g = run_attention_back(
            flag, grad, qkv, weights, context, out_w, h1
        )
        small_grad, result = run_last(
            flag, vec, small_grad, grad, grad_qkv, qkv_w, rows, grad_scores
        )
        low = run_output(flag, vec, dec_u, d2, down_w, low)
        small_grad = lax.psum(small_grad, "batch")
        cross_share, down_share, ffn_share, mixed_share = (
            lax.psum_scatter(pieces[0], "batch", scatter_dimension=0, tiled=True).astype(f32)
            for pieces in (cross_g, down_g, ffn_g, mixed_g)
        )
        cross_back = lax.ppermute(cross_share[:, 2 * width :], "section", [(1, 0)])
        cross_share = jnp.where(on_encoder, cross_back, cross_share[:, : 2 * width])
        cf_share, cs_share = cross_share[:, :width], cross_share[:, width:]
        out_share, qkv_share = mixed_share[:, :width], mixed_share[:, width:]
        vec_share = lax.dynamic_slice_in_dim(
            small_grad[:7], place * (width // devices), width // devices, 1
        )
        fbias_all = small_grad[8 : 8 + hidden // width].reshape(1, hidden)
        fbias_share = lax.dynamic_slice_in_dim(
            fbias_all, place * (hidden // devices), hidden // devices, 1
        )
        table_total = small_grad[16 : 16 + heads, :bucket_count].T
    else:

        def cross_steps(flag, kept, given):
            got = cross.to_core(given)
            return got, pair_sum(flag, kept, got, False)

        got, out = block_of(always, cross_steps, flag, *cross_g)
        flag = after(flag, out)

        def down_steps(out, kept, got, flag, down_w, slope, ffn_ins, *operands):
            far = cross.to_chip(out)
            small_grad, enc_grad, enc_low, pieces = run_down(flag, *operands)
            flag = after(flag, small_grad)
            enc_slope, down_got, out = beside(
                down, pieces, run_hidden, flag, enc_low, down_w, slope
            )
            down_held = (pieces[0], down_got, down.to_chip(out))
            flag = after(flag, out)
            small_grad, pieces = run_ffn(flag, small_grad, enc_slope)
            flag = after(flag, small_grad)
            *outs, cross_own = cross.sums(flag, kept, got, far)
            flag = after(flag, *outs)
            cross_last = (*cross.along(outs), cross_own)
            sums = beside(
                ffn, pieces, run_hidden_back, flag, vec, small_grad, enc_slope, *ffn_ins[:4],
                enc_grad, ffn_ins[4],
            )
            outs = down.sums(after(flag, sums[2]), *down_held)
            return outs, cross_last, pieces[0], sums

        down_outs, cross_last, kept, sums = block_of(
            always, down_steps, out, cross_g[0], got, flag, down_w, slope,
            (ffn_w, dq, first_w, x1, grad), vec, small_grad, returned, cot, e2, u, dec_u,
        )
        (small_grad, grad), got, ffn_out = sums
        ffn_held = (kept, got)
        flag = after(flag, ffn_out, *down_outs)

        def attention_steps(flag, ffn_out, outs, *operands):
            far = ffn.to_chip(ffn_out)
            moved = down.along(outs)
            grad_qkv, grad_scores, pieces = run_attention_back(flag, *operands)

            def swap(flag, kept, given):
                got = mixed.to_core(given)
                return got, pair_sum(flag, kept, got, True)

            swapped = block_of(always, swap, after(flag, grad_qkv), *pieces)
            return moved, far, grad_qkv, grad_scores, pieces[0], swapped

        moved, ffn_far, grad_qkv, grad_scores, kept, swapped = block_of(
            always, attention_steps, flag, ffn_out, down_outs[:3], grad, qkv, weights, context, out_w,
            h1,
        )
        down_last = (*moved, down_outs[3])
        got, out = swapped
        flag = after(flag, out)

        def swapped_small(small_grad, away):
            pairs = [(i, i ^ away) for i in range(devices)]
            return small_grad + lax.ppermute(small_grad, "batch", pairs)

        def last_steps(flag, out, held, mixed_held, *operands):
            far = mixed.to_chip(out)
            *outs, own = ffn.sums(flag, *held)
            moved = (*ffn.along(outs), own)
            small_grad, result = run_last(after(flag, *outs), *operands)

            small_grad = block_of(always, lambda s: swapped_small(s, 1), small_grad)
            outs = mixed.sums(after(flag, small_grad), *mixed_held, far)
            return outs, moved, small_grad, result

        (*outs, own), ffn_last, small_grad, result = block_of(
            always, last_steps, flag, out, (*ffn_held, ffn_far), (kept, got), vec, small_grad,
            grad, grad_qkv, qkv_w, rows, grad_scores,
        )

        moved = mixed.along(outs)

        def end_steps(small_grad, cross_last, down_last, ffn_last, flag, *operands):
            back, cross_share, down_share, ffn_share = [
                sum(part[:, at].astype(f32) for part in parts)
                for parts, at in (
                    (cross_last, slice(2 * width, 4 * width)),
                    (cross_last, slice(0, 2 * width)),
                    (down_last, slice(None)),
                    (ffn_last, slice(None)),
                )
            ]
            back = lax.ppermute(back, "section", [(1, 0)])
            small_grad = swapped_small(small_grad, 2)
            low = run_output(after(flag, small_grad), *operands)
            small_grad = swapped_small(small_grad, 4)
            return small_grad, low, back, cross_share, down_share, ffn_share

        small_grad, low, back, cross_share, down_share, ffn_share = block_of(
            always, end_steps, after(small_grad, *outs), cross_last, down_last, ffn_last, flag, vec,
            dec_u, d2, down_w, low,
        )
        small_other = lax.ppermute(small_grad, "batch", [(i, i ^ 8) for i in range(devices)])
        one = (width // devices, width)
        qkv_share, out_share, cf_share, cs_share = pl.pallas_call(
            finish_body,
            in_specs=[SMEM] + [VMEM] * 6,
            out_specs=[VMEM] * 4,
            out_shape=[shape_of((width // devices, 3 * width), f32)] + [shape_of(one, f32)] * 3,
            name="finish",
        )(flag, *moved, own, cross_share, back)
        small_other = after(small_other, qkv_share)
        vec_share, fbias_share, table_total = pl.pallas_call(
            small_body,
            in_specs=[SMEM] + [VMEM] * 2,
            out_specs=[VMEM] * 3,
            out_shape=[
                shape_of((7, 1, width // devices), f32), shape_of((1, hidden // devices), f32),
                shape_of((heads, 1, bucket_count), f32),
            ],
            name="small",
        )(place[None], small_grad, small_other)
        vec_share = jnp.transpose(vec_share, (1, 0, 2))[0]
        table_total = jnp.transpose(table_total, (1, 2, 0))[0]
    return (
        low.reshape((1, row_count, length, width)),
        result.reshape((1, row_count, length, width)),
        qkv_share[None],
        out_share[None],
        ffn_share[None],
        down_share[None],
        cf_share[None],
        cs_share[None],
        vec_share[None],
        fbias_share,
        table_total[None],
    )


def solution(mesh):
    return jax.shard_map(
        per_device,
        mesh=mesh,
        in_specs=(
            P("section", "batch", None, None),
            P("section", "batch", None, None),
            P(None, "batch", None),
            P(),
            P("section", None, None),
            P("section", None, None),
            P("section", None, None),
            P("section", None, None),
            P("section", None, None),
            P("section", None, None),
            P("section", None, None),
            P("section", None),
            P("section", None, None),
        ),
        out_specs=(
            P("section", "batch", None, None),
            P("section", "batch", None, None),
            P("section", "batch", None),
            P("section", "batch", None),
            P("section", "batch", None),
            P("section", "batch", None),
            P("section", "batch", None),
            P("section", "batch", None),
            P("section", None, "batch"),
            P("section", "batch"),
            P("section", None, None),
        ),
        check_vma=False,
    )
```

```python
import functools

import jax
import jax.numpy as jnp
from jax import lax
from jax.experimental import pallas as pl
from jax.experimental.pallas import tpu as pltpu
from jax.sharding import PartitionSpec as P

norm_epsilon = 1e-05
masked_score = -1e30
half_root = 0.7071067811865476
density_scale = 0.3989422804014327
tile = 768
chunk = 256
rotations = (2, 3, 1)
spare_bytes = 8 * 1024 * 1024
all_bytes = 62 * 1024 * 1024

f32 = jnp.float32
bf16 = jnp.bfloat16
ANY = pl.BlockSpec(memory_space=pl.ANY)
SMEM = pl.BlockSpec(memory_space=pltpu.SMEM)
VMEM = pl.BlockSpec(memory_space=pltpu.VMEM)


def mm(left, right):
    return jnp.dot(left, right, preferred_element_type=f32)


def mm_nt(left, right):
    return lax.dot_general(left, right, (((1,), (1,)), ((), ())), preferred_element_type=f32)


def mm_tn(left, right):
    return lax.dot_general(left, right, (((0,), (0,)), ((), ())), preferred_element_type=f32)


def mean_of(values):
    return jnp.sum(values, axis=-1, keepdims=True) * (1.0 / values.shape[-1])


def normalised(values):
    centre = values - mean_of(values)
    rate = lax.rsqrt(mean_of(centre * centre) + norm_epsilon)
    return centre * rate, rate


def each_rows(count, body):
    @pl.loop(0, count // chunk)
    def _(step):
        body(pl.ds(pl.multiple_of(step * chunk, chunk), chunk))


def each_tile(count, body, width=tile):
    if count == width:
        body(pl.ds(0, width))
        return

    @pl.loop(0, count // width)
    def _(step):
        body(pl.ds(pl.multiple_of(step * width, width), width))


def norm_forward(source, gain, offset, target, also=None):
    def rows(at):
        unit, _ = normalised(source[at, :].astype(f32))
        normed = unit * gain + offset
        target[at, :] = normed.astype(target.dtype)

    each_rows(source.shape[0], rows)


def norm_backward(
    source, grad_normed, gain, upstream, target, gain_sum, offset_sum, low=None
):
    gain_sum[...] = jnp.zeros_like(gain_sum)
    offset_sum[...] = jnp.zeros_like(offset_sum)

    def rows(at):
        unit, rate = normalised(source[at, :].astype(f32))
        upper = grad_normed[at, :]
        product = upper * unit
        gain_sum[...] += jnp.sum(product.reshape(-1, 8, product.shape[1]), axis=0)
        offset_sum[...] += jnp.sum(upper.reshape(-1, 8, upper.shape[1]), axis=0)
        scaled = upper * gain
        inner = mean_of(scaled)
        along = mean_of(product * gain)
        result = rate * (scaled - inner - unit * along)
        if upstream is not None:
            result = result + upstream[at, :].astype(f32)
        target[at, :] = result
        if low is not None:
            low[at, :] = result.astype(bf16)

    each_rows(source.shape[0], rows)


def column_sum(partial):
    return jnp.sum(partial[...], axis=0, keepdims=True)


def lower_lanes(shape):
    return lax.broadcasted_iota(jnp.int32, shape, 1) < shape[1] // 2


def split_pair(block):
    lower = lower_lanes(block.shape)
    zero = jnp.zeros_like(block)
    return jnp.concatenate([jnp.where(lower, block, zero), jnp.where(lower, zero, block)], axis=0)


def join_pair(stacked):
    rows = stacked.shape[0] // 2
    lower = lower_lanes((rows, stacked.shape[1]))
    return jnp.where(lower, stacked[:rows], stacked[rows:])


def attend_pair(queries, key_rows, values, additions, scale):
    length = queries.shape[0]
    scores = mm_nt((queries * scale).astype(bf16), split_pair(key_rows))
    parts = []
    for head in range(2):
        part = scores[:, head * length : (head + 1) * length] + additions[head]
        exponent = jnp.exp(part - jnp.max(part, axis=-1, keepdims=True))
        parts.append(exponent * (1.0 / jnp.sum(exponent, axis=-1, keepdims=True)))
    weights = jnp.concatenate(parts, axis=1).astype(bf16)
    return weights, mm(weights, split_pair(values))


def attend_pair_back(weights, queries, key_rows, values, context, grad_context, scale):
    length = queries.shape[0]
    grad_weights = mm_nt(grad_context, split_pair(values))
    product = grad_context.astype(f32) * context.astype(f32)
    lower = lower_lanes(product.shape)
    parts = []
    for head in range(2):
        at = slice(head * length, (head + 1) * length)
        own = jnp.where(lower, product, 0.0) if head == 0 else jnp.where(lower, 0.0, product)
        centred = jnp.sum(own, axis=-1, keepdims=True)
        parts.append(weights[:, at].astype(f32) * (grad_weights[:, at] - centred))
    grad_raw = jnp.concatenate(parts, axis=1).astype(bf16)
    grad_queries = mm(grad_raw, split_pair(key_rows)) * scale
    grad_keys = join_pair(mm_tn(grad_raw, queries)) * scale
    grad_values = join_pair(mm_tn(weights, grad_context))
    return grad_queries, grad_keys, grad_values, parts


def same_sentence(query_ids, key_ids):
    length = query_ids.shape[1]
    across = jnp.broadcast_to(key_ids.astype(f32), (length, length))
    down = jnp.broadcast_to(query_ids.astype(f32), (length, length)).T
    return across == down


class Move:
    def __init__(self, sources, target, semaphores):
        self.sources, self.target, self.semaphores = sources, target, semaphores

    def copies(self, sources):
        if not isinstance(sources, tuple):
            yield pltpu.make_async_copy(sources, self.target, self.semaphores[0])
            return
        rows = self.target.shape[0] // len(sources)
        for part, source in enumerate(sources):
            target = self.target.at[pl.ds(part * rows, rows)]
            yield pltpu.make_async_copy(source, target, self.semaphores[part])

    def start(self, sources=None):
        for copy in self.copies(self.sources if sources is None else sources):
            copy.start()

    def wait(self, sources=None):
        for copy in self.copies(self.sources if sources is None else sources):
            copy.wait()


class Mover:
    def __init__(self, semaphores):
        self.semaphores = semaphores
        self.used = 0

    def note(self, source, target):
        count = len(source) if isinstance(source, tuple) else 1
        semaphores = [self.semaphores.at[self.used + part] for part in range(count)]
        self.used += count
        return Move(source, target, semaphores)

    def start(self, source, target):
        move = self.note(source, target)
        move.start()
        return move


def wait_all(moves):
    for move in moves:
        move.wait()


def gelu_parts(hidden):
    share = 0.5 + 0.5 * lax.erf(hidden * half_root)
    slope = share + hidden * (density_scale * jnp.exp(hidden * hidden * -0.5))
    return hidden * share, slope


def feed_forward(normed, ffn_w, in_bias, ahead, use):
    tiles = spans(ffn_w.shape[1], tile)
    ahead[0] = mm(normed[...], ffn_w[:, tiles[0]])
    for step, at in enumerate(tiles):
        if step + 1 < len(tiles):
            ahead[(step + 1) % 2] = mm(normed[...], ffn_w[:, tiles[step + 1]])
        use(at, ahead[step % 2] + in_bias[:, at])


def first_body(
    heads, row, flag, ids, offsets, table, vectors, in_bias, rows_in, cot_in, qkv_in, out_in, ffn_in,
    down_in, first_in,
    x1_out, h1_out, qkv_out, weights_out, context_out, h2_out, u_out, slope_out, e2_out, low_out,
    hc_out, qc_out,
    rows, qkv_w, out_w, ffn_w, down_w, first_w, cot, normed, qkv, weights, context, x1, h2, u, slope,
    e2, low, bias_rows, mask, context_wide, ahead, loads, stores,
):
    length, width = rows.shape
    hidden_width = ffn_w.shape[1]
    on_encoder = flag[0] == 1
    own_rows = pl.ds(row * length, length)
    load = Mover(loads)
    store = Mover(stores)
    got_rows = load.start(rows_in.at[own_rows], rows)
    got_qkv = load.start(qkv_in, qkv_w)
    got_out = load.start(out_in, out_w)
    got_down = load.note(down_in, down_w)
    got_ffn = load.note(ffn_in, ffn_w)
    got_first = load.note(first_in, first_w)
    got_cot = load.note(cot_in.at[own_rows], cot)

    @pl.when(on_encoder)
    def _():
        got_ffn.start()
        got_down.start()

    @pl.when(jnp.logical_not(on_encoder))
    def _():
        got_first.start()
        got_cot.start()
        got_down.start()

    one_hot = (offsets[...] == lax.broadcasted_iota(jnp.int32, (table.shape[1], 2 * length), 0)).astype(f32)
    by_offset = lax.dot_general(
        table[...], one_hot, (((1,), (0,)), ((), ())), precision=lax.Precision.HIGHEST,
        preferred_element_type=f32,
    )
    bias_rows[...] = pltpu.roll(by_offset, length + 1, 1)
    own_group = jnp.where(on_encoder, 0, 1)
    causal = lax.broadcasted_iota(jnp.int32, (length, length), 0) >= lax.broadcasted_iota(
        jnp.int32, (length, length), 1
    )
    own = ids[pl.ds(own_group, 1), row, :]
    allowed = same_sentence(own, own) & (causal | on_encoder)
    mask[...] = jnp.where(allowed, 0.0, masked_score)

    got_rows.wait()
    norm_forward(rows, vectors[0], vectors[1], normed)
    got_qkv.wait()

    def project(at):
        qkv[:, at] = mm(normed[...], qkv_w[:, at]).astype(bf16)

    each_tile(3 * width, project)
    out_copies = [store.start(normed, h1_out), store.start(qkv, qkv_out)]
    scale = (width // heads) ** (-0.5)

    @pl.loop(0, heads // 2, unroll=heads // 2)
    def _(pair):
        lanes = pl.multiple_of(pair * 128, 128)
        additions = []
        for head in range(2):
            spread = jnp.broadcast_to(bias_rows[pl.ds(pair * 2 + head, 1), :], (length, 2 * length))
            skewed = pltpu.roll(spread, 0, 1, stride=1, stride_axis=0)
            additions.append(skewed[:, :length] + mask[...])
        part, mixed = attend_pair(
            qkv[:, pl.ds(lanes, 128)],
            qkv[:, pl.ds(width + lanes, 128)],
            qkv[:, pl.ds(2 * width + lanes, 128)],
            additions,
            scale,
        )
        weights[0, pair] = part
        context_wide[:, pl.ds(lanes, 128)] = mixed
        context[:, pl.ds(lanes, 128)] = mixed.astype(bf16)

    out_copies += [store.start(weights, weights_out), store.start(context_wide, context_out)]
    got_out.wait()
    x1[...] = rows[...].astype(f32) + mm(context[...], out_w[...])
    out_copies.append(store.start(x1, x1_out))

    @pl.when(on_encoder)
    def _():
        norm_forward(x1, vectors[2], vectors[3], h2)
        got_ffn.wait()

        def feed(at, hidden):
            value, rate = gelu_parts(hidden)
            u[:, at] = value.astype(bf16)
            slope[:, at] = rate.astype(bf16)

        feed_forward(h2, ffn_w, in_bias, ahead, feed)
        copies = [store.start(h2, h2_out), store.start(u, u_out), store.start(slope, slope_out)]
        got_down.wait()
        e2[...] = x1[...] + (mm(u[...], down_w[...]) + vectors[6])
        copies.append(store.start(e2, e2_out))
        norm_forward(e2, vectors[4], vectors[5], low)
        copies.append(store.start(low, low_out))
        wait_all(copies)

    @pl.when(jnp.logical_not(on_encoder))
    def _():
        norm_forward(x1, vectors[2], vectors[3], h2)
        got_first.wait()
        low[...] = mm(h2[...], first_w[...]).astype(bf16)
        copies = [store.start(h2, hc_out), store.start(low, qc_out)]
        got_down.wait()
        got_cot.wait()

        def back(at):
            slope[:, at] = mm_nt(cot[...], down_w[at, :]).astype(bf16)

        each_tile(hidden_width, back)
        copies.append(store.start(slope, slope_out))
        wait_all(copies)

    wait_all(out_copies)


def cross_body(
    heads, row, flag, ids, vectors, in_bias, small_in,
    memory_in, sent_in, other_in, second_in, x1_in, qc_in, cot_in, ffn_in, slope_in, earlier,
    small_out, h2_out, u_out, slope_out, d2_out, grad_out, cc_out, dq_out, dk_out, dv_out, dm_out,
    low_out, pieces, memory, keys_w, values_w, second_w, x1, qc, cot, ffn_w, keys, values, weights, cc, d2, h2, u,
    slope, grad_normed, grad, grad_low, dq, dk, dv, dm, mask, gain_sum, offset_sum, cc_wide, ahead, *rest
):
    *products, loads, stores = rest
    length, width = memory.shape
    small_out[...] = jnp.zeros_like(small_out) if row == 0 else small_in[...]

    @pl.when(flag[0] == 0)
    def _():
        load = Mover(loads)
        store = Mover(stores)
        got_memory = load.start(memory_in, memory)
        got_keys = load.note(sent_in, keys_w)
        got_values = load.note(sent_in, values_w)
        for core, (keys_in, values_in) in enumerate(((sent_in, other_in), (other_in, sent_in))):

            @pl.when(flag[1] == core)
            def _(keys_in=keys_in, values_in=values_in):
                got_keys.start(keys_in)
                got_values.start(values_in)

        got_query = load.start(qc_in, qc)
        got_second = [load.start(second_in, second_w), load.start(x1_in, x1)]
        got_ffn = [load.start(ffn_in, ffn_w), load.start(slope_in, slope)]
        got_cot = load.start(cot_in.at[pl.ds(row * length, length)], cot)
        if products:
            got_earlier = []
            for sources, whole in zip(earlier, products):
                if not sources:
                    continue
                rows = len(sources) * length
                got_earlier.append(load.start(tuple(sources), whole.at[pl.ds(0, rows)]))
        mask[...] = jnp.where(same_sentence(ids[1:2, row, :], ids[0:1, row, :]), 0.0, masked_score)
        got_memory.wait()
        got_keys.wait()
        keys[...] = mm(memory[...], keys_w[...]).astype(bf16)
        got_values.wait()
        values[...] = mm(memory[...], values_w[...]).astype(bf16)
        got_query.wait()
        scale = (width // heads) ** (-0.5)

        @pl.loop(0, heads // 2, unroll=3)
        def _(pair):
            lanes = pl.ds(pl.multiple_of(pair * 128, 128), 128)
            part, mixed = attend_pair(
                qc[:, lanes], keys[:, lanes], values[:, lanes], [mask[...], mask[...]], scale
            )
            weights[0, pair] = part
            cc_wide[:, lanes] = mixed
            cc[:, lanes] = mixed.astype(bf16)

        copies = [store.start(cc, cc_out)]
        wait_all(got_second)
        d2[...] = x1[...] + mm(cc[...], second_w[...])
        copies.append(store.start(d2, d2_out))
        norm_forward(d2, vectors[4], vectors[5], h2)
        copies.append(store.start(h2, h2_out))
        wait_all(got_ffn)

        def feed(at, hidden):
            value, rate = gelu_parts(hidden)
            u[:, at] = value.astype(bf16)
            slope[:, at] = (slope[:, at].astype(f32) * rate).astype(bf16)

        feed_forward(h2, ffn_w, in_bias, ahead, feed)
        copies += [store.start(u, u_out), store.start(slope, slope_out)]
        grad_normed[...] = mm_nt(slope[...], ffn_w[...])
        got_cot.wait()
        norm_backward(
            d2, grad_normed, vectors[4], cot, grad, gain_sum, offset_sum, grad_low
        )
        small_out[4:5, :] += column_sum(gain_sum)
        small_out[5:6, :] += column_sum(offset_sum)
        copies += [store.start(grad, grad_out), store.start(grad_low, low_out)]
        dm[...] = mm_nt(grad_low[...], second_w[...]).astype(bf16)

        @pl.loop(0, heads // 2, unroll=3)
        def _(pair):
            lanes = pl.ds(pl.multiple_of(pair * 128, 128), 128)
            grad_q, grad_k, grad_v, _ = attend_pair_back(
                weights[0, pair], qc[:, lanes], keys[:, lanes], values[:, lanes], cc_wide[:, lanes],
                dm[:, lanes], scale,
            )
            dq[:, lanes] = grad_q.astype(bf16)
            dk[:, lanes] = grad_k.astype(bf16)
            dv[:, lanes] = grad_v.astype(bf16)

        copies += [store.start(dq, dq_out), store.start(dk, dk_out), store.start(dv, dv_out)]
        dm[...] = (mm_nt(dk[...], keys_w[...]) + mm_nt(dv[...], values_w[...])).astype(bf16)
        copies.append(store.start(dm, dm_out))
        if products:
            *wholes, cross_g = products
            hc, *others = wholes
            own = pl.ds(hc.shape[0] - length, length)
            for whole, part in zip(others, (dq, cc, grad_low, memory, dk, dv)):
                whole[own, :] = part[...]
            wait_all(got_earlier)
            hc, dq_all, cc_all, low_all, memory_all, dk_all, dv_all = wholes
            query, out, key, value = spans(4 * width, width)
            cross_g[:, query] = mm_tn(hc[...], dq_all[...]).astype(bf16)
            cross_g[:, out] = mm_tn(cc_all[...], low_all[...]).astype(bf16)
            copies += put_columns(store, cross_g, pieces, flag[1], pl.ds(0, 2 * width))
            cross_g[:, key] = mm_tn(memory_all[...], dk_all[...]).astype(bf16)
            cross_g[:, value] = mm_tn(memory_all[...], dv_all[...]).astype(bf16)
            copies += put_columns(store, cross_g, pieces, flag[1], pl.ds(2 * width, 2 * width))
        wait_all(copies)


def put_rows(store, stage, targets, core, rows):
    if len(targets) == 1:
        return [store.start(stage.at[rows], targets[0].at[rows])]
    depth = targets[0].shape[1]
    copies = []
    for chip in range(rows.start // (2 * depth), (rows.start + rows.size) // (2 * depth)):
        for target, which in zip(targets, (core, 1 - core)):
            at = pl.multiple_of((2 * chip + which) * depth, depth)
            copies.append(store.start(stage.at[pl.ds(at, depth)], target.at[chip]))
    return copies


def put_columns(store, stage, targets, core, columns):
    if len(targets) == 1:
        return [store.start(stage.at[:, columns], targets[0].at[:, columns])]
    chips, depth = targets[0].shape[0], targets[0].shape[1]
    copies = []
    for chip in range(chips):
        for target, which in zip(targets, (core, 1 - core)):
            at = pl.multiple_of((2 * chip + which) * depth, depth)
            copies.append(
                store.start(stage.at[pl.ds(at, depth), columns], target.at[chip, :, columns])
            )
    return copies


def spans(count, width):
    return [pl.ds(start, width) for start in range(0, count, width)]


def down_body(flag, vectors, small_in, dm_in, cot_in, e2_in, enc_u_in, dec_u_in, *rest):
    small_out, grad_out, low_out, *rest = rest
    count = len(rest) - 11
    outs = rest[:count]
    dm, cot, e2, u, grad, grad_low, down_g, gain_sum, offset_sum, loads, stores = rest[count:]
    hidden_width, width = u.shape[1], cot.shape[1]
    small_out[...] = small_in[...]
    load = Mover(loads)
    store = Mover(stores)
    got_cot = load.start(cot_in, cot)
    got_u = load.note(enc_u_in, u)
    moved = [load.note(dm_in, dm), load.note(e2_in, e2)]
    kept = [store.note(grad, grad_out), store.note(grad_low, low_out)]

    @pl.when(flag[0] == 1)
    def _():
        for copy in moved:
            copy.start()
        got_cot.wait()
        wait_all(moved)
        got_u.start(enc_u_in)

        def total(at):
            grad[at, :] = dm[at, :].astype(f32) + cot[at, :].astype(f32)

        each_rows(grad.shape[0], total)
        norm_backward(e2, grad, vectors[4], None, grad, gain_sum, offset_sum, grad_low)
        small_out[4:5, :] = column_sum(gain_sum)
        small_out[5:6, :] = column_sum(offset_sum)
        for copy in kept:
            copy.start()

    @pl.when(flag[0] == 0)
    def _():
        got_u.start(dec_u_in)
        got_cot.wait()
        grad_low[...] = cot[...]

    got_u.wait()
    copies = []
    for rows in spans(hidden_width, tile):
        down_g[rows, :] = mm_tn(u[:, rows], grad_low[...]).astype(bf16)
        copies += put_rows(store, down_g, outs, flag[1], rows)
    small_out[6:7, :] = jnp.sum(grad_low[...].astype(f32), axis=0, keepdims=True)
    wait_all(copies)

    @pl.when(flag[0] == 1)
    def _():
        wait_all(kept)


def hidden_body(flag, low_in, down_in, slope_in, slope_out, grad_low, down_w, slope, loads, stores):
    @pl.when(flag[0] == 1)
    def _():
        load = Mover(loads)
        store = Mover(stores)
        hidden_width = slope.shape[1]
        got_low = load.start(low_in, grad_low)
        got_slope = load.start(slope_in, slope)
        got_down = [
            load.start(down_in.at[rows], down_w.at[rows]) for rows in spans(hidden_width, tile)
        ]
        got_low.wait()
        got_slope.wait()
        copies = []
        for at, got in zip(spans(hidden_width, tile), got_down):
            got.wait()
            part = mm_nt(grad_low[...], down_w[at, :]) * slope[:, at].astype(f32)
            slope[:, at] = part.astype(bf16)
            copies.append(store.start(slope.at[:, at], slope_out.at[:, at]))
        wait_all(copies)


def ffn_body(flag, small_in, enc_ins, dec_ins, *rest):
    small_out, *rest = rest
    count = len(rest) - 5
    outs = rest[:count]
    slope, h2, ffn_g, loads, stores = rest[count:]
    width, hidden_width = h2.shape[1], slope.shape[1]
    small_out[...] = small_in[...]
    load = Mover(loads)
    store = Mover(stores)
    moves = [load.note(source, target) for source, target in zip(dec_ins, (h2, slope))]
    for which, ins in enumerate((dec_ins, enc_ins)):

        @pl.when(flag[0] == which)
        def _(ins=ins):
            for move, source in zip(moves, ins):
                move.start(source)
            for move, source in zip(moves, ins):
                move.wait(source)

    copies = []
    for step, at in enumerate(spans(hidden_width, tile)):
        ffn_g[:, at] = mm_tn(h2[...], slope[:, at]).astype(bf16)
        if step % 2 == 1:
            both = pl.ds(at.start - tile, 2 * tile)
            copies += put_columns(store, ffn_g, outs, flag[1], both)
    for part in range(hidden_width // width):
        values = slope[:, part * width : (part + 1) * width].astype(f32)
        small_out[8 + part : 9 + part, :] = jnp.sum(values, axis=0, keepdims=True)
    wait_all(copies)


def hidden_back_body(
    flag, vectors, small_in, slope_in, ffn_in, dq_in, first_in, x1_in, enc_grad_in, dec_grad_in,
    small_out, grad_out,
    slope, ffn_w, dq, first_w, x1, grad, grad_normed, gain_sum, offset_sum, loads, stores,
):
    width = x1.shape[1]
    small_out[...] = small_in[...]
    load = Mover(loads)
    store = Mover(stores)
    got_x1 = load.note(x1_in, x1)
    got_grad = load.note(dec_grad_in, grad)

    @pl.when(flag[0] == 1)
    def _():
        got = [load.start(slope_in, slope), load.start(ffn_in, ffn_w)]
        got_x1.start()
        got_grad.start(enc_grad_in)
        wait_all(got)
        grad_normed[...] = mm_nt(slope[...], ffn_w[...])
        got_grad.wait(enc_grad_in)

    @pl.when(flag[0] == 0)
    def _():
        got = [load.start(dq_in, dq), load.start(first_in, first_w)]
        got_x1.start()
        got_grad.start(dec_grad_in)
        wait_all(got)
        grad_normed[...] = mm_nt(dq[...], first_w[...])
        got_grad.wait()

    got_x1.wait()
    norm_backward(x1, grad_normed, vectors[2], grad, grad, gain_sum, offset_sum)
    stored = store.start(grad, grad_out)
    small_out[2:3, :] = column_sum(gain_sum)
    small_out[3:4, :] = column_sum(offset_sum)
    stored.wait()


def attention_back_body(
    heads, flag, grad_in, qkv_in, weights_in, context_in, outw_in, h1_in, *rest
):
    grad_qkv_out, scores_out, *rest = rest
    count = len(rest) - 14
    outs = rest[:count]
    (
        grad, qkv, weights, context, out_w, h1, grad_low, grad_context, grad_qkv, mixed_g,
        grad_scores, context_low, loads, stores,
    ) = rest[count:]
    width = context.shape[1]
    row_count, length = weights.shape[0], weights.shape[2]
    load = Mover(loads)
    store = Mover(stores)
    got_grad = [load.start(grad_in, grad), load.start(outw_in, out_w)]
    got_context = load.start(context_in, context)
    got_attention = [load.start(weights_in, weights), load.start(qkv_in, qkv)]
    got_h1 = load.start(h1_in, h1)
    wait_all(got_grad)

    def lower(at):
        grad_low[at, :] = grad[at, :].astype(bf16)

    each_rows(grad.shape[0], lower)
    grad_context[...] = mm_nt(grad_low[...], out_w[...]).astype(bf16)
    got_context.wait()
    context_low[...] = context[...].astype(bf16)
    mixed_g[:, pl.ds(0, width)] = mm_tn(context_low[...], grad_low[...]).astype(bf16)
    wait_all(got_attention)
    scale = (width // heads) ** (-0.5)

    @pl.loop(0, heads // 2, unroll=6)
    def _(pair):
        lanes = pl.multiple_of(pair * 128, 128)
        totals = [None, None]
        for row in range(row_count):
            at = slice(row * length, (row + 1) * length)
            grad_q, grad_k, grad_v, parts = attend_pair_back(
                weights[row, pair],
                qkv[at, pl.ds(lanes, 128)],
                qkv[at, pl.ds(width + lanes, 128)],
                qkv[at, pl.ds(2 * width + lanes, 128)],
                context[at, pl.ds(lanes, 128)],
                grad_context[at, pl.ds(lanes, 128)],
                scale,
            )
            grad_qkv[at, pl.ds(lanes, 128)] = grad_q.astype(bf16)
            grad_qkv[at, pl.ds(width + lanes, 128)] = grad_k.astype(bf16)
            grad_qkv[at, pl.ds(2 * width + lanes, 128)] = grad_v.astype(bf16)
            totals = [p if t is None else t + p for t, p in zip(totals, parts)]
        for head in range(2):
            grad_scores[pair * 2 + head] = totals[head]

    got_h1.wait()
    copies = [store.start(grad_qkv, grad_qkv_out), store.start(grad_scores, scores_out)]
    for step, at in enumerate(spans(3 * width, width)):
        mixed_g[:, pl.ds(width + at.start, width)] = mm_tn(h1[...], grad_qkv[:, at]).astype(bf16)
        if step != 1:
            both = pl.ds(0 if step == 0 else 2 * width, 2 * width)
            copies += put_columns(store, mixed_g, outs, flag[1], both)
    wait_all(copies)


def sum_diagonals(grid):
    length = grid.shape[0]
    padded = jnp.concatenate([grid, jnp.zeros((length, length), f32)], axis=1)
    folded = padded[0:8, :]
    for block in range(1, length // 8):
        folded = folded + pltpu.roll(
            padded[block * 8 : (block + 1) * 8, :], 2 * length - block * 8, 1
        )
    line = folded[0:1, :]
    for sub in range(1, 8):
        line = line + pltpu.roll(folded[sub : sub + 1, :], 2 * length - sub, 1)
    return pltpu.roll(line, length - 1, 1)


def last_body(
    flag, offsets, vectors, small_in, grad_in, grad_qkv_in, qkvw_in, rows_in, scores_in,
    small_out, result_out,
    grad, grad_qkv, qkv_w, rows, grad_normed, grad_scores, diagonals, one_hot, gain_sum, offset_sum,
    loads, stores,
):
    small_out[...] = small_in[...]
    heads, bucket_count = grad_scores.shape[0], one_hot.shape[0]
    load = Mover(loads)
    store = Mover(stores)
    got = [load.start(grad_qkv_in, grad_qkv), load.start(qkvw_in, qkv_w)]
    got_rows = [load.start(rows_in, rows), load.start(grad_in, grad)]
    got_scores = load.start(scores_in, grad_scores)
    wait_all(got)
    grad_normed[...] = mm_nt(grad_qkv[...], qkv_w[...])
    wait_all(got_rows)
    norm_backward(rows, grad_normed, vectors[0], grad, grad, gain_sum, offset_sum)
    small_out[0:1, :] = column_sum(gain_sum)
    small_out[1:2, :] = column_sum(offset_sum)
    stored = store.start(grad, result_out)

    got_scores.wait()

    @pl.loop(0, heads)
    def _(head):
        diagonals[pl.ds(head, 1), :] = sum_diagonals(grad_scores[head])

    one_hot[...] = (offsets[...] == lax.broadcasted_iota(jnp.int32, one_hot.shape, 0)).astype(f32)
    small_out[pl.ds(16, heads), pl.ds(0, bucket_count)] = lax.dot_general(
        diagonals[...], one_hot[...], (((1,), (1,)), ((), ())), precision=lax.Precision.HIGHEST,
        preferred_element_type=f32,
    )
    stored.wait()


def output_body(
    flag, vectors, u_in, d2_in, down_in, low_in, low_out, u, d2, down_w, low, loads, stores
):
    load = Mover(loads)
    stored = Mover(stores).note(low, low_out)
    got_low = load.note(low_in, low)

    @pl.when(flag[0] == 1)
    def _():
        got_low.start()
        got_low.wait()
        stored.start()

    @pl.when(flag[0] == 0)
    def _():
        wait_all([load.start(u_in, u), load.start(d2_in, d2), load.start(down_in, down_w)])
        value = d2[...] + (mm(u[...], down_w[...]) + vectors[6])
        low[...] = value.astype(bf16)
        stored.start()

    stored.wait()


def pair_sum_body(everywhere, flag, kept_in, got_in, out, kept, got, total, loads, stores):
    @pl.when(jnp.logical_or(flag[0] == 0, everywhere))
    def _():
        load = Mover(loads)
        store = Mover(stores)
        blocks = out.shape[0]
        ready = []
        for step in range(blocks):
            block = 2 * step + 1 - flag[2]
            ready.append(
                (load.start(kept_in.at[block], kept.at[step]), load.start(got_in.at[block], got.at[step]))
            )
        copies = []
        for step in range(blocks):
            wait_all(ready[step])
            total[step] = (kept[step].astype(f32) + got[step].astype(f32)).astype(bf16)
            copies.append(store.start(total.at[step], out.at[step]))
        wait_all(copies)


def pair_sum(flag, kept, got, everywhere):
    chips, depth, width = kept.shape
    part = (chips // 2, depth, width)
    return run_kernel(
        functools.partial(pair_sum_body, everywhere),
        (flag, kept, got),
        [SMEM, ANY, ANY],
        [shape_of(part, bf16)],
        [ANY],
        [(part, bf16)] * 3,
        chips, chips // 2, "pair_sum",
    )[0]


def chip_sum_body(
    everywhere, flag, kept_in, got_in, far_in, first_out, second_out, third_out, own_out,
    kept, got, far, total, own, loads, stores,
):
    @pl.when(jnp.logical_or(flag[0] == 0, everywhere))
    def _():
        load = Mover(loads)
        store = Mover(stores)
        ready = []
        for step, away in enumerate((*rotations, 0)):
            place = lax.rem(flag[3] + away, 4)
            block = 2 * place + flag[2]
            ready.append(
                [
                    load.start(kept_in.at[block], kept.at[step]),
                    load.start(got_in.at[block], got.at[step]),
                    load.start(far_in.at[place], far.at[step]),
                ]
            )
        copies = []
        for step, out in enumerate((first_out, second_out, third_out, own_out)):
            wait_all(ready[step])
            value = kept[step].astype(f32) + got[step].astype(f32) + far[step].astype(f32)
            if step < 3:
                total[step] = value.astype(bf16)
                copies.append(store.start(total.at[step], out))
            else:
                own[...] = value
                copies.append(store.start(own, out))
        wait_all(copies)


def chip_sum(flag, kept, got, far, everywhere):
    _, depth, width = kept.shape
    one = (depth, width)
    return run_kernel(
        functools.partial(chip_sum_body, everywhere),
        (flag, kept, got, far),
        [SMEM, ANY, ANY, ANY],
        [shape_of(one, bf16)] * 3 + [shape_of(one, f32)],
        [ANY] * 4,
        [((4,) + one, bf16)] * 3 + [((3,) + one, bf16), (one, f32)],
        12, 4, "chip_sum",
    )


def pick_body(flag, first_in, second_in, out, held, loads, stores):
    @pl.when(flag[0] == 1)
    def _():
        got = Mover(loads).note(first_in, held)
        for core, source in enumerate((first_in, second_in)):

            @pl.when(flag[1] == core)
            def _(source=source):
                got.start(source)

        got.wait()
        Mover(stores).start(held, out).wait()


def finish_body(
    flag, first, second, third, own, cross, back, qkv_out, out_out, cf_out, cs_out
):
    width = out_out.shape[1]
    total = own[...]
    for part in (first, second, third):
        total = total + part[...].astype(f32)
    out_out[...] = total[:, :width]
    qkv_out[...] = total[:, width:]
    chosen = jnp.where(flag[0] == 1, back[...], cross[...])
    cf_out[...] = chosen[:, :width]
    cs_out[...] = chosen[:, width:]


def small_body(place, mine, other, vec_out, fbias_out, table_out):
    small = mine[...] + other[...]
    width = small.shape[1]
    share = vec_out.shape[2]
    turned = pltpu.roll(small[0:8, :], lax.rem(width - place[0] * share, width), 1)
    for row in range(vec_out.shape[0]):
        vec_out[row] = turned[row : row + 1, :share]
    share = fbias_out.shape[1]
    per_row = width // share
    row = mine[pl.ds(8 + lax.div(place[0], per_row), 1), :]
    row = row + other[pl.ds(8 + lax.div(place[0], per_row), 1), :]
    turned = pltpu.roll(row, lax.rem(width - lax.rem(place[0], per_row) * share, width), 1)
    fbias_out[...] = turned[:, :share]
    for head in range(table_out.shape[0]):
        table_out[head] = small[16 + head : 17 + head, : table_out.shape[2]]


def shape_of(dims, dtype):
    return jax.ShapeDtypeStruct(tuple(dims), dtype)


def size_of(dims, dtype):
    total = jnp.dtype(dtype).itemsize
    for dim in dims:
        total *= dim
    return total


def run_kernel(
    body, operands, places, outs, out_places, scratch, loads, stores, name, alone=False
):
    held = sum(size_of(dims, dtype) for dims, dtype in scratch)
    flat, form = jax.tree.flatten(operands)
    flat_places = [
        place for place, operand in zip(places, operands, strict=True) for _ in jax.tree.leaves(operand)
    ]

    flat_outs, out_form = jax.tree.flatten(outs)
    held_at = len(flat) + len(flat_outs)

    def kernel(*refs):
        results = out_form.unflatten(refs[len(flat) : held_at])
        return body(*form.unflatten(refs[: len(flat)]), *results, *refs[held_at:])

    results = pl.pallas_call(
        kernel,
        in_specs=flat_places,
        out_specs=out_places,
        out_shape=flat_outs,
        scratch_shapes=[pltpu.VMEM(dims, dtype) for dims, dtype in scratch]
        + [pltpu.SemaphoreType.DMA((loads,)), pltpu.SemaphoreType.DMA((stores,))],
        compiler_params=pltpu.CompilerParams(
            vmem_limit_bytes=all_bytes
        ),
        cost_estimate=pl.CostEstimate(flops=1, bytes_accessed=1, transcendentals=0),
        name=name,
    )(*flat)
    return out_form.unflatten(results)


def after(value, *others):
    return lax.optimization_barrier((value,) + others)[0]


def block_of(always, steps, *operands):
    shapes = jax.eval_shape(steps, *operands)

    def blank(*_):
        return jax.tree.map(lambda leaf: jnp.zeros(leaf.shape, leaf.dtype), shapes)

    return lax.cond(always, steps, blank, *operands)


class Ring:
    def __init__(self, devices, everywhere):
        self.devices = devices
        self.everywhere = everywhere

    def send(self, shard, moved):
        pairs = [(i, moved(i)) for i in range(self.devices)]
        if self.everywhere:
            return lax.ppermute(shard, "batch", pairs)
        pairs = [(self.devices + i, self.devices + j) for i, j in pairs]
        return lax.ppermute(shard, ("section", "batch"), pairs)

    def to_core(self, given):
        return self.send(given, lambda i: i ^ 1)

    def to_chip(self, out):
        return self.send(out, lambda i: i ^ 2)

    def sums(self, flag, *held):
        return chip_sum(flag, *held, self.everywhere)

    def along(self, outs):
        return [
            self.send(out, lambda i, away=away: (i + 4 * away) % 16)
            for away, out in zip(rotations, outs)
        ]


def per_device(
    inputs, cotangent, segments, buckets, qkv_weight, out_weight, in_weight, down_weight,
    cross_first, cross_second, vectors, ffn_bias, position_table,
):
    row_count, length, width = inputs.shape[1:]
    heads = position_table.shape[2]
    bucket_count = position_table.shape[1]
    hidden = in_weight.shape[2]
    tokens = row_count * length
    pairs = heads // 2
    on_encoder = lax.axis_index("section") == 0
    place = lax.axis_index("batch")
    core = lax.rem(place, 2)
    devices = lax.axis_size("batch")
    by_chip = devices == 16
    always = place < devices
    flag = jnp.stack(
        [on_encoder.astype(jnp.int32), core, lax.rem(lax.div(place, 2), 2), lax.div(place, 4)]
    )
    offsets = jnp.pad(buckets, (0, 1), constant_values=-1)[None]
    table = jnp.transpose(position_table, (2, 0, 1))[:, 0]
    rows = inputs.reshape(tokens, width)
    cot = cotangent.reshape(tokens, width)
    qkv_w, out_w, ffn_w, down_w = qkv_weight[0], out_weight[0], in_weight[0], down_weight[0]
    first_w, second_w = cross_first[0], cross_second[0]
    vec = jnp.transpose(vectors, (1, 0, 2))
    fbias = ffn_bias

    tw, th = (tokens, width), (tokens, hidden)
    wide = (tokens, 3 * width)
    square = (row_count, pairs, length, 2 * length)
    row_tw, row_th, row_wide = (length, width), (length, hidden), (length, 3 * width)
    row_square = (1, pairs, length, 2 * length)
    small = (32, width)

    (picked,) = run_kernel(
        pick_body, (flag, first_w, second_w), [SMEM, ANY, ANY], [shape_of((width, width), bf16)],
        [ANY], [((width, width), bf16)], 1, 1, "pick",
    )
    sent = lax.ppermute(picked, "section", [(0, 1)])
    flag = after(flag, picked)

    def piece(depth_rows, columns):
        if not by_chip:
            return [shape_of((depth_rows, columns), bf16)]
        return [shape_of((devices // 2, depth_rows // devices, columns), bf16)] * 2

    down_piece, ffn_piece = piece(hidden, width), piece(width, hidden)
    mixed_piece = piece(width, 4 * width)
    count = len(down_piece)
    share_copies = devices if by_chip else 1
    def run_first(row, flag):
        return run_kernel(
            functools.partial(first_body, heads, row),
            (flag, segments, offsets, table, vec, fbias, rows, cot, qkv_w, out_w, ffn_w,
             down_w, first_w),
            [SMEM] + [VMEM] * 5 + [ANY] * 7,
            [
                shape_of(row_tw, f32), shape_of(row_tw, bf16), shape_of(row_wide, bf16),
                shape_of(row_square, bf16), shape_of(row_tw, f32), shape_of(row_tw, bf16),
                shape_of(row_th, bf16), shape_of(row_th, bf16), shape_of(row_tw, f32),
                shape_of(row_tw, bf16), shape_of(row_tw, bf16), shape_of(row_tw, bf16),
            ],
            [ANY] * 12,
            [
                (row_tw, bf16), ((width, 3 * width), bf16), ((width, width), bf16),
                ((width, hidden), bf16), ((hidden, width), bf16), ((width, width), bf16),
                (row_tw, bf16), (row_tw, bf16), (row_wide, bf16), (row_square, bf16), (row_tw, bf16),
                (row_tw, f32), (row_tw, bf16), (row_th, bf16), (row_th, bf16), (row_tw, f32),
                (row_tw, bf16), ((heads, 2 * length), f32), ((length, length), f32),
                (row_tw, f32), ((2, length, tile), f32),
            ],
            7, 13, "first", True,
        )

    def run_cross(row, flag, small_grad, memory, sent, sent_other, own, earlier):
        x1, qc, slope = own
        last_row = row == row_count - 1
        products = [(tw, bf16)] * 7 + [((width, 4 * width), bf16)] if last_row else []
        return run_kernel(
            functools.partial(cross_body, heads, row),
            (flag, segments, vec, fbias, small_grad, memory, sent, sent_other, second_w, x1, qc, cot,
             ffn_w, slope, earlier if last_row else ()),
            [SMEM] + [VMEM] * 4 + [ANY] * 10,
            [shape_of(small, f32), shape_of(row_tw, bf16), shape_of(row_th, bf16),
             shape_of(row_th, bf16), shape_of(row_tw, f32), shape_of(row_tw, f32)]
            + [shape_of(row_tw, bf16)] * 6 + [mixed_piece if last_row else []],
            [VMEM] + [ANY] * (11 + (count if last_row else 0)),
            [
                (row_tw, bf16), ((width, width), bf16), ((width, width), bf16),
                ((width, width), bf16), (row_tw, f32), (row_tw, bf16), (row_tw, bf16),
                ((width, hidden), bf16), (row_tw, bf16), (row_tw, bf16), (row_square, bf16),
                (row_tw, bf16), (row_tw, f32), (row_tw, bf16), (row_th, bf16), (row_th, bf16),
                (row_tw, f32), (row_tw, f32), (row_tw, bf16), (row_tw, bf16), (row_tw, bf16),
                (row_tw, bf16), (row_tw, bf16), ((length, length), f32), ((8, width), f32),
                ((8, width), f32), (row_tw, f32), ((2, length, tile), f32),
            ] + products,
            9 + (7 * row_count if last_row else 0), 11 + 2 * share_copies, "cross", True,
        )

    def to_decoder(value):
        return lax.ppermute(value, "section", [(0, 1)])

    def to_encoder(value):
        return lax.ppermute(value, "section", [(1, 0)])

    kept_rows = [run_first(0, flag)]
    for row in range(1, row_count):

        def first_steps(low, flag, row=row):
            memory = to_decoder(low)
            return memory, run_first(row, flag)

        low = kept_rows[-1][9]
        memory, outs = block_of(always, first_steps, low, after(flag, low))
        kept_rows.append(outs)
        memories = (*memories, memory) if row > 1 else (memory,)

    def cross_steps(low, flag, first_memory, sent, own, first_earlier):
        memory = to_decoder(low)
        other = lax.ppermute(sent, "batch", [(i, i ^ 1) for i in range(devices)])
        return memory, other, run_cross(0, flag, fbias, first_memory, sent, other, own, first_earlier)

    def own_of(row):
        outs = kept_rows[row]
        return outs[0], outs[11], outs[7]

    def earlier_of(rows):
        hc = tuple(outs[10] for outs in kept_rows)
        return (
            hc,
            *(tuple(outs[part] for outs in rows) for part in (6, 5, 10)),
            tuple(memories[: len(rows)]),
            *(tuple(outs[part] for outs in rows) for part in (7, 8)),
        )

    low = kept_rows[-1][9]
    memory, sent_other, outs = block_of(
        always, cross_steps, low, after(flag, low), memories[0], sent, own_of(0), earlier_of(())
    )
    memories = (*memories, memory)
    small_grad, *outs = outs
    cross_rows, returned = [outs], ()
    for row in range(1, row_count):

        def return_steps(dm, flag, *operands, row=row):
            back = to_encoder(dm)
            return back, run_cross(row, flag, *operands)

        dm = cross_rows[-1][9]
        back, outs = block_of(
            always, return_steps, dm, after(flag, dm), small_grad, memories[row], sent, sent_other,
            own_of(row), earlier_of(cross_rows),
        )
        small_grad, *outs = outs
        cross_rows.append(outs)
        returned = (*returned, back)
    dm = cross_rows[-1][9]
    returned = (*returned, to_encoder(dm))
    x1, h1, qkv, weights, context, h2, u, slope, e2, low, hc, qc = zip(*kept_rows)
    dec_h2, dec_u, dec_slope, d2, grad, _, dq, _, _, dm, _, cross_gs = zip(*cross_rows)
    cross_g = cross_gs[-1]

    cross, down, ffn, mixed = (
        Ring(devices, name != "cross") for name in ("cross", "down", "ffn", "mixed")
    )

    flag = after(flag, *dm)

    def run_down(flag, vec, small_grad, returned, cot, e2, u, dec_u):
        small_grad, enc_grad, enc_low, *pieces = run_kernel(
            down_body,
            (flag, vec, small_grad, returned, cot, e2, u, dec_u),
            [SMEM] + [VMEM] * 2 + [ANY] * 5,
            [shape_of(small, f32), shape_of(tw, f32), shape_of(tw, bf16)] + down_piece,
            [VMEM] + [ANY] * (2 + count),
            [
                (tw, bf16), (tw, bf16), (tw, f32), (th, bf16), (tw, f32), (tw, bf16),
                ((hidden, width), bf16), ((8, width), f32), ((8, width), f32),
            ],
            1 + 3 * row_count, 2 + max(share_copies, hidden // tile), "down",
        )
        return small_grad, enc_grad, enc_low, pieces

    def run_hidden(flag, enc_low, down_w, slope):
        return run_kernel(
            hidden_body,
            (flag, enc_low, down_w, slope),
            [SMEM] + [ANY] * 3,
            [shape_of(th, bf16)],
            [ANY],
            [(tw, bf16), ((hidden, width), bf16), (th, bf16)],
            1 + row_count + hidden // tile, hidden // tile, "hidden",
        )[0]

    def run_ffn(flag, small_grad, enc_slope):
        small_grad, *pieces = run_kernel(
            ffn_body,
            (flag, small_grad, (h2, enc_slope), (dec_h2, dec_slope)),
            [SMEM, VMEM, ANY, ANY],
            [shape_of(small, f32)] + ffn_piece,
            [VMEM] + [ANY] * count,
            [(th, bf16), (tw, bf16), ((width, hidden), bf16)],
            2 * row_count, hidden // (2 * tile) * share_copies, "ffn",
        )
        return small_grad, pieces

    def run_hidden_back(flag, vec, small_grad, slope, ffn_w, dq, first_w, x1, enc_grad, grad):
        return run_kernel(
            hidden_back_body,
            (flag, vec, small_grad, slope, ffn_w, dq, first_w, x1, enc_grad, grad),
            [SMEM] + [VMEM] * 2 + [ANY] * 7,
            [shape_of(small, f32), shape_of(tw, f32)],
            [VMEM, ANY],
            [
                (th, bf16), ((width, hidden), bf16), (tw, bf16), ((width, width), bf16), (tw, f32),
                (tw, f32), (tw, f32), ((8, width), f32), ((8, width), f32),
            ],
            3 + 3 * row_count, 1, "hidden_back",
        )

    def run_attention_back(flag, grad, qkv, weights, context, out_w, h1):
        grad_qkv, grad_scores, *pieces = run_kernel(
            functools.partial(attention_back_body, heads),
            (flag, grad, qkv, weights, context, out_w, h1),
            [SMEM] + [ANY] * 6,
            [shape_of(wide, bf16), shape_of((heads, length, length), f32)] + mixed_piece,
            [ANY] * (2 + count),
            [
                (tw, f32), (wide, bf16), (square, bf16), (tw, f32), ((width, width), bf16),
                (tw, bf16), (tw, bf16), (tw, bf16), (wide, bf16), ((width, 4 * width), bf16),
                ((heads, length, length), f32), (tw, bf16),
            ],
            2 + 4 * row_count, 2 + 2 * share_copies, "attention_back",
        )
        return grad_qkv, grad_scores, pieces

    def run_last(flag, vec, small_grad, grad, grad_qkv, qkv_w, rows, grad_scores):
        return run_kernel(
            last_body,
            (flag, offsets, vec, small_grad, grad, grad_qkv, qkv_w, rows, grad_scores),
            [SMEM] + [VMEM] * 3 + [ANY] * 5,
            [shape_of(small, f32), shape_of(tw, f32)],
            [VMEM, ANY],
            [
                (tw, f32), (wide, bf16), ((width, 3 * width), bf16), (tw, bf16), (tw, f32),
                ((heads, length, length), f32), ((heads, 2 * length), f32),
                ((bucket_count, 2 * length), f32), ((8, width), f32), ((8, width), f32),
            ],
            5, 1, "last",
        )

    def run_output(flag, vec, dec_u, d2, down_w, low):
        return run_kernel(
            output_body,
            (flag, vec, dec_u, d2, down_w, low),
            [SMEM, VMEM] + [ANY] * 4,
            [shape_of(tw, bf16)],
            [ANY],
            [(th, bf16), (tw, f32), ((hidden, width), bf16), (tw, bf16)],
            1 + 3 * row_count, 1, "output",
        )[0]

    def beside(ring, pieces, kernel, *operands):
        def steps(kept, given, flag, *operands):
            got = ring.to_core(given)
            outs = kernel(flag, *operands)
            out = pair_sum(after(flag, *jax.tree.leaves(outs)), kept, got, ring.everywhere)
            return outs, got, out

        return block_of(always, steps, *pieces, *operands)

    if not by_chip:
        small_grad, enc_grad, enc_low, down_g = run_down(
            flag, vec, small_grad, returned, cot, e2, u, dec_u
        )
        enc_slope = run_hidden(flag, enc_low, down_w, slope)
        small_grad, ffn_g = run_ffn(flag, small_grad, enc_slope)
        small_grad, grad = run_hidden_back(
            flag, vec, small_grad, enc_slope, ffn_w, dq, first_w, x1, enc_grad, grad
        )
        grad_qkv, grad_scores, mixed_g = run_attention_back(
            flag, grad, qkv, weights, context, out_w, h1
        )
        small_grad, result = run_last(
            flag, vec, small_grad, grad, grad_qkv, qkv_w, rows, grad_scores
        )
        low = run_output(flag, vec, dec_u, d2, down_w, low)
        small_grad = lax.psum(small_grad, "batch")
        cross_share, down_share, ffn_share, mixed_share = (
            lax.psum_scatter(pieces[0], "batch", scatter_dimension=0, tiled=True).astype(f32)
            for pieces in (cross_g, down_g, ffn_g, mixed_g)
        )
        cross_back = lax.ppermute(cross_share[:, 2 * width :], "section", [(1, 0)])
        cross_share = jnp.where(on_encoder, cross_back, cross_share[:, : 2 * width])
        cf_share, cs_share = cross_share[:, :width], cross_share[:, width:]
        out_share, qkv_share = mixed_share[:, :width], mixed_share[:, width:]
        vec_share = lax.dynamic_slice_in_dim(
            small_grad[:7], place * (width // devices), width // devices, 1
        )
        fbias_all = small_grad[8 : 8 + hidden // width].reshape(1, hidden)
        fbias_share = lax.dynamic_slice_in_dim(
            fbias_all, place * (hidden // devices), hidden // devices, 1
        )
        table_total = small_grad[16 : 16 + heads, :bucket_count].T
    else:

        def cross_steps(flag, kept, given):
            got = cross.to_core(given)
            return got, pair_sum(flag, kept, got, False)

        got, out = block_of(always, cross_steps, flag, *cross_g)
        flag = after(flag, out)

        def down_steps(out, kept, got, flag, down_w, slope, ffn_ins, *operands):
            far = cross.to_chip(out)
            small_grad, enc_grad, enc_low, pieces = run_down(flag, *operands)
            flag = after(flag, small_grad)
            enc_slope, down_got, out = beside(
                down, pieces, run_hidden, flag, enc_low, down_w, slope
            )
            down_held = (pieces[0], down_got, down.to_chip(out))
            flag = after(flag, out)
            small_grad, pieces = run_ffn(flag, small_grad, enc_slope)
            flag = after(flag, small_grad)
            *outs, cross_own = cross.sums(flag, kept, got, far)
            flag = after(flag, *outs)
            cross_last = (*cross.along(outs), cross_own)
            sums = beside(
                ffn, pieces, run_hidden_back, flag, vec, small_grad, enc_slope, *ffn_ins[:4],
                enc_grad, ffn_ins[4],
            )
            outs = down.sums(after(flag, sums[2]), *down_held)
            return outs, cross_last, pieces[0], sums

        down_outs, cross_last, kept, sums = block_of(
            always, down_steps, out, cross_g[0], got, flag, down_w, slope,
            (ffn_w, dq, first_w, x1, grad), vec, small_grad, returned, cot, e2, u, dec_u,
        )
        (small_grad, grad), got, ffn_out = sums
        ffn_held = (kept, got)
        flag = after(flag, ffn_out, *down_outs)

        def attention_steps(flag, ffn_out, outs, *operands):
            far = ffn.to_chip(ffn_out)
            moved = down.along(outs)
            grad_qkv, grad_scores, pieces = run_attention_back(flag, *operands)

            def swap(flag, kept, given):
                got = mixed.to_core(given)
                return got, pair_sum(flag, kept, got, True)

            swapped = block_of(always, swap, after(flag, grad_qkv), *pieces)
            return moved, far, grad_qkv, grad_scores, pieces[0], swapped

        moved, ffn_far, grad_qkv, grad_scores, kept, swapped = block_of(
            always, attention_steps, flag, ffn_out, down_outs[:3], grad, qkv, weights, context, out_w,
            h1,
        )
        down_last = (*moved, down_outs[3])
        got, out = swapped
        flag = after(flag, out)

        def swapped_small(small_grad, away):
            pairs = [(i, i ^ away) for i in range(devices)]
            return small_grad + lax.ppermute(small_grad, "batch", pairs)

        def last_steps(flag, out, held, mixed_held, *operands):
            far = mixed.to_chip(out)
            *outs, own = ffn.sums(flag, *held)
            moved = (*ffn.along(outs), own)
            small_grad, result = run_last(after(flag, *outs), *operands)

            small_grad = block_of(always, lambda s: swapped_small(s, 1), small_grad)
            outs = mixed.sums(after(flag, small_grad), *mixed_held, far)
            return outs, moved, small_grad, result

        (*outs, own), ffn_last, small_grad, result = block_of(
            always, last_steps, flag, out, (*ffn_held, ffn_far), (kept, got), vec, small_grad,
            grad, grad_qkv, qkv_w, rows, grad_scores,
        )

        moved = mixed.along(outs)

        def end_steps(small_grad, cross_last, down_last, ffn_last, flag, *operands):
            back, cross_share, down_share, ffn_share = [
                sum(part[:, at].astype(f32) for part in parts)
                for parts, at in (
                    (cross_last, slice(2 * width, 4 * width)),
                    (cross_last, slice(0, 2 * width)),
                    (down_last, slice(None)),
                    (ffn_last, slice(None)),
                )
            ]
            back = lax.ppermute(back, "section", [(1, 0)])
            small_grad = swapped_small(small_grad, 2)
            low = run_output(after(flag, small_grad), *operands)
            small_grad = swapped_small(small_grad, 4)
            return small_grad, low, back, cross_share, down_share, ffn_share

        small_grad, low, back, cross_share, down_share, ffn_share = block_of(
            always, end_steps, after(small_grad, *outs), cross_last, down_last, ffn_last, flag, vec,
            dec_u, d2, down_w, low,
        )
        small_other = lax.ppermute(small_grad, "batch", [(i, i ^ 8) for i in range(devices)])
        one = (width // devices, width)
        qkv_share, out_share, cf_share, cs_share = pl.pallas_call(
            finish_body,
            in_specs=[SMEM] + [VMEM] * 6,
            out_specs=[VMEM] * 4,
            out_shape=[shape_of((width // devices, 3 * width), f32)] + [shape_of(one, f32)] * 3,
            name="finish",
        )(flag, *moved, own, cross_share, back)
        small_other = after(small_other, qkv_share)
        vec_share, fbias_share, table_total = pl.pallas_call(
            small_body,
            in_specs=[SMEM] + [VMEM] * 2,
            out_specs=[VMEM] * 3,
            out_shape=[
                shape_of((7, 1, width // devices), f32), shape_of((1, hidden // devices), f32),
                shape_of((heads, 1, bucket_count), f32),
            ],
            name="small",
        )(place[None], small_grad, small_other)
        vec_share = jnp.transpose(vec_share, (1, 0, 2))[0]
        table_total = jnp.transpose(table_total, (1, 2, 0))[0]
    return (
        low.reshape((1, row_count, length, width)),
        result.reshape((1, row_count, length, width)),
        qkv_share[None],
        out_share[None],
        ffn_share[None],
        down_share[None],
        cf_share[None],
        cs_share[None],
        vec_share[None],
        fbias_share,
        table_total[None],
    )


def solution(mesh):
    return jax.shard_map(
        per_device,
        mesh=mesh,
        in_specs=(
            P("section", "batch", None, None),
            P("section", "batch", None, None),
            P(None, "batch", None),
            P(),
            P("section", None, None),
            P("section", None, None),
            P("section", None, None),
            P("section", None, None),
            P("section", None, None),
            P("section", None, None),
            P("section", None, None),
            P("section", None),
            P("section", None, None),
        ),
        out_specs=(
            P("section", "batch", None, None),
            P("section", "batch", None, None),
            P("section", "batch", None),
            P("section", "batch", None),
            P("section", "batch", None),
            P("section", "batch", None),
            P("section", "batch", None),
            P("section", "batch", None),
            P("section", None, "batch"),
            P("section", "batch"),
            P("section", None, None),
        ),
        check_vma=False,
    )
```
